32 devices in a mesh: heads: 4 (over y, x), blk: 8 (over z, core).
Axes of the slice: x: 2, y: 2, z: 4, core: 2. Of those that a mesh axis runs over, the one named last changes fastest.
Arguments:
- inputs: bfloat16 [16384, 2048], P(('blk', 'heads')), may hold values from -6 to 6
- positions: int32 [16384], P('blk'), may hold values from 0 to 1999, as said below
- attn_gain: bfloat16 [2048], P(('heads', 'blk')), may hold values from 0.25 to 1.75
- qkv_weight: bfloat16 [2048, 1536], P(('heads', 'blk')), may hold values from -0.125 to 0.125
- q_gain: bfloat16 [64], replicated, may hold values from 0.796875 to 1.796875
- k_gain: bfloat16 [64], replicated, may hold values from 0.796875 to 1.796875
- out_weight: bfloat16 [1024, 2048], P(('heads', 'blk')), may hold values from -1.5 to 1.5
- ffn_gain: bfloat16 [2048], P(('heads', 'blk')), may hold values from 0.25 to 1.75
- ffn_in_weight: bfloat16 [2048, 10240], P(('heads', 'blk')), may hold values from -0.125 to 0.125
- ffn_out_weight: bfloat16 [5120, 2048], P(('heads', 'blk')), may hold values from -0.078125 to 0.078125
- cotangent: bfloat16 [16384, 2048], P(('blk', 'heads')), may hold values from -6 to 6
Outputs:
- layer_out: bfloat16 [16384, 2048], P(('blk', 'heads'))
- input_grad: float32 [16384, 2048], P(('blk', 'heads'))
- attn_gain_grad: float32 [2048], P(('heads', 'blk'))
- qkv_grad: float32 [2048, 1536], P(('heads', 'blk'))
- q_gain_grad: float32 [64], replicated
- k_gain_grad: float32 [64], replicated
- out_grad: float32 [1024, 2048], P(('heads', 'blk'))
- ffn_gain_grad: float32 [2048], P(('heads', 'blk'))
- ffn_in_grad: float32 [2048, 10240], P(('heads', 'blk'))
- ffn_out_grad: float32 [5120, 2048], P(('heads', 'blk'))
The draws below stay inside these ranges and needn't reach their ends.
Inputs may be any that keep to these rules, and one draw needn't show every extreme that they name: `positions`: positions count up by one along a document and start at 0 where a new one begins; a document begins at every multiple of 8192 tokens; no document has more than 2000 tokens and the first of the stream has exactly 2000; a document that a sequence's end does not cut has at least 200 tokens.
All inputs are finite; a program needn't handle non-finite values.
Results may differ from the reference program's by a relative error of at most 0.015.
Values may be sent and summed in bfloat16 or wider, within the bound.
A program may use at most 320 MiB of HBM per device.

```python
import jax
import jax.numpy as jnp
from jax import lax

D = 2048
HEADS = 16
KV_HEADS = 4
HEAD_DIM = 64
FF = 5120
SEQ = 8192
DOC_MAX = 2000
DOC_MIN = 200
TOKENS = 16384


def draw_positions(key, part):
    tosses = jax.random.randint(key, (TOKENS,), 0, 1 << 20)
    token_index = jnp.arange(TOKENS, dtype=jnp.int32)
    chance = (1 << 20) // max(DOC_MAX // 2, 1)

    def advance(current, element):
        toss, position_index = element
        begins = (position_index % SEQ == 0) | (current >= DOC_MAX - 1)
        begins = begins | (current >= DOC_MIN - 1) & (toss < chance) & (position_index >= DOC_MAX)
        renewed = jnp.where(begins, 0, current + 1).astype(jnp.int32)
        return (renewed, renewed)
    _, positions = lax.scan(advance, jnp.int32(-1), (tosses, token_index))
    return positions.astype(jnp.int32)


def shard_levels(own_key, shape, split, smallest, top_value):
    def one(dim, parts):
        steps = jax.random.uniform(jax.random.fold_in(jax.random.fold_in(own_key, 6), dim), (parts,), jnp.float32, smallest / len(split), top_value / len(split))
        return jnp.repeat(jnp.exp(steps), shape[dim] // parts).reshape((-1,) + (1,) * (len(shape) - dim - 1))

    gain = one(*split[0])
    for cut in split[1:]:
        gain = gain * one(*cut)
    return gain


def gaussian(key, extent, width, reach, split=(), held_as=jnp.bfloat16):
    level = shard_levels(key, extent, split, -0.22, 0.18) if split else 1.0
    drawn = jax.random.normal(key, extent, jnp.float32) * width * level
    return jnp.minimum(jnp.maximum(drawn, -reach), reach).astype(held_as)


def setup_inputs(seed: int = 0) -> dict:
    arg_keys = jax.random.split(jax.random.key(seed), 12)
    inputs = gaussian(arg_keys[0], (TOKENS, D), 1.0, 6.0, ((0, 32),))
    positions = draw_positions(jax.random.fold_in(arg_keys[11], 71), 0)
    attn_gain = jnp.clip(1.0 + 0.15 * jax.random.normal(arg_keys[2], (D,), jnp.float32), 0.25, 1.75).astype(jnp.bfloat16)
    qkv_weight = gaussian(arg_keys[3], (D, (HEADS + 2 * KV_HEADS) * HEAD_DIM), D ** -0.5, 0.125, ((0, 32),))
    q_gain = jnp.clip(jax.random.uniform(arg_keys[4], (HEAD_DIM,), jnp.float32, 0.796875, 1.796875), 0.796875, 1.796875).astype(jnp.bfloat16)
    k_gain = jnp.clip(jax.random.uniform(arg_keys[5], (HEAD_DIM,), jnp.float32, 0.796875, 1.796875), 0.796875, 1.796875).astype(jnp.bfloat16)
    out_weight = gaussian(arg_keys[6], (HEADS * HEAD_DIM, D), (HEADS * HEAD_DIM // 64) ** -0.5, 1.5, ((0, 32),))
    ffn_gain = jnp.clip(1.0 + 0.15 * jax.random.normal(arg_keys[7], (D,), jnp.float32), 0.25, 1.75).astype(jnp.bfloat16)
    ffn_in_weight = gaussian(arg_keys[8], (D, 2 * FF), D ** -0.5, 0.125, ((0, 32),))
    ffn_out_weight = gaussian(arg_keys[9], (FF, D), FF ** -0.5, 0.078125, ((0, 32),))
    cotangent = gaussian(arg_keys[10], (TOKENS, D), 1.0, 6.0, ((0, 32),))
    return dict(inputs=inputs, positions=positions, attn_gain=attn_gain, qkv_weight=qkv_weight, q_gain=q_gain, k_gain=k_gain, out_weight=out_weight, ffn_gain=ffn_gain, ffn_in_weight=ffn_in_weight, ffn_out_weight=ffn_out_weight, cotangent=cotangent)


EPS = 1e-06
ROPE_BASE = 10000.0
NEG = -1e+30

@jax.custom_vjp
def low(v):
    return lax.optimization_barrier(v.astype(jnp.bfloat16)).astype(jnp.float32)

@jax.custom_vjp
def low_back(v):
    return v

def low_keep(v):
    return (low(v), None)

def low_pass(kept, grad):
    return (grad,)

def back_keep(v):
    return (v, None)

def back_low(kept, grad):
    return (low(grad),)
low.defvjp(low_keep, low_pass)
low_back.defvjp(back_keep, back_low)

def matmul_high(left, right):
    return jnp.dot(left, right, precision=lax.Precision.HIGHEST, preferred_element_type=jnp.float32)

def rms_scale(values, scaling):
    return values * lax.rsqrt(lax.optimization_barrier(jnp.mean(values * values, axis=-1, keepdims=True)) + EPS) * scaling

def rotation(positions):
    half_width = HEAD_DIM // 2
    frequency = ROPE_BASE ** (-2.0 * jnp.arange(half_width, dtype=jnp.float32) / HEAD_DIM)
    angles = positions.astype(jnp.float32)[:, None] * frequency[None, :]
    return (jnp.cos(angles)[:, None, :], jnp.sin(angles)[:, None, :])

def rotate(values, cosine, sine):
    half_width = values.shape[-1] // 2
    front_half = values[..., :half_width]
    second = values[..., half_width:]
    return jnp.concatenate([front_half * cosine - second * sine, second * cosine + front_half * sine], axis=-1)

def sequence_attention(query_seq, key_seq, value_seq, position_seq):
    group_size = HEADS // KV_HEADS
    query_rows = min(512, SEQ)
    score_scale = HEAD_DIM ** (-0.5)
    key_rows = jnp.repeat(key_seq, group_size, axis=1)
    value_rows = jnp.repeat(value_seq, group_size, axis=1)
    key_index = jnp.arange(SEQ, dtype=jnp.int32)

    def block(row_start):
        query_part = lax.dynamic_slice_in_dim(query_seq, row_start, query_rows, 0)
        position_part = lax.dynamic_slice_in_dim(position_seq, row_start, query_rows, 0)
        query_index = row_start + jnp.arange(query_rows, dtype=jnp.int32)
        allowed = (key_index[None, :] <= query_index[:, None]) & (key_index[None, :] >= (query_index - position_part)[:, None])
        scores = jnp.einsum('qhd,khd->hqk', query_part, key_rows, precision=lax.Precision.HIGHEST) * score_scale
        scores = low_back(scores)
        scores = jnp.where(allowed[None], scores, NEG)
        top = lax.optimization_barrier(jnp.max(scores, axis=-1, keepdims=True))
        expo = jnp.exp(scores - top)
        probs = low(expo / lax.optimization_barrier(jnp.sum(expo, axis=-1, keepdims=True)))
        return jnp.einsum('hqk,khd->qhd', probs, value_rows, precision=lax.Precision.HIGHEST)
    starts = jnp.arange(SEQ // query_rows, dtype=jnp.int32) * query_rows
    mixed = lax.map(jax.checkpoint(block), starts)
    return mixed.reshape(SEQ, HEADS, HEAD_DIM)

def attention(queries, key_rows, value_rows, positions):
    count = queries.shape[0] // SEQ

    def per_sequence(carried, element):
        return (carried, sequence_attention(element[0], element[1], element[2], element[3]))
    _, mixed = lax.scan(jax.checkpoint(per_sequence), jnp.zeros((), jnp.float32), (queries.reshape(count, SEQ, HEADS, HEAD_DIM), key_rows.reshape(count, SEQ, KV_HEADS, HEAD_DIM), value_rows.reshape(count, SEQ, KV_HEADS, HEAD_DIM), positions.reshape(count, SEQ)))
    return mixed.reshape(count * SEQ, HEADS, HEAD_DIM)

def layer(hidden_in, attn_gain, qkv_weight, q_gain, k_gain, out_weight, ffn_gain, ffn_in_weight, ffn_out_weight, positions):
    token_count = hidden_in.shape[0]
    query_width = HEADS * HEAD_DIM
    key_width = KV_HEADS * HEAD_DIM
    normed = low(rms_scale(hidden_in, attn_gain))
    projected = low_back(matmul_high(normed, qkv_weight))
    query_raw = projected[:, :query_width].reshape(token_count, HEADS, HEAD_DIM)
    key_raw = projected[:, query_width:query_width + key_width].reshape(token_count, KV_HEADS, HEAD_DIM)
    value_raw = projected[:, query_width + key_width:].reshape(token_count, KV_HEADS, HEAD_DIM)
    cosine, sine = rotation(positions)
    queries = low(low_back(rotate(rms_scale(query_raw, q_gain), cosine, sine)))
    key_rows = low(low_back(rotate(rms_scale(key_raw, k_gain), cosine, sine)))
    value_rows = low(low_back(value_raw))
    attended = attention(queries, key_rows, value_rows, positions)
    attended = low(low_back(attended.reshape(token_count, query_width)))
    residual = hidden_in + low_back(matmul_high(attended, out_weight))
    ffn_normed = low(rms_scale(residual, ffn_gain))
    gate_up = low_back(matmul_high(ffn_normed, ffn_in_weight))
    hidden = low(jax.nn.silu(gate_up[:, :FF]) * gate_up[:, FF:])
    return residual + low_back(matmul_high(hidden, ffn_out_weight))

def reference(inputs, positions, attn_gain, qkv_weight, q_gain, k_gain, out_weight, ffn_gain, ffn_in_weight, ffn_out_weight, cotangent):

    def forward(hidden_in, gain_one, weight_one, gain_two, gain_three, weight_two, gain_four, weight_three, weight_four):
        return layer(hidden_in, gain_one, weight_one, gain_two, gain_three, weight_two, gain_four, weight_three, weight_four, positions)
    output, pullback = jax.vjp(forward, inputs.astype(jnp.float32), attn_gain.astype(jnp.float32), qkv_weight.astype(jnp.float32), q_gain.astype(jnp.float32), k_gain.astype(jnp.float32), out_weight.astype(jnp.float32), ffn_gain.astype(jnp.float32), ffn_in_weight.astype(jnp.float32), ffn_out_weight.astype(jnp.float32))
    grads = pullback(cotangent.astype(jnp.float32))
    return (output.astype(jnp.bfloat16), grads[0], grads[1], grads[2], grads[3], grads[4], grads[5], grads[6], grads[7], grads[8])
```

```python
import jax
import jax.numpy as jnp
from jax import lax
from jax.sharding import PartitionSpec as P

HEADS = 16
KV_HEADS = 4
DOC_MAX = 2000


EPS = 1e-06
ROPE_BASE = 10000.0
NEG = -1e30


def from_behind(block, axis, distance):
    devices = range(lax.axis_size(axis))
    route = [(i - distance, i) for i in devices if i - distance in devices]
    return lax.ppermute(block, axis, route)


def rms_scale(values, scaling):
    return values * lax.rsqrt(jnp.mean(values * values, axis=-1, keepdims=True) + EPS) * scaling


def norm_back(values, scaling, gradient):
    inverse = lax.rsqrt(jnp.mean(values * values, axis=-1, keepdims=True) + EPS)
    scaled = gradient * scaling
    moment = jnp.mean(scaled * values, axis=-1, keepdims=True)
    return (
        inverse * scaled - values * inverse * inverse * inverse * moment,
        gradient * values * inverse,
    )


def rotation(positions, head_dim):
    half_width = head_dim // 2
    frequency = ROPE_BASE ** (-2.0 * jnp.arange(half_width, dtype=jnp.float32) / head_dim)
    angles = positions.astype(jnp.float32)[:, None] * frequency[None, :]
    return (jnp.cos(angles)[:, None, :], jnp.sin(angles)[:, None, :])


def rotate(values, cosine, sine):
    half_width = values.shape[-1] // 2
    front_half = values[..., :half_width]
    second = values[..., half_width:]
    return jnp.concatenate(
        [front_half * cosine - second * sine, second * cosine + front_half * sine], axis=-1
    )


def peers_exchange(pieces, axis):
    size = lax.axis_size(axis)
    return [pieces[0]] + [
        lax.ppermute(pieces[k], axis, [(i, i ^ k) for i in range(size)]) for k in range(1, size)
    ]


def place(parts, axis, dim):
    own = lax.axis_index(axis)
    extent = parts[0].shape[dim]
    shape = list(parts[0].shape)
    shape[dim] = extent * len(parts)
    whole = jnp.zeros(shape, parts[0].dtype)
    for k, part in enumerate(parts):
        whole = lax.dynamic_update_slice_in_dim(whole, part, (own ^ k) * extent, dim)
    return whole


def gather_peers(block, axis, dim):
    return place(peers_exchange([block] * lax.axis_size(axis), axis), axis, dim)


def slices_for(block, axis, dim):
    own = lax.axis_index(axis)
    size = lax.axis_size(axis)
    extent = block.shape[dim] // size
    return [
        lax.dynamic_slice_in_dim(block, (own ^ k) * extent, extent, dim) for k in range(size)
    ]


def local(
    inputs,
    positions,
    attn_gain,
    qkv_weight,
    q_gain,
    k_gain,
    out_weight,
    ffn_gain,
    ffn_in_weight,
    ffn_out_weight,
    cotangent,
):
    token_count, width = inputs.shape
    depth = qkv_weight.shape[0]
    head_dim = q_gain.shape[0]
    group_size = HEADS // KV_HEADS
    score_scale = head_dim ** (-0.5)
    heads_size = lax.axis_size("heads")
    blk_size = lax.axis_size("blk")
    query_width = HEADS * head_dim // heads_size
    key_width = KV_HEADS * head_dim // heads_size
    own_head = lax.axis_index("heads")
    block_len = token_count * heads_size
    hidden_units = ffn_out_weight.shape[0] * blk_size

    qkv_parts = jnp.concatenate(
        [
            qkv_weight[:, : HEADS * head_dim].reshape(depth, heads_size, query_width),
            qkv_weight[:, HEADS * head_dim : (HEADS + KV_HEADS) * head_dim].reshape(
                depth, heads_size, key_width
            ),
            qkv_weight[:, (HEADS + KV_HEADS) * head_dim :].reshape(depth, heads_size, key_width),
            jnp.broadcast_to(attn_gain[:, None, None], (depth, heads_size, 64)),
            jnp.broadcast_to(ffn_gain[:, None, None], (depth, heads_size, 64)),
        ],
        axis=-1,
    )
    joined_width = qkv_parts.shape[-1]
    qkv_parts = qkv_parts.transpose(1, 0, 2)

    def to_group(parts):
        sent = slices_for(parts, "heads", 0)
        return place(peers_exchange(sent, "heads"), "heads", 0)

    qkv_group = lax.all_gather(to_group(qkv_parts), "blk", axis=1, tiled=True).reshape(
        width, joined_width
    )
    qkv_width = query_width + 2 * key_width
    attn_scaling = qkv_group[:, qkv_width].astype(jnp.float32)
    ffn_scaling = qkv_group[:, qkv_width + 64].astype(jnp.float32)
    qkv_group = qkv_group[:, :qkv_width]
    in_parts = ffn_in_weight.reshape(depth, 2, heads_size, hidden_units).transpose(2, 0, 1, 3)
    in_group = lax.all_gather(
        to_group(in_parts.reshape(heads_size, depth, 2 * hidden_units)), "blk", axis=1, tiled=True
    ).reshape(width, 2 * hidden_units)
    out_group = lax.all_gather(out_weight, "blk", axis=0, tiled=True)
    down_group = lax.all_gather(ffn_out_weight, "blk", axis=0, tiled=True)

    inputs_blk = gather_peers(inputs, "heads", 0)
    hidden_in = inputs_blk.astype(jnp.float32)
    cosine, sine = rotation(positions, head_dim)
    normed = rms_scale(hidden_in, attn_scaling).astype(jnp.bfloat16)
    projected = jnp.dot(normed, qkv_group, preferred_element_type=jnp.float32)
    query_raw = projected[:, :query_width].reshape(block_len, -1, head_dim)
    key_raw = projected[:, query_width : query_width + key_width].reshape(block_len, -1, head_dim)
    value_raw = projected[:, query_width + key_width :].reshape(block_len, -1, head_dim)
    query_scaling = q_gain.astype(jnp.float32)
    key_scaling = k_gain.astype(jnp.float32)
    query_low = rotate(rms_scale(query_raw, query_scaling), cosine, sine).astype(jnp.bfloat16)
    key_low = rotate(rms_scale(key_raw, key_scaling), cosine, sine).astype(jnp.bfloat16)
    pair_blk = jnp.concatenate([key_low, value_raw.astype(jnp.bfloat16)], axis=-1)
    local_groups = pair_blk.shape[1]
    prior_pair = from_behind(pair_blk, "blk", 1)
    pair_all = jnp.concatenate([prior_pair, pair_blk], axis=0)
    query_rows = min(512, block_len)
    window = min(block_len, -(-DOC_MAX // 128) * 128)
    key_span = window + query_rows
    queries = query_low.reshape(block_len, local_groups, group_size, head_dim)
    starts = jnp.arange(block_len // query_rows, dtype=jnp.int32) * query_rows

    def scores_at(row_start):
        query_part = lax.dynamic_slice_in_dim(queries, row_start, query_rows, 0)
        window_start = row_start + block_len - window
        pair_part = lax.dynamic_slice_in_dim(pair_all, window_start, key_span, 0)
        key_part = pair_part[..., :head_dim]
        value_part = pair_part[..., head_dim:]
        position_part = lax.dynamic_slice_in_dim(positions, row_start, query_rows, 0)
        query_index = row_start + block_len + jnp.arange(query_rows, dtype=jnp.int32)
        key_index = window_start + jnp.arange(key_span, dtype=jnp.int32)
        allowed = (key_index[None, :] <= query_index[:, None]) & (
            key_index[None, :] >= (query_index - position_part)[:, None]
        )
        scores = (
            jnp.einsum("qcgd,kcd->cgqk", query_part, key_part, preferred_element_type=jnp.float32)
            * score_scale
        )
        return (query_part, key_part, value_part, window_start, jnp.where(allowed, scores, NEG))

    def attend(row_start):
        query_part, key_part, value_part, window_start, scores = scores_at(row_start)
        top = jnp.max(scores, axis=-1, keepdims=True)
        expo = jnp.exp(scores - top)
        total = jnp.sum(expo, axis=-1, keepdims=True)
        probs = (expo / total).astype(jnp.bfloat16)
        mixed = jnp.einsum("cgqk,kcd->qcgd", probs, value_part, preferred_element_type=jnp.float32)
        return (mixed.astype(jnp.bfloat16), top + jnp.log(total))

    attended, log_sums = lax.map(attend, starts)
    attended_blk = attended.reshape(block_len, query_width)
    attended_all = gather_peers(attended_blk, "heads", 1)
    out_full = gather_peers(out_group, "heads", 0)
    residual = hidden_in + jnp.dot(attended_all, out_full, preferred_element_type=jnp.float32)
    ffn_normed = rms_scale(residual, ffn_scaling).astype(jnp.bfloat16)
    residual_own = lax.dynamic_slice_in_dim(residual, own_head * token_count, token_count, 0)
    attended_own = lax.dynamic_slice_in_dim(attended_all, own_head * token_count, token_count, 0)
    cotangent_blk = gather_peers(cotangent, "heads", 0)

    gate_up = jnp.dot(ffn_normed, in_group, preferred_element_type=jnp.float32)
    gate = gate_up[:, :hidden_units]
    upward = gate_up[:, hidden_units:]
    sigmoid = jax.nn.sigmoid(gate)
    activated = gate * sigmoid
    hidden = (activated * upward).astype(jnp.bfloat16)
    hidden_grad = jnp.dot(cotangent_blk, down_group.T, preferred_element_type=jnp.float32)
    gate_up_grad = jnp.concatenate(
        [
            hidden_grad * upward * sigmoid * (1.0 + gate * (1.0 - sigmoid)),
            hidden_grad * activated,
        ],
        axis=-1,
    ).astype(jnp.bfloat16)

    def sum_peers(block):
        got = peers_exchange(slices_for(block, "heads", 0), "heads")
        return sum(part.astype(jnp.float32) for part in got)

    normed_grad_part = jnp.dot(gate_up_grad, in_group.T, preferred_element_type=jnp.float32)
    ffn_normed_grad = sum_peers(normed_grad_part.astype(jnp.bfloat16))
    output_part = jnp.dot(hidden, down_group, preferred_element_type=jnp.float32)
    layer_out = (residual_own + sum_peers(output_part.astype(jnp.bfloat16))).astype(jnp.bfloat16)
    down_grad = jnp.dot(hidden.T, cotangent_blk, preferred_element_type=jnp.float32)
    ffn_out_grad = lax.psum_scatter(
        down_grad.astype(jnp.bfloat16), "blk", scatter_dimension=0, tiled=True
    ).astype(jnp.float32)
    up_grad = jnp.dot(ffn_normed.T, gate_up_grad, preferred_element_type=jnp.float32)
    up_grad = lax.psum_scatter(
        up_grad.astype(jnp.bfloat16).reshape(heads_size, blk_size * depth, 2 * hidden_units),
        "blk",
        scatter_dimension=1,
        tiled=True,
    )
    ffn_in_grad = place(
        [
            part.reshape(depth, 2, 1, hidden_units)
            for part in peers_exchange(
                [piece[0] for piece in slices_for(up_grad, "heads", 0)], "heads"
            )
        ],
        "heads",
        2,
    ).reshape(depth, 2 * heads_size * hidden_units).astype(jnp.float32)

    residual_norm_grad, ffn_gain_terms = norm_back(residual_own, ffn_scaling, ffn_normed_grad)
    residual_grad = cotangent.astype(jnp.float32) + residual_norm_grad
    branch_grad = residual_grad.astype(jnp.bfloat16)
    out_proj_grad = jnp.dot(attended_own.T, branch_grad, preferred_element_type=jnp.float32)
    out_grad = lax.psum_scatter(
        sum_peers(out_proj_grad.astype(jnp.bfloat16)).astype(jnp.bfloat16),
        "blk",
        scatter_dimension=0,
        tiled=True,
    ).astype(jnp.float32)
    attended_grad = jnp.dot(branch_grad, out_full.T, preferred_element_type=jnp.float32).astype(
        jnp.bfloat16
    )
    attended_grad_blk = place(
        peers_exchange(slices_for(attended_grad, "heads", 1), "heads"), "heads", 0
    ).reshape(block_len, local_groups, group_size, head_dim)

    def attend_back(pair_sum, element):
        row_start, log_sum = element
        query_part, key_part, value_part, window_start, scores = scores_at(row_start)
        probs = jnp.exp(scores - log_sum)
        grad_part = lax.dynamic_slice_in_dim(attended_grad_blk, row_start, query_rows, 0)
        prob_grad = jnp.einsum(
            "qcgd,kcd->cgqk", grad_part, value_part, preferred_element_type=jnp.float32
        )
        inner = jnp.sum(probs * prob_grad, axis=-1, keepdims=True)
        score_grad = (probs * (prob_grad - inner)).astype(jnp.bfloat16)
        query_grad = (
            jnp.einsum("cgqk,kcd->qcgd", score_grad, key_part, preferred_element_type=jnp.float32)
            * score_scale
        )
        key_grad = (
            jnp.einsum("cgqk,qcgd->kcd", score_grad, query_part, preferred_element_type=jnp.float32)
            * score_scale
        )
        value_grad = jnp.einsum(
            "cgqk,qcgd->kcd",
            probs.astype(jnp.bfloat16),
            grad_part,
            preferred_element_type=jnp.float32,
        )
        window_sum = lax.dynamic_slice_in_dim(
            pair_sum, window_start, key_span, 0
        ) + jnp.concatenate([key_grad, value_grad], axis=-1)
        return (lax.dynamic_update_slice_in_dim(pair_sum, window_sum, window_start, 0), query_grad)

    pair_zero = jnp.zeros((2 * block_len, local_groups, 2 * head_dim), jnp.float32)
    pair_sum, query_grads = lax.scan(attend_back, pair_zero, (starts, log_sums))
    returned = from_behind(pair_sum[:block_len], "blk", -1)
    pair_grad_blk = (pair_sum[block_len:] + returned).astype(jnp.bfloat16)
    query_rot_grad = (
        query_grads.reshape(block_len, -1, head_dim).astype(jnp.bfloat16).astype(jnp.float32)
    )
    key_rot_grad = pair_grad_blk[..., :head_dim].astype(jnp.float32)
    value_grad = pair_grad_blk[..., head_dim:]
    query_raw_grad, query_gain_terms = norm_back(
        query_raw, query_scaling, rotate(query_rot_grad, cosine, -sine)
    )
    key_raw_grad, key_gain_terms = norm_back(
        key_raw, key_scaling, rotate(key_rot_grad, cosine, -sine)
    )
    projected_grad = jnp.concatenate(
        [
            query_raw_grad.reshape(block_len, query_width).astype(jnp.bfloat16),
            key_raw_grad.reshape(block_len, key_width).astype(jnp.bfloat16),
            value_grad.reshape(block_len, key_width),
        ],
        axis=-1,
    )
    qkv_grad_part = jnp.dot(normed.T, projected_grad, preferred_element_type=jnp.float32)
    qkv_sum = lax.psum_scatter(
        qkv_grad_part.astype(jnp.bfloat16).reshape(heads_size, blk_size * depth, qkv_width),
        "blk",
        scatter_dimension=1,
        tiled=True,
    )
    qkv_got = place(
        [
            part[:, None, :]
            for part in peers_exchange(
                [piece[0] for piece in slices_for(qkv_sum, "heads", 0)], "heads"
            )
        ],
        "heads",
        1,
    ).astype(jnp.float32)
    qkv_grad = jnp.concatenate(
        [
            qkv_got[:, :, :query_width].reshape(depth, -1),
            qkv_got[:, :, query_width : query_width + key_width].reshape(depth, -1),
            qkv_got[:, :, query_width + key_width :].reshape(depth, -1),
        ],
        axis=-1,
    )
    qkv_all = gather_peers(qkv_group, "heads", 1)
    projected_grad_own = place(
        peers_exchange(slices_for(projected_grad, "heads", 0), "heads"), "heads", 1
    )
    normed_in_grad = jnp.dot(projected_grad_own, qkv_all.T, preferred_element_type=jnp.float32)
    input_norm_grad, attn_gain_terms = norm_back(
        inputs.astype(jnp.float32), attn_scaling, normed_in_grad
    )
    input_grad = residual_grad + input_norm_grad
    gains = lax.psum(
        jnp.concatenate(
            [
                jnp.sum(attn_gain_terms, axis=0),
                jnp.sum(ffn_gain_terms, axis=0),
                jnp.sum(query_gain_terms, axis=(0, 1)),
                jnp.sum(key_gain_terms, axis=(0, 1)),
            ]
        ),
        ("heads", "blk"),
    )
    own_rows = (own_head * blk_size + lax.axis_index("blk")) * depth
    attn_gain_grad = lax.dynamic_slice_in_dim(gains, own_rows, depth, 0)
    ffn_gain_grad = lax.dynamic_slice_in_dim(gains, width + own_rows, depth, 0)
    q_gain_grad = gains[2 * width : 2 * width + head_dim]
    k_gain_grad = gains[2 * width + head_dim :]
    return (
        layer_out,
        input_grad,
        attn_gain_grad,
        qkv_grad,
        q_gain_grad,
        k_gain_grad,
        out_grad,
        ffn_gain_grad,
        ffn_in_grad,
        ffn_out_grad,
    )


def solution(mesh):
    placed = (
        P(("blk", "heads"), None),
        P("blk"),
        P(("heads", "blk")),
        P(("heads", "blk"), None),
        P(),
        P(),
        P(("heads", "blk"), None),
        P(("heads", "blk")),
        P(("heads", "blk"), None),
        P(("heads", "blk"), None),
        P(("blk", "heads"), None),
    )
    return jax.shard_map(
        local,
        mesh=mesh,
        in_specs=placed,
        out_specs=(
            P(("blk", "heads"), None),
            P(("blk", "heads"), None),
            P(("heads", "blk")),
            P(("heads", "blk"), None),
            P(),
            P(),
            P(("heads", "blk"), None),
            P(("heads", "blk")),
            P(("heads", "blk"), None),
            P(("heads", "blk"), None),
        ),
        check_vma=False,
    )
```

```python
import functools

import jax
import jax.numpy as jnp
from jax import lax
from jax.experimental import pallas as pl
from jax.experimental.pallas import tpu as pltpu
from jax.sharding import PartitionSpec as P

HEADS = 16
KV_HEADS = 4


EPS = 1e-06
ROPE_BASE = 10000.0
NEG = -1e30
MESH = pl.DeviceIdType.MESH
ROWS_IN_BOTH = (((1,), (1,)), ((), ()))


def from_behind(block, axis, distance):
    devices = range(lax.axis_size(axis))
    route = [(i - distance, i) for i in devices if i - distance in devices]
    return lax.ppermute(block, axis, route)


def rotation(positions, head_dim):
    half_width = head_dim // 2
    frequency = ROPE_BASE ** (-2.0 * jnp.arange(half_width, dtype=jnp.float32) / head_dim)
    angles = positions.astype(jnp.float32)[:, None] * frequency[None, :]
    return (jnp.cos(angles)[:, None, :], jnp.sin(angles)[:, None, :])


def stack_heads(tile, heads, first):
    turned = tile.T
    dim = turned.shape[0] // heads
    wide = jnp.concatenate([turned[h * dim : (h + 1) * dim] for h in range(heads)], axis=1)
    zero = jnp.zeros_like(wide)
    return jnp.concatenate([wide, zero] if first else [zero, wide], axis=0)


def unstack_heads(wide, heads):
    count = wide.shape[1] // heads
    return jnp.concatenate([wide[:, h * count : (h + 1) * count] for h in range(heads)], axis=0).T


def scores_at(pair, query_ext, low, first_query, key_start, heads):
    scores = jnp.dot(pair, query_ext, preferred_element_type=jnp.float32)
    rows, columns = scores.shape
    shape = (rows, columns // heads)
    key = key_start + lax.broadcasted_iota(jnp.int32, shape, 0)
    query = first_query + lax.broadcasted_iota(jnp.int32, shape, 1)
    bias = jnp.where((key <= query) & (key >= low), 0.0, NEG)
    return scores + jnp.concatenate([bias] * heads, axis=1)


def transpose_into(pair_ref, turned_ref):
    for start in range(0, pair_ref.shape[0], 512):
        turned_ref[:, start : start + 512] = pair_ref[start : start + 512, :].T


def attend_kernel(
    heads, key_rows, scale, first_ref, query_ref, low_ref, pair_ref, out_ref, log_ref, turned_ref,
    mixed_ref, total_ref
):
    step = pl.program_id(0)
    query_rows = query_ref.shape[0]

    @pl.when(step == 0)
    def _():
        transpose_into(pair_ref, turned_ref)

    query_ext = stack_heads(query_ref[...] * jnp.bfloat16(scale), heads, True)
    low = low_ref[...]
    base = pair_ref.shape[0] // 2 + step * query_rows
    mixed_ref[...] = jnp.zeros_like(mixed_ref)
    total_ref[...] = jnp.zeros_like(total_ref)

    def tile(index, carried):
        start = pl.multiple_of(index * key_rows, key_rows)
        expo = jnp.exp(
            scores_at(pair_ref[pl.ds(start, key_rows), :], query_ext, low, base, start, heads)
        )
        total_ref[...] += jnp.sum(expo, axis=0, keepdims=True)
        mixed_ref[...] += jnp.dot(
            turned_ref[:, pl.ds(start, key_rows)],
            expo.astype(jnp.bfloat16),
            preferred_element_type=jnp.float32,
        )
        return carried

    lax.fori_loop(first_ref[step], (base + query_rows - 1) // key_rows + 1, tile, 0)
    total = total_ref[...]
    dim = pair_ref.shape[1] // 2
    out_ref[...] = unstack_heads(mixed_ref[dim:] / total, heads).astype(out_ref.dtype)
    log_ref[...] = jnp.log(total)[None]


def attend_back_kernel(
    heads, key_rows, scale, first_ref, query_ref, low_ref, pair_ref, out_ref, log_ref, *refs
):
    *grad_refs, query_grad_ref, pair_grad_ref, turned_ref, sum_ref = refs
    step = pl.program_id(0)
    peer = first_ref[pl.num_programs(0)] ^ step
    grad = grad_refs[0][...]
    for k in range(1, len(grad_refs)):
        grad = jnp.where(peer == k, grad_refs[k][...], grad)
    query_rows = query_ref.shape[0]
    dim = pair_ref.shape[1] // 2

    @pl.when(step == 0)
    def _():
        pair_grad_ref[...] = jnp.zeros_like(pair_grad_ref)
        transpose_into(pair_ref, turned_ref)

    query_ext = stack_heads(query_ref[...] * jnp.bfloat16(scale), heads, True)
    grad_ext = stack_heads(grad, heads, False)
    out_ext = stack_heads(out_ref[...], heads, False)
    inner = jnp.sum(
        grad_ext.astype(jnp.float32) * out_ext.astype(jnp.float32), axis=0, keepdims=True
    )
    log_sum = log_ref[0]
    low = low_ref[...]
    base = pair_ref.shape[0] // 2 + step * query_rows
    sum_ref[...] = jnp.zeros_like(sum_ref)

    def tile(index, carried):
        start = pl.multiple_of(index * key_rows, key_rows)
        pair = pair_ref[pl.ds(start, key_rows), :]
        probs = jnp.exp(scores_at(pair, query_ext, low, base, start, heads) - log_sum)
        probs_grad = jnp.dot(pair, grad_ext, preferred_element_type=jnp.float32)
        score_grad = (probs * (probs_grad - inner)).astype(jnp.bfloat16)
        sum_ref[...] += jnp.dot(
            turned_ref[:dim, pl.ds(start, key_rows)], score_grad, preferred_element_type=jnp.float32
        )
        pair_grad_ref[pl.ds(start, key_rows), :] += lax.dot_general(
            score_grad, query_ext, ROWS_IN_BOTH, preferred_element_type=jnp.float32
        ) + lax.dot_general(
            probs.astype(jnp.bfloat16), grad_ext, ROWS_IN_BOTH, preferred_element_type=jnp.float32
        )
        return carried

    lax.fori_loop(first_ref[step], (base + query_rows - 1) // key_rows + 1, tile, 0)
    query_grad_ref[...] = unstack_heads(sum_ref[...] * scale, heads).astype(query_grad_ref.dtype)


def attention_specs(queries, pair, query_rows, heads):
    width = queries.shape[1]
    return (
        pl.BlockSpec((query_rows, width), lambda i, first: (i, 0)),
        pl.BlockSpec((1, query_rows), lambda i, first: (0, i)),
        pl.BlockSpec(pair.shape, lambda i, first: (0, 0)),
        pl.BlockSpec((1, 1, heads * query_rows), lambda i, first: (i, 0, 0)),
    )


def attend(queries, pair, first, low, heads, query_rows, key_rows):
    count, width = queries.shape
    tile, row, whole, logs = attention_specs(queries, pair, query_rows, heads)
    columns = heads * query_rows
    return pl.pallas_call(
        functools.partial(attend_kernel, heads, key_rows, (width // heads) ** -0.5),
        grid_spec=pltpu.PrefetchScalarGridSpec(
            num_scalar_prefetch=1,
            grid=(count // query_rows,),
            in_specs=[tile, row, whole],
            out_specs=[tile, logs],
            scratch_shapes=[
                pltpu.VMEM(pair.shape[::-1], jnp.bfloat16),
                pltpu.VMEM((pair.shape[1], columns), jnp.float32),
                pltpu.VMEM((1, columns), jnp.float32),
            ],
        ),
        out_shape=[
            jax.ShapeDtypeStruct((count, width), jnp.bfloat16),
            jax.ShapeDtypeStruct((count // query_rows, 1, columns), jnp.float32),
        ],
        compiler_params=pltpu.CompilerParams(vmem_limit_bytes=48 << 20),
        cost_estimate=pl.CostEstimate(
            flops=20_000_000_000, bytes_accessed=8_000_000, transcendentals=0
        ),
        name="attend",
    )(first, queries, low, pair)


def attend_back(queries, pair, first, low, grads, out, logs, heads, query_rows, key_rows):
    count, width = queries.shape
    tile, row, whole, log_spec = attention_specs(queries, pair, query_rows, heads)
    columns = heads * query_rows
    return pl.pallas_call(
        functools.partial(attend_back_kernel, heads, key_rows, (width // heads) ** -0.5),
        grid_spec=pltpu.PrefetchScalarGridSpec(
            num_scalar_prefetch=1,
            grid=(count // query_rows,),
            in_specs=[tile, row, whole, tile, log_spec]
            + [pl.BlockSpec((query_rows, width), lambda i, first: (0, 0))] * len(grads),
            out_specs=[tile, whole],
            scratch_shapes=[
                pltpu.VMEM(pair.shape[::-1], jnp.bfloat16),
                pltpu.VMEM((pair.shape[1] // 2, columns), jnp.float32),
            ],
        ),
        out_shape=[
            jax.ShapeDtypeStruct((count, width), jnp.bfloat16),
            jax.ShapeDtypeStruct(pair.shape, jnp.float32),
        ],
        compiler_params=pltpu.CompilerParams(vmem_limit_bytes=48 << 20),
        cost_estimate=pl.CostEstimate(
            flops=40_000_000_000, bytes_accessed=12_000_000, transcendentals=0
        ),
        name="attend_back",
    )(first, queries, low, pair, out, logs, *grads)


def heads_apart(wide, dim):
    rows = wide.shape[0]
    return jnp.concatenate(
        [
            jnp.broadcast_to(
                jnp.mean(jnp.square(wide[:, c : c + dim]), axis=-1, keepdims=True), (rows, dim)
            )
            for c in range(0, wide.shape[1], dim)
        ],
        axis=1,
    )


def spread_mean(wide, dim):
    rows = wide.shape[0]
    return jnp.concatenate(
        [
            jnp.broadcast_to(jnp.mean(wide[:, c : c + dim], axis=-1, keepdims=True), (rows, dim))
            for c in range(0, wide.shape[1], dim)
        ],
        axis=1,
    )


def turn(wide, cosine, sine, dim):
    count = wide.shape[1] // dim
    half = dim // 2
    swapped = jnp.concatenate(
        [
            wide[:, c + shift : c + shift + half]
            for c in range(0, wide.shape[1], dim)
            for shift in (half, 0)
        ],
        axis=1,
    )
    return wide * jnp.concatenate([cosine] * count, axis=1) + swapped * jnp.concatenate(
        [sine] * count, axis=1
    )


def project_kernel(
    dim, own_ref, x_ref, weight_ref, head_gain_ref, cosine_ref, sine_ref, query_ref, pair_ref,
    raw_ref, normed_ref, gain_ref, ffn_gain_ref
):
    columns = raw_ref.shape[1]

    @pl.when(pl.program_id(0) == 0)
    def _():
        gains = weight_ref[:, columns:].T.astype(jnp.float32)
        gain_ref[...] = gains[:1]
        ffn_gain_ref[...] = gains[64:65]

    values = x_ref[...].astype(jnp.float32)
    normed = values * lax.rsqrt(jnp.mean(values * values, axis=-1, keepdims=True) + EPS)
    normed = (normed * gain_ref[...]).astype(jnp.bfloat16)
    normed_ref[...] = normed
    raw = jnp.dot(normed, weight_ref[:, :columns], preferred_element_type=jnp.float32)
    raw_ref[...] = raw
    turned_width = raw.shape[1] - pair_ref.shape[1] // 2
    heads = raw[:, :turned_width]
    heads = heads * lax.rsqrt(heads_apart(heads, dim) + EPS) * head_gain_ref[...]
    heads = turn(heads, cosine_ref[...], sine_ref[...], dim).astype(jnp.bfloat16)
    query_width = query_ref.shape[1]
    query_ref[...] = heads[:, :query_width]
    pair_ref[...] = jnp.concatenate(
        [heads[:, query_width:], raw[:, turned_width:].astype(jnp.bfloat16)], axis=1
    )


def project(own, x, weight, head_gain, cosine, sine, size, query_width, rows):
    count, width = x.shape
    out_width = weight.shape[1] - 128
    pair_width = out_width - query_width
    dim = cosine.shape[1]
    tiles = count // size // rows

    def apart(i, own):
        return ((own[0] ^ (i // tiles)) * tiles + i % tiles, 0)

    def there(i, own):
        return (i, 0)

    def whole(i, own):
        return (0, 0)

    return pl.pallas_call(
        functools.partial(project_kernel, dim),
        grid_spec=pltpu.PrefetchScalarGridSpec(
            num_scalar_prefetch=1,
            grid=(count // rows,),
            in_specs=[
                pl.BlockSpec((rows, width), there),
                pl.BlockSpec(weight.shape, whole),
                pl.BlockSpec(head_gain.shape, whole),
                pl.BlockSpec((rows, dim), apart),
                pl.BlockSpec((rows, dim), apart),
            ],
            out_specs=[
                pl.BlockSpec((rows, query_width), apart),
                pl.BlockSpec((rows, pair_width), apart),
                pl.BlockSpec((rows, out_width), apart),
                pl.BlockSpec((rows, width), there),
                pl.BlockSpec((1, width), whole),
                pl.BlockSpec((1, width), whole),
            ],
        ),
        out_shape=[
            jax.ShapeDtypeStruct((count, query_width), jnp.bfloat16),
            jax.ShapeDtypeStruct((count, pair_width), jnp.bfloat16),
            jax.ShapeDtypeStruct((count, out_width), jnp.float32),
            jax.ShapeDtypeStruct((count, width), jnp.bfloat16),
            jax.ShapeDtypeStruct((1, width), jnp.float32),
            jax.ShapeDtypeStruct((1, width), jnp.float32),
        ],
        compiler_params=pltpu.CompilerParams(vmem_limit_bytes=48 << 20),
        cost_estimate=pl.CostEstimate(
            flops=4 * count * width * out_width, bytes_accessed=30_000_000, transcendentals=0
        ),
        name="project",
    )(own, x, weight, head_gain, cosine, sine)


def project_back_kernel(
    dim, own_ref, query_grad_ref, pair_grad_ref, returned_ref, raw_ref, head_gain_ref, cosine_ref,
    sine_ref, grad_ref, gain_grad_ref
):
    @pl.when(pl.program_id(0) == 0)
    def _():
        gain_grad_ref[...] = jnp.zeros_like(gain_grad_ref)

    pair_grad = pair_grad_ref[...] + returned_ref[...].astype(jnp.float32)
    pair_grad = pair_grad.astype(jnp.bfloat16)
    half = pair_grad.shape[1] // 2
    grads = jnp.concatenate([query_grad_ref[...], pair_grad[:, :half]], axis=1).astype(jnp.float32)
    grads = turn(grads, cosine_ref[...], -sine_ref[...], dim)
    values = raw_ref[:, : grads.shape[1]]
    inverse = lax.rsqrt(heads_apart(values, dim) + EPS)
    gain_grad_ref[...] += jnp.sum(grads * values * inverse, axis=0, keepdims=True)
    scaled = grads * head_gain_ref[...]
    moment = spread_mean(scaled * values, dim)
    back = inverse * scaled - values * inverse * inverse * inverse * moment
    grad_ref[...] = jnp.concatenate([back.astype(jnp.bfloat16), pair_grad[:, half:]], axis=1)


def project_back(own, query_grad, pair_sum, returned, raw, head_gain, cosine, sine, size, rows):
    count, query_width = query_grad.shape
    pair_width = pair_sum.shape[1]
    out_width = raw.shape[1]
    dim = cosine.shape[1]
    tiles = count // size // rows

    def apart(i, own):
        return ((own[0] ^ (i // tiles)) * tiles + i % tiles, 0)

    def behind(i, own):
        return (apart(i, own)[0] + count // rows, 0)

    def whole(i, own):
        return (0, 0)

    return pl.pallas_call(
        functools.partial(project_back_kernel, dim),
        grid_spec=pltpu.PrefetchScalarGridSpec(
            num_scalar_prefetch=1,
            grid=(count // rows,),
            in_specs=[
                pl.BlockSpec((rows, query_width), apart),
                pl.BlockSpec((rows, pair_width), behind),
                pl.BlockSpec((rows, pair_width), apart),
                pl.BlockSpec((rows, out_width), apart),
                pl.BlockSpec(head_gain.shape, whole),
                pl.BlockSpec((rows, dim), apart),
                pl.BlockSpec((rows, dim), apart),
            ],
            out_specs=[
                pl.BlockSpec((rows, out_width), lambda i, own: (i, 0)),
                pl.BlockSpec(head_gain.shape, whole),
            ],
        ),
        out_shape=[
            jax.ShapeDtypeStruct((count, out_width), jnp.bfloat16),
            jax.ShapeDtypeStruct(head_gain.shape, jnp.float32),
        ],
        compiler_params=pltpu.CompilerParams(vmem_limit_bytes=48 << 20),
        cost_estimate=pl.CostEstimate(
            flops=8_000_000_000, bytes_accessed=8_000_000, transcendentals=0
        ),
        name="project_back",
    )(own, query_grad, pair_sum, returned, raw, head_gain, cosine, sine)


def join_kernel(half_tiles, x_ref, *refs):
    *part_refs, top_ref, bottom_ref, weight_ref, gain_ref, residual_ref, normed_ref = refs
    tile = pl.program_id(0)
    far = jnp.where((tile // half_tiles) % 2 == 1, top_ref[...], bottom_ref[...])
    attended = jnp.concatenate([ref[...] for ref in part_refs] + [far], axis=1)
    residual = x_ref[...].astype(jnp.float32) + jnp.dot(
        attended, weight_ref[...], preferred_element_type=jnp.float32
    )
    residual_ref[...] = residual
    normed = residual * lax.rsqrt(jnp.mean(residual * residual, axis=-1, keepdims=True) + EPS)
    normed_ref[...] = (normed * gain_ref[...]).astype(jnp.bfloat16)


def join(x, parts, top, bottom, weight, gain, rows):
    count, width = x.shape
    columns = parts[0].shape[1]
    tiles = count // 4 // rows

    def part_map(k):
        return lambda i: ((k ^ (i // tiles)) * tiles + i % tiles, 0)

    def far_map(i):
        return (((3 ^ (i // tiles)) % 2) * tiles + i % tiles, 0)

    def there(i):
        return (i, 0)

    def whole(i):
        return (0, 0)

    return pl.pallas_call(
        functools.partial(join_kernel, 2 * tiles),
        grid=(count // rows,),
        in_specs=[pl.BlockSpec((rows, width), there)]
        + [pl.BlockSpec((rows, columns), part_map(k)) for k in range(3)]
        + [pl.BlockSpec((rows, columns), far_map)] * 2
        + [pl.BlockSpec(weight.shape, whole), pl.BlockSpec((1, width), whole)],
        out_specs=[pl.BlockSpec((rows, width), there)] * 2,
        out_shape=[
            jax.ShapeDtypeStruct((count, width), jnp.float32),
            jax.ShapeDtypeStruct((count, width), jnp.bfloat16),
        ],
        compiler_params=pltpu.CompilerParams(vmem_limit_bytes=48 << 20),
        cost_estimate=pl.CostEstimate(
            flops=2 * count * width * weight.shape[0],
            bytes_accessed=50_000_000,
            transcendentals=0,
        ),
        name="join",
    )(x, *parts, top, bottom, weight, gain)


def settle_kernel(size, own_ref, *refs):
    *part_refs, out_ref = refs
    for k, part_ref in enumerate(part_refs):

        @pl.when(pl.program_id(0) % size == k)
        def _(part_ref=part_ref):
            out_ref[...] = part_ref[...].astype(out_ref.dtype)


def settle(own, parts, pieces):
    size = len(parts)
    rows, width = parts[0].shape
    piece = width // pieces
    return pl.pallas_call(
        functools.partial(settle_kernel, size),
        grid_spec=pltpu.PrefetchScalarGridSpec(
            num_scalar_prefetch=1,
            grid=(pieces * size,),
            in_specs=[pl.BlockSpec((rows, piece), lambda i, own: (0, i // size))] * size,
            out_specs=pl.BlockSpec(
                (rows, piece), lambda i, own: (0, i // size * size + (own[0] ^ (i % size)))
            ),
        ),
        out_shape=jax.ShapeDtypeStruct((rows, width * size), jnp.float32),
        name="settle",
    )(own, *parts)


def begin_kernel(
    x_ref, qkv_ref, in_ref, x_out, qkv_out, in_out, local_sem, x_send, x_recv, q_send, q_recv,
    w_send, w_recv, b_send, b_recv
):
    head, blk = lax.axis_index("heads"), lax.axis_index("blk")
    size, blk_size = lax.axis_size("heads"), lax.axis_size("blk")
    count, depth = x_ref.shape[0], qkv_ref.shape[1]
    half = count // 2
    units = in_out.shape[2] // 2
    barrier = pltpu.get_barrier_semaphore()
    for k in range(1, size):
        pl.semaphore_signal(barrier, inc=1, device_id=(head ^ k, blk), device_id_type=MESH)

    def greet(k, carried):
        pl.semaphore_signal(
            barrier, inc=1, device_id=(head, lax.rem(blk + k, blk_size)), device_id_type=MESH
        )
        return carried

    lax.fori_loop(1, blk_size, greet, 0)
    pl.semaphore_wait(barrier, size + blk_size - 2)

    def send(source, target, k, send_sem, recv_sem):
        return pltpu.make_async_remote_copy(
            src_ref=source,
            dst_ref=target,
            send_sem=send_sem,
            recv_sem=recv_sem,
            device_id=(head ^ k, blk),
            device_id_type=MESH,
        )

    rows = pl.ds(pl.multiple_of(blk * depth, depth), depth)
    qkv_copies = [
        send(
            qkv_ref.at[head ^ k], qkv_out.at[head, rows], k, q_send.at[k - 1], q_recv.at[k - 1]
        )
        for k in range(1, size)
    ]

    def columns(part, owner):
        return pl.ds(pl.multiple_of((part * size + owner) * units, units), units)

    in_copies = [
        send(
            in_ref.at[:, columns(part, head ^ k)],
            in_out.at[head, :, pl.ds(part * units, units)],
            k,
            w_send.at[2 * k - 2 + part],
            w_recv.at[2 * k - 2 + part],
        )
        for k in range(1, size)
        for part in range(2)
    ]
    near = [
        send(x_ref, x_out.at[pl.ds(k * count, count)], k, x_send.at[k - 1], x_recv.at[k - 1])
        for k in (1, 2)
    ]
    far = [
        send(
            x_out.at[pl.ds(count, half)],
            x_out.at[pl.ds(3 * count, half)],
            2,
            x_send.at[2],
            x_recv.at[2],
        ),
        send(
            x_out.at[pl.ds(2 * count + half, half)],
            x_out.at[pl.ds(3 * count + half, half)],
            1,
            x_send.at[3],
            x_recv.at[3],
        ),
    ]
    own = [
        pltpu.make_async_copy(qkv_ref.at[head], qkv_out.at[head, rows], local_sem.at[0]),
        pltpu.make_async_copy(x_ref, x_out.at[pl.ds(0, count)], local_sem.at[1]),
    ] + [
        pltpu.make_async_copy(
            in_ref.at[:, columns(part, head)],
            in_out.at[head, :, pl.ds(part * units, units)],
            local_sem.at[2 + part],
        )
        for part in range(2)
    ]
    for copy in qkv_copies + near + in_copies + own:
        copy.start()

    def along(k):
        return pltpu.make_async_remote_copy(
            src_ref=qkv_out.at[:, rows],
            dst_ref=qkv_out.at[:, rows],
            send_sem=b_send.at[k],
            recv_sem=b_recv.at[k],
            device_id=(head, lax.rem(blk + k, blk_size)),
            device_id_type=MESH,
        )

    def arrived(k):
        source = pl.ds(
            pl.multiple_of(lax.rem(blk + blk_size - k, blk_size) * depth, depth), depth
        )
        return pltpu.make_async_remote_copy(
            src_ref=qkv_out.at[:, rows],
            dst_ref=qkv_out.at[:, source],
            send_sem=b_send.at[k],
            recv_sem=b_recv.at[k],
            device_id=(head, lax.rem(blk + k, blk_size)),
            device_id_type=MESH,
        )

    def start(k, carried):
        along(k).start()
        return carried

    def finish(k, carried):
        along(k).wait_send()
        arrived(k).wait_recv()
        return carried

    own[0].wait()
    for copy in qkv_copies:
        copy.wait_recv()
    lax.fori_loop(1, blk_size, start, 0)
    for first, second in zip(near, far):
        first.wait_recv()
        second.start()
    for copy in qkv_copies + near:
        copy.wait_send()
    for copy in in_copies + far:
        copy.wait()
    for copy in own[1:]:
        copy.wait()
    lax.fori_loop(1, blk_size, finish, 0)


def begin(x, qkv_parts, in_weight):
    size, blk_size = lax.axis_size("heads"), lax.axis_size("blk")
    count, width = x.shape
    depth, joined = qkv_parts.shape[1:]
    anywhere = pl.BlockSpec(memory_space=pl.ANY)
    sems = pltpu.SemaphoreType.DMA
    return pl.pallas_call(
        begin_kernel,
        out_shape=[
            jax.ShapeDtypeStruct((size * count, width), x.dtype),
            jax.ShapeDtypeStruct((size, blk_size * depth, joined), x.dtype),
            jax.ShapeDtypeStruct((size, depth, in_weight.shape[1] // size), x.dtype),
        ],
        in_specs=[anywhere] * 3,
        out_specs=[anywhere] * 3,
        scratch_shapes=[
            sems((4,)),
            sems((4,)),
            sems((4,)),
            sems((size - 1,)),
            sems((size - 1,)),
            sems((2 * size - 2,)),
            sems((2 * size - 2,)),
            sems((blk_size,)),
            sems((blk_size,)),
        ],
        compiler_params=pltpu.CompilerParams(collective_id=1, has_side_effects=True),
        name="begin",
    )(x, qkv_parts, in_weight)


def hidden_kernel(
    normed_ref, gate_ref, up_ref, cot_ref, down_ref, hidden_ref, gate_grad_ref, up_grad_ref
):
    normed = normed_ref[...]
    gate = jnp.dot(normed, gate_ref[...], preferred_element_type=jnp.float32)
    upward = jnp.dot(normed, up_ref[...], preferred_element_type=jnp.float32)
    grad = lax.dot_general(
        cot_ref[...], down_ref[...], ROWS_IN_BOTH, preferred_element_type=jnp.float32
    )
    sigmoid = jax.nn.sigmoid(gate)
    activated = gate * sigmoid
    hidden_ref[...] = (activated * upward).astype(jnp.bfloat16)
    gate_grad_ref[...] = (grad * upward * sigmoid * (1.0 + gate * (1.0 - sigmoid))).astype(
        jnp.bfloat16
    )
    up_grad_ref[...] = (grad * activated).astype(jnp.bfloat16)


def hidden_pass(normed, weight, cot, down, rows, units):
    count, width = normed.shape
    total = down.shape[0]
    tiles = total // units
    out_spec = pl.BlockSpec((rows, units), lambda i, j: (i, j))
    out_shape = jax.ShapeDtypeStruct((count, total), jnp.bfloat16)
    return pl.pallas_call(
        hidden_kernel,
        grid=(count // rows, tiles),
        in_specs=[
            pl.BlockSpec((rows, width), lambda i, j: (i, 0)),
            pl.BlockSpec((width, units), lambda i, j: (0, j)),
            pl.BlockSpec((width, units), lambda i, j: (0, tiles + j)),
            pl.BlockSpec((rows, width), lambda i, j: (i, 0)),
            pl.BlockSpec((units, width), lambda i, j: (j, 0)),
        ],
        out_specs=[out_spec] * 3,
        out_shape=[out_shape] * 3,
        compiler_params=pltpu.CompilerParams(vmem_limit_bytes=58 << 20),
        cost_estimate=pl.CostEstimate(
            flops=6 * count * width * total, bytes_accessed=70_000_000, transcendentals=0
        ),
        name="hidden_pass",
    )(normed, weight, weight, cot, down)


def shares_kernel(compute, order_ref, *refs):
    *in_refs, one_ref, two_ref, rest_ref = refs
    step = pl.program_id(0)
    value = compute(*in_refs).astype(jnp.bfloat16)

    @pl.when(step < 2)
    def _():
        one_ref[...] = value

    @pl.when((step >= 2) & (step < 4))
    def _():
        two_ref[...] = value

    @pl.when(step >= 4)
    def _():
        rest_ref[...] = value


def shares(compute, left, right, right_specs, flops, name):
    rows = left[0].shape[0] // 8
    width = right[0].shape[0] if name == "back_pass" else right[0].shape[1]
    order = jnp.array([2, 6, 5, 7, 0, 1, 4, 3], jnp.int32)
    return pl.pallas_call(
        functools.partial(shares_kernel, compute),
        grid_spec=pltpu.PrefetchScalarGridSpec(
            num_scalar_prefetch=1,
            grid=(8,),
            in_specs=[
                pl.BlockSpec((rows, a.shape[1]), lambda i, order: (order[i], 0)) for a in left
            ]
            + right_specs,
            out_specs=[
                pl.BlockSpec((rows, width), lambda i, order: (jnp.minimum(i, 1), 0)),
                pl.BlockSpec((rows, width), lambda i, order: (jnp.clip(i - 2, 0, 1), 0)),
                pl.BlockSpec((rows, width), lambda i, order: (jnp.clip(i - 4, 0, 3), 0)),
            ],
        ),
        out_shape=[
            jax.ShapeDtypeStruct((count * rows, width), jnp.bfloat16) for count in (2, 2, 4)
        ],
        compiler_params=pltpu.CompilerParams(vmem_limit_bytes=58 << 20),
        cost_estimate=pl.CostEstimate(flops=flops, bytes_accessed=40_000_000, transcendentals=0),
        name=name,
    )(order, *left, *right)


def back_product(gate_ref, up_ref, gate_weight_ref, up_weight_ref):
    return lax.dot_general(
        gate_ref[...], gate_weight_ref[...], ROWS_IN_BOTH, preferred_element_type=jnp.float32
    ) + lax.dot_general(
        up_ref[...], up_weight_ref[...], ROWS_IN_BOTH, preferred_element_type=jnp.float32
    )


def back_pass(gate_grad, up_grad, weight):
    width, total = weight.shape[0], gate_grad.shape[1]
    specs = [
        pl.BlockSpec((width, total), lambda i, order: (0, 0)),
        pl.BlockSpec((width, total), lambda i, order: (0, 1)),
    ]
    flops = 4 * gate_grad.shape[0] * width * total
    return shares(back_product, [gate_grad, up_grad], [weight] * 2, specs, flops, "back_pass")


def down_product(hidden_ref, weight_ref):
    return jnp.dot(hidden_ref[...], weight_ref[...], preferred_element_type=jnp.float32)


def down_pass(hidden, weight):
    specs = [pl.BlockSpec(weight.shape, lambda i, order: (0, 0))]
    flops = 2 * hidden.shape[0] * weight.shape[0] * weight.shape[1]
    return shares(down_product, [hidden], [weight], specs, flops, "down_pass")


def residual_back_kernel(
    keep_ref, top_ref, bottom_ref, top_last_ref, bottom_last_ref, residual_ref, cot_ref, gain_ref,
    *refs
):
    *weight_refs, grad_ref, branch_ref, gain_grad_ref, attended_ref = refs
    step = pl.program_id(0)
    first = step < pl.num_programs(0) // 2

    @pl.when(step == 0)
    def _():
        gain_grad_ref[...] = jnp.zeros_like(gain_grad_ref)

    def wide(ref):
        return ref[...].astype(jnp.float32)

    gradient = wide(keep_ref) + jnp.where(
        first, wide(top_ref) + wide(top_last_ref), wide(bottom_ref) + wide(bottom_last_ref)
    )
    values = residual_ref[...]
    inverse = lax.rsqrt(jnp.mean(values * values, axis=-1, keepdims=True) + EPS)
    gain_grad_ref[...] += jnp.sum(gradient * values * inverse, axis=0, keepdims=True)
    scaled = gradient * gain_ref[...]
    moment = jnp.mean(scaled * values, axis=-1, keepdims=True)
    total = wide(cot_ref) + inverse * scaled - values * (inverse * inverse * inverse * moment)
    grad_ref[...] = total
    branch = total.astype(jnp.bfloat16)
    branch_ref[...] = branch
    for k, weight_ref in enumerate(weight_refs):
        attended_ref[k] = lax.dot_general(
            branch, weight_ref[...], ROWS_IN_BOTH, preferred_element_type=jnp.float32
        ).astype(jnp.bfloat16)


def residual_back(keep, top, bottom, top_last, bottom_last, residual, cot, gain, weights, rows):
    count, width = cot.shape
    columns = weights[0].shape[0]
    tiles = count // 2 // rows

    def there(i):
        return (i, 0)

    def in_half(i):
        return (i % tiles, 0)

    def whole(i):
        return (0, 0)

    tile = pl.BlockSpec((rows, width), there)
    half = pl.BlockSpec((rows, width), in_half)
    row = pl.BlockSpec((1, width), whole)
    return pl.pallas_call(
        residual_back_kernel,
        grid=(count // rows,),
        in_specs=[tile, half, half, half, half, tile, tile, row]
        + [pl.BlockSpec(weight.shape, whole) for weight in weights],
        out_specs=[
            tile,
            tile,
            row,
            pl.BlockSpec((len(weights), rows, columns), lambda i: (0, i, 0)),
        ],
        out_shape=[
            jax.ShapeDtypeStruct((count, width), jnp.float32),
            jax.ShapeDtypeStruct((count, width), jnp.bfloat16),
            jax.ShapeDtypeStruct((1, width), jnp.float32),
            jax.ShapeDtypeStruct((len(weights), count, columns), jnp.bfloat16),
        ],
        compiler_params=pltpu.CompilerParams(vmem_limit_bytes=48 << 20),
        cost_estimate=pl.CostEstimate(
            flops=2 * count * width * columns * len(weights),
            bytes_accessed=30_000_000,
            transcendentals=0,
        ),
        name="residual_back",
    )(keep, top, bottom, top_last, bottom_last, residual, cot, gain, *weights)


def turned_kernel(left_ref, right_ref, out_ref):
    out_ref[...] = lax.dot_general(
        left_ref[...], right_ref[...], (((0,), (0,)), ((), ())), preferred_element_type=jnp.float32
    ).astype(out_ref.dtype)


def turned_product(left, right, rows):
    count, height = left.shape
    width = right.shape[1]
    return pl.pallas_call(
        turned_kernel,
        grid=(height // rows,),
        in_specs=[
            pl.BlockSpec((count, rows), lambda i: (0, i)),
            pl.BlockSpec((count, width), lambda i: (0, 0)),
        ],
        out_specs=pl.BlockSpec((rows, width), lambda i: (i, 0)),
        out_shape=jax.ShapeDtypeStruct((height, width), jnp.bfloat16),
        compiler_params=pltpu.CompilerParams(vmem_limit_bytes=58 << 20),
        cost_estimate=pl.CostEstimate(
            flops=2 * count * height * width, bytes_accessed=20_000_000, transcendentals=0
        ),
        name="turned_product",
    )(left, right)


def finish_kernel(
    query_width, dim, sent_ref, qkv_ref, x_ref, residual_ref, gain_ref, ffn_ref, head_ref, *refs
):
    size, blk_size = lax.axis_size("heads"), lax.axis_size("blk")
    weight_refs, refs = refs[:size], refs[size:]
    (
        grad_ref, qkv_grad_ref, gains_ref, got_ref, qkv_got_ref, part_ref, gain_got_ref, s_send,
        s_recv, q_send, q_recv, g_send, g_recv,
    ) = refs
    devices = size * blk_size
    head, blk = lax.axis_index("heads"), lax.axis_index("blk")
    own = head * blk_size + blk
    count, width = x_ref.shape
    depth = width // devices
    barrier = pltpu.get_barrier_semaphore()

    def place_of(index):
        return (index // blk_size, lax.rem(index, blk_size))

    def greet(k, carried):
        pl.semaphore_signal(
            barrier, inc=1, device_id=place_of(lax.rem(own + k, devices)), device_id_type=MESH
        )
        return carried

    lax.fori_loop(1, devices, greet, 0)
    pl.semaphore_wait(barrier, devices - 1)

    sends = [
        pltpu.make_async_remote_copy(
            src_ref=sent_ref.at[pl.ds(k * count, count)],
            dst_ref=got_ref.at[k - 1],
            send_sem=s_send.at[k - 1],
            recv_sem=s_recv.at[k - 1],
            device_id=(head ^ k, blk),
            device_id_type=MESH,
        )
        for k in range(1, size)
    ]
    for copy in sends:
        copy.start()

    def rows_of(index):
        return pl.ds(pl.multiple_of(index * depth, depth), depth)

    def qkv_copy(k, slot):
        other = lax.rem(own + k, devices)
        return pltpu.make_async_remote_copy(
            src_ref=qkv_ref.at[rows_of(other)],
            dst_ref=qkv_got_ref.at[slot],
            send_sem=q_send.at[k],
            recv_sem=q_recv.at[slot],
            device_id=place_of(other),
            device_id_type=MESH,
        )

    def gain_copy(k, slot):
        other = lax.rem(own + k, devices)
        return pltpu.make_async_remote_copy(
            src_ref=part_ref.at[other],
            dst_ref=gain_got_ref.at[slot],
            send_sem=g_send.at[k],
            recv_sem=g_recv.at[slot],
            device_id=place_of(other),
            device_id_type=MESH,
        )

    def start_qkv(k, carried):
        qkv_copy(k, own).start()
        return carried

    lax.fori_loop(1, devices, start_qkv, 0)
    qkv_got_ref[own] = qkv_ref[rows_of(own)]
    for copy in sends:
        copy.wait_recv()

    rows = min(128, count)

    def tile(index, gain_sum):
        here = pl.ds(pl.multiple_of(index * rows, rows), rows)
        normed_grad = lax.dot_general(
            sent_ref[here], weight_refs[0][...], ROWS_IN_BOTH, preferred_element_type=jnp.float32
        )
        for k in range(1, size):
            normed_grad += lax.dot_general(
                got_ref[k - 1, here],
                weight_refs[k][...],
                ROWS_IN_BOTH,
                preferred_element_type=jnp.float32,
            )
        values = x_ref[here].astype(jnp.float32)
        inverse = lax.rsqrt(jnp.mean(values * values, axis=-1, keepdims=True) + EPS)
        scaled = normed_grad * gain_ref[...]
        moment = jnp.mean(scaled * values, axis=-1, keepdims=True)
        grad_ref[here] = (
            residual_ref[here]
            + inverse * scaled
            - values * (inverse * inverse * inverse * moment)
        )
        return gain_sum + jnp.sum(normed_grad * values * inverse, axis=0, keepdims=True)

    attn_sum = lax.fori_loop(0, count // rows, tile, jnp.zeros((1, width), jnp.float32))

    def by_device(row):
        lanes = jnp.concatenate(
            [row[:, d * depth : (d + 1) * depth] for d in range(devices)], axis=0
        )
        if depth < 64:
            lanes = jnp.concatenate(
                [lanes, jnp.zeros((devices, 64 - depth), jnp.float32)], axis=1
            )
        return lanes

    head_row = head_ref[...]
    query_sum = head_row[:, :dim]
    for c in range(dim, query_width, dim):
        query_sum += head_row[:, c : c + dim]
    key_sum = head_row[:, query_width : query_width + dim]
    for c in range(query_width + dim, head_row.shape[1], dim):
        key_sum += head_row[:, c : c + dim]
    both = jnp.concatenate([query_sum, key_sum], axis=1)
    part_ref[...] = jnp.zeros_like(part_ref)
    part_ref[:, 0, :] = jnp.concatenate([by_device(attn_sum), by_device(ffn_ref[...])], axis=1)
    part_ref[:, 1, :] = jnp.broadcast_to(both, (devices, 2 * dim))

    def start_gain(k, carried):
        gain_copy(k, own).start()
        return carried

    lax.fori_loop(1, devices, start_gain, 0)
    gain_got_ref[own] = part_ref[own]

    def finish(k, carried):
        source = lax.rem(own + devices - k, devices)
        qkv_copy(k, source).wait()
        gain_copy(k, source).wait()
        return carried

    lax.fori_loop(1, devices, finish, 0)
    for copy in sends:
        copy.wait_send()
    gains_ref[...] = jnp.sum(gain_got_ref[...], axis=0)

    def group_sum(h):
        total = qkv_got_ref[h * blk_size].astype(jnp.float32)
        for b in range(1, blk_size):
            total += qkv_got_ref[h * blk_size + b].astype(jnp.float32)
        return total

    sums = [group_sum(h) for h in range(size)]
    key_end = query_width + (sums[0].shape[1] - query_width) // 2
    qkv_grad_ref[...] = jnp.concatenate(
        [total[:, :query_width] for total in sums]
        + [total[:, query_width:key_end] for total in sums]
        + [total[:, key_end:] for total in sums],
        axis=1,
    )


def finish(sent, qkv_part, x, residual_grad, gain, ffn_sum, head_sum, weights, query_width, dim):
    size, blk_size = lax.axis_size("heads"), lax.axis_size("blk")
    devices = size * blk_size
    count, width = x.shape
    depth, joined = width // devices, sent.shape[1]
    vmem = pl.BlockSpec(memory_space=pltpu.VMEM)
    sems = pltpu.SemaphoreType.DMA
    return pl.pallas_call(
        functools.partial(finish_kernel, query_width, dim),
        out_shape=[
            jax.ShapeDtypeStruct((count, width), jnp.float32),
            jax.ShapeDtypeStruct((depth, size * joined), jnp.float32),
            jax.ShapeDtypeStruct((8, 128), jnp.float32),
        ],
        in_specs=[vmem] * (7 + size),
        out_specs=[vmem] * 3,
        scratch_shapes=[
            pltpu.VMEM((size - 1, count, joined), jnp.bfloat16),
            pltpu.VMEM((devices, depth, joined), jnp.bfloat16),
            pltpu.VMEM((devices, 8, 128), jnp.float32),
            pltpu.VMEM((devices, 8, 128), jnp.float32),
            sems((size - 1,)),
            sems((size - 1,)),
            sems((devices,)),
            sems((devices,)),
            sems((devices,)),
            sems((devices,)),
        ],
        compiler_params=pltpu.CompilerParams(
            collective_id=0, has_side_effects=True, vmem_limit_bytes=56 << 20
        ),
        name="finish",
    )(sent, qkv_part, x, residual_grad, gain, ffn_sum, head_sum, *weights)


def permute(block, axis, k):
    return lax.ppermute(block, axis, [(i, i ^ k) for i in range(lax.axis_size(axis))])


def after(value, *done):
    return lax.optimization_barrier((value, *done))[0]


def pick(block, k, axis, dim):
    extent = block.shape[dim] // lax.axis_size(axis)
    return lax.dynamic_slice_in_dim(block, (lax.axis_index(axis) ^ k) * extent, extent, dim)


def gather_near(block, *done):
    half = block.shape[0] // 2
    one, two = permute(block, "heads", 1), permute(block, "heads", 2)
    if done:
        one, two = lax.optimization_barrier((one, two, *done))[:2]
    top = permute(one[:half], "heads", 2)
    bottom = permute(two[half:], "heads", 1)
    return block, one, two, top, bottom


def wide(block):
    return block.astype(jnp.float32)


def local(
    inputs,
    positions,
    attn_gain,
    qkv_weight,
    q_gain,
    k_gain,
    out_weight,
    ffn_gain,
    ffn_in_weight,
    ffn_out_weight,
    cotangent,
):
    token_count, width = inputs.shape
    depth = qkv_weight.shape[0]
    head_dim = q_gain.shape[0]
    group_size = HEADS // KV_HEADS
    size = lax.axis_size("heads")
    blk_size = lax.axis_size("blk")
    query_all, key_all = HEADS * head_dim, KV_HEADS * head_dim
    query_width, key_width = query_all // size, key_all // size
    qkv_width = query_width + 2 * key_width
    block_len = token_count * size
    half = token_count // 2
    own = lax.axis_index("heads").astype(jnp.int32).reshape(1)

    qkv_parts = jnp.concatenate(
        [
            qkv_weight[:, :query_all].reshape(depth, size, query_width),
            qkv_weight[:, query_all : query_all + key_all].reshape(depth, size, key_width),
            qkv_weight[:, query_all + key_all :].reshape(depth, size, key_width),
            jnp.broadcast_to(attn_gain[:, None, None], (depth, size, 64)),
            jnp.broadcast_to(ffn_gain[:, None, None], (depth, size, 64)),
        ],
        axis=-1,
    ).transpose(1, 0, 2)
    out_group = lax.all_gather(out_weight, "blk", axis=0, tiled=True)
    down_group = lax.all_gather(ffn_out_weight, "blk", axis=0, tiled=True)

    inputs_blk, qkv_rows, in_rows = begin(inputs, qkv_parts, ffn_in_weight)
    in_group = lax.all_gather(in_rows, "blk", axis=1, tiled=True).reshape(width, -1)
    qkv_rows = qkv_rows.reshape(width, -1)
    cosine, sine = rotation(positions, head_dim)
    cosine = jnp.concatenate([cosine[:, 0], cosine[:, 0]], axis=-1)
    sine = jnp.concatenate([-sine[:, 0], sine[:, 0]], axis=-1)
    head_gain = jnp.concatenate(
        [jnp.tile(q_gain, HEADS // size), jnp.tile(k_gain, KV_HEADS // size)]
    ).astype(jnp.float32)[None, :]
    query_low, pair_blk, raw, normed, attn_scaling, ffn_scaling = project(
        own, inputs_blk, qkv_rows, head_gain, cosine, sine, size, query_width, 256
    )
    pair_all = jnp.concatenate([from_behind(pair_blk, "blk", 1), pair_blk], axis=0)
    query_rows, key_rows = token_count, 256
    low = block_len + jnp.arange(block_len, dtype=jnp.int32) - positions
    first = jnp.concatenate([low[::query_rows] // key_rows, own])
    low = low[None, :]
    attended_blk, logs = attend(query_low, pair_all, first, low, group_size, query_rows, key_rows)

    mine = jnp.concatenate([pick(attended_blk, k, "heads", 0) for k in range(size)], axis=0)
    out_near = gather_near(after(out_group, inputs_blk))
    out_all = (*out_near[:3], jnp.concatenate(out_near[3:], axis=0))
    near = gather_near(mine)
    residual, ffn_normed = join(
        inputs_blk, near[:3], *near[3:], jnp.concatenate(out_all, axis=0), ffn_scaling, 256
    )
    residual_own = residual[:token_count]
    cotangent_near = gather_near(after(cotangent, inputs_blk), near[1])
    cotangent_blk = jnp.concatenate(cotangent_near, axis=0)

    hidden, gate_grad, up_grad = hidden_pass(
        ffn_normed, in_group, cotangent_blk, down_group, block_len // 2, 256
    )
    one, two, rest = back_pass(gate_grad, up_grad, in_group)
    top, bottom = permute(one, "heads", 1), permute(two, "heads", 2)
    down_sum = turned_product(after(hidden, rest), cotangent_blk, 256)
    ffn_out_grad = wide(lax.psum_scatter(down_sum, "blk", scatter_dimension=0, tiled=True))
    gate_up_grad = jnp.concatenate([gate_grad, up_grad], axis=1)
    in_sum = turned_product(ffn_normed, after(gate_up_grad, down_sum), 256)
    in_part = lax.psum_scatter(
        in_sum.reshape(size, blk_size * depth, -1), "blk", scatter_dimension=1, tiled=True
    )
    top, bottom, in_sum = lax.optimization_barrier((top, bottom, in_sum))
    top_send = (wide(rest[2 * half : 3 * half]) + wide(top[half:])).astype(jnp.bfloat16)
    bottom_send = (wide(rest[3 * half :]) + wide(bottom[half:])).astype(jnp.bfloat16)
    top_last, bottom_last = permute(top_send, "heads", 2), permute(bottom_send, "heads", 1)
    out_one, out_two, out_rest = down_pass(after(hidden, top_send, bottom_send), down_group)
    top_last, bottom_last, out_rest = lax.optimization_barrier((top_last, bottom_last, out_rest))

    residual_grad, branch_grad, ffn_sum, attended_grad = residual_back(
        rest, top, bottom, top_last, bottom_last, residual_own, cotangent, ffn_scaling, out_all,
        min(128, half)
    )
    grads = [attended_grad[0]] + [permute(attended_grad[k], "heads", k) for k in range(1, size)]
    attended_own = jnp.concatenate(
        [
            near[0][:token_count],
            near[1][token_count : 2 * token_count],
            near[2][2 * token_count : 3 * token_count],
            near[4][token_count:],
        ],
        axis=1,
    )
    out_sum = turned_product(attended_own, branch_grad, 256)
    *grads, out_sum, out_one, out_two = lax.optimization_barrier(
        (*grads, out_sum, out_one, out_two)
    )
    out_top, out_bottom = permute(out_one, "heads", 1), permute(out_two, "heads", 2)
    query_grad, pair_sum = attend_back(
        query_low, pair_all, first, low, grads, attended_blk, logs, group_size, query_rows, key_rows
    )
    returned = from_behind(pair_sum[:block_len].astype(jnp.bfloat16), "blk", -1)
    out_peers = [
        permute(out_sum[k * query_width : (k + 1) * query_width], "heads", k)
        for k in range(1, size)
    ]
    out_part = sum(wide(part) for part in out_peers) + wide(out_sum[:query_width])
    out_grad = wide(
        lax.psum_scatter(out_part.astype(jnp.bfloat16), "blk", scatter_dimension=0, tiled=True)
    )
    out_top, out_bottom, returned = lax.optimization_barrier((out_top, out_bottom, returned))
    top_send = (wide(out_rest[2 * half : 3 * half]) + wide(out_top[half:])).astype(jnp.bfloat16)
    bottom_send = (wide(out_rest[3 * half :]) + wide(out_bottom[half:])).astype(jnp.bfloat16)
    out_top_last = permute(top_send, "heads", 2)
    out_bottom_last = permute(bottom_send, "heads", 1)
    layer_out = jnp.concatenate(
        [
            residual_own[:half] + wide(out_rest[:half]) + wide(out_top[:half]) + wide(out_top_last),
            residual_own[half:]
            + wide(out_rest[half : 2 * half])
            + wide(out_bottom[:half])
            + wide(out_bottom_last),
        ],
        axis=0,
    ).astype(jnp.bfloat16)

    projected_grad, head_sum = project_back(
        own, query_grad, pair_sum, returned, raw, head_gain, cosine, sine, size, 256
    )
    qkv_part = turned_product(normed, projected_grad, 512)
    qkv_near = gather_near(after(qkv_rows[:, :qkv_width], out_near[1], near[1], cotangent_blk))
    qkv_all = (*qkv_near[:3], jnp.concatenate(qkv_near[3:], axis=0))
    input_grad, qkv_grad, gains = finish(
        projected_grad, qkv_part, inputs, residual_grad, attn_scaling, ffn_sum, head_sum, qkv_all,
        query_width, head_dim
    )
    in_pieces = [pick(in_part, k, "heads", 0)[0] for k in range(size)]
    ffn_in_grad = settle(
        own,
        [in_pieces[0]] + [permute(in_pieces[k], "heads", k) for k in range(1, size)],
        2,
    )
    return (
        layer_out,
        input_grad,
        gains[0, :depth],
        qkv_grad,
        gains[1, :head_dim],
        gains[1, head_dim : 2 * head_dim],
        out_grad,
        gains[0, 64 : 64 + depth],
        ffn_in_grad,
        ffn_out_grad,
    )


def solution(mesh):
    placed = (
        P(("blk", "heads"), None),
        P("blk"),
        P(("heads", "blk")),
        P(("heads", "blk"), None),
        P(),
        P(),
        P(("heads", "blk"), None),
        P(("heads", "blk")),
        P(("heads", "blk"), None),
        P(("heads", "blk"), None),
        P(("blk", "heads"), None),
    )
    return jax.shard_map(
        local,
        mesh=mesh,
        in_specs=placed,
        out_specs=(
            P(("blk", "heads"), None),
            P(("blk", "heads"), None),
            P(("heads", "blk")),
            P(("heads", "blk"), None),
            P(),
            P(),
            P(("heads", "blk"), None),
            P(("heads", "blk")),
            P(("heads", "blk"), None),
            P(("heads", "blk"), None),
        ),
        check_vma=False,
    )
```

```python
import functools

import jax
import jax.numpy as jnp
from jax import lax
from jax.experimental import pallas as pl
from jax.experimental.pallas import tpu as pltpu
from jax.sharding import PartitionSpec as P

HEADS = 16
KV_HEADS = 4


EPS = 1e-06
ROPE_BASE = 10000.0
NEG = -1e30
MESH = pl.DeviceIdType.MESH
ROWS_IN_BOTH = (((1,), (1,)), ((), ()))


def from_behind(block, axis, distance):
    devices = range(lax.axis_size(axis))
    route = [(i - distance, i) for i in devices if i - distance in devices]
    return lax.ppermute(block, axis, route)


def rotation(positions, head_dim):
    half_width = head_dim // 2
    frequency = ROPE_BASE ** (-2.0 * jnp.arange(half_width, dtype=jnp.float32) / head_dim)
    angles = positions.astype(jnp.float32)[:, None] * frequency[None, :]
    return (jnp.cos(angles)[:, None, :], jnp.sin(angles)[:, None, :])


def stack_heads(tile, heads, first):
    turned = tile.T
    dim = turned.shape[0] // heads
    wide = jnp.concatenate([turned[h * dim : (h + 1) * dim] for h in range(heads)], axis=1)
    zero = jnp.zeros_like(wide)
    return jnp.concatenate([wide, zero] if first else [zero, wide], axis=0)


def unstack_heads(wide, heads):
    count = wide.shape[1] // heads
    return jnp.concatenate([wide[:, h * count : (h + 1) * count] for h in range(heads)], axis=0).T


def scores_at(pair, query_ext, low, first_query, key_start, heads):
    scores = jnp.dot(pair, query_ext, preferred_element_type=jnp.float32)
    rows, columns = scores.shape
    shape = (rows, columns // heads)
    key = key_start + lax.broadcasted_iota(jnp.int32, shape, 0)
    query = first_query + lax.broadcasted_iota(jnp.int32, shape, 1)
    bias = jnp.where((key <= query) & (key >= low), 0.0, NEG)
    return scores + jnp.concatenate([bias] * heads, axis=1)


def transpose_into(pair_ref, turned_ref):
    for start in range(0, pair_ref.shape[0], 512):
        turned_ref[:, start : start + 512] = pair_ref[start : start + 512, :].T


def attend_kernel(
    heads, key_rows, scale, first_ref, query_ref, low_ref, pair_ref, out_ref, log_ref, turned_ref,
    mixed_ref, total_ref
):
    step = pl.program_id(0)
    query_rows = query_ref.shape[0]

    @pl.when(step == 0)
    def _():
        transpose_into(pair_ref, turned_ref)

    query_ext = stack_heads(query_ref[...] * jnp.bfloat16(scale), heads, True)
    low = low_ref[...]
    base = pair_ref.shape[0] // 2 + step * query_rows
    mixed_ref[...] = jnp.zeros_like(mixed_ref)
    total_ref[...] = jnp.zeros_like(total_ref)

    def tile(index, carried):
        start = pl.multiple_of(index * key_rows, key_rows)
        expo = jnp.exp(
            scores_at(pair_ref[pl.ds(start, key_rows), :], query_ext, low, base, start, heads)
        )
        total_ref[...] += jnp.sum(expo, axis=0, keepdims=True)
        mixed_ref[...] += jnp.dot(
            turned_ref[:, pl.ds(start, key_rows)],
            expo.astype(jnp.bfloat16),
            preferred_element_type=jnp.float32,
        )
        return carried

    lax.fori_loop(first_ref[step], (base + query_rows - 1) // key_rows + 1, tile, 0)
    total = total_ref[...]
    dim = pair_ref.shape[1] // 2
    out_ref[...] = unstack_heads(mixed_ref[dim:] / total, heads).astype(out_ref.dtype)
    log_ref[...] = jnp.log(total)[None]


def attend_back_kernel(
    heads, key_rows, scale, first_ref, query_ref, low_ref, pair_ref, out_ref, log_ref, *refs
):
    grads_ref, query_grad_ref, pair_grad_ref, turned_ref, sum_ref = refs
    step = pl.program_id(0)
    grad = grads_ref[first_ref[pl.num_programs(0)] ^ step]
    query_rows = query_ref.shape[0]
    dim = pair_ref.shape[1] // 2

    @pl.when(step == 0)
    def _():
        pair_grad_ref[...] = jnp.zeros_like(pair_grad_ref)
        transpose_into(pair_ref, turned_ref)

    query_ext = stack_heads(query_ref[...] * jnp.bfloat16(scale), heads, True)
    grad_ext = stack_heads(grad, heads, False)
    out_ext = stack_heads(out_ref[...], heads, False)
    inner = jnp.sum(
        grad_ext.astype(jnp.float32) * out_ext.astype(jnp.float32), axis=0, keepdims=True
    )
    log_sum = log_ref[0]
    low = low_ref[...]
    base = pair_ref.shape[0] // 2 + step * query_rows
    sum_ref[...] = jnp.zeros_like(sum_ref)

    def tile(index, carried):
        start = pl.multiple_of(index * key_rows, key_rows)
        pair = pair_ref[pl.ds(start, key_rows), :]
        probs = jnp.exp(scores_at(pair, query_ext, low, base, start, heads) - log_sum)
        probs_grad = jnp.dot(pair, grad_ext, preferred_element_type=jnp.float32)
        score_grad = (probs * (probs_grad - inner)).astype(jnp.bfloat16)
        sum_ref[...] += jnp.dot(
            turned_ref[:dim, pl.ds(start, key_rows)], score_grad, preferred_element_type=jnp.float32
        )
        pair_grad_ref[pl.ds(start, key_rows), :] += lax.dot_general(
            score_grad, query_ext, ROWS_IN_BOTH, preferred_element_type=jnp.float32
        ) + lax.dot_general(
            probs.astype(jnp.bfloat16), grad_ext, ROWS_IN_BOTH, preferred_element_type=jnp.float32
        )
        return carried

    lax.fori_loop(first_ref[step], (base + query_rows - 1) // key_rows + 1, tile, 0)
    query_grad_ref[...] = unstack_heads(sum_ref[...] * scale, heads).astype(query_grad_ref.dtype)


def attention_specs(queries, pair, query_rows, heads):
    width = queries.shape[1]
    return (
        pl.BlockSpec((query_rows, width), lambda i, first: (i, 0)),
        pl.BlockSpec((1, query_rows), lambda i, first: (0, i)),
        pl.BlockSpec(pair.shape, lambda i, first: (0, 0)),
        pl.BlockSpec((1, 1, heads * query_rows), lambda i, first: (i, 0, 0)),
    )


def attend(queries, pair, first, low, heads, query_rows, key_rows):
    count, width = queries.shape
    tile, row, whole, logs = attention_specs(queries, pair, query_rows, heads)
    columns = heads * query_rows
    return pl.pallas_call(
        functools.partial(attend_kernel, heads, key_rows, (width // heads) ** -0.5),
        grid_spec=pltpu.PrefetchScalarGridSpec(
            num_scalar_prefetch=1,
            grid=(count // query_rows,),
            in_specs=[tile, row, whole],
            out_specs=[tile, logs],
            scratch_shapes=[
                pltpu.VMEM(pair.shape[::-1], jnp.bfloat16),
                pltpu.VMEM((pair.shape[1], columns), jnp.float32),
                pltpu.VMEM((1, columns), jnp.float32),
            ],
        ),
        out_shape=[
            jax.ShapeDtypeStruct((count, width), jnp.bfloat16),
            jax.ShapeDtypeStruct((count // query_rows, 1, columns), jnp.float32),
        ],
        compiler_params=pltpu.CompilerParams(vmem_limit_bytes=48 << 20),
        cost_estimate=pl.CostEstimate(
            flops=20_000_000_000, bytes_accessed=8_000_000, transcendentals=0
        ),
        name="attend",
    )(first, queries, low, pair)


def attend_back(queries, pair, first, low, grads, out, logs, heads, query_rows, key_rows):
    count, width = queries.shape
    tile, row, whole, log_spec = attention_specs(queries, pair, query_rows, heads)
    columns = heads * query_rows
    return pl.pallas_call(
        functools.partial(attend_back_kernel, heads, key_rows, (width // heads) ** -0.5),
        grid_spec=pltpu.PrefetchScalarGridSpec(
            num_scalar_prefetch=1,
            grid=(count // query_rows,),
            in_specs=[tile, row, whole, tile, log_spec]
            + [pl.BlockSpec(grads.shape, lambda i, first: (0, 0, 0))],
            out_specs=[tile, whole],
            scratch_shapes=[
                pltpu.VMEM(pair.shape[::-1], jnp.bfloat16),
                pltpu.VMEM((pair.shape[1] // 2, columns), jnp.float32),
            ],
        ),
        out_shape=[
            jax.ShapeDtypeStruct((count, width), jnp.bfloat16),
            jax.ShapeDtypeStruct(pair.shape, jnp.float32),
        ],
        compiler_params=pltpu.CompilerParams(vmem_limit_bytes=48 << 20),
        cost_estimate=pl.CostEstimate(
            flops=40_000_000_000, bytes_accessed=12_000_000, transcendentals=0
        ),
        name="attend_back",
    )(first, queries, low, pair, out, logs, grads)


def heads_apart(wide, dim):
    rows = wide.shape[0]
    return jnp.concatenate(
        [
            jnp.broadcast_to(
                jnp.mean(jnp.square(wide[:, c : c + dim]), axis=-1, keepdims=True), (rows, dim)
            )
            for c in range(0, wide.shape[1], dim)
        ],
        axis=1,
    )


def spread_mean(wide, dim):
    rows = wide.shape[0]
    return jnp.concatenate(
        [
            jnp.broadcast_to(jnp.mean(wide[:, c : c + dim], axis=-1, keepdims=True), (rows, dim))
            for c in range(0, wide.shape[1], dim)
        ],
        axis=1,
    )


def turn(wide, cosine, sine, dim):
    count = wide.shape[1] // dim
    half = dim // 2
    swapped = jnp.concatenate(
        [
            wide[:, c + shift : c + shift + half]
            for c in range(0, wide.shape[1], dim)
            for shift in (half, 0)
        ],
        axis=1,
    )
    return wide * jnp.concatenate([cosine] * count, axis=1) + swapped * jnp.concatenate(
        [sine] * count, axis=1
    )


def project_kernel(
    dim, own_ref, x_ref, weight_ref, head_gain_ref, cosine_ref, sine_ref, query_ref, pair_ref,
    raw_ref, normed_ref, gain_ref, ffn_gain_ref
):
    columns = raw_ref.shape[1]

    @pl.when(pl.program_id(0) == 0)
    def _():
        gains = weight_ref[:, columns:].T.astype(jnp.float32)
        gain_ref[...] = gains[:1]
        ffn_gain_ref[...] = gains[64:65]

    values = x_ref[...].astype(jnp.float32)
    normed = values * lax.rsqrt(jnp.mean(values * values, axis=-1, keepdims=True) + EPS)
    normed = (normed * gain_ref[...]).astype(jnp.bfloat16)
    normed_ref[...] = normed
    raw = jnp.dot(normed, weight_ref[:, :columns], preferred_element_type=jnp.float32)
    raw_ref[...] = raw
    turned_width = raw.shape[1] - pair_ref.shape[1] // 2
    heads = raw[:, :turned_width]
    heads = heads * lax.rsqrt(heads_apart(heads, dim) + EPS) * head_gain_ref[...]
    heads = turn(heads, cosine_ref[...], sine_ref[...], dim).astype(jnp.bfloat16)
    query_width = query_ref.shape[1]
    query_ref[...] = heads[:, :query_width]
    pair_ref[...] = jnp.concatenate(
        [heads[:, query_width:], raw[:, turned_width:].astype(jnp.bfloat16)], axis=1
    )


def project(own, x, weight, head_gain, cosine, sine, size, query_width, rows):
    count, width = x.shape
    out_width = weight.shape[1] - 128
    pair_width = out_width - query_width
    dim = cosine.shape[1]
    tiles = count // size // rows

    def apart(i, own):
        return ((own[0] ^ (i // tiles)) * tiles + i % tiles, 0)

    def there(i, own):
        return (i, 0)

    def whole(i, own):
        return (0, 0)

    return pl.pallas_call(
        functools.partial(project_kernel, dim),
        grid_spec=pltpu.PrefetchScalarGridSpec(
            num_scalar_prefetch=1,
            grid=(count // rows,),
            in_specs=[
                pl.BlockSpec((rows, width), there),
                pl.BlockSpec(weight.shape, whole),
                pl.BlockSpec(head_gain.shape, whole),
                pl.BlockSpec((rows, dim), apart),
                pl.BlockSpec((rows, dim), apart),
            ],
            out_specs=[
                pl.BlockSpec((rows, query_width), apart),
                pl.BlockSpec((rows, pair_width), apart),
                pl.BlockSpec((rows, out_width), apart),
                pl.BlockSpec((rows, width), there),
                pl.BlockSpec((1, width), whole),
                pl.BlockSpec((1, width), whole),
            ],
        ),
        out_shape=[
            jax.ShapeDtypeStruct((count, query_width), jnp.bfloat16),
            jax.ShapeDtypeStruct((count, pair_width), jnp.bfloat16),
            jax.ShapeDtypeStruct((count, out_width), jnp.float32),
            jax.ShapeDtypeStruct((count, width), jnp.bfloat16),
            jax.ShapeDtypeStruct((1, width), jnp.float32),
            jax.ShapeDtypeStruct((1, width), jnp.float32),
        ],
        compiler_params=pltpu.CompilerParams(vmem_limit_bytes=48 << 20),
        cost_estimate=pl.CostEstimate(
            flops=4 * count * width * out_width, bytes_accessed=30_000_000, transcendentals=0
        ),
        name="project",
    )(own, x, weight, head_gain, cosine, sine)


def project_back_kernel(
    dim, own_ref, query_grad_ref, pair_grad_ref, returned_ref, raw_ref, head_gain_ref, cosine_ref,
    sine_ref, grad_ref, gain_grad_ref
):
    @pl.when(pl.program_id(0) == 0)
    def _():
        gain_grad_ref[...] = jnp.zeros_like(gain_grad_ref)

    pair_grad = pair_grad_ref[...] + returned_ref[...].astype(jnp.float32)
    pair_grad = pair_grad.astype(jnp.bfloat16)
    half = pair_grad.shape[1] // 2
    grads = jnp.concatenate([query_grad_ref[...], pair_grad[:, :half]], axis=1).astype(jnp.float32)
    grads = turn(grads, cosine_ref[...], -sine_ref[...], dim)
    values = raw_ref[:, : grads.shape[1]]
    inverse = lax.rsqrt(heads_apart(values, dim) + EPS)
    gain_grad_ref[...] += jnp.sum(grads * values * inverse, axis=0, keepdims=True)
    scaled = grads * head_gain_ref[...]
    moment = spread_mean(scaled * values, dim)
    back = inverse * scaled - values * inverse * inverse * inverse * moment
    grad_ref[...] = jnp.concatenate([back.astype(jnp.bfloat16), pair_grad[:, half:]], axis=1)


def project_back(own, query_grad, pair_sum, returned, raw, head_gain, cosine, sine, size, rows):
    count, query_width = query_grad.shape
    pair_width = pair_sum.shape[1]
    out_width = raw.shape[1]
    dim = cosine.shape[1]
    tiles = count // size // rows

    def apart(i, own):
        return ((own[0] ^ (i // tiles)) * tiles + i % tiles, 0)

    def behind(i, own):
        return (apart(i, own)[0] + count // rows, 0)

    def whole(i, own):
        return (0, 0)

    return pl.pallas_call(
        functools.partial(project_back_kernel, dim),
        grid_spec=pltpu.PrefetchScalarGridSpec(
            num_scalar_prefetch=1,
            grid=(count // rows,),
            in_specs=[
                pl.BlockSpec((rows, query_width), apart),
                pl.BlockSpec((rows, pair_width), behind),
                pl.BlockSpec((rows, pair_width), apart),
                pl.BlockSpec((rows, out_width), apart),
                pl.BlockSpec(head_gain.shape, whole),
                pl.BlockSpec((rows, dim), apart),
                pl.BlockSpec((rows, dim), apart),
            ],
            out_specs=[
                pl.BlockSpec((rows, out_width), lambda i, own: (i, 0)),
                pl.BlockSpec(head_gain.shape, whole),
            ],
        ),
        out_shape=[
            jax.ShapeDtypeStruct((count, out_width), jnp.bfloat16),
            jax.ShapeDtypeStruct(head_gain.shape, jnp.float32),
        ],
        compiler_params=pltpu.CompilerParams(vmem_limit_bytes=48 << 20),
        cost_estimate=pl.CostEstimate(
            flops=8_000_000_000, bytes_accessed=8_000_000, transcendentals=0
        ),
        name="project_back",
    )(own, query_grad, pair_sum, returned, raw, head_gain, cosine, sine)


def join_kernel(half_tiles, x_ref, *refs):
    *part_refs, top_ref, bottom_ref, weight_ref, gain_ref, residual_ref, normed_ref = refs
    tile = pl.program_id(0)
    far = jnp.where((tile // half_tiles) % 2 == 1, top_ref[...], bottom_ref[...])
    attended = jnp.concatenate([ref[...] for ref in part_refs] + [far], axis=1)
    residual = x_ref[...].astype(jnp.float32) + jnp.dot(
        attended, weight_ref[...], preferred_element_type=jnp.float32
    )
    residual_ref[...] = residual
    normed = residual * lax.rsqrt(jnp.mean(residual * residual, axis=-1, keepdims=True) + EPS)
    normed_ref[...] = (normed * gain_ref[...]).astype(jnp.bfloat16)


def join(x, parts, top, bottom, weight, gain, rows):
    count, width = x.shape
    columns = parts[0].shape[1]
    tiles = count // 4 // rows

    def part_map(k):
        return lambda i: ((k ^ (i // tiles)) * tiles + i % tiles, 0)

    def far_map(i):
        return (((3 ^ (i // tiles)) % 2) * tiles + i % tiles, 0)

    def there(i):
        return (i, 0)

    def whole(i):
        return (0, 0)

    return pl.pallas_call(
        functools.partial(join_kernel, 2 * tiles),
        grid=(count // rows,),
        in_specs=[pl.BlockSpec((rows, width), there)]
        + [pl.BlockSpec((rows, columns), part_map(k)) for k in range(3)]
        + [pl.BlockSpec((rows, columns), far_map)] * 2
        + [pl.BlockSpec(weight.shape, whole), pl.BlockSpec((1, width), whole)],
        out_specs=[pl.BlockSpec((rows, width), there)] * 2,
        out_shape=[
            jax.ShapeDtypeStruct((count, width), jnp.float32),
            jax.ShapeDtypeStruct((count, width), jnp.bfloat16),
        ],
        compiler_params=pltpu.CompilerParams(vmem_limit_bytes=48 << 20),
        cost_estimate=pl.CostEstimate(
            flops=2 * count * width * weight.shape[0],
            bytes_accessed=50_000_000,
            transcendentals=0,
        ),
        name="join",
    )(x, *parts, top, bottom, weight, gain)


def settle_kernel(size, own_ref, *refs):
    *part_refs, out_ref = refs
    for k, part_ref in enumerate(part_refs):

        @pl.when(pl.program_id(0) % size == k)
        def _(part_ref=part_ref):
            out_ref[...] = part_ref[...].astype(out_ref.dtype)


def settle(own, parts, pieces):
    size = len(parts)
    rows, width = parts[0].shape
    piece = width // pieces
    return pl.pallas_call(
        functools.partial(settle_kernel, size),
        grid_spec=pltpu.PrefetchScalarGridSpec(
            num_scalar_prefetch=1,
            grid=(pieces * size,),
            in_specs=[pl.BlockSpec((rows, piece), lambda i, own: (0, i // size))] * size,
            out_specs=pl.BlockSpec(
                (rows, piece), lambda i, own: (0, i // size * size + (own[0] ^ (i % size)))
            ),
        ),
        out_shape=jax.ShapeDtypeStruct((rows, width * size), jnp.float32),
        name="settle",
    )(own, *parts)


def begin_kernel(
    x_ref, qkv_ref, in_ref, x_out, qkv_out, in_out, local_sem, x_send, x_recv, q_send, q_recv,
    w_send, w_recv, b_send, b_recv
):
    head, blk = lax.axis_index("heads"), lax.axis_index("blk")
    size, blk_size = lax.axis_size("heads"), lax.axis_size("blk")
    count, depth = x_ref.shape[0], qkv_ref.shape[1]
    half = count // 2
    units = in_out.shape[2] // 2
    barrier = pltpu.get_barrier_semaphore()
    for k in range(1, size):
        pl.semaphore_signal(barrier, inc=1, device_id=(head ^ k, blk), device_id_type=MESH)

    def greet(k, carried):
        pl.semaphore_signal(
            barrier, inc=1, device_id=(head, lax.rem(blk + k, blk_size)), device_id_type=MESH
        )
        return carried

    lax.fori_loop(1, blk_size, greet, 0)
    pl.semaphore_wait(barrier, size + blk_size - 2)

    def send(source, target, k, send_sem, recv_sem):
        return pltpu.make_async_remote_copy(
            src_ref=source,
            dst_ref=target,
            send_sem=send_sem,
            recv_sem=recv_sem,
            device_id=(head ^ k, blk),
            device_id_type=MESH,
        )

    rows = pl.ds(pl.multiple_of(blk * depth, depth), depth)
    qkv_copies = [
        send(
            qkv_ref.at[head ^ k], qkv_out.at[head, rows], k, q_send.at[k - 1], q_recv.at[k - 1]
        )
        for k in range(1, size)
    ]

    def columns(part, owner):
        return pl.ds(pl.multiple_of((part * size + owner) * units, units), units)

    in_copies = [
        send(
            in_ref.at[:, columns(part, head ^ k)],
            in_out.at[head, :, pl.ds(part * units, units)],
            k,
            w_send.at[2 * k - 2 + part],
            w_recv.at[2 * k - 2 + part],
        )
        for k in range(1, size)
        for part in range(2)
    ]
    near = [
        send(x_ref, x_out.at[pl.ds(k * count, count)], k, x_send.at[k - 1], x_recv.at[k - 1])
        for k in (1, 2)
    ]
    far = [
        send(
            x_out.at[pl.ds(count, half)],
            x_out.at[pl.ds(3 * count, half)],
            2,
            x_send.at[2],
            x_recv.at[2],
        ),
        send(
            x_out.at[pl.ds(2 * count + half, half)],
            x_out.at[pl.ds(3 * count + half, half)],
            1,
            x_send.at[3],
            x_recv.at[3],
        ),
    ]
    own = [
        pltpu.make_async_copy(qkv_ref.at[head], qkv_out.at[head, rows], local_sem.at[0]),
        pltpu.make_async_copy(x_ref, x_out.at[pl.ds(0, count)], local_sem.at[1]),
    ] + [
        pltpu.make_async_copy(
            in_ref.at[:, columns(part, head)],
            in_out.at[head, :, pl.ds(part * units, units)],
            local_sem.at[2 + part],
        )
        for part in range(2)
    ]
    for copy in qkv_copies + near + in_copies + own:
        copy.start()

    def along(k):
        return pltpu.make_async_remote_copy(
            src_ref=qkv_out.at[:, rows],
            dst_ref=qkv_out.at[:, rows],
            send_sem=b_send.at[k],
            recv_sem=b_recv.at[k],
            device_id=(head, lax.rem(blk + k, blk_size)),
            device_id_type=MESH,
        )

    def arrived(k):
        source = pl.ds(
            pl.multiple_of(lax.rem(blk + blk_size - k, blk_size) * depth, depth), depth
        )
        return pltpu.make_async_remote_copy(
            src_ref=qkv_out.at[:, rows],
            dst_ref=qkv_out.at[:, source],
            send_sem=b_send.at[k],
            recv_sem=b_recv.at[k],
            device_id=(head, lax.rem(blk + k, blk_size)),
            device_id_type=MESH,
        )

    def start(k, carried):
        along(k).start()
        return carried

    def finish(k, carried):
        along(k).wait_send()
        arrived(k).wait_recv()
        return carried

    own[0].wait()
    for copy in qkv_copies:
        copy.wait_recv()
    lax.fori_loop(1, blk_size, start, 0)
    for first, second in zip(near, far):
        first.wait_recv()
        second.start()
    for copy in qkv_copies + near:
        copy.wait_send()
    for copy in in_copies + far:
        copy.wait()
    for copy in own[1:]:
        copy.wait()
    lax.fori_loop(1, blk_size, finish, 0)


def begin(x, qkv_parts, in_weight):
    size, blk_size = lax.axis_size("heads"), lax.axis_size("blk")
    count, width = x.shape
    depth, joined = qkv_parts.shape[1:]
    anywhere = pl.BlockSpec(memory_space=pl.ANY)
    sems = pltpu.SemaphoreType.DMA
    return pl.pallas_call(
        begin_kernel,
        out_shape=[
            jax.ShapeDtypeStruct((size * count, width), x.dtype),
            jax.ShapeDtypeStruct((size, blk_size * depth, joined), x.dtype),
            jax.ShapeDtypeStruct((size, depth, in_weight.shape[1] // size), x.dtype),
        ],
        in_specs=[anywhere] * 3,
        out_specs=[anywhere] * 3,
        scratch_shapes=[
            sems((4,)),
            sems((4,)),
            sems((4,)),
            sems((size - 1,)),
            sems((size - 1,)),
            sems((2 * size - 2,)),
            sems((2 * size - 2,)),
            sems((blk_size,)),
            sems((blk_size,)),
        ],
        compiler_params=pltpu.CompilerParams(collective_id=1, has_side_effects=True),
        name="begin",
    )(x, qkv_parts, in_weight)


def spread_copies(source_ref, target_ref, send_sem, recv_sem):
    head, blk = lax.axis_index("heads"), lax.axis_index("blk")
    rows = source_ref.shape[0] // 2
    quarter = rows // 2
    start = pl.multiple_of(lax.rem(blk, 2) * rows, rows)
    half = pl.ds(start, rows)
    count = [0]

    def copy(source, target, place):
        index = count[0]
        count[0] += 1
        return pltpu.make_async_remote_copy(
            src_ref=source,
            dst_ref=target,
            send_sem=send_sem.at[index],
            recv_sem=recv_sem.at[index],
            device_id=place,
            device_id_type=MESH,
        )

    near = [
        copy(source_ref.at[half], target_ref.at[k - 1, half], (head ^ k, blk)) for k in (1, 2)
    ]
    upper = pl.ds(start, quarter)
    lower = pl.ds(pl.multiple_of(start + quarter, quarter), quarter)
    far = [
        copy(target_ref.at[0, upper], target_ref.at[2, upper], (head ^ 2, blk)),
        copy(target_ref.at[1, lower], target_ref.at[2, lower], (head ^ 1, blk)),
    ]
    other = [
        copy(target_ref.at[k, half], target_ref.at[k, half], (head, blk ^ 1)) for k in range(3)
    ]
    return near, far, other


def greet_near(partner):
    head, blk = lax.axis_index("heads"), lax.axis_index("blk")
    barrier = pltpu.get_barrier_semaphore()
    places = [(head ^ 1, blk), (head ^ 2, blk)] + ([(head, blk ^ 1)] if partner else [])
    for place in places:
        pl.semaphore_signal(barrier, inc=1, device_id=place, device_id_type=MESH)
    pl.semaphore_wait(barrier, len(places))


def spread_job(step, marks, source_ref, target_ref, send_sem, recv_sem):
    near, far, other = spread_copies(source_ref, target_ref, send_sem, recv_sem)
    begin_at, far_at, other_at = marks

    @pl.when(step == begin_at)
    def _():
        greet_near(True)
        for copy in near:
            copy.start()

    @pl.when(step == far_at)
    def _():
        for k in range(2):
            near[k].wait_recv()
            far[k].start()
            other[k].start()

    @pl.when(step == other_at)
    def _():
        for copy in far:
            copy.wait_recv()
        other[2].start()

    def end():
        for copy in near + far:
            copy.wait_send()
        for copy in other:
            copy.wait()

    return end


SPREAD_COUNT = 7


def hidden_kernel(
    normed_ref, gate_ref, up_ref, cot_ref, down_ref, side_ref, hidden_ref, gate_grad_ref,
    up_grad_ref, spread_ref, send_sem, recv_sem
):
    steps = pl.num_programs(0) * pl.num_programs(1)
    step = pl.program_id(0) * pl.num_programs(1) + pl.program_id(1)
    marks = (0, steps // 2, steps - 2)
    end = spread_job(step, marks, side_ref, spread_ref, send_sem, recv_sem)
    normed = normed_ref[...]
    gate = jnp.dot(normed, gate_ref[...], preferred_element_type=jnp.float32)
    upward = jnp.dot(normed, up_ref[...], preferred_element_type=jnp.float32)
    grad = lax.dot_general(
        cot_ref[...], down_ref[...], ROWS_IN_BOTH, preferred_element_type=jnp.float32
    )
    sigmoid = jax.nn.sigmoid(gate)
    activated = gate * sigmoid
    hidden_ref[...] = (activated * upward).astype(jnp.bfloat16)
    gate_grad_ref[...] = (grad * upward * sigmoid * (1.0 + gate * (1.0 - sigmoid))).astype(
        jnp.bfloat16
    )
    up_grad_ref[...] = (grad * activated).astype(jnp.bfloat16)
    pl.when(step == steps - 1)(end)


def hidden_pass(normed, weight, cot, down, side, rows, units):
    count, width = normed.shape
    total = down.shape[0]
    tiles = total // units
    out_spec = pl.BlockSpec((rows, units), lambda i, j: (i, j))
    out_shape = jax.ShapeDtypeStruct((count, total), jnp.bfloat16)
    anywhere = pl.BlockSpec(memory_space=pl.ANY)
    return pl.pallas_call(
        hidden_kernel,
        grid=(count // rows, tiles),
        in_specs=[
            pl.BlockSpec((rows, width), lambda i, j: (i, 0)),
            pl.BlockSpec((width, units), lambda i, j: (0, j)),
            pl.BlockSpec((width, units), lambda i, j: (0, tiles + j)),
            pl.BlockSpec((rows, width), lambda i, j: (i, 0)),
            pl.BlockSpec((units, width), lambda i, j: (j, 0)),
            anywhere,
        ],
        out_specs=[out_spec] * 3 + [anywhere],
        out_shape=[out_shape] * 3 + [jax.ShapeDtypeStruct((3, *side.shape), side.dtype)],
        scratch_shapes=[pltpu.SemaphoreType.DMA((SPREAD_COUNT,))] * 2,
        compiler_params=pltpu.CompilerParams(
            collective_id=2, has_side_effects=True, vmem_limit_bytes=58 << 20
        ),
        cost_estimate=pl.CostEstimate(
            flops=6 * count * width * total, bytes_accessed=70_000_000, transcendentals=0
        ),
        name="hidden_pass",
    )(normed, weight, weight, cot, down, side)


def in_order(step):
    value = 3
    for index, half in enumerate((2, 6, 5, 7, 0, 1, 4)):
        value = jnp.where(step == index, half, value)
    return value


def tail_kernel(
    normed_ref, gate_ref, up_ref, hidden_ref, in_hbm, down_hbm, in_sum_ref, out_ref, grad_ref,
    weight_ref, one_ref, two_ref, rest_ref, top_ref, bottom_ref, last_ref, last_got_ref,
    weight_sem, send_sem, recv_sem
):
    step = pl.program_id(0)
    head, blk = lax.axis_index("heads"), lax.axis_index("blk")
    rows, total = hidden_ref.shape
    width = grad_ref.shape[1]
    load_in = pltpu.make_async_copy(in_hbm, weight_ref, weight_sem.at[0])
    load_down = pltpu.make_async_copy(
        down_hbm, weight_ref.at[pl.ds(0, total), pl.ds(0, width)], weight_sem.at[1]
    )

    def copy(source, target, k, index):
        return pltpu.make_async_remote_copy(
            src_ref=source,
            dst_ref=target,
            send_sem=send_sem.at[index],
            recv_sem=recv_sem.at[index],
            device_id=(head ^ k, blk),
            device_id_type=MESH,
        )

    send_one = copy(one_ref, top_ref, 1, 0)
    send_two = copy(two_ref, bottom_ref, 2, 1)
    send_top = copy(last_ref.at[0], last_got_ref.at[0], 2, 2)
    send_bottom = copy(last_ref.at[1], last_got_ref.at[1], 1, 3)

    def wide_of(block):
        return block.astype(jnp.float32)

    @pl.when(step == 0)
    def _():
        load_in.start()
        greet_near(False)
        load_in.wait()

    @pl.when(step < 8)
    def _():
        here = pl.ds(pl.multiple_of(in_order(step) * rows, rows), rows)
        value = lax.dot_general(
            gate_ref[here], weight_ref[:, :total], ROWS_IN_BOTH, preferred_element_type=jnp.float32
        ) + lax.dot_general(
            up_ref[here], weight_ref[:, total:], ROWS_IN_BOTH, preferred_element_type=jnp.float32
        )
        value = value.astype(jnp.bfloat16)

        def rows_from(first):
            return pl.ds(pl.multiple_of((step - first) * rows, rows), rows)

        @pl.when(step < 2)
        def _():
            one_ref[rows_from(0)] = value

        @pl.when((step >= 2) & (step < 4))
        def _():
            two_ref[rows_from(2)] = value

        @pl.when(step >= 4)
        def _():
            rest_ref[rows_from(4)] = value

        @pl.when(step == 1)
        def _():
            send_one.start()

        @pl.when(step == 3)
        def _():
            send_two.start()

        @pl.when(step == 7)
        def _():
            load_down.start()

    @pl.when((step >= 8) & (step < 16))
    def _():
        for part, ref in enumerate((gate_ref, up_ref)):
            in_sum_ref[:, part * total : (part + 1) * total] = lax.dot_general(
                normed_ref[...], ref[...], (((0,), (0,)), ((), ())),
                preferred_element_type=jnp.float32,
            ).astype(jnp.bfloat16)

        @pl.when(step == 13)
        def _():
            send_one.wait_recv()
            last_ref[0] = (
                wide_of(rest_ref[2 * rows : 3 * rows]) + wide_of(top_ref[rows:])
            ).astype(jnp.bfloat16)
            send_top.start()

        @pl.when(step == 15)
        def _():
            send_two.wait_recv()
            last_ref[1] = (wide_of(rest_ref[3 * rows :]) + wide_of(bottom_ref[rows:])).astype(
                jnp.bfloat16
            )
            send_bottom.start()
            load_down.wait()

    @pl.when(step >= 16)
    def _():
        out_ref[...] = jnp.dot(
            hidden_ref[...], weight_ref[:total, :width], preferred_element_type=jnp.float32
        ).astype(jnp.bfloat16)

    @pl.when(step == pl.num_programs(0) - 1)
    def _():
        send_top.wait_recv()
        send_bottom.wait_recv()
        grad_ref[:rows] = (
            wide_of(rest_ref[:rows]) + wide_of(top_ref[:rows]) + wide_of(last_got_ref[0])
        )
        grad_ref[rows:] = (
            wide_of(rest_ref[rows : 2 * rows]) + wide_of(bottom_ref[:rows]) + wide_of(last_got_ref[1])
        )
        for sent in (send_one, send_two, send_top, send_bottom):
            sent.wait_send()


def feed_tail(normed, gate_grad, up_grad, hidden, weight, down):
    count, width = normed.shape
    total = hidden.shape[1]
    rows = count // 8
    anywhere = pl.BlockSpec(memory_space=pl.ANY)
    once = pl.Buffered(1)

    def stage(i, first):
        return jnp.clip(i - first, 0, 7)

    low = jnp.bfloat16
    return pl.pallas_call(
        tail_kernel,
        grid=(24,),
        in_specs=[
            pl.BlockSpec((count, rows), lambda i: (0, stage(i, 8))),
            pl.BlockSpec((count, total), lambda i: (0, 0), pipeline_mode=once),
            pl.BlockSpec((count, total), lambda i: (0, 0), pipeline_mode=once),
            pl.BlockSpec((rows, total), lambda i: (in_order(stage(i, 16)), 0)),
            anywhere,
            anywhere,
        ],
        out_specs=[
            pl.BlockSpec((rows, 2 * total), lambda i: (stage(i, 8), 0)),
            pl.BlockSpec((rows, width), lambda i: (stage(i, 16), 0)),
            pl.BlockSpec((2 * rows, width), lambda i: (0, 0), pipeline_mode=once),
        ],
        out_shape=[
            jax.ShapeDtypeStruct((width, 2 * total), low),
            jax.ShapeDtypeStruct((count, width), low),
            jax.ShapeDtypeStruct((2 * rows, width), jnp.float32),
        ],
        scratch_shapes=[
            pltpu.VMEM(weight.shape, low),
            pltpu.VMEM((2 * rows, width), low),
            pltpu.VMEM((2 * rows, width), low),
            pltpu.VMEM((4 * rows, width), low),
            pltpu.VMEM((2 * rows, width), low),
            pltpu.VMEM((2 * rows, width), low),
            pltpu.VMEM((2, rows, width), low),
            pltpu.VMEM((2, rows, width), low),
            pltpu.SemaphoreType.DMA((2,)),
            pltpu.SemaphoreType.DMA((4,)),
            pltpu.SemaphoreType.DMA((4,)),
        ],
        compiler_params=pltpu.CompilerParams(
            collective_id=3, has_side_effects=True, vmem_limit_bytes=60 << 20
        ),
        cost_estimate=pl.CostEstimate(
            flops=10 * count * width * total, bytes_accessed=70_000_000, transcendentals=0
        ),
        name="feed_tail",
    )(normed, gate_grad, up_grad, hidden, weight, down)


def residual_back_kernel(
    grad_sum_ref, residual_ref, cot_ref, gain_ref, attended_ref, *refs
):
    size = lax.axis_size("heads")
    weight_refs, refs = refs[:size], refs[size:]
    (
        grad_ref, gain_grad_ref, out_sum_ref, pieces_ref, branch_ref, mine_ref, own_sem, send_sem,
        recv_sem,
    ) = refs
    step = pl.program_id(0)
    last = pl.num_programs(0) - 1
    head, blk = lax.axis_index("heads"), lax.axis_index("blk")
    rows = cot_ref.shape[0]
    copies = [
        pltpu.make_async_remote_copy(
            src_ref=mine_ref.at[k],
            dst_ref=pieces_ref.at[k],
            send_sem=send_sem.at[k - 1],
            recv_sem=recv_sem.at[k - 1],
            device_id=(head ^ k, blk),
            device_id_type=MESH,
        )
        for k in range(1, size)
    ]
    keep = pltpu.make_async_copy(mine_ref.at[0], pieces_ref.at[0], own_sem)

    @pl.when(step == 0)
    def _():
        gain_grad_ref[...] = jnp.zeros_like(gain_grad_ref)
        barrier = pltpu.get_barrier_semaphore()
        for k in range(1, size):
            pl.semaphore_signal(barrier, inc=1, device_id=(head ^ k, blk), device_id_type=MESH)
        pl.semaphore_wait(barrier, size - 1)

    @pl.when(step < last)
    def _():
        here = pl.ds(pl.multiple_of(step * rows, rows), rows)
        gradient = grad_sum_ref[...]
        values = residual_ref[...]
        inverse = lax.rsqrt(jnp.mean(values * values, axis=-1, keepdims=True) + EPS)
        gain_grad_ref[...] += jnp.sum(gradient * values * inverse, axis=0, keepdims=True)
        scaled = gradient * gain_ref[...]
        moment = jnp.mean(scaled * values, axis=-1, keepdims=True)
        total = cot_ref[...].astype(jnp.float32) + (
            inverse * scaled - values * (inverse * inverse * inverse * moment)
        )
        grad_ref[...] = total
        branch = total.astype(jnp.bfloat16)
        branch_ref[here] = branch
        for k, weight_ref in enumerate(weight_refs):
            mine_ref[k, here] = lax.dot_general(
                branch, weight_ref[...], ROWS_IN_BOTH, preferred_element_type=jnp.float32
            ).astype(jnp.bfloat16)

    @pl.when(step == last)
    def _():
        for copy in copies:
            copy.start()
        keep.start()
        columns = attended_ref.shape[1] // size
        for k in range(size):
            out_sum_ref[k * columns : (k + 1) * columns] = lax.dot_general(
                attended_ref[:, k * columns : (k + 1) * columns],
                branch_ref[...],
                (((0,), (0,)), ((), ())),
                preferred_element_type=jnp.float32,
            ).astype(jnp.bfloat16)
        for copy in copies:
            copy.wait()
        keep.wait()


def residual_back(grad_sum, residual, cot, gain, attended, weights, rows):
    count, width = cot.shape
    size = len(weights)
    columns = weights[0].shape[0]
    tiles = count // rows

    def there(i):
        return (jnp.minimum(i, tiles - 1), 0)

    def whole(i):
        return (0, 0)

    tile = pl.BlockSpec((rows, width), there)
    row = pl.BlockSpec((1, width), whole)
    pieces = (size, count, columns)
    return pl.pallas_call(
        residual_back_kernel,
        grid=(tiles + 1,),
        in_specs=[tile, tile, tile, row, pl.BlockSpec(attended.shape, whole)]
        + [pl.BlockSpec(weight.shape, whole) for weight in weights],
        out_specs=[
            tile,
            row,
            pl.BlockSpec((size * columns, width), whole),
            pl.BlockSpec(memory_space=pl.ANY),
        ],
        out_shape=[
            jax.ShapeDtypeStruct((count, width), jnp.float32),
            jax.ShapeDtypeStruct((1, width), jnp.float32),
            jax.ShapeDtypeStruct((size * columns, width), jnp.bfloat16),
            jax.ShapeDtypeStruct(pieces, jnp.bfloat16),
        ],
        scratch_shapes=[
            pltpu.VMEM((count, width), jnp.bfloat16),
            pltpu.VMEM(pieces, jnp.bfloat16),
            pltpu.SemaphoreType.DMA,
            pltpu.SemaphoreType.DMA((size - 1,)),
            pltpu.SemaphoreType.DMA((size - 1,)),
        ],
        compiler_params=pltpu.CompilerParams(
            collective_id=4, has_side_effects=True, vmem_limit_bytes=56 << 20
        ),
        cost_estimate=pl.CostEstimate(
            flops=4 * count * width * columns * size, bytes_accessed=30_000_000, transcendentals=0
        ),
        name="residual_back",
    )(grad_sum, residual, cot, gain, attended, *weights)


def turned_kernel(left_ref, right_ref, out_ref):
    out_ref[...] = lax.dot_general(
        left_ref[...], right_ref[...], (((0,), (0,)), ((), ())), preferred_element_type=jnp.float32
    ).astype(out_ref.dtype)


def turned_product(left, right, rows):
    count, height = left.shape
    width = right.shape[1]
    return pl.pallas_call(
        turned_kernel,
        grid=(height // rows,),
        in_specs=[
            pl.BlockSpec((count, rows), lambda i: (0, i)),
            pl.BlockSpec((count, width), lambda i: (0, 0)),
        ],
        out_specs=pl.BlockSpec((rows, width), lambda i: (i, 0)),
        out_shape=jax.ShapeDtypeStruct((height, width), jnp.bfloat16),
        compiler_params=pltpu.CompilerParams(vmem_limit_bytes=58 << 20),
        cost_estimate=pl.CostEstimate(
            flops=2 * count * height * width, bytes_accessed=20_000_000, transcendentals=0
        ),
        name="turned_product",
    )(left, right)


def finish_kernel(
    query_width, dim, sent_ref, qkv_ref, x_ref, residual_ref, gain_ref, ffn_ref, head_ref,
    weight_ref, weights_ref, *refs
):
    size, blk_size = lax.axis_size("heads"), lax.axis_size("blk")
    out_refs, refs = refs[:size], refs[size:]
    (
        grad_ref, qkv_grad_ref, gains_ref, out_grad_ref, got_ref, qkv_got_ref, part_ref,
        gain_got_ref, out_part_ref, out_got_ref, s_send, s_recv, q_send, q_recv, g_send, g_recv,
        o_send, o_recv,
    ) = refs
    devices = size * blk_size
    head, blk = lax.axis_index("heads"), lax.axis_index("blk")
    own = head * blk_size + blk
    count, width = x_ref.shape
    depth = width // devices
    barrier = pltpu.get_barrier_semaphore()

    def place_of(index):
        return (index // blk_size, lax.rem(index, blk_size))

    def greet(k, carried):
        pl.semaphore_signal(
            barrier, inc=1, device_id=place_of(lax.rem(own + k, devices)), device_id_type=MESH
        )
        return carried

    lax.fori_loop(1, devices, greet, 0)
    pl.semaphore_wait(barrier, devices - 1)

    sends = [
        pltpu.make_async_remote_copy(
            src_ref=sent_ref.at[pl.ds(k * count, count)],
            dst_ref=got_ref.at[k - 1],
            send_sem=s_send.at[k - 1],
            recv_sem=s_recv.at[k - 1],
            device_id=(head ^ k, blk),
            device_id_type=MESH,
        )
        for k in range(1, size)
    ]
    for copy in sends:
        copy.start()

    def rows_of(index):
        return pl.ds(pl.multiple_of(index * depth, depth), depth)

    def qkv_copy(k, slot):
        other = lax.rem(own + k, devices)
        return pltpu.make_async_remote_copy(
            src_ref=qkv_ref.at[rows_of(other)],
            dst_ref=qkv_got_ref.at[slot],
            send_sem=q_send.at[k],
            recv_sem=q_recv.at[slot],
            device_id=place_of(other),
            device_id_type=MESH,
        )

    out_rows = out_grad_ref.shape[0]

    def out_copy(k, slot):
        other = lax.rem(blk + k, blk_size)
        return pltpu.make_async_remote_copy(
            src_ref=out_part_ref.at[other],
            dst_ref=out_got_ref.at[slot],
            send_sem=o_send.at[k],
            recv_sem=o_recv.at[slot],
            device_id=(head, other),
            device_id_type=MESH,
        )

    def gain_copy(k, slot):
        other = lax.rem(own + k, devices)
        return pltpu.make_async_remote_copy(
            src_ref=part_ref.at[other],
            dst_ref=gain_got_ref.at[slot],
            send_sem=g_send.at[k],
            recv_sem=g_recv.at[slot],
            device_id=place_of(other),
            device_id_type=MESH,
        )

    def start_qkv(k, carried):
        qkv_copy(k, own).start()
        return carried

    lax.fori_loop(1, devices, start_qkv, 0)
    qkv_got_ref[own] = qkv_ref[rows_of(own)]

    def out_sum(index, carried):
        here = pl.ds(pl.multiple_of(index * out_rows, out_rows), out_rows)
        total = out_refs[0][here].astype(jnp.float32)
        for ref in out_refs[1:]:
            total += ref[here].astype(jnp.float32)
        out_part_ref[index, :out_rows] = total.astype(jnp.bfloat16)
        return carried

    lax.fori_loop(0, blk_size, out_sum, 0)

    def start_out(k, carried):
        out_copy(k, blk).start()
        return carried

    lax.fori_loop(1, blk_size, start_out, 0)
    out_got_ref[blk] = out_part_ref[blk]
    for copy in sends:
        copy.wait_recv()

    rows = min(128, count)

    def tile(index, gain_sum):
        here = pl.ds(pl.multiple_of(index * rows, rows), rows)
        normed_grad = lax.dot_general(
            sent_ref[here], weight_ref[...], ROWS_IN_BOTH, preferred_element_type=jnp.float32
        )
        for k in range(1, size):
            normed_grad += lax.dot_general(
                got_ref[k - 1, here],
                weights_ref[k - 1],
                ROWS_IN_BOTH,
                preferred_element_type=jnp.float32,
            )
        values = x_ref[here].astype(jnp.float32)
        inverse = lax.rsqrt(jnp.mean(values * values, axis=-1, keepdims=True) + EPS)
        scaled = normed_grad * gain_ref[...]
        moment = jnp.mean(scaled * values, axis=-1, keepdims=True)
        grad_ref[here] = (
            residual_ref[here]
            + inverse * scaled
            - values * (inverse * inverse * inverse * moment)
        )
        return gain_sum + jnp.sum(normed_grad * values * inverse, axis=0, keepdims=True)

    attn_sum = lax.fori_loop(0, count // rows, tile, jnp.zeros((1, width), jnp.float32))

    def by_device(row):
        lanes = jnp.concatenate(
            [row[:, d * depth : (d + 1) * depth] for d in range(devices)], axis=0
        )
        if depth < 64:
            lanes = jnp.concatenate(
                [lanes, jnp.zeros((devices, 64 - depth), jnp.float32)], axis=1
            )
        return lanes

    head_row = head_ref[...]
    query_sum = head_row[:, :dim]
    for c in range(dim, query_width, dim):
        query_sum += head_row[:, c : c + dim]
    key_sum = head_row[:, query_width : query_width + dim]
    for c in range(query_width + dim, head_row.shape[1], dim):
        key_sum += head_row[:, c : c + dim]
    both = jnp.concatenate([query_sum, key_sum], axis=1)
    part_ref[...] = jnp.zeros_like(part_ref)
    part_ref[:, 0, :] = jnp.concatenate([by_device(attn_sum), by_device(ffn_ref[...])], axis=1)
    part_ref[:, 1, :] = jnp.broadcast_to(both, (devices, 2 * dim))

    def start_gain(k, carried):
        gain_copy(k, own).start()
        return carried

    lax.fori_loop(1, devices, start_gain, 0)
    gain_got_ref[own] = part_ref[own]

    def finish(k, carried):
        source = lax.rem(own + devices - k, devices)
        qkv_copy(k, source).wait()
        gain_copy(k, source).wait()
        return carried

    lax.fori_loop(1, devices, finish, 0)

    def finish_out(k, carried):
        out_copy(k, lax.rem(blk + blk_size - k, blk_size)).wait()
        return carried

    lax.fori_loop(1, blk_size, finish_out, 0)
    for copy in sends:
        copy.wait_send()
    out_total = out_got_ref[0, :out_rows].astype(jnp.float32)
    for b in range(1, blk_size):
        out_total += out_got_ref[b, :out_rows].astype(jnp.float32)
    out_grad_ref[...] = out_total
    gains_ref[...] = jnp.sum(gain_got_ref[...], axis=0)

    def group_sum(h):
        total = qkv_got_ref[h * blk_size].astype(jnp.float32)
        for b in range(1, blk_size):
            total += qkv_got_ref[h * blk_size + b].astype(jnp.float32)
        return total

    sums = [group_sum(h) for h in range(size)]
    key_end = query_width + (sums[0].shape[1] - query_width) // 2
    qkv_grad_ref[...] = jnp.concatenate(
        [total[:, :query_width] for total in sums]
        + [total[:, query_width:key_end] for total in sums]
        + [total[:, key_end:] for total in sums],
        axis=1,
    )


def finish(
    sent, qkv_part, x, residual_grad, gain, ffn_sum, head_sum, weight, weights, outs, query_width, dim
):
    size, blk_size = lax.axis_size("heads"), lax.axis_size("blk")
    devices = size * blk_size
    count, width = x.shape
    depth, joined = width // devices, sent.shape[1]
    out_rows = outs[0].shape[0] // blk_size
    held_rows = -(-out_rows // 16) * 16
    vmem = pl.BlockSpec(memory_space=pltpu.VMEM)
    sems = pltpu.SemaphoreType.DMA
    return pl.pallas_call(
        functools.partial(finish_kernel, query_width, dim),
        out_shape=[
            jax.ShapeDtypeStruct((count, width), jnp.float32),
            jax.ShapeDtypeStruct((depth, size * joined), jnp.float32),
            jax.ShapeDtypeStruct((8, 128), jnp.float32),
            jax.ShapeDtypeStruct((out_rows, width), jnp.float32),
        ],
        in_specs=[vmem] * (9 + size),
        out_specs=[vmem] * 4,
        scratch_shapes=[
            pltpu.VMEM((size - 1, count, joined), jnp.bfloat16),
            pltpu.VMEM((devices, depth, joined), jnp.bfloat16),
            pltpu.VMEM((devices, 8, 128), jnp.float32),
            pltpu.VMEM((devices, 8, 128), jnp.float32),
            pltpu.VMEM((blk_size, held_rows, width), jnp.bfloat16),
            pltpu.VMEM((blk_size, held_rows, width), jnp.bfloat16),
            sems((size - 1,)),
            sems((size - 1,)),
            sems((devices,)),
            sems((devices,)),
            sems((devices,)),
            sems((devices,)),
            sems((blk_size,)),
            sems((blk_size,)),
        ],
        compiler_params=pltpu.CompilerParams(
            collective_id=0, has_side_effects=True, vmem_limit_bytes=56 << 20
        ),
        name="finish",
    )(sent, qkv_part, x, residual_grad, gain, ffn_sum, head_sum, weight, weights, *outs)


def permute(block, axis, k):
    return lax.ppermute(block, axis, [(i, i ^ k) for i in range(lax.axis_size(axis))])


def after(value, *done):
    return lax.optimization_barrier((value, *done))[0]


def pick(block, k, axis, dim):
    extent = block.shape[dim] // lax.axis_size(axis)
    return lax.dynamic_slice_in_dim(block, (lax.axis_index(axis) ^ k) * extent, extent, dim)


def gather_near(block, *done):
    half = block.shape[0] // 2
    one, two = permute(block, "heads", 1), permute(block, "heads", 2)
    if done:
        one, two = lax.optimization_barrier((one, two, *done))[:2]
    top = permute(one[:half], "heads", 2)
    bottom = permute(two[half:], "heads", 1)
    return block, one, two, top, bottom


def wide(block):
    return block.astype(jnp.float32)


def local(
    inputs,
    positions,
    attn_gain,
    qkv_weight,
    q_gain,
    k_gain,
    out_weight,
    ffn_gain,
    ffn_in_weight,
    ffn_out_weight,
    cotangent,
):
    token_count, width = inputs.shape
    depth = qkv_weight.shape[0]
    head_dim = q_gain.shape[0]
    group_size = HEADS // KV_HEADS
    size = lax.axis_size("heads")
    blk_size = lax.axis_size("blk")
    query_all, key_all = HEADS * head_dim, KV_HEADS * head_dim
    query_width, key_width = query_all // size, key_all // size
    qkv_width = query_width + 2 * key_width
    block_len = token_count * size
    half = token_count // 2
    own = lax.axis_index("heads").astype(jnp.int32).reshape(1)

    qkv_parts = jnp.concatenate(
        [
            qkv_weight[:, :query_all].reshape(depth, size, query_width),
            qkv_weight[:, query_all : query_all + key_all].reshape(depth, size, key_width),
            qkv_weight[:, query_all + key_all :].reshape(depth, size, key_width),
            jnp.broadcast_to(attn_gain[:, None, None], (depth, size, 64)),
            jnp.broadcast_to(ffn_gain[:, None, None], (depth, size, 64)),
        ],
        axis=-1,
    ).transpose(1, 0, 2)
    out_group = lax.all_gather(out_weight, "blk", axis=0, tiled=True)
    down_group = lax.all_gather(ffn_out_weight, "blk", axis=0, tiled=True)

    inputs_blk, qkv_rows, in_rows = begin(inputs, qkv_parts, ffn_in_weight)
    in_group = lax.all_gather(in_rows, "blk", axis=1, tiled=True).reshape(width, -1)
    qkv_rows = qkv_rows.reshape(width, -1)
    cosine, sine = rotation(positions, head_dim)
    cosine = jnp.concatenate([cosine[:, 0], cosine[:, 0]], axis=-1)
    sine = jnp.concatenate([-sine[:, 0], sine[:, 0]], axis=-1)
    head_gain = jnp.concatenate(
        [jnp.tile(q_gain, HEADS // size), jnp.tile(k_gain, KV_HEADS // size)]
    ).astype(jnp.float32)[None, :]
    query_low, pair_blk, raw, normed, attn_scaling, ffn_scaling = project(
        own, inputs_blk, qkv_rows, head_gain, cosine, sine, size, query_width, 256
    )
    pair_all = jnp.concatenate([from_behind(pair_blk, "blk", 1), pair_blk], axis=0)
    query_rows, key_rows = token_count, 256
    low = block_len + jnp.arange(block_len, dtype=jnp.int32) - positions
    first = jnp.concatenate([low[::query_rows] // key_rows, own])
    low = low[None, :]
    attended_blk, logs = attend(query_low, pair_all, first, low, group_size, query_rows, key_rows)

    mine = jnp.concatenate([pick(attended_blk, k, "heads", 0) for k in range(size)], axis=0)
    out_near = gather_near(after(out_group, inputs_blk))
    out_all = (*out_near[:3], jnp.concatenate(out_near[3:], axis=0))
    near = gather_near(mine)
    residual, ffn_normed = join(
        inputs_blk, near[:3], *near[3:], jnp.concatenate(out_all, axis=0), ffn_scaling, 256
    )
    residual_own = residual[:token_count]
    cotangent_near = gather_near(after(cotangent, inputs_blk), near[1])
    cotangent_blk = jnp.concatenate(cotangent_near, axis=0)

    qkv_group = qkv_rows[:, :qkv_width]
    hidden, gate_grad, up_grad, qkv_peers = hidden_pass(
        ffn_normed, in_group, cotangent_blk, down_group, qkv_group, block_len // 2, 256
    )
    down_sum = turned_product(hidden, cotangent_blk, 256)
    ffn_out_grad = lax.psum_scatter(down_sum, "blk", scatter_dimension=0, tiled=True)
    in_sum, out_terms, grad_sum = feed_tail(
        ffn_normed, gate_grad, up_grad, after(hidden, down_sum), in_group, down_group
    )
    in_sum, ffn_out_grad = lax.optimization_barrier((in_sum, ffn_out_grad))
    in_part = lax.psum_scatter(
        in_sum.reshape(size, blk_size * depth, -1), "blk", scatter_dimension=1, tiled=True
    )
    ffn_out_grad = wide(ffn_out_grad)
    attended_own = jnp.concatenate(
        [
            near[0][:token_count],
            near[1][token_count : 2 * token_count],
            near[2][2 * token_count : 3 * token_count],
            near[4][token_count:],
        ],
        axis=1,
    )
    residual_grad, ffn_sum, out_sum, grads = residual_back(
        grad_sum, residual_own, cotangent, ffn_scaling, attended_own, out_all, min(128, half)
    )
    out_one, out_two, out_rest = (
        out_terms[: 2 * half],
        out_terms[2 * half : 4 * half],
        out_terms[4 * half :],
    )
    out_one, out_two, grads = lax.optimization_barrier((out_one, out_two, grads))
    out_top, out_bottom = permute(out_one, "heads", 1), permute(out_two, "heads", 2)
    out_slices = [out_sum[k * query_width : (k + 1) * query_width] for k in range(size)]
    out_slices = [out_slices[0]] + [permute(out_slices[k], "heads", k) for k in range(1, size)]
    query_grad, pair_sum = attend_back(
        query_low, pair_all, first, low, grads, attended_blk, logs, group_size, query_rows, key_rows
    )
    returned = from_behind(pair_sum[:block_len].astype(jnp.bfloat16), "blk", -1)
    out_top, out_bottom, returned = lax.optimization_barrier((out_top, out_bottom, returned))
    top_send = (wide(out_rest[2 * half : 3 * half]) + wide(out_top[half:])).astype(jnp.bfloat16)
    bottom_send = (wide(out_rest[3 * half :]) + wide(out_bottom[half:])).astype(jnp.bfloat16)
    out_top_last = permute(top_send, "heads", 2)
    out_bottom_last = permute(bottom_send, "heads", 1)
    layer_out = jnp.concatenate(
        [
            residual_own[:half] + wide(out_rest[:half]) + wide(out_top[:half]) + wide(out_top_last),
            residual_own[half:]
            + wide(out_rest[half : 2 * half])
            + wide(out_bottom[:half])
            + wide(out_bottom_last),
        ],
        axis=0,
    ).astype(jnp.bfloat16)

    projected_grad, head_sum = project_back(
        own, query_grad, pair_sum, returned, raw, head_gain, cosine, sine, size, 256
    )
    qkv_part = turned_product(normed, projected_grad, 512)
    input_grad, qkv_grad, gains, out_grad = finish(
        projected_grad, qkv_part, inputs, residual_grad, attn_scaling, ffn_sum, head_sum, qkv_group,
        qkv_peers, out_slices, query_width, head_dim
    )
    in_pieces = [pick(in_part, k, "heads", 0)[0] for k in range(size)]
    ffn_in_grad = settle(
        own,
        [in_pieces[0]] + [permute(in_pieces[k], "heads", k) for k in range(1, size)],
        2,
    )
    return (
        layer_out,
        input_grad,
        gains[0, :depth],
        qkv_grad,
        gains[1, :head_dim],
        gains[1, head_dim : 2 * head_dim],
        out_grad,
        gains[0, 64 : 64 + depth],
        ffn_in_grad,
        ffn_out_grad,
    )


def solution(mesh):
    placed = (
        P(("blk", "heads"), None),
        P("blk"),
        P(("heads", "blk")),
        P(("heads", "blk"), None),
        P(),
        P(),
        P(("heads", "blk"), None),
        P(("heads", "blk")),
        P(("heads", "blk"), None),
        P(("heads", "blk"), None),
        P(("blk", "heads"), None),
    )
    return jax.shard_map(
        local,
        mesh=mesh,
        in_specs=placed,
        out_specs=(
            P(("blk", "heads"), None),
            P(("blk", "heads"), None),
            P(("heads", "blk")),
            P(("heads", "blk"), None),
            P(),
            P(),
            P(("heads", "blk"), None),
            P(("heads", "blk")),
            P(("heads", "blk"), None),
            P(("heads", "blk"), None),
        ),
        check_vma=False,
    )
```

```python
import functools

import jax
import jax.numpy as jnp
from jax import lax
from jax.experimental import pallas as pl
from jax.experimental.pallas import tpu as pltpu
from jax.sharding import PartitionSpec as P

HEADS = 16
KV_HEADS = 4


EPS = 1e-06
ROPE_BASE = 10000.0
NEG = -1e30
MESH = pl.DeviceIdType.MESH
ROWS_IN_BOTH = (((1,), (1,)), ((), ()))


def from_behind(block, axis, distance):
    devices = range(lax.axis_size(axis))
    route = [(i - distance, i) for i in devices if i - distance in devices]
    return lax.ppermute(block, axis, route)


def rotation(positions, head_dim):
    half_width = head_dim // 2
    frequency = ROPE_BASE ** (-2.0 * jnp.arange(half_width, dtype=jnp.float32) / head_dim)
    angles = positions.astype(jnp.float32)[:, None] * frequency[None, :]
    return (jnp.cos(angles)[:, None, :], jnp.sin(angles)[:, None, :])


def stack_heads(tile, heads, first):
    turned = tile.T
    dim = turned.shape[0] // heads
    wide = jnp.concatenate([turned[h * dim : (h + 1) * dim] for h in range(heads)], axis=1)
    zero = jnp.zeros_like(wide)
    return jnp.concatenate([wide, zero] if first else [zero, wide], axis=0)


def unstack_heads(wide, heads):
    count = wide.shape[1] // heads
    return jnp.concatenate([wide[:, h * count : (h + 1) * count] for h in range(heads)], axis=0).T


def scores_at(pair, query_ext, low, first_query, key_start, heads):
    scores = jnp.dot(pair, query_ext, preferred_element_type=jnp.float32)
    rows, columns = scores.shape
    shape = (rows, columns // heads)
    key = key_start + lax.broadcasted_iota(jnp.int32, shape, 0)
    query = first_query + lax.broadcasted_iota(jnp.int32, shape, 1)
    bias = jnp.where((key <= query) & (key >= low), 0.0, NEG)
    return scores + jnp.concatenate([bias] * heads, axis=1)


def transpose_into(pair_ref, turned_ref):
    for start in range(0, pair_ref.shape[0], 512):
        turned_ref[:, start : start + 512] = pair_ref[start : start + 512, :].T


def attend_kernel(
    heads, key_rows, scale, first_ref, query_ref, low_ref, pair_ref, out_ref, log_ref, turned_ref,
    mixed_ref, total_ref
):
    step = pl.program_id(0)
    query_rows = query_ref.shape[0]

    @pl.when(step == 0)
    def _():
        transpose_into(pair_ref, turned_ref)

    query_ext = stack_heads(query_ref[...] * jnp.bfloat16(scale), heads, True)
    low = low_ref[...]
    base = pair_ref.shape[0] // 2 + step * query_rows
    mixed_ref[...] = jnp.zeros_like(mixed_ref)
    total_ref[...] = jnp.zeros_like(total_ref)

    def tile(index, carried):
        start = pl.multiple_of(index * key_rows, key_rows)
        expo = jnp.exp(
            scores_at(pair_ref[pl.ds(start, key_rows), :], query_ext, low, base, start, heads)
        )
        total_ref[...] += jnp.sum(expo, axis=0, keepdims=True)
        mixed_ref[...] += jnp.dot(
            turned_ref[:, pl.ds(start, key_rows)],
            expo.astype(jnp.bfloat16),
            preferred_element_type=jnp.float32,
        )
        return carried

    lax.fori_loop(first_ref[step], (base + query_rows - 1) // key_rows + 1, tile, 0)
    total = total_ref[...]
    dim = pair_ref.shape[1] // 2
    out_ref[...] = unstack_heads(mixed_ref[dim:] / total, heads).astype(out_ref.dtype)
    log_ref[...] = jnp.log(total)[None]


def attend_back_kernel(
    heads, key_rows, scale, first_ref, query_ref, low_ref, pair_ref, out_ref, log_ref, *refs
):
    grads_ref, query_grad_ref, pair_grad_ref, turned_ref, sum_ref = refs
    step = pl.program_id(0)
    grad = grads_ref[first_ref[pl.num_programs(0)] ^ step]
    query_rows = query_ref.shape[0]
    dim = pair_ref.shape[1] // 2

    @pl.when(step == 0)
    def _():
        pair_grad_ref[...] = jnp.zeros_like(pair_grad_ref)
        transpose_into(pair_ref, turned_ref)

    query_ext = stack_heads(query_ref[...] * jnp.bfloat16(scale), heads, True)
    grad_ext = stack_heads(grad, heads, False)
    out_ext = stack_heads(out_ref[...], heads, False)
    inner = jnp.sum(
        grad_ext.astype(jnp.float32) * out_ext.astype(jnp.float32), axis=0, keepdims=True
    )
    log_sum = log_ref[0]
    low = low_ref[...]
    base = pair_ref.shape[0] // 2 + step * query_rows
    sum_ref[...] = jnp.zeros_like(sum_ref)

    def tile(index, carried):
        start = pl.multiple_of(index * key_rows, key_rows)
        pair = pair_ref[pl.ds(start, key_rows), :]
        probs = jnp.exp(scores_at(pair, query_ext, low, base, start, heads) - log_sum)
        probs_grad = jnp.dot(pair, grad_ext, preferred_element_type=jnp.float32)
        score_grad = (probs * (probs_grad - inner)).astype(jnp.bfloat16)
        sum_ref[...] += jnp.dot(
            turned_ref[:dim, pl.ds(start, key_rows)], score_grad, preferred_element_type=jnp.float32
        )
        pair_grad_ref[pl.ds(start, key_rows), :] += lax.dot_general(
            score_grad, query_ext, ROWS_IN_BOTH, preferred_element_type=jnp.float32
        ) + lax.dot_general(
            probs.astype(jnp.bfloat16), grad_ext, ROWS_IN_BOTH, preferred_element_type=jnp.float32
        )
        return carried

    lax.fori_loop(first_ref[step], (base + query_rows - 1) // key_rows + 1, tile, 0)
    query_grad_ref[...] = unstack_heads(sum_ref[...] * scale, heads).astype(query_grad_ref.dtype)


def attention_specs(queries, pair, query_rows, heads):
    width = queries.shape[1]
    return (
        pl.BlockSpec((query_rows, width), lambda i, first: (i, 0)),
        pl.BlockSpec((1, query_rows), lambda i, first: (0, i)),
        pl.BlockSpec(pair.shape, lambda i, first: (0, 0)),
        pl.BlockSpec((1, 1, heads * query_rows), lambda i, first: (i, 0, 0)),
    )


def attend(queries, pair, first, low, heads, query_rows, key_rows):
    count, width = queries.shape
    tile, row, whole, logs = attention_specs(queries, pair, query_rows, heads)
    columns = heads * query_rows
    return pl.pallas_call(
        functools.partial(attend_kernel, heads, key_rows, (width // heads) ** -0.5),
        grid_spec=pltpu.PrefetchScalarGridSpec(
            num_scalar_prefetch=1,
            grid=(count // query_rows,),
            in_specs=[tile, row, whole],
            out_specs=[tile, logs],
            scratch_shapes=[
                pltpu.VMEM(pair.shape[::-1], jnp.bfloat16),
                pltpu.VMEM((pair.shape[1], columns), jnp.float32),
                pltpu.VMEM((1, columns), jnp.float32),
            ],
        ),
        out_shape=[
            jax.ShapeDtypeStruct((count, width), jnp.bfloat16),
            jax.ShapeDtypeStruct((count // query_rows, 1, columns), jnp.float32),
        ],
        compiler_params=pltpu.CompilerParams(vmem_limit_bytes=48 << 20),
        cost_estimate=pl.CostEstimate(
            flops=20_000_000_000, bytes_accessed=8_000_000, transcendentals=0
        ),
        name="attend",
    )(first, queries, low, pair)


def attend_back(queries, pair, first, low, grads, out, logs, heads, query_rows, key_rows):
    count, width = queries.shape
    tile, row, whole, log_spec = attention_specs(queries, pair, query_rows, heads)
    columns = heads * query_rows
    return pl.pallas_call(
        functools.partial(attend_back_kernel, heads, key_rows, (width // heads) ** -0.5),
        grid_spec=pltpu.PrefetchScalarGridSpec(
            num_scalar_prefetch=1,
            grid=(count // query_rows,),
            in_specs=[tile, row, whole, tile, log_spec]
            + [pl.BlockSpec(grads.shape, lambda i, first: (0, 0, 0))],
            out_specs=[tile, whole],
            scratch_shapes=[
                pltpu.VMEM(pair.shape[::-1], jnp.bfloat16),
                pltpu.VMEM((pair.shape[1] // 2, columns), jnp.float32),
            ],
        ),
        out_shape=[
            jax.ShapeDtypeStruct((count, width), jnp.bfloat16),
            jax.ShapeDtypeStruct(pair.shape, jnp.float32),
        ],
        compiler_params=pltpu.CompilerParams(vmem_limit_bytes=48 << 20),
        cost_estimate=pl.CostEstimate(
            flops=40_000_000_000, bytes_accessed=12_000_000, transcendentals=0
        ),
        name="attend_back",
    )(first, queries, low, pair, out, logs, grads)


def heads_apart(wide, dim):
    rows = wide.shape[0]
    return jnp.concatenate(
        [
            jnp.broadcast_to(
                jnp.mean(jnp.square(wide[:, c : c + dim]), axis=-1, keepdims=True), (rows, dim)
            )
            for c in range(0, wide.shape[1], dim)
        ],
        axis=1,
    )


def spread_mean(wide, dim):
    rows = wide.shape[0]
    return jnp.concatenate(
        [
            jnp.broadcast_to(jnp.mean(wide[:, c : c + dim], axis=-1, keepdims=True), (rows, dim))
            for c in range(0, wide.shape[1], dim)
        ],
        axis=1,
    )


def turn(wide, cosine, sine, dim):
    count = wide.shape[1] // dim
    half = dim // 2
    swapped = jnp.concatenate(
        [
            wide[:, c + shift : c + shift + half]
            for c in range(0, wide.shape[1], dim)
            for shift in (half, 0)
        ],
        axis=1,
    )
    return wide * jnp.concatenate([cosine] * count, axis=1) + swapped * jnp.concatenate(
        [sine] * count, axis=1
    )


def project_kernel(
    dim, x_ref, weight_ref, head_gain_ref, cosine_ref, sine_ref, side_ref, query_ref, pair_ref,
    raw_ref, normed_ref, gain_ref, ffn_gain_ref, spread_ref, send_sem, recv_sem
):
    columns = raw_ref.shape[1]
    step, steps = pl.program_id(0), pl.num_programs(0)
    marks = (0, steps // 2, steps - 2)
    end = spread_job(step, marks, side_ref, spread_ref, send_sem, recv_sem)

    @pl.when(pl.program_id(0) == 0)
    def _():
        gains = weight_ref[:, columns:].T.astype(jnp.float32)
        gain_ref[...] = gains[:1]
        ffn_gain_ref[...] = gains[64:65]

    values = x_ref[...].astype(jnp.float32)
    normed = values * lax.rsqrt(jnp.mean(values * values, axis=-1, keepdims=True) + EPS)
    normed = (normed * gain_ref[...]).astype(jnp.bfloat16)
    normed_ref[...] = normed
    raw = jnp.dot(normed, weight_ref[:, :columns], preferred_element_type=jnp.float32)
    raw_ref[...] = raw
    turned_width = raw.shape[1] - pair_ref.shape[1] // 2
    heads = raw[:, :turned_width]
    heads = heads * lax.rsqrt(heads_apart(heads, dim) + EPS) * head_gain_ref[...]
    heads = turn(heads, cosine_ref[...], sine_ref[...], dim).astype(jnp.bfloat16)
    query_width = query_ref.shape[1]
    query_ref[...] = heads[:, :query_width]
    pair_ref[...] = jnp.concatenate(
        [heads[:, query_width:], raw[:, turned_width:].astype(jnp.bfloat16)], axis=1
    )
    pl.when(step == steps - 1)(end)


def project(x, weight, head_gain, cosine, sine, side, size, query_width, rows):
    count, width = x.shape
    out_width = weight.shape[1] - 128
    pair_width = out_width - query_width
    dim = cosine.shape[1]
    tiles = count // size // rows

    def apart(i):
        return ((lax.axis_index("heads") ^ (i // tiles)) * tiles + i % tiles, 0)

    def there(i):
        return (i, 0)

    def whole(i):
        return (0, 0)

    anywhere = pl.BlockSpec(memory_space=pl.ANY)

    return pl.pallas_call(
        functools.partial(project_kernel, dim),
        grid=(count // rows,),
        in_specs=[
            pl.BlockSpec((rows, width), there),
            pl.BlockSpec(weight.shape, whole),
            pl.BlockSpec(head_gain.shape, whole),
            pl.BlockSpec((rows, dim), apart),
            pl.BlockSpec((rows, dim), apart),
            anywhere,
        ],
        out_specs=[
            pl.BlockSpec((rows, query_width), apart),
            pl.BlockSpec((rows, pair_width), apart),
            pl.BlockSpec((rows, out_width), apart),
            pl.BlockSpec((rows, width), there),
            pl.BlockSpec((1, width), whole),
            pl.BlockSpec((1, width), whole),
            anywhere,
        ],
        out_shape=[
            jax.ShapeDtypeStruct((count, query_width), jnp.bfloat16),
            jax.ShapeDtypeStruct((count, pair_width), jnp.bfloat16),
            jax.ShapeDtypeStruct((count, out_width), jnp.float32),
            jax.ShapeDtypeStruct((count, width), jnp.bfloat16),
            jax.ShapeDtypeStruct((1, width), jnp.float32),
            jax.ShapeDtypeStruct((1, width), jnp.float32),
            jax.ShapeDtypeStruct((3, *side.shape), side.dtype),
        ],
        scratch_shapes=[pltpu.SemaphoreType.DMA((SPREAD_COUNT,))] * 2,
        compiler_params=pltpu.CompilerParams(
            collective_id=5, has_side_effects=True, vmem_limit_bytes=48 << 20
        ),
        cost_estimate=pl.CostEstimate(
            flops=4 * count * width * out_width, bytes_accessed=30_000_000, transcendentals=0
        ),
        name="project",
    )(x, weight, head_gain, cosine, sine, side)


def project_back_kernel(
    dim, own_ref, query_grad_ref, pair_grad_ref, returned_ref, raw_ref, head_gain_ref, cosine_ref,
    sine_ref, grad_ref, gain_grad_ref
):
    @pl.when(pl.program_id(0) == 0)
    def _():
        gain_grad_ref[...] = jnp.zeros_like(gain_grad_ref)

    pair_grad = pair_grad_ref[...] + returned_ref[...].astype(jnp.float32)
    pair_grad = pair_grad.astype(jnp.bfloat16)
    half = pair_grad.shape[1] // 2
    grads = jnp.concatenate([query_grad_ref[...], pair_grad[:, :half]], axis=1).astype(jnp.float32)
    grads = turn(grads, cosine_ref[...], -sine_ref[...], dim)
    values = raw_ref[:, : grads.shape[1]]
    inverse = lax.rsqrt(heads_apart(values, dim) + EPS)
    gain_grad_ref[...] += jnp.sum(grads * values * inverse, axis=0, keepdims=True)
    scaled = grads * head_gain_ref[...]
    moment = spread_mean(scaled * values, dim)
    back = inverse * scaled - values * inverse * inverse * inverse * moment
    grad_ref[...] = jnp.concatenate([back.astype(jnp.bfloat16), pair_grad[:, half:]], axis=1)


def project_back(own, query_grad, pair_sum, returned, raw, head_gain, cosine, sine, size, rows):
    count, query_width = query_grad.shape
    pair_width = pair_sum.shape[1]
    out_width = raw.shape[1]
    dim = cosine.shape[1]
    tiles = count // size // rows

    def apart(i, own):
        return ((own[0] ^ (i // tiles)) * tiles + i % tiles, 0)

    def behind(i, own):
        return (apart(i, own)[0] + count // rows, 0)

    def whole(i, own):
        return (0, 0)

    return pl.pallas_call(
        functools.partial(project_back_kernel, dim),
        grid_spec=pltpu.PrefetchScalarGridSpec(
            num_scalar_prefetch=1,
            grid=(count // rows,),
            in_specs=[
                pl.BlockSpec((rows, query_width), apart),
                pl.BlockSpec((rows, pair_width), behind),
                pl.BlockSpec((rows, pair_width), apart),
                pl.BlockSpec((rows, out_width), apart),
                pl.BlockSpec(head_gain.shape, whole),
                pl.BlockSpec((rows, dim), apart),
                pl.BlockSpec((rows, dim), apart),
            ],
            out_specs=[
                pl.BlockSpec((rows, out_width), lambda i, own: (i, 0)),
                pl.BlockSpec(head_gain.shape, whole),
            ],
        ),
        out_shape=[
            jax.ShapeDtypeStruct((count, out_width), jnp.bfloat16),
            jax.ShapeDtypeStruct(head_gain.shape, jnp.float32),
        ],
        compiler_params=pltpu.CompilerParams(vmem_limit_bytes=48 << 20),
        cost_estimate=pl.CostEstimate(
            flops=8_000_000_000, bytes_accessed=8_000_000, transcendentals=0
        ),
        name="project_back",
    )(own, query_grad, pair_sum, returned, raw, head_gain, cosine, sine)


def join_kernel(
    x_ref, weight_ref, weights_ref, gain_ref, mine_ref, cot_ref, residual_ref,
    normed_ref, attended_ref, cot_one_ref, cot_two_ref, held_ref, local_sem, send_sem, recv_sem
):
    step = pl.program_id(0)
    head, blk = lax.axis_index("heads"), lax.axis_index("blk")
    rows = x_ref.shape[0]
    count = held_ref.shape[1] // 4
    tiles = count // rows

    def copy(source, target, k, index):
        return pltpu.make_async_remote_copy(
            src_ref=source,
            dst_ref=target,
            send_sem=send_sem.at[index],
            recv_sem=recv_sem.at[index],
            device_id=(head ^ k, blk),
            device_id_type=MESH,
        )

    upper, lower = pl.ds(0, 2 * count), pl.ds(2 * count, 2 * count)
    near = [copy(mine_ref, held_ref.at[k], k, k - 1) for k in (1, 2)]
    far = [
        copy(held_ref.at[1, upper], held_ref.at[3, upper], 2, 2),
        copy(held_ref.at[2, lower], held_ref.at[3, lower], 1, 3),
    ]
    half = count // 2
    cot_near = [
        copy(cot_ref.at[pl.ds(half, half)], cot_one_ref, 1, 4),
        copy(cot_ref.at[pl.ds(0, half)], cot_two_ref, 2, 5),
    ]
    own = pltpu.make_async_copy(mine_ref, held_ref.at[0], local_sem)

    @pl.when(step == 0)
    def _():
        own.start()
        greet_near(False)
        for first in near:
            first.start()
        for first, second in zip(near, far):
            first.wait_recv()
            second.start()
        own.wait()
        for second in far:
            second.wait_recv()
        for last in cot_near:
            last.start()

    chunk = step // tiles
    parts = []
    total = x_ref[...].astype(jnp.float32)
    for k in range(4):
        start = ((chunk ^ k) * tiles + lax.rem(step, tiles)) * rows
        part = held_ref[k, pl.ds(pl.multiple_of(start, rows), rows)]
        weight = weight_ref[...] if k == 0 else weights_ref[k - 1]
        total += jnp.dot(part, weight, preferred_element_type=jnp.float32)
        parts.append(part)
    residual_ref[...] = total
    normed = total * lax.rsqrt(jnp.mean(total * total, axis=-1, keepdims=True) + EPS)
    normed_ref[...] = (normed * gain_ref[...]).astype(jnp.bfloat16)

    @pl.when(chunk == 0)
    def _():
        attended_ref[...] = jnp.concatenate(parts, axis=1)

    @pl.when(step == pl.num_programs(0) - 1)
    def _():
        for first in near + far:
            first.wait_send()
        for last in cot_near:
            last.wait()


def join(x, mine, weight, weights, gain, cot, rows):
    count, width = x.shape
    tokens = count // 4
    columns = mine.shape[1]
    tiles = tokens // rows
    anywhere = pl.BlockSpec(memory_space=pl.ANY)

    def there(i):
        return (i, 0)

    def whole(i):
        return (0, 0)

    sems = pltpu.SemaphoreType.DMA
    return pl.pallas_call(
        join_kernel,
        grid=(count // rows,),
        in_specs=[
            pl.BlockSpec((rows, width), there),
            pl.BlockSpec(weight.shape, whole),
            pl.BlockSpec(weights.shape, lambda i: (0, 0, 0)),
            pl.BlockSpec((1, width), whole),
            anywhere,
            anywhere,
        ],
        out_specs=[
            pl.BlockSpec((rows, width), there),
            pl.BlockSpec((rows, width), there),
            pl.BlockSpec((rows, 4 * columns), lambda i: (jnp.minimum(i, tiles - 1), 0)),
            anywhere,
            anywhere,
        ],
        out_shape=[
            jax.ShapeDtypeStruct((count, width), jnp.float32),
            jax.ShapeDtypeStruct((count, width), jnp.bfloat16),
            jax.ShapeDtypeStruct((tokens, 4 * columns), jnp.bfloat16),
            jax.ShapeDtypeStruct((tokens // 2, width), jnp.bfloat16),
            jax.ShapeDtypeStruct((tokens // 2, width), jnp.bfloat16),
        ],
        scratch_shapes=[
            pltpu.VMEM((4, count, columns), jnp.bfloat16),
            sems,
            sems((6,)),
            sems((6,)),
        ],
        compiler_params=pltpu.CompilerParams(
            collective_id=6, has_side_effects=True, vmem_limit_bytes=56 << 20
        ),
        cost_estimate=pl.CostEstimate(
            flops=16 * count * width * columns, bytes_accessed=50_000_000, transcendentals=0
        ),
        name="join",
    )(x, weight, weights, gain, mine, cot)


def begin_kernel(
    x_ref, qkv_ref, in_ref, x_out, qkv_out, in_out, local_sem, x_send, x_recv, q_send, q_recv,
    w_send, w_recv, b_send, b_recv
):
    head, blk = lax.axis_index("heads"), lax.axis_index("blk")
    size, blk_size = lax.axis_size("heads"), lax.axis_size("blk")
    count, depth = x_ref.shape[0], qkv_ref.shape[1]
    half = count // 2
    units = in_out.shape[2] // 2
    barrier = pltpu.get_barrier_semaphore()
    for k in range(1, size):
        pl.semaphore_signal(barrier, inc=1, device_id=(head ^ k, blk), device_id_type=MESH)

    def greet(k, carried):
        pl.semaphore_signal(
            barrier, inc=1, device_id=(head, lax.rem(blk + k, blk_size)), device_id_type=MESH
        )
        return carried

    lax.fori_loop(1, blk_size, greet, 0)
    pl.semaphore_wait(barrier, size + blk_size - 2)

    def send(source, target, k, send_sem, recv_sem):
        return pltpu.make_async_remote_copy(
            src_ref=source,
            dst_ref=target,
            send_sem=send_sem,
            recv_sem=recv_sem,
            device_id=(head ^ k, blk),
            device_id_type=MESH,
        )

    rows = pl.ds(pl.multiple_of(blk * depth, depth), depth)
    qkv_copies = [
        send(
            qkv_ref.at[head ^ k], qkv_out.at[head, rows], k, q_send.at[k - 1], q_recv.at[k - 1]
        )
        for k in range(1, size)
    ]

    def columns(part, owner):
        return pl.ds(pl.multiple_of((part * size + owner) * units, units), units)

    in_copies = [
        send(
            in_ref.at[:, columns(part, head ^ k)],
            in_out.at[head, :, pl.ds(part * units, units)],
            k,
            w_send.at[2 * k - 2 + part],
            w_recv.at[2 * k - 2 + part],
        )
        for k in range(1, size)
        for part in range(2)
    ]
    near = [
        send(x_ref, x_out.at[pl.ds(k * count, count)], k, x_send.at[k - 1], x_recv.at[k - 1])
        for k in (1, 2)
    ]
    far = [
        send(
            x_out.at[pl.ds(count, half)],
            x_out.at[pl.ds(3 * count, half)],
            2,
            x_send.at[2],
            x_recv.at[2],
        ),
        send(
            x_out.at[pl.ds(2 * count + half, half)],
            x_out.at[pl.ds(3 * count + half, half)],
            1,
            x_send.at[3],
            x_recv.at[3],
        ),
    ]
    own = [
        pltpu.make_async_copy(qkv_ref.at[head], qkv_out.at[head, rows], local_sem.at[0]),
        pltpu.make_async_copy(x_ref, x_out.at[pl.ds(0, count)], local_sem.at[1]),
    ] + [
        pltpu.make_async_copy(
            in_ref.at[:, columns(part, head)],
            in_out.at[head, :, pl.ds(part * units, units)],
            local_sem.at[2 + part],
        )
        for part in range(2)
    ]
    for copy in qkv_copies + near + in_copies + own:
        copy.start()

    def along(k):
        return pltpu.make_async_remote_copy(
            src_ref=qkv_out.at[:, rows],
            dst_ref=qkv_out.at[:, rows],
            send_sem=b_send.at[k],
            recv_sem=b_recv.at[k],
            device_id=(head, lax.rem(blk + k, blk_size)),
            device_id_type=MESH,
        )

    def arrived(k):
        source = pl.ds(
            pl.multiple_of(lax.rem(blk + blk_size - k, blk_size) * depth, depth), depth
        )
        return pltpu.make_async_remote_copy(
            src_ref=qkv_out.at[:, rows],
            dst_ref=qkv_out.at[:, source],
            send_sem=b_send.at[k],
            recv_sem=b_recv.at[k],
            device_id=(head, lax.rem(blk + k, blk_size)),
            device_id_type=MESH,
        )

    def start(k, carried):
        along(k).start()
        return carried

    def finish(k, carried):
        along(k).wait_send()
        arrived(k).wait_recv()
        return carried

    own[0].wait()
    for copy in qkv_copies:
        copy.wait_recv()
    lax.fori_loop(1, blk_size, start, 0)
    for first, second in zip(near, far):
        first.wait_recv()
        second.start()
    for copy in qkv_copies + near:
        copy.wait_send()
    for copy in in_copies + far:
        copy.wait()
    for copy in own[1:]:
        copy.wait()
    lax.fori_loop(1, blk_size, finish, 0)


def begin(x, qkv_parts, in_weight):
    size, blk_size = lax.axis_size("heads"), lax.axis_size("blk")
    count, width = x.shape
    depth, joined = qkv_parts.shape[1:]
    anywhere = pl.BlockSpec(memory_space=pl.ANY)
    sems = pltpu.SemaphoreType.DMA
    return pl.pallas_call(
        begin_kernel,
        out_shape=[
            jax.ShapeDtypeStruct((size * count, width), x.dtype),
            jax.ShapeDtypeStruct((size, blk_size * depth, joined), x.dtype),
            jax.ShapeDtypeStruct((size, depth, in_weight.shape[1] // size), x.dtype),
        ],
        in_specs=[anywhere] * 3,
        out_specs=[anywhere] * 3,
        scratch_shapes=[
            sems((4,)),
            sems((4,)),
            sems((4,)),
            sems((size - 1,)),
            sems((size - 1,)),
            sems((2 * size - 2,)),
            sems((2 * size - 2,)),
            sems((blk_size,)),
            sems((blk_size,)),
        ],
        compiler_params=pltpu.CompilerParams(collective_id=1, has_side_effects=True),
        name="begin",
    )(x, qkv_parts, in_weight)


def spread_copies(source_ref, target_ref, send_sem, recv_sem):
    head, blk = lax.axis_index("heads"), lax.axis_index("blk")
    rows = source_ref.shape[0] // 2
    quarter = rows // 2
    start = pl.multiple_of(lax.rem(blk, 2) * rows, rows)
    half = pl.ds(start, rows)
    count = [0]

    def copy(source, target, place):
        index = count[0]
        count[0] += 1
        return pltpu.make_async_remote_copy(
            src_ref=source,
            dst_ref=target,
            send_sem=send_sem.at[index],
            recv_sem=recv_sem.at[index],
            device_id=place,
            device_id_type=MESH,
        )

    near = [
        copy(source_ref.at[half], target_ref.at[k - 1, half], (head ^ k, blk)) for k in (1, 2)
    ]
    upper = pl.ds(start, quarter)
    lower = pl.ds(pl.multiple_of(start + quarter, quarter), quarter)
    far = [
        copy(target_ref.at[0, upper], target_ref.at[2, upper], (head ^ 2, blk)),
        copy(target_ref.at[1, lower], target_ref.at[2, lower], (head ^ 1, blk)),
    ]
    other = [
        copy(target_ref.at[k, half], target_ref.at[k, half], (head, blk ^ 1)) for k in range(3)
    ]
    return near, far, other


def greet_near(partner):
    head, blk = lax.axis_index("heads"), lax.axis_index("blk")
    barrier = pltpu.get_barrier_semaphore()
    places = [(head ^ 1, blk), (head ^ 2, blk)] + ([(head, blk ^ 1)] if partner else [])
    for place in places:
        pl.semaphore_signal(barrier, inc=1, device_id=place, device_id_type=MESH)
    pl.semaphore_wait(barrier, len(places))


def spread_job(step, marks, source_ref, target_ref, send_sem, recv_sem, greet=True):
    near, far, other = spread_copies(source_ref, target_ref, send_sem, recv_sem)
    begin_at, far_at, other_at = marks

    @pl.when(step == begin_at)
    def _():
        if greet:
            greet_near(True)
        for copy in near:
            copy.start()

    @pl.when(step == far_at)
    def _():
        for k in range(2):
            near[k].wait_recv()
            far[k].start()
            other[k].start()

    @pl.when(step == other_at)
    def _():
        for copy in far:
            copy.wait_recv()
        other[2].start()

    def end():
        for copy in near + far:
            copy.wait_send()
        for copy in other:
            copy.wait()

    return end


SPREAD_COUNT = 7


def hidden_kernel(
    tiles, normed_ref, gate_ref, up_ref, down_ref, side_ref, cot_ref, one_top_ref, one_bottom_ref,
    two_top_ref, two_bottom_ref, hidden_ref, gate_grad_ref, up_grad_ref, down_sum_ref, spread_ref,
    held_ref, hidden_all_ref, load_sem, far_send, far_recv, send_sem, recv_sem
):
    step, steps = pl.program_id(0), pl.num_programs(0)
    head, blk = lax.axis_index("heads"), lax.axis_index("blk")
    count = cot_ref.shape[0]
    half = count // 2
    rows, units = hidden_ref.shape
    far = [
        pltpu.make_async_remote_copy(
            src_ref=ref,
            dst_ref=held_ref.at[pl.ds(3 * count + part * half, half)],
            send_sem=far_send.at[part],
            recv_sem=far_recv.at[part],
            device_id=(head ^ k, blk),
            device_id_type=MESH,
        )
        for part, (ref, k) in enumerate(((one_top_ref, 2), (two_bottom_ref, 1)))
    ]
    near = ((one_top_ref, 2), (one_bottom_ref, 3), (two_top_ref, 4), (two_bottom_ref, 5))
    loads = [pltpu.make_async_copy(cot_ref, held_ref.at[pl.ds(0, count)], load_sem.at[0])] + [
        pltpu.make_async_copy(ref, held_ref.at[pl.ds(half * place, half)], load_sem.at[place - 1])
        for ref, place in near
    ]

    @pl.when(step == 0)
    def _():
        for load in loads:
            load.start()
        greet_near(True)
        for copy in far:
            copy.start()
        for load in loads:
            load.wait()

    @pl.when(step == tiles)
    def _():
        for copy in far:
            copy.wait()

    marks = (tiles, 2 * tiles, 2 * tiles + 2)
    end = spread_job(step, marks, side_ref, spread_ref, send_sem, recv_sem, False)

    @pl.when(step < 2 * tiles)
    def _():
        here = pl.ds(pl.multiple_of(step // tiles * rows, rows), rows)
        normed = normed_ref[...]
        gate = jnp.dot(normed, gate_ref[...], preferred_element_type=jnp.float32)
        upward = jnp.dot(normed, up_ref[...], preferred_element_type=jnp.float32)
        grad = lax.dot_general(
            held_ref[here], down_ref[...], ROWS_IN_BOTH, preferred_element_type=jnp.float32
        )
        sigmoid = jax.nn.sigmoid(gate)
        activated = gate * sigmoid
        hidden = (activated * upward).astype(jnp.bfloat16)
        hidden_ref[...] = hidden
        hidden_all_ref[here, pl.ds(pl.multiple_of(lax.rem(step, tiles) * units, units), units)] = (
            hidden
        )
        gate_grad_ref[...] = (grad * upward * sigmoid * (1.0 + gate * (1.0 - sigmoid))).astype(
            jnp.bfloat16
        )
        up_grad_ref[...] = (grad * activated).astype(jnp.bfloat16)

    @pl.when(step >= 2 * tiles)
    def _():
        there = pl.ds(pl.multiple_of((step - 2 * tiles) * units, units), units)
        down_sum_ref[...] = lax.dot_general(
            hidden_all_ref[:, there],
            held_ref[...],
            (((0,), (0,)), ((), ())),
            preferred_element_type=jnp.float32,
        ).astype(jnp.bfloat16)

    pl.when(step == steps - 1)(end)


def hidden_pass(normed, weight, cot, cot_near, down, side, units):
    count, width = normed.shape
    total = down.shape[0]
    tiles = total // units
    rows = count // 2

    def row(s):
        return jnp.minimum(s // tiles, 1)

    def column(s):
        return jnp.where(s < 2 * tiles, lax.rem(s, tiles), tiles - 1)

    out_spec = pl.BlockSpec((rows, units), lambda s: (row(s), column(s)))
    out_shape = jax.ShapeDtypeStruct((count, total), jnp.bfloat16)
    anywhere = pl.BlockSpec(memory_space=pl.ANY)
    sems = pltpu.SemaphoreType.DMA
    return pl.pallas_call(
        functools.partial(hidden_kernel, tiles),
        grid=(3 * tiles,),
        in_specs=[
            pl.BlockSpec((rows, width), lambda s: (row(s), 0)),
            pl.BlockSpec((width, units), lambda s: (0, column(s))),
            pl.BlockSpec((width, units), lambda s: (0, tiles + column(s))),
            pl.BlockSpec((units, width), lambda s: (column(s), 0)),
        ]
        + [anywhere] * 6,
        out_specs=[out_spec] * 3
        + [
            pl.BlockSpec((units, width), lambda s: (jnp.maximum(s - 2 * tiles, 0), 0)),
            anywhere,
        ],
        out_shape=[out_shape] * 3
        + [
            jax.ShapeDtypeStruct((total, width), jnp.bfloat16),
            jax.ShapeDtypeStruct((3, *side.shape), side.dtype),
        ],
        scratch_shapes=[
            pltpu.VMEM((count, width), jnp.bfloat16),
            pltpu.VMEM((count, total), jnp.bfloat16),
            sems((5,)),
            sems((2,)),
            sems((2,)),
            sems((SPREAD_COUNT,)),
            sems((SPREAD_COUNT,)),
        ],
        compiler_params=pltpu.CompilerParams(
            collective_id=2, has_side_effects=True, vmem_limit_bytes=58 << 20
        ),
        cost_estimate=pl.CostEstimate(
            flops=8 * count * width * total, bytes_accessed=70_000_000, transcendentals=0
        ),
        name="hidden_pass",
    )(normed, weight, weight, down, side, cot, *cot_near)


def in_order(step):
    value = 3
    for index, half in enumerate((2, 6, 5, 7, 0, 1, 4)):
        value = jnp.where(step == index, half, value)
    return value


def tail_kernel(
    normed_ref, gate_ref, up_ref, hidden_ref, in_hbm, down_hbm, in_sum_ref, out_one_ref,
    out_two_ref, out_rest_ref, grad_ref,
    weight_ref, one_ref, two_ref, rest_ref, top_ref, bottom_ref, last_ref, last_got_ref,
    weight_sem, send_sem, recv_sem
):
    step = pl.program_id(0)
    head, blk = lax.axis_index("heads"), lax.axis_index("blk")
    rows, total = hidden_ref.shape
    width = grad_ref.shape[1]
    load_in = pltpu.make_async_copy(in_hbm, weight_ref, weight_sem.at[0])
    load_down = pltpu.make_async_copy(
        down_hbm, weight_ref.at[pl.ds(0, total), pl.ds(0, width)], weight_sem.at[1]
    )

    def copy(source, target, k, index):
        return pltpu.make_async_remote_copy(
            src_ref=source,
            dst_ref=target,
            send_sem=send_sem.at[index],
            recv_sem=recv_sem.at[index],
            device_id=(head ^ k, blk),
            device_id_type=MESH,
        )

    send_one = copy(one_ref, top_ref, 1, 0)
    send_two = copy(two_ref, bottom_ref, 2, 1)
    send_top = copy(last_ref.at[0], last_got_ref.at[0], 2, 2)
    send_bottom = copy(last_ref.at[1], last_got_ref.at[1], 1, 3)

    def wide_of(block):
        return block.astype(jnp.float32)

    @pl.when(step == 0)
    def _():
        load_in.start()
        greet_near(False)
        load_in.wait()

    @pl.when(step < 8)
    def _():
        here = pl.ds(pl.multiple_of(in_order(step) * rows, rows), rows)
        value = lax.dot_general(
            gate_ref[here], weight_ref[:, :total], ROWS_IN_BOTH, preferred_element_type=jnp.float32
        ) + lax.dot_general(
            up_ref[here], weight_ref[:, total:], ROWS_IN_BOTH, preferred_element_type=jnp.float32
        )
        value = value.astype(jnp.bfloat16)

        def rows_from(first):
            return pl.ds(pl.multiple_of((step - first) * rows, rows), rows)

        @pl.when(step < 2)
        def _():
            one_ref[rows_from(0)] = value

        @pl.when((step >= 2) & (step < 4))
        def _():
            two_ref[rows_from(2)] = value

        @pl.when(step >= 4)
        def _():
            rest_ref[rows_from(4)] = value

        @pl.when(step == 1)
        def _():
            send_one.start()

        @pl.when(step == 3)
        def _():
            send_two.start()

        @pl.when(step == 7)
        def _():
            load_down.start()

    @pl.when((step >= 8) & (step < 16))
    def _():
        for part, ref in enumerate((gate_ref, up_ref)):
            in_sum_ref[:, part * total : (part + 1) * total] = lax.dot_general(
                normed_ref[...], ref[...], (((0,), (0,)), ((), ())),
                preferred_element_type=jnp.float32,
            ).astype(jnp.bfloat16)

        @pl.when(step == 13)
        def _():
            send_one.wait_recv()
            last_ref[0] = (
                wide_of(rest_ref[2 * rows : 3 * rows]) + wide_of(top_ref[rows:])
            ).astype(jnp.bfloat16)
            send_top.start()

        @pl.when(step == 15)
        def _():
            send_two.wait_recv()
            last_ref[1] = (wide_of(rest_ref[3 * rows :]) + wide_of(bottom_ref[rows:])).astype(
                jnp.bfloat16
            )
            send_bottom.start()
            load_down.wait()

    @pl.when(step >= 16)
    def _():
        terms = jnp.dot(
            hidden_ref[...], weight_ref[:total, :width], preferred_element_type=jnp.float32
        ).astype(jnp.bfloat16)

        @pl.when(step < 18)
        def _():
            out_one_ref[...] = terms

        @pl.when((step >= 18) & (step < 20))
        def _():
            out_two_ref[...] = terms

        @pl.when(step >= 20)
        def _():
            out_rest_ref[...] = terms

    @pl.when(step == pl.num_programs(0) - 1)
    def _():
        send_top.wait_recv()
        send_bottom.wait_recv()
        grad_ref[:rows] = (
            wide_of(rest_ref[:rows]) + wide_of(top_ref[:rows]) + wide_of(last_got_ref[0])
        )
        grad_ref[rows:] = (
            wide_of(rest_ref[rows : 2 * rows]) + wide_of(bottom_ref[:rows]) + wide_of(last_got_ref[1])
        )
        for sent in (send_one, send_two, send_top, send_bottom):
            sent.wait_send()


def feed_tail(normed, gate_grad, up_grad, hidden, weight, down):
    count, width = normed.shape
    total = hidden.shape[1]
    rows = count // 8
    anywhere = pl.BlockSpec(memory_space=pl.ANY)
    once = pl.Buffered(1)

    def stage(i, first):
        return jnp.clip(i - first, 0, 7)

    low = jnp.bfloat16
    return pl.pallas_call(
        tail_kernel,
        grid=(24,),
        in_specs=[
            pl.BlockSpec((count, rows), lambda i: (0, stage(i, 8))),
            pl.BlockSpec((count, total), lambda i: (0, 0), pipeline_mode=once),
            pl.BlockSpec((count, total), lambda i: (0, 0), pipeline_mode=once),
            pl.BlockSpec((rows, total), lambda i: (in_order(stage(i, 16)), 0)),
            anywhere,
            anywhere,
        ],
        out_specs=[
            pl.BlockSpec((rows, 2 * total), lambda i: (stage(i, 8), 0)),
            pl.BlockSpec((rows, width), lambda i: (jnp.clip(i - 16, 0, 1), 0)),
            pl.BlockSpec((rows, width), lambda i: (jnp.clip(i - 18, 0, 1), 0)),
            pl.BlockSpec((rows, width), lambda i: (jnp.clip(i - 20, 0, 3), 0)),
            pl.BlockSpec((2 * rows, width), lambda i: (0, 0), pipeline_mode=once),
        ],
        out_shape=[
            jax.ShapeDtypeStruct((width, 2 * total), low),
            jax.ShapeDtypeStruct((2 * rows, width), low),
            jax.ShapeDtypeStruct((2 * rows, width), low),
            jax.ShapeDtypeStruct((4 * rows, width), low),
            jax.ShapeDtypeStruct((2 * rows, width), jnp.float32),
        ],
        scratch_shapes=[
            pltpu.VMEM(weight.shape, low),
            pltpu.VMEM((2 * rows, width), low),
            pltpu.VMEM((2 * rows, width), low),
            pltpu.VMEM((4 * rows, width), low),
            pltpu.VMEM((2 * rows, width), low),
            pltpu.VMEM((2 * rows, width), low),
            pltpu.VMEM((2, rows, width), low),
            pltpu.VMEM((2, rows, width), low),
            pltpu.SemaphoreType.DMA((2,)),
            pltpu.SemaphoreType.DMA((4,)),
            pltpu.SemaphoreType.DMA((4,)),
        ],
        compiler_params=pltpu.CompilerParams(
            collective_id=3, has_side_effects=True, vmem_limit_bytes=60 << 20
        ),
        cost_estimate=pl.CostEstimate(
            flops=10 * count * width * total, bytes_accessed=70_000_000, transcendentals=0
        ),
        name="feed_tail",
    )(normed, gate_grad, up_grad, hidden, weight, down)


def residual_back_kernel(
    grad_sum_ref, residual_ref, cot_ref, gain_ref, attended_ref, weight_ref, weights_ref, grad_ref,
    gain_grad_ref, out_sum_ref, pieces_ref, branch_ref, mine_ref, terms_ref, terms_got_ref, own_sem,
    send_sem, recv_sem
):
    size = lax.axis_size("heads")
    core = lax.rem(lax.axis_index("blk"), 2)
    step = pl.program_id(0)
    last = pl.num_programs(0) - 1
    head, blk = lax.axis_index("heads"), lax.axis_index("blk")
    rows = cot_ref.shape[0]
    copies = [
        pltpu.make_async_remote_copy(
            src_ref=mine_ref.at[k],
            dst_ref=pieces_ref.at[k],
            send_sem=send_sem.at[k - 1],
            recv_sem=recv_sem.at[k - 1],
            device_id=(head ^ k, blk),
            device_id_type=MESH,
        )
        for k in range(1, size)
    ]
    keep = pltpu.make_async_copy(mine_ref.at[0], pieces_ref.at[0], own_sem)
    across = pltpu.make_async_remote_copy(
        src_ref=terms_ref.at[:, 1 - core],
        dst_ref=terms_got_ref,
        send_sem=send_sem.at[size - 1],
        recv_sem=recv_sem.at[size - 1],
        device_id=(head, blk ^ 1),
        device_id_type=MESH,
    )

    @pl.when(step == 0)
    def _():
        gain_grad_ref[...] = jnp.zeros_like(gain_grad_ref)
        barrier = pltpu.get_barrier_semaphore()
        for k in range(1, size):
            pl.semaphore_signal(barrier, inc=1, device_id=(head ^ k, blk), device_id_type=MESH)
        pl.semaphore_signal(barrier, inc=1, device_id=(head, blk ^ 1), device_id_type=MESH)
        pl.semaphore_wait(barrier, size)

    @pl.when(step < last)
    def _():
        here = pl.ds(pl.multiple_of(step * rows, rows), rows)
        gradient = grad_sum_ref[...]
        values = residual_ref[...]
        inverse = lax.rsqrt(jnp.mean(values * values, axis=-1, keepdims=True) + EPS)
        gain_grad_ref[...] += jnp.sum(gradient * values * inverse, axis=0, keepdims=True)
        scaled = gradient * gain_ref[...]
        moment = jnp.mean(scaled * values, axis=-1, keepdims=True)
        total = cot_ref[...].astype(jnp.float32) + (
            inverse * scaled - values * (inverse * inverse * inverse * moment)
        )
        grad_ref[...] = total
        branch = total.astype(jnp.bfloat16)
        branch_ref[here] = branch
        for k in range(size):
            weight = weight_ref[...] if k == 0 else weights_ref[k - 1]
            mine_ref[k, here] = lax.dot_general(
                branch, weight, ROWS_IN_BOTH, preferred_element_type=jnp.float32
            ).astype(jnp.bfloat16)

    @pl.when(step == last)
    def _():
        for copy in copies:
            copy.start()
        keep.start()
        columns = attended_ref.shape[1] // size
        pairs = terms_ref.shape[0] // size
        for k in range(size):
            terms = lax.dot_general(
                attended_ref[:, k * columns : (k + 1) * columns],
                branch_ref[...],
                (((0,), (0,)), ((), ())),
                preferred_element_type=jnp.float32,
            ).astype(jnp.bfloat16)
            terms_ref[k * pairs : (k + 1) * pairs] = terms.reshape(pairs, *terms_ref.shape[1:])
        across.start()
        across.wait()

        def add(index, carried):
            out_sum_ref[index] = (
                terms_ref[index, core].astype(jnp.float32)
                + terms_got_ref[index].astype(jnp.float32)
            ).astype(jnp.bfloat16)
            return carried

        lax.fori_loop(0, terms_ref.shape[0], add, 0)
        for copy in copies:
            copy.wait()
        keep.wait()


def residual_back(grad_sum, residual, cot, gain, attended, weight, weights, rows):
    count, width = cot.shape
    size, blk_size = lax.axis_size("heads"), lax.axis_size("blk")
    columns = weight.shape[0]
    pairs, held = size * blk_size // 2, columns // blk_size
    tiles = count // rows

    def there(i):
        return (jnp.minimum(i, tiles - 1), 0)

    def whole(i):
        return (0, 0)

    tile = pl.BlockSpec((rows, width), there)
    row = pl.BlockSpec((1, width), whole)
    pieces = (size, count, columns)
    return pl.pallas_call(
        residual_back_kernel,
        grid=(tiles + 1,),
        in_specs=[
            tile,
            tile,
            tile,
            row,
            pl.BlockSpec(attended.shape, whole),
            pl.BlockSpec(weight.shape, whole),
            pl.BlockSpec(weights.shape, lambda i: (0, 0, 0)),
        ],
        out_specs=[
            tile,
            row,
            pl.BlockSpec((pairs, held, width), lambda i: (0, 0, 0)),
            pl.BlockSpec(memory_space=pl.ANY),
        ],
        out_shape=[
            jax.ShapeDtypeStruct((count, width), jnp.float32),
            jax.ShapeDtypeStruct((1, width), jnp.float32),
            jax.ShapeDtypeStruct((pairs, held, width), jnp.bfloat16),
            jax.ShapeDtypeStruct(pieces, jnp.bfloat16),
        ],
        scratch_shapes=[
            pltpu.VMEM((count, width), jnp.bfloat16),
            pltpu.VMEM(pieces, jnp.bfloat16),
            pltpu.VMEM((pairs, 2, held, width), jnp.bfloat16),
            pltpu.VMEM((pairs, held, width), jnp.bfloat16),
            pltpu.SemaphoreType.DMA,
            pltpu.SemaphoreType.DMA((size,)),
            pltpu.SemaphoreType.DMA((size,)),
        ],
        compiler_params=pltpu.CompilerParams(
            collective_id=4, has_side_effects=True, vmem_limit_bytes=56 << 20
        ),
        cost_estimate=pl.CostEstimate(
            flops=4 * count * width * columns * size, bytes_accessed=30_000_000, transcendentals=0
        ),
        name="residual_back",
    )(grad_sum, residual, cot, gain, attended, weight, weights)


def turned_kernel(left_ref, *refs):
    *right_refs, out_ref, held_ref, load_sem = refs
    count = right_refs[0].shape[0]

    @pl.when(pl.program_id(0) == 0)
    def _():
        loads = [
            pltpu.make_async_copy(ref, held_ref.at[pl.ds(k * count, count)], load_sem.at[k])
            for k, ref in enumerate(right_refs)
        ]
        for load in loads:
            load.start()
        for load in loads:
            load.wait()

    out_ref[...] = lax.dot_general(
        left_ref[...], held_ref[...], (((0,), (0,)), ((), ())), preferred_element_type=jnp.float32
    ).astype(out_ref.dtype)


def turned_product(left, rights, rows):
    count, height = left.shape
    width = rights[0].shape[1]
    return pl.pallas_call(
        turned_kernel,
        grid=(height // rows,),
        in_specs=[pl.BlockSpec((count, rows), lambda i: (0, i))]
        + [pl.BlockSpec(memory_space=pl.ANY)] * len(rights),
        out_specs=pl.BlockSpec((rows, width), lambda i: (i, 0)),
        out_shape=jax.ShapeDtypeStruct((height, width), jnp.bfloat16),
        scratch_shapes=[
            pltpu.VMEM((count, width), jnp.bfloat16),
            pltpu.SemaphoreType.DMA((len(rights),)),
        ],
        compiler_params=pltpu.CompilerParams(vmem_limit_bytes=58 << 20),
        cost_estimate=pl.CostEstimate(
            flops=2 * count * height * width, bytes_accessed=20_000_000, transcendentals=0
        ),
        name="turned_product",
    )(left, *rights)


def finish_kernel(
    query_width, dim, sent_ref, qkv_ref, gain_ref, ffn_ref, head_ref, weight_ref, out_own_ref,
    out_one_ref, out_two_ref, out_three_ref, *refs
):
    size, blk_size = lax.axis_size("heads"), lax.axis_size("blk")
    out_refs = (out_own_ref, out_one_ref, out_two_ref, out_three_ref)
    sources, refs = refs[:4], refs[4:]
    (
        grad_ref, qkv_grad_ref, gains_ref, out_grad_ref, in_grad_ref, *refs
    ) = refs
    held, refs = refs[:4], refs[4:]
    weights_ref, x_ref, residual_grad_ref, in_ref = held
    (
        got_ref, qkv_other_ref, qkv_sum_ref, qkv_got_ref, part_ref, gain_got_ref, out_part_ref,
        out_got_ref, in_got_ref, load_sem, s_send, s_recv, c_send, c_recv, q_send, q_recv, g_send,
        g_recv, o_send, o_recv, i_send, i_recv,
    ) = refs
    devices = size * blk_size
    pairs = blk_size // 2
    head, blk = lax.axis_index("heads"), lax.axis_index("blk")
    core, pair = lax.rem(blk, 2), blk // 2
    own = head * blk_size + blk
    own_pair = head * pairs + pair
    count, width = x_ref.shape
    depth = width // devices
    barrier = pltpu.get_barrier_semaphore()
    loads = [
        pltpu.make_async_copy(source, target, load_sem.at[index])
        for index, (source, target) in enumerate(zip(sources, held))
    ]
    for load in loads:
        load.start()

    def place_of(index):
        return (index // blk_size, lax.rem(index, blk_size))

    def greet(k, carried):
        pl.semaphore_signal(
            barrier, inc=1, device_id=place_of(lax.rem(own + k, devices)), device_id_type=MESH
        )
        return carried

    lax.fori_loop(1, devices, greet, 0)
    pl.semaphore_wait(barrier, devices - 1)

    def copy(source, target, place, send, recv):
        return pltpu.make_async_remote_copy(
            src_ref=source,
            dst_ref=target,
            send_sem=send,
            recv_sem=recv,
            device_id=place,
            device_id_type=MESH,
        )

    across = copy(qkv_ref.at[:, 1 - core], qkv_other_ref, (head, blk ^ 1), c_send, c_recv)
    across.start()
    sends = [
        copy(
            sent_ref.at[pl.ds(k * count, count)],
            got_ref.at[k - 1],
            (head ^ k, blk),
            s_send.at[k - 1],
            s_recv.at[k - 1],
        )
        for k in range(1, size)
    ]
    for sent in sends:
        sent.start()

    def wide_of(block):
        return block.astype(jnp.float32)

    across.wait_recv()

    def qkv_copy(k, slot):
        other = lax.rem(own_pair + k, size * pairs)
        return copy(
            qkv_sum_ref.at[other],
            qkv_got_ref.at[slot],
            (other // pairs, lax.rem(other, pairs) * 2 + core),
            q_send.at[k],
            q_recv.at[slot],
        )

    def qkv_sum(index, carried):
        qkv_sum_ref[index] = (
            wide_of(qkv_ref[index, core]) + wide_of(qkv_other_ref[index])
        ).astype(jnp.bfloat16)
        return carried

    def start_qkv(k, carried):
        qkv_copy(k, own_pair).start()
        return carried

    lax.fori_loop(0, size * pairs, qkv_sum, 0)
    lax.fori_loop(1, size * pairs, start_qkv, 0)
    qkv_got_ref[own_pair] = qkv_sum_ref[own_pair]

    def out_copy(k, slot):
        other = lax.rem(pair + k, pairs)
        return copy(
            out_part_ref.at[other],
            out_got_ref.at[slot],
            (head, other * 2 + core),
            o_send.at[k],
            o_recv.at[slot],
        )

    out_rows = out_grad_ref.shape[0]

    def out_sum(index, carried):
        here = pl.ds(pl.multiple_of(index * out_rows, out_rows), out_rows)
        total = wide_of(out_refs[0][here])
        for ref in out_refs[1:]:
            total += wide_of(ref[here])
        out_part_ref[index, :out_rows] = total.astype(jnp.bfloat16)
        return carried

    def start_out(k, carried):
        out_copy(k, pair).start()
        return carried

    lax.fori_loop(0, pairs, out_sum, 0)
    lax.fori_loop(1, pairs, start_out, 0)
    out_got_ref[pair] = out_part_ref[pair]

    loads[3].wait()
    in_sends = [
        copy(
            in_ref.at[head ^ k],
            in_got_ref.at[k - 1],
            (head ^ k, blk),
            i_send.at[k - 1],
            i_recv.at[k - 1],
        )
        for k in range(1, size)
    ]
    for sent in in_sends:
        sent.start()

    for index in (0, 1, 2):
        loads[index].wait()
    for sent in sends:
        sent.wait_recv()
    rows = min(128, count)

    def tile(index, gain_sum):
        here = pl.ds(pl.multiple_of(index * rows, rows), rows)
        normed_grad = lax.dot_general(
            sent_ref[here], weight_ref[...], ROWS_IN_BOTH, preferred_element_type=jnp.float32
        )
        for k in range(1, size):
            normed_grad += lax.dot_general(
                got_ref[k - 1, here],
                weights_ref[k - 1],
                ROWS_IN_BOTH,
                preferred_element_type=jnp.float32,
            )
        values = wide_of(x_ref[here])
        inverse = lax.rsqrt(jnp.mean(values * values, axis=-1, keepdims=True) + EPS)
        scaled = normed_grad * gain_ref[...]
        moment = jnp.mean(scaled * values, axis=-1, keepdims=True)
        grad_ref[here] = (
            residual_grad_ref[here]
            + inverse * scaled
            - values * (inverse * inverse * inverse * moment)
        )
        return gain_sum + jnp.sum(normed_grad * values * inverse, axis=0, keepdims=True)

    attn_sum = lax.fori_loop(0, count // rows, tile, jnp.zeros((1, width), jnp.float32))

    def by_device(row):
        lanes = jnp.concatenate(
            [row[:, d * depth : (d + 1) * depth] for d in range(devices)], axis=0
        )
        if depth < 64:
            lanes = jnp.concatenate(
                [lanes, jnp.zeros((devices, 64 - depth), jnp.float32)], axis=1
            )
        return lanes

    head_row = head_ref[...]
    query_sum = head_row[:, :dim]
    for c in range(dim, query_width, dim):
        query_sum += head_row[:, c : c + dim]
    key_sum = head_row[:, query_width : query_width + dim]
    for c in range(query_width + dim, head_row.shape[1], dim):
        key_sum += head_row[:, c : c + dim]
    both = jnp.concatenate([query_sum, key_sum], axis=1)
    part_ref[...] = jnp.zeros_like(part_ref)
    part_ref[:, 0, :] = jnp.concatenate([by_device(attn_sum), by_device(ffn_ref[...])], axis=1)
    part_ref[:, 1, :] = jnp.broadcast_to(both, (devices, 2 * dim))

    def gain_copy(k, slot):
        other = lax.rem(own + k, devices)
        return copy(
            part_ref.at[other], gain_got_ref.at[slot], place_of(other), g_send.at[k], g_recv.at[slot]
        )

    def start_gain(k, carried):
        gain_copy(k, own).start()
        return carried

    lax.fori_loop(1, devices, start_gain, 0)
    gain_got_ref[own] = part_ref[own]

    units = in_ref.shape[2] // 2
    for k in range(size):
        if k:
            in_sends[k - 1].wait_recv()
        for part in range(2):
            columns = pl.ds(pl.multiple_of((part * size + (head ^ k)) * units, units), units)
            piece = slice(part * units, (part + 1) * units)
            got = in_got_ref[k - 1, :, piece] if k else in_ref[head, :, piece]
            in_grad_ref[:, columns] = wide_of(got)

    def finish_qkv(k, carried):
        qkv_copy(k, lax.rem(own_pair + size * pairs - k, size * pairs)).wait()
        return carried

    lax.fori_loop(1, size * pairs, finish_qkv, 0)

    def group_sum(h):
        total = wide_of(qkv_got_ref[h * pairs])
        for b in range(1, pairs):
            total += wide_of(qkv_got_ref[h * pairs + b])
        return total

    sums = [group_sum(h) for h in range(size)]
    key_end = query_width + (sums[0].shape[1] - query_width) // 2
    qkv_grad_ref[...] = jnp.concatenate(
        [total[:, :query_width] for total in sums]
        + [total[:, query_width:key_end] for total in sums]
        + [total[:, key_end:] for total in sums],
        axis=1,
    )

    def finish_out(k, carried):
        out_copy(k, lax.rem(pair + pairs - k, pairs)).wait()
        return carried

    lax.fori_loop(1, pairs, finish_out, 0)
    out_total = wide_of(out_got_ref[0, :out_rows])
    for b in range(1, pairs):
        out_total += wide_of(out_got_ref[b, :out_rows])
    out_grad_ref[...] = out_total

    def finish_gain(k, carried):
        gain_copy(k, lax.rem(own + devices - k, devices)).wait()
        return carried

    lax.fori_loop(1, devices, finish_gain, 0)
    gains_ref[...] = jnp.sum(gain_got_ref[...], axis=0)
    across.wait_send()
    for sent in sends + in_sends:
        sent.wait_send()


def finish(
    sent, qkv_part, x, residual_grad, gain, ffn_sum, head_sum, weight, weights, outs, in_part,
    query_width, dim
):
    size, blk_size = lax.axis_size("heads"), lax.axis_size("blk")
    devices = size * blk_size
    pairs = blk_size // 2
    count, width = x.shape
    depth, joined = width // devices, sent.shape[1]
    out_rows = outs[0].shape[0] // pairs
    held_rows = -(-out_rows // 16) * 16
    units = in_part.shape[2]
    vmem = pl.BlockSpec(memory_space=pltpu.VMEM)
    anywhere = pl.BlockSpec(memory_space=pl.ANY)
    sems = pltpu.SemaphoreType.DMA
    low = jnp.bfloat16
    loaded = (weights, x, residual_grad, in_part)
    return pl.pallas_call(
        functools.partial(finish_kernel, query_width, dim),
        out_shape=[
            jax.ShapeDtypeStruct((count, width), jnp.float32),
            jax.ShapeDtypeStruct((depth, size * joined), jnp.float32),
            jax.ShapeDtypeStruct((8, 128), jnp.float32),
            jax.ShapeDtypeStruct((out_rows, width), jnp.float32),
            jax.ShapeDtypeStruct((depth, size * units), jnp.float32),
        ],
        in_specs=[vmem] * (6 + size) + [anywhere] * 4,
        out_specs=[vmem] * 5,
        scratch_shapes=[pltpu.VMEM(array.shape, array.dtype) for array in loaded]
        + [
            pltpu.VMEM((size - 1, count, joined), low),
            pltpu.VMEM((size * pairs, depth, joined), low),
            pltpu.VMEM((size * pairs, depth, joined), low),
            pltpu.VMEM((size * pairs, depth, joined), low),
            pltpu.VMEM((devices, 8, 128), jnp.float32),
            pltpu.VMEM((devices, 8, 128), jnp.float32),
            pltpu.VMEM((pairs, held_rows, width), low),
            pltpu.VMEM((pairs, held_rows, width), low),
            pltpu.VMEM((size - 1, depth, units), low),
            sems((4,)),
            sems((size - 1,)),
            sems((size - 1,)),
            sems,
            sems,
            sems((size * pairs,)),
            sems((size * pairs,)),
            sems((devices,)),
            sems((devices,)),
            sems((pairs,)),
            sems((pairs,)),
            sems((size - 1,)),
            sems((size - 1,)),
        ],
        compiler_params=pltpu.CompilerParams(
            collective_id=0, has_side_effects=True, vmem_limit_bytes=60 << 20
        ),
        name="finish",
    )(
        sent, qkv_part.reshape(size * pairs, 2, depth, joined), gain, ffn_sum, head_sum, weight,
        *outs, *loaded
    )


def permute(block, axis, k):
    return lax.ppermute(block, axis, [(i, i ^ k) for i in range(lax.axis_size(axis))])


def after(value, *done):
    return lax.optimization_barrier((value, *done))[0]


def pick(block, k, axis, dim):
    extent = block.shape[dim] // lax.axis_size(axis)
    return lax.dynamic_slice_in_dim(block, (lax.axis_index(axis) ^ k) * extent, extent, dim)


def wide(block):
    return block.astype(jnp.float32)


def local(
    inputs,
    positions,
    attn_gain,
    qkv_weight,
    q_gain,
    k_gain,
    out_weight,
    ffn_gain,
    ffn_in_weight,
    ffn_out_weight,
    cotangent,
):
    token_count, width = inputs.shape
    depth = qkv_weight.shape[0]
    head_dim = q_gain.shape[0]
    group_size = HEADS // KV_HEADS
    size = lax.axis_size("heads")
    blk_size = lax.axis_size("blk")
    query_all, key_all = HEADS * head_dim, KV_HEADS * head_dim
    query_width, key_width = query_all // size, key_all // size
    qkv_width = query_width + 2 * key_width
    block_len = token_count * size
    half = token_count // 2
    own = lax.axis_index("heads").astype(jnp.int32).reshape(1)

    qkv_parts = jnp.concatenate(
        [
            qkv_weight[:, :query_all].reshape(depth, size, query_width),
            qkv_weight[:, query_all : query_all + key_all].reshape(depth, size, key_width),
            qkv_weight[:, query_all + key_all :].reshape(depth, size, key_width),
            jnp.broadcast_to(attn_gain[:, None, None], (depth, size, 64)),
            jnp.broadcast_to(ffn_gain[:, None, None], (depth, size, 64)),
        ],
        axis=-1,
    ).transpose(1, 0, 2)
    out_group = lax.all_gather(out_weight, "blk", axis=0, tiled=True)
    down_group = lax.all_gather(ffn_out_weight, "blk", axis=0, tiled=True)

    inputs_blk, qkv_rows, in_rows = begin(inputs, qkv_parts, ffn_in_weight)
    in_group = lax.all_gather(in_rows, "blk", axis=1, tiled=True).reshape(width, -1)
    qkv_rows = qkv_rows.reshape(width, -1)
    cosine, sine = rotation(positions, head_dim)
    cosine = jnp.concatenate([cosine[:, 0], cosine[:, 0]], axis=-1)
    sine = jnp.concatenate([-sine[:, 0], sine[:, 0]], axis=-1)
    head_gain = jnp.concatenate(
        [jnp.tile(q_gain, HEADS // size), jnp.tile(k_gain, KV_HEADS // size)]
    ).astype(jnp.float32)[None, :]
    query_low, pair_blk, raw, normed, attn_scaling, ffn_scaling, out_peers = project(
        inputs_blk, qkv_rows, head_gain, cosine, sine, out_group, size, query_width, 256
    )
    pair_all = jnp.concatenate([from_behind(pair_blk, "blk", 1), pair_blk], axis=0)
    query_rows, key_rows = token_count, 256
    low = block_len + jnp.arange(block_len, dtype=jnp.int32) - positions
    first = jnp.concatenate([low[::query_rows] // key_rows, own])
    low = low[None, :]
    attended_blk, logs = attend(query_low, pair_all, first, low, group_size, query_rows, key_rows)

    mine = jnp.concatenate([pick(attended_blk, k, "heads", 0) for k in range(size)], axis=0)
    late = after(cotangent, inputs_blk)
    one_top, two_bottom = permute(late[:half], "heads", 1), permute(late[half:], "heads", 2)
    residual, ffn_normed, attended_own, one_bottom, two_top = join(
        inputs_blk, mine, out_group, out_peers, ffn_scaling, cotangent, 256
    )
    residual_own = residual[:token_count]
    qkv_group = qkv_rows[:, :qkv_width]
    hidden, gate_grad, up_grad, down_sum, qkv_peers = hidden_pass(
        ffn_normed,
        in_group,
        cotangent,
        (one_top, one_bottom, two_top, two_bottom),
        down_group,
        qkv_group,
        256,
    )
    ffn_out_grad = lax.psum_scatter(down_sum, "blk", scatter_dimension=0, tiled=True)
    in_sum, out_one, out_two, out_rest, grad_sum = feed_tail(
        ffn_normed, gate_grad, up_grad, hidden, in_group, down_group
    )
    in_sum, ffn_out_grad = lax.optimization_barrier((in_sum, ffn_out_grad))
    in_part = lax.psum_scatter(
        in_sum.reshape(size, blk_size * depth, -1), "blk", scatter_dimension=1, tiled=True
    )
    ffn_out_grad = wide(ffn_out_grad)
    residual_grad, ffn_sum, out_sum, grads = residual_back(
        grad_sum, residual, cotangent, ffn_scaling, attended_own, out_group, out_peers,
        min(128, half)
    )
    out_one, out_two, grads = lax.optimization_barrier((out_one, out_two, grads))
    out_top, out_bottom = permute(out_one, "heads", 1), permute(out_two, "heads", 2)
    out_slices = jnp.split(out_sum.reshape(size, -1, width), size, axis=0)
    out_slices = [piece[0] for piece in out_slices]
    out_slices = [out_slices[0]] + [permute(out_slices[k], "heads", k) for k in range(1, size)]
    query_grad, pair_sum = attend_back(
        query_low, pair_all, first, low, grads, attended_blk, logs, group_size, query_rows, key_rows
    )
    returned = from_behind(pair_sum[:block_len].astype(jnp.bfloat16), "blk", -1)
    out_top, out_bottom, returned = lax.optimization_barrier((out_top, out_bottom, returned))
    top_send = (wide(out_rest[2 * half : 3 * half]) + wide(out_top[half:])).astype(jnp.bfloat16)
    bottom_send = (wide(out_rest[3 * half :]) + wide(out_bottom[half:])).astype(jnp.bfloat16)
    out_top_last = permute(top_send, "heads", 2)
    out_bottom_last = permute(bottom_send, "heads", 1)
    layer_out = jnp.concatenate(
        [
            residual_own[:half] + wide(out_rest[:half]) + wide(out_top[:half]) + wide(out_top_last),
            residual_own[half:]
            + wide(out_rest[half : 2 * half])
            + wide(out_bottom[:half])
            + wide(out_bottom_last),
        ],
        axis=0,
    ).astype(jnp.bfloat16)

    projected_grad, head_sum = project_back(
        own, query_grad, pair_sum, returned, raw, head_gain, cosine, sine, size, 256
    )
    qkv_part = turned_product(normed, [projected_grad], 512)
    input_grad, qkv_grad, gains, out_grad, ffn_in_grad = finish(
        projected_grad, qkv_part, inputs, residual_grad, attn_scaling, ffn_sum, head_sum, qkv_group,
        qkv_peers, out_slices, in_part, query_width, head_dim
    )
    return (
        layer_out,
        input_grad,
        gains[0, :depth],
        qkv_grad,
        gains[1, :head_dim],
        gains[1, head_dim : 2 * head_dim],
        out_grad,
        gains[0, 64 : 64 + depth],
        ffn_in_grad,
        ffn_out_grad,
    )


def solution(mesh):
    placed = (
        P(("blk", "heads"), None),
        P("blk"),
        P(("heads", "blk")),
        P(("heads", "blk"), None),
        P(),
        P(),
        P(("heads", "blk"), None),
        P(("heads", "blk")),
        P(("heads", "blk"), None),
        P(("heads", "blk"), None),
        P(("blk", "heads"), None),
    )
    return jax.shard_map(
        local,
        mesh=mesh,
        in_specs=placed,
        out_specs=(
            P(("blk", "heads"), None),
            P(("blk", "heads"), None),
            P(("heads", "blk")),
            P(("heads", "blk"), None),
            P(),
            P(),
            P(("heads", "blk"), None),
            P(("heads", "blk")),
            P(("heads", "blk"), None),
            P(("heads", "blk"), None),
        ),
        check_vma=False,
    )
```

```python
import functools

import jax
import jax.numpy as jnp
from jax import lax
from jax.experimental import pallas as pl
from jax.experimental.pallas import tpu as pltpu
from jax.sharding import PartitionSpec as P

HEADS = 16
KV_HEADS = 4


EPS = 1e-06
ROPE_BASE = 10000.0
NEG = -1e30
MESH = pl.DeviceIdType.MESH
ROWS_IN_BOTH = (((1,), (1,)), ((), ()))


def from_behind(block, axis, distance):
    devices = range(lax.axis_size(axis))
    route = [(i - distance, i) for i in devices if i - distance in devices]
    return lax.ppermute(block, axis, route)


def rotation(positions, head_dim):
    half_width = head_dim // 2
    frequency = ROPE_BASE ** (-2.0 * jnp.arange(half_width, dtype=jnp.float32) / head_dim)
    angles = positions.astype(jnp.float32)[:, None] * frequency[None, :]
    return (jnp.cos(angles)[:, None, :], jnp.sin(angles)[:, None, :])


def stack_heads(tile, heads, first):
    turned = tile.T
    dim = turned.shape[0] // heads
    wide = jnp.concatenate([turned[h * dim : (h + 1) * dim] for h in range(heads)], axis=1)
    zero = jnp.zeros_like(wide)
    return jnp.concatenate([wide, zero] if first else [zero, wide], axis=0)


def unstack_heads(wide, heads):
    count = wide.shape[1] // heads
    return jnp.concatenate([wide[:, h * count : (h + 1) * count] for h in range(heads)], axis=0).T


def scores_at(pair, query_ext, low, first_query, key_start, heads):
    scores = jnp.dot(pair, query_ext, preferred_element_type=jnp.float32)
    rows, columns = scores.shape
    shape = (rows, columns // heads)
    key = key_start + lax.broadcasted_iota(jnp.int32, shape, 0)
    query = first_query + lax.broadcasted_iota(jnp.int32, shape, 1)
    bias = jnp.where((key <= query) & (key >= low), 0.0, NEG)
    return scores + jnp.concatenate([bias] * heads, axis=1)


def transpose_into(pair_ref, turned_ref):
    for start in range(0, pair_ref.shape[0], 512):
        turned_ref[:, start : start + 512] = pair_ref[start : start + 512, :].T


def attend_kernel(
    heads, key_rows, scale, first_ref, query_ref, low_ref, pair_ref, out_ref, log_ref, turned_ref,
    mixed_ref, total_ref
):
    step = pl.program_id(0)
    query_rows = query_ref.shape[0]

    @pl.when(step == 0)
    def _():
        transpose_into(pair_ref, turned_ref)

    query_ext = stack_heads(query_ref[...] * jnp.bfloat16(scale), heads, True)
    low = low_ref[...]
    base = pair_ref.shape[0] // 2 + step * query_rows
    mixed_ref[...] = jnp.zeros_like(mixed_ref)
    total_ref[...] = jnp.zeros_like(total_ref)

    def tile(index, carried):
        start = pl.multiple_of(index * key_rows, key_rows)
        expo = jnp.exp(
            scores_at(pair_ref[pl.ds(start, key_rows), :], query_ext, low, base, start, heads)
        )
        total_ref[...] += jnp.sum(expo, axis=0, keepdims=True)
        mixed_ref[...] += jnp.dot(
            turned_ref[:, pl.ds(start, key_rows)],
            expo.astype(jnp.bfloat16),
            preferred_element_type=jnp.float32,
        )
        return carried

    lax.fori_loop(first_ref[step], (base + query_rows - 1) // key_rows + 1, tile, 0)
    total = total_ref[...]
    dim = pair_ref.shape[1] // 2
    out_ref[...] = unstack_heads(mixed_ref[dim:] / total, heads).astype(out_ref.dtype)
    log_ref[...] = jnp.log(total)[None]


def attend_back_kernel(
    heads, key_rows, scale, first_ref, query_ref, low_ref, pair_ref, out_ref, log_ref, *refs
):
    grads_ref, query_grad_ref, pair_grad_ref, behind_ref, turned_ref, sum_ref = refs
    step = pl.program_id(0)
    grad = grads_ref[first_ref[pl.num_programs(0)] ^ step]
    query_rows = query_ref.shape[0]
    dim = pair_ref.shape[1] // 2

    @pl.when(step == 0)
    def _():
        pair_grad_ref[...] = jnp.zeros_like(pair_grad_ref)
        transpose_into(pair_ref, turned_ref)

    query_ext = stack_heads(query_ref[...] * jnp.bfloat16(scale), heads, True)
    grad_ext = stack_heads(grad, heads, False)
    out_ext = stack_heads(out_ref[...], heads, False)
    inner = jnp.sum(
        grad_ext.astype(jnp.float32) * out_ext.astype(jnp.float32), axis=0, keepdims=True
    )
    log_sum = log_ref[0]
    low = low_ref[...]
    base = pair_ref.shape[0] // 2 + step * query_rows
    sum_ref[...] = jnp.zeros_like(sum_ref)

    def tile(index, carried):
        start = pl.multiple_of(index * key_rows, key_rows)
        pair = pair_ref[pl.ds(start, key_rows), :]
        probs = jnp.exp(scores_at(pair, query_ext, low, base, start, heads) - log_sum)
        probs_grad = jnp.dot(pair, grad_ext, preferred_element_type=jnp.float32)
        score_grad = (probs * (probs_grad - inner)).astype(jnp.bfloat16)
        sum_ref[...] += jnp.dot(
            turned_ref[:dim, pl.ds(start, key_rows)], score_grad, preferred_element_type=jnp.float32
        )
        pair_grad_ref[pl.ds(start, key_rows), :] += lax.dot_general(
            score_grad, query_ext, ROWS_IN_BOTH, preferred_element_type=jnp.float32
        ) + lax.dot_general(
            probs.astype(jnp.bfloat16), grad_ext, ROWS_IN_BOTH, preferred_element_type=jnp.float32
        )
        return carried

    lax.fori_loop(first_ref[step], (base + query_rows - 1) // key_rows + 1, tile, 0)
    query_grad_ref[...] = unstack_heads(sum_ref[...] * scale, heads).astype(query_grad_ref.dtype)

    @pl.when(step == pl.num_programs(0) - 1)
    def _():
        behind_ref[...] = pair_grad_ref[: behind_ref.shape[0]].astype(behind_ref.dtype)


def attention_specs(queries, pair, query_rows, heads):
    width = queries.shape[1]
    return (
        pl.BlockSpec((query_rows, width), lambda i, first: (i, 0)),
        pl.BlockSpec((1, query_rows), lambda i, first: (0, i)),
        pl.BlockSpec(pair.shape, lambda i, first: (0, 0)),
        pl.BlockSpec((1, 1, heads * query_rows), lambda i, first: (i, 0, 0)),
    )


def attend(queries, pair, first, low, heads, query_rows, key_rows):
    count, width = queries.shape
    tile, row, whole, logs = attention_specs(queries, pair, query_rows, heads)
    columns = heads * query_rows
    return pl.pallas_call(
        functools.partial(attend_kernel, heads, key_rows, (width // heads) ** -0.5),
        grid_spec=pltpu.PrefetchScalarGridSpec(
            num_scalar_prefetch=1,
            grid=(count // query_rows,),
            in_specs=[tile, row, whole],
            out_specs=[tile, logs],
            scratch_shapes=[
                pltpu.VMEM(pair.shape[::-1], jnp.bfloat16),
                pltpu.VMEM((pair.shape[1], columns), jnp.float32),
                pltpu.VMEM((1, columns), jnp.float32),
            ],
        ),
        out_shape=[
            jax.ShapeDtypeStruct((count, width), jnp.bfloat16),
            jax.ShapeDtypeStruct((count // query_rows, 1, columns), jnp.float32),
        ],
        compiler_params=pltpu.CompilerParams(vmem_limit_bytes=48 << 20),
        cost_estimate=pl.CostEstimate(
            flops=20_000_000_000, bytes_accessed=8_000_000, transcendentals=0
        ),
        name="attend",
    )(first, queries, low, pair)


def attend_back(queries, pair, first, low, grads, out, logs, heads, query_rows, key_rows):
    count, width = queries.shape
    tile, row, whole, log_spec = attention_specs(queries, pair, query_rows, heads)
    columns = heads * query_rows
    behind = (pair.shape[0] // 2, pair.shape[1])
    return pl.pallas_call(
        functools.partial(attend_back_kernel, heads, key_rows, (width // heads) ** -0.5),
        grid_spec=pltpu.PrefetchScalarGridSpec(
            num_scalar_prefetch=1,
            grid=(count // query_rows,),
            in_specs=[tile, row, whole, tile, log_spec]
            + [pl.BlockSpec(grads.shape, lambda i, first: (0, 0, 0))],
            out_specs=[tile, whole, pl.BlockSpec(behind, lambda i, first: (0, 0))],
            scratch_shapes=[
                pltpu.VMEM(pair.shape[::-1], jnp.bfloat16),
                pltpu.VMEM((pair.shape[1] // 2, columns), jnp.float32),
            ],
        ),
        out_shape=[
            jax.ShapeDtypeStruct((count, width), jnp.bfloat16),
            jax.ShapeDtypeStruct(pair.shape, jnp.float32),
            jax.ShapeDtypeStruct(behind, jnp.bfloat16),
        ],
        compiler_params=pltpu.CompilerParams(vmem_limit_bytes=48 << 20),
        cost_estimate=pl.CostEstimate(
            flops=40_000_000_000, bytes_accessed=12_000_000, transcendentals=0
        ),
        name="attend_back",
    )(first, queries, low, pair, out, logs, grads)


def heads_apart(wide, dim):
    rows = wide.shape[0]
    return jnp.concatenate(
        [
            jnp.broadcast_to(
                jnp.mean(jnp.square(wide[:, c : c + dim]), axis=-1, keepdims=True), (rows, dim)
            )
            for c in range(0, wide.shape[1], dim)
        ],
        axis=1,
    )


def spread_mean(wide, dim):
    rows = wide.shape[0]
    return jnp.concatenate(
        [
            jnp.broadcast_to(jnp.mean(wide[:, c : c + dim], axis=-1, keepdims=True), (rows, dim))
            for c in range(0, wide.shape[1], dim)
        ],
        axis=1,
    )


def turn(wide, cosine, sine, dim):
    count = wide.shape[1] // dim
    half = dim // 2
    swapped = jnp.concatenate(
        [
            wide[:, c + shift : c + shift + half]
            for c in range(0, wide.shape[1], dim)
            for shift in (half, 0)
        ],
        axis=1,
    )
    return wide * jnp.concatenate([cosine] * count, axis=1) + swapped * jnp.concatenate(
        [sine] * count, axis=1
    )


def project_kernel(
    dim, x_ref, weight_ref, head_gain_ref, cosine_ref, sine_ref, side_ref, query_ref, pair_ref,
    raw_ref, normed_ref, gain_ref, ffn_gain_ref, spread_ref, send_sem, recv_sem
):
    columns = raw_ref.shape[1]
    step, steps = pl.program_id(0), pl.num_programs(0)
    marks = (0, steps // 2, steps - 2)
    end = spread_job(step, marks, side_ref, spread_ref, send_sem, recv_sem)

    @pl.when(pl.program_id(0) == 0)
    def _():
        gains = weight_ref[:, columns:].T.astype(jnp.float32)
        gain_ref[...] = gains[:1]
        ffn_gain_ref[...] = gains[64:65]

    values = x_ref[...].astype(jnp.float32)
    normed = values * lax.rsqrt(jnp.mean(values * values, axis=-1, keepdims=True) + EPS)
    normed = (normed * gain_ref[...]).astype(jnp.bfloat16)
    normed_ref[...] = normed
    raw = jnp.dot(normed, weight_ref[:, :columns], preferred_element_type=jnp.float32)
    raw_ref[...] = raw
    turned_width = raw.shape[1] - pair_ref.shape[1] // 2
    heads = raw[:, :turned_width]
    heads = heads * lax.rsqrt(heads_apart(heads, dim) + EPS) * head_gain_ref[...]
    heads = turn(heads, cosine_ref[...], sine_ref[...], dim).astype(jnp.bfloat16)
    query_width = query_ref.shape[1]
    query_ref[...] = heads[:, :query_width]
    pair_ref[...] = jnp.concatenate(
        [heads[:, query_width:], raw[:, turned_width:].astype(jnp.bfloat16)], axis=1
    )
    pl.when(step == steps - 1)(end)


def project(x, weight, head_gain, cosine, sine, side, size, query_width, rows):
    count, width = x.shape
    out_width = weight.shape[1] - 128
    pair_width = out_width - query_width
    dim = cosine.shape[1]
    tiles = count // size // rows

    def apart(i):
        return ((lax.axis_index("heads") ^ (i // tiles)) * tiles + i % tiles, 0)

    def there(i):
        return (i, 0)

    def whole(i):
        return (0, 0)

    anywhere = pl.BlockSpec(memory_space=pl.ANY)

    return pl.pallas_call(
        functools.partial(project_kernel, dim),
        grid=(count // rows,),
        in_specs=[
            pl.BlockSpec((rows, width), there),
            pl.BlockSpec(weight.shape, whole),
            pl.BlockSpec(head_gain.shape, whole),
            pl.BlockSpec((rows, dim), apart),
            pl.BlockSpec((rows, dim), apart),
            anywhere,
        ],
        out_specs=[
            pl.BlockSpec((rows, query_width), apart),
            pl.BlockSpec((rows, pair_width), apart),
            pl.BlockSpec((rows, out_width), apart),
            pl.BlockSpec((rows, width), there),
            pl.BlockSpec((1, width), whole),
            pl.BlockSpec((1, width), whole),
            anywhere,
        ],
        out_shape=[
            jax.ShapeDtypeStruct((count, query_width), jnp.bfloat16),
            jax.ShapeDtypeStruct((count, pair_width), jnp.bfloat16),
            jax.ShapeDtypeStruct((count, out_width), jnp.float32),
            jax.ShapeDtypeStruct((count, width), jnp.bfloat16),
            jax.ShapeDtypeStruct((1, width), jnp.float32),
            jax.ShapeDtypeStruct((1, width), jnp.float32),
            jax.ShapeDtypeStruct((3, *side.shape), side.dtype),
        ],
        scratch_shapes=[pltpu.SemaphoreType.DMA((SPREAD_COUNT,))] * 2,
        compiler_params=pltpu.CompilerParams(
            collective_id=5, has_side_effects=True, vmem_limit_bytes=48 << 20
        ),
        cost_estimate=pl.CostEstimate(
            flops=4 * count * width * out_width, bytes_accessed=30_000_000, transcendentals=0
        ),
        name="project",
    )(x, weight, head_gain, cosine, sine, side)


def project_back_kernel(
    dim, size, query_grad_ref, pair_grad_ref, raw_ref, head_gain_ref, cosine_ref, sine_ref,
    behind_ref, grad_ref, gain_grad_ref, returned_ref, send_sem, recv_sem
):
    step = pl.program_id(0)
    head, blk = lax.axis_index("heads"), lax.axis_index("blk")
    last = lax.axis_size("blk") - 1
    rows = raw_ref.shape[0]
    tiles = returned_ref.shape[0] // size // rows
    back = pltpu.make_async_remote_copy(
        src_ref=behind_ref,
        dst_ref=returned_ref,
        send_sem=send_sem,
        recv_sem=recv_sem,
        device_id=(head, jnp.maximum(blk - 1, 0)),
        device_id_type=MESH,
    )

    @pl.when(step == 0)
    def _():
        barrier = pltpu.get_barrier_semaphore()

        @pl.when(blk < last)
        def _():
            pl.semaphore_signal(
                barrier, inc=1, device_id=(head, blk + 1), device_id_type=MESH
            )

        @pl.when(blk > 0)
        def _():
            pl.semaphore_wait(barrier, 1)
            back.start()

        @pl.when(blk == last)
        def _():
            returned_ref[...] = jnp.zeros_like(returned_ref)

        @pl.when(blk < last)
        def _():
            back.wait_recv()

        gain_grad_ref[...] = jnp.zeros_like(gain_grad_ref)

    place = ((head ^ (step // tiles)) * tiles + lax.rem(step, tiles)) * rows
    returned = returned_ref[pl.ds(pl.multiple_of(place, rows), rows)]
    pair_grad = pair_grad_ref[...] + returned.astype(jnp.float32)
    pair_grad = pair_grad.astype(jnp.bfloat16)
    half = pair_grad.shape[1] // 2
    grads = jnp.concatenate([query_grad_ref[...], pair_grad[:, :half]], axis=1).astype(jnp.float32)
    grads = turn(grads, cosine_ref[...], -sine_ref[...], dim)
    values = raw_ref[:, : grads.shape[1]]
    inverse = lax.rsqrt(heads_apart(values, dim) + EPS)
    gain_grad_ref[...] += jnp.sum(grads * values * inverse, axis=0, keepdims=True)
    scaled = grads * head_gain_ref[...]
    moment = spread_mean(scaled * values, dim)
    values_grad = inverse * scaled - values * inverse * inverse * inverse * moment
    grad_ref[...] = jnp.concatenate([values_grad.astype(jnp.bfloat16), pair_grad[:, half:]], axis=1)

    @pl.when((step == pl.num_programs(0) - 1) & (blk > 0))
    def _():
        back.wait_send()


def project_back(query_grad, pair_sum, behind, raw, head_gain, cosine, sine, size, rows):
    count, query_width = query_grad.shape
    pair_width = pair_sum.shape[1]
    out_width = raw.shape[1]
    dim = cosine.shape[1]
    tiles = count // size // rows

    def apart(i):
        return ((lax.axis_index("heads") ^ (i // tiles)) * tiles + i % tiles, 0)

    def after_behind(i):
        return (apart(i)[0] + count // rows, 0)

    def whole(i):
        return (0, 0)

    return pl.pallas_call(
        functools.partial(project_back_kernel, dim, size),
        grid=(count // rows,),
        in_specs=[
            pl.BlockSpec((rows, query_width), apart),
            pl.BlockSpec((rows, pair_width), after_behind),
            pl.BlockSpec((rows, out_width), apart),
            pl.BlockSpec(head_gain.shape, whole),
            pl.BlockSpec((rows, dim), apart),
            pl.BlockSpec((rows, dim), apart),
            pl.BlockSpec(memory_space=pl.ANY),
        ],
        out_specs=[
            pl.BlockSpec((rows, out_width), lambda i: (i, 0)),
            pl.BlockSpec(head_gain.shape, whole),
        ],
        scratch_shapes=[
            pltpu.VMEM(behind.shape, behind.dtype),
            pltpu.SemaphoreType.DMA,
            pltpu.SemaphoreType.DMA,
        ],
        out_shape=[
            jax.ShapeDtypeStruct((count, out_width), jnp.bfloat16),
            jax.ShapeDtypeStruct(head_gain.shape, jnp.float32),
        ],
        compiler_params=pltpu.CompilerParams(
            collective_id=9, has_side_effects=True, vmem_limit_bytes=48 << 20
        ),
        cost_estimate=pl.CostEstimate(
            flops=8_000_000_000, bytes_accessed=8_000_000, transcendentals=0
        ),
        name="project_back",
    )(query_grad, pair_sum, raw, head_gain, cosine, sine, behind)


def join_kernel(
    x_ref, weight_ref, weights_ref, gain_ref, mine_ref, cot_ref, residual_ref,
    normed_ref, attended_ref, cot_one_ref, cot_two_ref, held_ref, local_sem, send_sem, recv_sem
):
    step = pl.program_id(0)
    head, blk = lax.axis_index("heads"), lax.axis_index("blk")
    rows = x_ref.shape[0]
    count = held_ref.shape[1] // 4
    tiles = count // rows

    def copy(source, target, k, index):
        return pltpu.make_async_remote_copy(
            src_ref=source,
            dst_ref=target,
            send_sem=send_sem.at[index],
            recv_sem=recv_sem.at[index],
            device_id=(head ^ k, blk),
            device_id_type=MESH,
        )

    upper, lower = pl.ds(0, 2 * count), pl.ds(2 * count, 2 * count)
    near = [copy(mine_ref, held_ref.at[k], k, k - 1) for k in (1, 2)]
    far = [
        copy(held_ref.at[1, upper], held_ref.at[3, upper], 2, 2),
        copy(held_ref.at[2, lower], held_ref.at[3, lower], 1, 3),
    ]
    half = count // 2
    cot_near = [
        copy(cot_ref.at[pl.ds(half, half)], cot_one_ref, 1, 4),
        copy(cot_ref.at[pl.ds(0, half)], cot_two_ref, 2, 5),
    ]
    own = pltpu.make_async_copy(mine_ref, held_ref.at[0], local_sem)

    @pl.when(step == 0)
    def _():
        own.start()
        greet_near(False)
        for first in near:
            first.start()
        for first, second in zip(near, far):
            first.wait_recv()
            second.start()
        own.wait()
        for second in far:
            second.wait_recv()
        for last in cot_near:
            last.start()

    chunk = step // tiles
    parts = []
    total = x_ref[...].astype(jnp.float32)
    for k in range(4):
        start = ((chunk ^ k) * tiles + lax.rem(step, tiles)) * rows
        part = held_ref[k, pl.ds(pl.multiple_of(start, rows), rows)]
        weight = weight_ref[...] if k == 0 else weights_ref[k - 1]
        total += jnp.dot(part, weight, preferred_element_type=jnp.float32)
        parts.append(part)
    residual_ref[...] = total
    normed = total * lax.rsqrt(jnp.mean(total * total, axis=-1, keepdims=True) + EPS)
    normed_ref[...] = (normed * gain_ref[...]).astype(jnp.bfloat16)

    @pl.when(chunk == 0)
    def _():
        attended_ref[...] = jnp.concatenate(parts, axis=1)

    @pl.when(step == pl.num_programs(0) - 1)
    def _():
        for first in near + far:
            first.wait_send()
        for last in cot_near:
            last.wait()


def join(x, mine, weight, weights, gain, cot, rows):
    count, width = x.shape
    tokens = count // 4
    columns = mine.shape[1]
    tiles = tokens // rows
    anywhere = pl.BlockSpec(memory_space=pl.ANY)

    def there(i):
        return (i, 0)

    def whole(i):
        return (0, 0)

    sems = pltpu.SemaphoreType.DMA
    return pl.pallas_call(
        join_kernel,
        grid=(count // rows,),
        in_specs=[
            pl.BlockSpec((rows, width), there),
            pl.BlockSpec(weight.shape, whole),
            pl.BlockSpec(weights.shape, lambda i: (0, 0, 0)),
            pl.BlockSpec((1, width), whole),
            anywhere,
            anywhere,
        ],
        out_specs=[
            pl.BlockSpec((rows, width), there),
            pl.BlockSpec((rows, width), there),
            pl.BlockSpec((rows, 4 * columns), lambda i: (jnp.minimum(i, tiles - 1), 0)),
            anywhere,
            anywhere,
        ],
        out_shape=[
            jax.ShapeDtypeStruct((count, width), jnp.float32),
            jax.ShapeDtypeStruct((count, width), jnp.bfloat16),
            jax.ShapeDtypeStruct((tokens, 4 * columns), jnp.bfloat16),
            jax.ShapeDtypeStruct((tokens // 2, width), jnp.bfloat16),
            jax.ShapeDtypeStruct((tokens // 2, width), jnp.bfloat16),
        ],
        scratch_shapes=[
            pltpu.VMEM((4, count, columns), jnp.bfloat16),
            sems,
            sems((6,)),
            sems((6,)),
        ],
        compiler_params=pltpu.CompilerParams(
            collective_id=6, has_side_effects=True, vmem_limit_bytes=56 << 20
        ),
        cost_estimate=pl.CostEstimate(
            flops=16 * count * width * columns, bytes_accessed=50_000_000, transcendentals=0
        ),
        name="join",
    )(x, weight, weights, gain, mine, cot)


def trade_kernel(in_ref, out_ref, send_sem, recv_sem):
    head, blk = lax.axis_index("heads"), lax.axis_index("blk")
    size = lax.axis_size("heads")
    units = out_ref.shape[2] // 2
    barrier = pltpu.get_barrier_semaphore()
    for k in range(1, size):
        pl.semaphore_signal(barrier, inc=1, device_id=(head ^ k, blk), device_id_type=MESH)
    pl.semaphore_wait(barrier, size - 1)

    def columns(part, owner):
        return pl.ds(pl.multiple_of((part * size + owner) * units, units), units)

    copies = [
        pltpu.make_async_remote_copy(
            src_ref=in_ref.at[:, columns(part, head ^ k)],
            dst_ref=out_ref.at[head, :, pl.ds(part * units, units)],
            send_sem=send_sem.at[2 * k - 2 + part],
            recv_sem=recv_sem.at[2 * k - 2 + part],
            device_id=(head ^ k, blk),
            device_id_type=MESH,
        )
        for k in range(1, size)
        for part in range(2)
    ]
    for copy in copies:
        copy.start()
    for part in range(2):
        out_ref[head, :, part * units : (part + 1) * units] = in_ref[:, columns(part, head)]
    for copy in copies:
        copy.wait()


def trade(weight):
    size = lax.axis_size("heads")
    depth, width = weight.shape
    vmem = pl.BlockSpec(memory_space=pltpu.VMEM)
    return pl.pallas_call(
        trade_kernel,
        out_shape=jax.ShapeDtypeStruct((size, depth, width // size), weight.dtype),
        in_specs=[vmem],
        out_specs=vmem,
        scratch_shapes=[pltpu.SemaphoreType.DMA((2 * size - 2,))] * 2,
        compiler_params=pltpu.CompilerParams(
            collective_id=8, has_side_effects=True, vmem_limit_bytes=16 << 20
        ),
        name="trade",
    )(weight)


def begin_kernel(
    x_ref, qkv_ref, x_out, qkv_out, local_sem, x_send, x_recv, q_send, q_recv, b_send, b_recv,
    c_send, c_recv
):
    head, blk = lax.axis_index("heads"), lax.axis_index("blk")
    size, blk_size = lax.axis_size("heads"), lax.axis_size("blk")
    pairs = blk_size // 2
    count, depth = x_ref.shape[0], qkv_ref.shape[1]
    half = count // 2
    barrier = pltpu.get_barrier_semaphore()
    for k in range(1, size):
        pl.semaphore_signal(barrier, inc=1, device_id=(head ^ k, blk), device_id_type=MESH)
    pl.semaphore_signal(barrier, inc=1, device_id=(head, blk ^ 1), device_id_type=MESH)

    def same_core(k):
        return lax.rem(blk + 2 * k, blk_size)

    def greet(k, carried):
        pl.semaphore_signal(barrier, inc=1, device_id=(head, same_core(k)), device_id_type=MESH)
        return carried

    lax.fori_loop(1, pairs, greet, 0)
    pl.semaphore_wait(barrier, size + pairs - 1)

    def send(source, target, k, send_sem, recv_sem):
        return pltpu.make_async_remote_copy(
            src_ref=source,
            dst_ref=target,
            send_sem=send_sem,
            recv_sem=recv_sem,
            device_id=(head ^ k, blk),
            device_id_type=MESH,
        )

    def rows_of(index):
        return pl.ds(pl.multiple_of(index * depth, depth), depth)

    rows = rows_of(blk)
    qkv_copies = [
        send(
            qkv_ref.at[head ^ k], qkv_out.at[head, rows], k, q_send.at[k - 1], q_recv.at[k - 1]
        )
        for k in range(1, size)
    ]
    near = [
        send(x_ref, x_out.at[pl.ds(k * count, count)], k, x_send.at[k - 1], x_recv.at[k - 1])
        for k in (1, 2)
    ]
    far = [
        send(
            x_out.at[pl.ds(count, half)],
            x_out.at[pl.ds(3 * count, half)],
            2,
            x_send.at[2],
            x_recv.at[2],
        ),
        send(
            x_out.at[pl.ds(2 * count + half, half)],
            x_out.at[pl.ds(3 * count + half, half)],
            1,
            x_send.at[3],
            x_recv.at[3],
        ),
    ]
    own = [
        pltpu.make_async_copy(qkv_ref.at[head], qkv_out.at[head, rows], local_sem.at[0]),
        pltpu.make_async_copy(x_ref, x_out.at[pl.ds(0, count)], local_sem.at[1]),
    ]
    for copy in qkv_copies + near + own:
        copy.start()

    def along(k, source):
        return pltpu.make_async_remote_copy(
            src_ref=qkv_out.at[:, rows],
            dst_ref=qkv_out.at[:, rows_of(source)],
            send_sem=b_send.at[k],
            recv_sem=b_recv.at[k],
            device_id=(head, same_core(k)),
            device_id_type=MESH,
        )

    def behind(k):
        return lax.rem(blk + blk_size - 2 * k, blk_size)

    def across(k, core):
        source = behind(k) ^ core
        return pltpu.make_async_remote_copy(
            src_ref=qkv_out.at[:, rows_of(behind(k))],
            dst_ref=qkv_out.at[:, rows_of(source)],
            send_sem=c_send.at[k],
            recv_sem=c_recv.at[k],
            device_id=(head, blk ^ 1),
            device_id_type=MESH,
        )

    def start(k, carried):
        along(k, blk).start()
        return carried

    def pass_on(k, carried):
        along(k, behind(k)).wait_recv()
        across(k, 0).start()
        return carried

    def finish(k, carried):
        across(k, 0).wait_send()
        across(k, 1).wait_recv()
        return carried

    def sent(k, carried):
        along(k, blk).wait_send()
        return carried

    own[0].wait()
    for copy in qkv_copies:
        copy.wait_recv()
    lax.fori_loop(1, pairs, start, 0)
    across(0, 0).start()
    lax.fori_loop(1, pairs, pass_on, 0)
    for first, second in zip(near, far):
        first.wait_recv()
        second.start()
    for copy in qkv_copies + near:
        copy.wait_send()
    for copy in far:
        copy.wait()
    own[1].wait()
    lax.fori_loop(1, pairs, sent, 0)
    lax.fori_loop(0, pairs, finish, 0)


def begin(x, qkv_parts):
    size, blk_size = lax.axis_size("heads"), lax.axis_size("blk")
    count, width = x.shape
    depth, joined = qkv_parts.shape[1:]
    anywhere = pl.BlockSpec(memory_space=pl.ANY)
    sems = pltpu.SemaphoreType.DMA
    return pl.pallas_call(
        begin_kernel,
        out_shape=[
            jax.ShapeDtypeStruct((size * count, width), x.dtype),
            jax.ShapeDtypeStruct((size, blk_size * depth, joined), x.dtype),
        ],
        in_specs=[anywhere] * 2,
        out_specs=[anywhere] * 2,
        scratch_shapes=[
            sems((2,)),
            sems((4,)),
            sems((4,)),
            sems((size - 1,)),
            sems((size - 1,)),
            sems((blk_size // 2,)),
            sems((blk_size // 2,)),
            sems((blk_size // 2,)),
            sems((blk_size // 2,)),
        ],
        compiler_params=pltpu.CompilerParams(collective_id=1, has_side_effects=True),
        name="begin",
    )(x, qkv_parts)


def spread_copies(source_ref, target_ref, send_sem, recv_sem):
    head, blk = lax.axis_index("heads"), lax.axis_index("blk")
    rows = source_ref.shape[0] // 2
    quarter = rows // 2
    start = pl.multiple_of(lax.rem(blk, 2) * rows, rows)
    half = pl.ds(start, rows)
    first = source_ref.at[half, pl.ds(0, target_ref.shape[2])]
    count = [0]

    def copy(source, target, place):
        index = count[0]
        count[0] += 1
        return pltpu.make_async_remote_copy(
            src_ref=source,
            dst_ref=target,
            send_sem=send_sem.at[index],
            recv_sem=recv_sem.at[index],
            device_id=place,
            device_id_type=MESH,
        )

    near = [
        copy(first, target_ref.at[k - 1, half], (head ^ k, blk)) for k in (1, 2)
    ]
    upper = pl.ds(start, quarter)
    lower = pl.ds(pl.multiple_of(start + quarter, quarter), quarter)
    far = [
        copy(target_ref.at[0, upper], target_ref.at[2, upper], (head ^ 2, blk)),
        copy(target_ref.at[1, lower], target_ref.at[2, lower], (head ^ 1, blk)),
    ]
    other = [
        copy(target_ref.at[k, half], target_ref.at[k, half], (head, blk ^ 1)) for k in range(3)
    ]
    return near, far, other


def greet_near(partner):
    head, blk = lax.axis_index("heads"), lax.axis_index("blk")
    barrier = pltpu.get_barrier_semaphore()
    places = [(head ^ 1, blk), (head ^ 2, blk)] + ([(head, blk ^ 1)] if partner else [])
    for place in places:
        pl.semaphore_signal(barrier, inc=1, device_id=place, device_id_type=MESH)
    pl.semaphore_wait(barrier, len(places))


def spread_job(step, marks, source_ref, target_ref, send_sem, recv_sem, greet=True):
    near, far, other = spread_copies(source_ref, target_ref, send_sem, recv_sem)
    begin_at, far_at, other_at = marks

    @pl.when(step == begin_at)
    def _():
        if greet:
            greet_near(True)
        for copy in near:
            copy.start()

    @pl.when(step == far_at)
    def _():
        for k in range(2):
            near[k].wait_recv()
            far[k].start()
            other[k].start()

    @pl.when(step == other_at)
    def _():
        for copy in far:
            copy.wait_recv()
        other[2].start()

    def end():
        for copy in near + far:
            copy.wait_send()
        for copy in other:
            copy.wait()

    return end


SPREAD_COUNT = 7


def hidden_kernel(
    tiles, normed_ref, gate_ref, up_ref, down_ref, turned_ref, side_ref, cot_ref, one_top_ref,
    one_bottom_ref, two_top_ref, two_bottom_ref, hidden_ref, gate_grad_ref, up_grad_ref, in_sum_ref,
    cot_far_ref, spread_ref, held_ref, grads_ref, load_sem, far_send, far_recv, send_sem, recv_sem
):
    step, steps = pl.program_id(0), pl.num_programs(0)
    head, blk = lax.axis_index("heads"), lax.axis_index("blk")
    count = cot_ref.shape[0]
    half = count // 2
    rows, units = hidden_ref.shape
    far = [
        pltpu.make_async_remote_copy(
            src_ref=ref,
            dst_ref=held_ref.at[pl.ds(3 * count + part * half, half)],
            send_sem=far_send.at[part],
            recv_sem=far_recv.at[part],
            device_id=(head ^ k, blk),
            device_id_type=MESH,
        )
        for part, (ref, k) in enumerate(((one_top_ref, 2), (two_bottom_ref, 1)))
    ]
    keep = pltpu.make_async_copy(
        held_ref.at[pl.ds(3 * count, count)], cot_far_ref, load_sem.at[5]
    )
    near = ((one_top_ref, 2), (one_bottom_ref, 3), (two_top_ref, 4), (two_bottom_ref, 5))
    loads = [pltpu.make_async_copy(cot_ref, held_ref.at[pl.ds(0, count)], load_sem.at[0])] + [
        pltpu.make_async_copy(ref, held_ref.at[pl.ds(half * place, half)], load_sem.at[place - 1])
        for ref, place in near
    ]

    @pl.when(step == 0)
    def _():
        for load in loads:
            load.start()
        greet_near(True)
        for copy in far:
            copy.start()
        for load in loads:
            load.wait()

    @pl.when(step == tiles)
    def _():
        for copy in far:
            copy.wait()
        keep.start()

    marks = (tiles, 2 * tiles, 2 * tiles + 4)
    end = spread_job(step, marks, side_ref, spread_ref, send_sem, recv_sem, False)

    @pl.when(step < 2 * tiles)
    def _():
        here = pl.ds(pl.multiple_of(step // tiles * rows, rows), rows)
        normed = normed_ref[...]
        gate = jnp.dot(normed, gate_ref[...], preferred_element_type=jnp.float32)
        upward = jnp.dot(normed, up_ref[...], preferred_element_type=jnp.float32)
        grad = lax.dot_general(
            held_ref[here], down_ref[...], ROWS_IN_BOTH, preferred_element_type=jnp.float32
        )
        sigmoid = jax.nn.sigmoid(gate)
        activated = gate * sigmoid
        hidden_ref[...] = (activated * upward).astype(jnp.bfloat16)
        gate_grad = (grad * upward * sigmoid * (1.0 + gate * (1.0 - sigmoid))).astype(jnp.bfloat16)
        up_grad = (grad * activated).astype(jnp.bfloat16)
        gate_grad_ref[...] = gate_grad
        up_grad_ref[...] = up_grad
        for part, value in enumerate((gate_grad, up_grad)):
            place = (part * tiles + lax.rem(step, tiles)) * units
            grads_ref[here, pl.ds(pl.multiple_of(place, units), units)] = value

    @pl.when(step >= 2 * tiles)
    def _():
        in_sum_ref[...] = lax.dot_general(
            turned_ref[...],
            grads_ref[...],
            (((0,), (0,)), ((), ())),
            preferred_element_type=jnp.float32,
        ).astype(jnp.bfloat16)

    @pl.when(step == steps - 1)
    def _():
        end()
        keep.wait()


def hidden_pass(normed, weight, cot, cot_near, down, side, side_columns, units):
    count, width = normed.shape
    total = down.shape[0]
    tiles = total // units
    rows = count // 2
    columns = width // 8

    def row(s):
        return jnp.minimum(s // tiles, 1)

    def column(s):
        return jnp.where(s < 2 * tiles, lax.rem(s, tiles), tiles - 1)

    out_spec = pl.BlockSpec((rows, units), lambda s: (row(s), column(s)))
    out_shape = jax.ShapeDtypeStruct((count, total), jnp.bfloat16)
    anywhere = pl.BlockSpec(memory_space=pl.ANY)
    sems = pltpu.SemaphoreType.DMA
    return pl.pallas_call(
        functools.partial(hidden_kernel, tiles),
        grid=(2 * tiles + 8,),
        in_specs=[
            pl.BlockSpec((rows, width), lambda s: (row(s), 0)),
            pl.BlockSpec((width, units), lambda s: (0, column(s))),
            pl.BlockSpec((width, units), lambda s: (0, tiles + column(s))),
            pl.BlockSpec((units, width), lambda s: (column(s), 0)),
            pl.BlockSpec((count, columns), lambda s: (0, jnp.maximum(s - 2 * tiles, 0))),
        ]
        + [anywhere] * 6,
        out_specs=[out_spec] * 3
        + [
            pl.BlockSpec((columns, 2 * total), lambda s: (jnp.maximum(s - 2 * tiles, 0), 0)),
            anywhere,
            anywhere,
        ],
        out_shape=[out_shape] * 3
        + [
            jax.ShapeDtypeStruct((width, 2 * total), jnp.bfloat16),
            jax.ShapeDtypeStruct(cot.shape, jnp.bfloat16),
            jax.ShapeDtypeStruct((3, side.shape[0], side_columns), side.dtype),
        ],
        scratch_shapes=[
            pltpu.VMEM((count, width), jnp.bfloat16),
            pltpu.VMEM((count, 2 * total), jnp.bfloat16),
            sems((6,)),
            sems((2,)),
            sems((2,)),
            sems((SPREAD_COUNT,)),
            sems((SPREAD_COUNT,)),
        ],
        compiler_params=pltpu.CompilerParams(
            collective_id=2, has_side_effects=True, vmem_limit_bytes=58 << 20
        ),
        cost_estimate=pl.CostEstimate(
            flops=10 * count * width * total, bytes_accessed=70_000_000, transcendentals=0
        ),
        name="hidden_pass",
    )(normed, weight, weight, down, normed, side, cot, *cot_near)


def in_order(step):
    value = 1
    for index, half in enumerate((6, 7, 2, 5, 4, 3, 0)):
        value = jnp.where(step == index, half, value)
    return value


def tail_kernel(
    gate_ref, up_ref, hidden_ref, turned_ref, in_hbm, down_hbm, cot_ref, one_top_ref, one_bottom_ref,
    two_top_ref, two_bottom_ref, cot_far_ref, down_sum_ref, *refs
):
    first_refs, (out_rest_ref, grad_ref, *refs) = refs[:4], refs[4:]
    (
        weight_ref, down_ref, first_ref, rest_ref, got_ref, last_ref, last_got_ref, weight_sem,
        send_sem, recv_sem,
    ) = refs
    step = pl.program_id(0)
    head, blk = lax.axis_index("heads"), lax.axis_index("blk")
    rows, total = hidden_ref.shape
    width = grad_ref.shape[1]
    load_in = pltpu.make_async_copy(in_hbm, weight_ref, weight_sem.at[0])
    load_down = pltpu.make_async_copy(down_hbm, down_ref, weight_sem.at[1])
    pieces = (
        (cot_ref, 0, 2),
        (one_top_ref, 2, 1),
        (one_bottom_ref, 3, 1),
        (two_top_ref, 4, 1),
        (two_bottom_ref, 5, 1),
        (cot_far_ref, 6, 2),
    )
    cot_loads = [
        pltpu.make_async_copy(
            ref,
            weight_ref.at[pl.ds(place * rows, length * rows), pl.ds(0, width)],
            weight_sem.at[2 + index],
        )
        for index, (ref, place, length) in enumerate(pieces)
    ]

    def copy(source, target, k, index):
        return pltpu.make_async_remote_copy(
            src_ref=source,
            dst_ref=target,
            send_sem=send_sem.at[index],
            recv_sem=recv_sem.at[index],
            device_id=(head ^ k, blk),
            device_id_type=MESH,
        )

    firsts = [
        copy(first_ref.at[index], got_ref.at[index], k, index)
        for index, k in enumerate((1, 2, 1, 2))
    ]
    lasts = [copy(last_ref.at[part], last_got_ref.at[part], 2 - part, 4 + part) for part in range(2)]

    def wide_of(block):
        return block.astype(jnp.float32)

    @pl.when(step == 0)
    def _():
        load_in.start()
        load_down.start()
        greet_near(False)
        load_in.wait()

    @pl.when(step < 8)
    def _():
        value = lax.dot_general(
            gate_ref[...], weight_ref[:, :total], ROWS_IN_BOTH, preferred_element_type=jnp.float32
        ) + lax.dot_general(
            up_ref[...], weight_ref[:, total:], ROWS_IN_BOTH, preferred_element_type=jnp.float32
        )
        value = value.astype(jnp.bfloat16)

        for index in range(4):

            @pl.when(step == index)
            def _(index=index):
                first_ref[index] = value
                firsts[index].start()

        @pl.when(step >= 4)
        def _():
            rest_ref[pl.ds(pl.multiple_of((step - 4) * rows, rows), rows)] = value

        @pl.when(step == 7)
        def _():
            load_down.wait()
            for load in cot_loads:
                load.start()

    @pl.when((step >= 8) & (step < 16))
    def _():
        terms = jnp.dot(
            hidden_ref[...], down_ref[...], preferred_element_type=jnp.float32
        ).astype(jnp.bfloat16)

        for index, ref in enumerate(first_refs):

            @pl.when(step == 8 + index)
            def _(ref=ref):
                ref[...] = terms

        @pl.when(step >= 12)
        def _():
            out_rest_ref[...] = terms

        @pl.when(step == 15)
        def _():
            for load in cot_loads:
                load.wait()

    @pl.when(step >= 16)
    def _():
        down_sum_ref[...] = lax.dot_general(
            turned_ref[...],
            weight_ref[:, :width],
            (((0,), (0,)), ((), ())),
            preferred_element_type=jnp.float32,
        ).astype(jnp.bfloat16)

    for part, when in enumerate((8, 9)):

        @pl.when(step == when)
        def _(part=part):
            firsts[part].wait_recv()
            last_ref[part] = (
                wide_of(rest_ref[part * rows : (part + 1) * rows]) + wide_of(got_ref[part])
            ).astype(jnp.bfloat16)
            lasts[part].start()

    @pl.when(step == pl.num_programs(0) - 1)
    def _():
        for part in range(2):
            firsts[2 + part].wait_recv()
            lasts[part].wait_recv()
            grad_ref[part * rows : (part + 1) * rows] = (
                wide_of(rest_ref[(2 + part) * rows : (3 + part) * rows])
                + wide_of(got_ref[2 + part])
                + wide_of(last_got_ref[part])
            )
        for sent in firsts + lasts:
            sent.wait_send()


def feed_tail(gate_grad, up_grad, hidden, weight, down, cots):
    count, total = hidden.shape
    width = weight.shape[0]
    rows = count // 8
    units = 256
    anywhere = pl.BlockSpec(memory_space=pl.ANY)

    def stage(i, first, last):
        return jnp.clip(i - first, 0, last)

    def first_rows(i):
        return (in_order(stage(i, 0, 7)), 0)

    low = jnp.bfloat16
    return pl.pallas_call(
        tail_kernel,
        grid=(16 + total // units,),
        in_specs=[
            pl.BlockSpec((rows, total), first_rows),
            pl.BlockSpec((rows, total), first_rows),
            pl.BlockSpec((rows, total), lambda i: (in_order(stage(i, 8, 7)), 0)),
            pl.BlockSpec((count, units), lambda i: (0, jnp.maximum(i - 16, 0))),
        ]
        + [anywhere] * 8,
        out_specs=[
            pl.BlockSpec((units, width), lambda i: (jnp.maximum(i - 16, 0), 0)),
            *[pl.BlockSpec((rows, width), lambda i: (0, 0), pipeline_mode=pl.Buffered(1))] * 4,
            pl.BlockSpec((rows, width), lambda i: (stage(i, 12, 3), 0)),
            pl.BlockSpec((2 * rows, width), lambda i: (0, 0), pipeline_mode=pl.Buffered(1)),
        ],
        out_shape=[
            jax.ShapeDtypeStruct((total, width), low),
            *[jax.ShapeDtypeStruct((rows, width), low)] * 4,
            jax.ShapeDtypeStruct((4 * rows, width), low),
            jax.ShapeDtypeStruct((2 * rows, width), jnp.float32),
        ],
        scratch_shapes=[
            pltpu.VMEM(weight.shape, low),
            pltpu.VMEM(down.shape, low),
            pltpu.VMEM((4, rows, width), low),
            pltpu.VMEM((4 * rows, width), low),
            pltpu.VMEM((4, rows, width), low),
            pltpu.VMEM((2, rows, width), low),
            pltpu.VMEM((2, rows, width), low),
            pltpu.SemaphoreType.DMA((8,)),
            pltpu.SemaphoreType.DMA((6,)),
            pltpu.SemaphoreType.DMA((6,)),
        ],
        compiler_params=pltpu.CompilerParams(
            collective_id=3, has_side_effects=True, vmem_limit_bytes=60 << 20
        ),
        cost_estimate=pl.CostEstimate(
            flops=8 * count * width * total, bytes_accessed=70_000_000, transcendentals=0
        ),
        name="feed_tail",
    )(gate_grad, up_grad, hidden, hidden, weight, down, *cots)


def residual_back_kernel(
    grad_sum_ref, residual_ref, cot_ref, gain_ref, attended_ref, weight_ref, weights_ref, grad_ref,
    gain_grad_ref, pieces_ref, *refs
):
    *out_refs, branch_ref, mine_ref, terms_ref, terms_got_ref, own_sem, send_sem, recv_sem = refs
    size = lax.axis_size("heads")
    core = lax.rem(lax.axis_index("blk"), 2)
    step = pl.program_id(0)
    last = pl.num_programs(0) - 1
    head, blk = lax.axis_index("heads"), lax.axis_index("blk")
    rows = cot_ref.shape[0]
    copies = [
        pltpu.make_async_remote_copy(
            src_ref=mine_ref.at[k],
            dst_ref=pieces_ref.at[k],
            send_sem=send_sem.at[k - 1],
            recv_sem=recv_sem.at[k - 1],
            device_id=(head ^ k, blk),
            device_id_type=MESH,
        )
        for k in range(1, size)
    ]
    keep = pltpu.make_async_copy(mine_ref.at[0], pieces_ref.at[0], own_sem)
    across = pltpu.make_async_remote_copy(
        src_ref=terms_ref.at[:, 1 - core],
        dst_ref=terms_got_ref,
        send_sem=send_sem.at[size - 1],
        recv_sem=recv_sem.at[size - 1],
        device_id=(head, blk ^ 1),
        device_id_type=MESH,
    )

    @pl.when(step == 0)
    def _():
        gain_grad_ref[...] = jnp.zeros_like(gain_grad_ref)
        barrier = pltpu.get_barrier_semaphore()
        for k in range(1, size):
            pl.semaphore_signal(barrier, inc=1, device_id=(head ^ k, blk), device_id_type=MESH)
        pl.semaphore_signal(barrier, inc=1, device_id=(head, blk ^ 1), device_id_type=MESH)
        pl.semaphore_wait(barrier, size)

    @pl.when(step < last)
    def _():
        here = pl.ds(pl.multiple_of(step * rows, rows), rows)
        gradient = grad_sum_ref[...]
        values = residual_ref[...]
        inverse = lax.rsqrt(jnp.mean(values * values, axis=-1, keepdims=True) + EPS)
        gain_grad_ref[...] += jnp.sum(gradient * values * inverse, axis=0, keepdims=True)
        scaled = gradient * gain_ref[...]
        moment = jnp.mean(scaled * values, axis=-1, keepdims=True)
        total = cot_ref[...].astype(jnp.float32) + (
            inverse * scaled - values * (inverse * inverse * inverse * moment)
        )
        grad_ref[...] = total
        branch = total.astype(jnp.bfloat16)
        branch_ref[here] = branch
        for k in range(size):
            weight = weight_ref[...] if k == 0 else weights_ref[k - 1]
            mine_ref[k, here] = lax.dot_general(
                branch, weight, ROWS_IN_BOTH, preferred_element_type=jnp.float32
            ).astype(jnp.bfloat16)

    @pl.when(step == last)
    def _():
        for copy in copies:
            copy.start()
        keep.start()
        columns = attended_ref.shape[1] // size
        pairs = terms_ref.shape[0] // size
        for k in range(size):
            terms = lax.dot_general(
                attended_ref[:, k * columns : (k + 1) * columns],
                branch_ref[...],
                (((0,), (0,)), ((), ())),
                preferred_element_type=jnp.float32,
            ).astype(jnp.bfloat16)
            terms_ref[k * pairs : (k + 1) * pairs] = terms.reshape(pairs, *terms_ref.shape[1:])
        across.start()
        across.wait()

        for k, out_ref in enumerate(out_refs):

            def add(index, carried, k=k, out_ref=out_ref):
                out_ref[index] = (
                    terms_ref[k * pairs + index, core].astype(jnp.float32)
                    + terms_got_ref[k * pairs + index].astype(jnp.float32)
                ).astype(jnp.bfloat16)
                return carried

            lax.fori_loop(0, pairs, add, 0)
        for copy in copies:
            copy.wait()
        keep.wait()


def residual_back(grad_sum, residual, cot, gain, attended, weight, weights, rows):
    count, width = cot.shape
    size, blk_size = lax.axis_size("heads"), lax.axis_size("blk")
    columns = weight.shape[0]
    pairs, held = size * blk_size // 2, columns // blk_size
    tiles = count // rows

    def there(i):
        return (jnp.minimum(i, tiles - 1), 0)

    def whole(i):
        return (0, 0)

    tile = pl.BlockSpec((rows, width), there)
    row = pl.BlockSpec((1, width), whole)
    pieces = (size, count, columns)
    return pl.pallas_call(
        residual_back_kernel,
        grid=(tiles + 1,),
        in_specs=[
            tile,
            tile,
            tile,
            row,
            pl.BlockSpec(attended.shape, whole),
            pl.BlockSpec(weight.shape, whole),
            pl.BlockSpec(weights.shape, lambda i: (0, 0, 0)),
        ],
        out_specs=[
            tile,
            row,
            pl.BlockSpec(memory_space=pl.ANY),
            *[pl.BlockSpec((pairs // size, held, width), lambda i: (0, 0, 0))] * size,
        ],
        out_shape=[
            jax.ShapeDtypeStruct((count, width), jnp.float32),
            jax.ShapeDtypeStruct((1, width), jnp.float32),
            jax.ShapeDtypeStruct(pieces, jnp.bfloat16),
            *[jax.ShapeDtypeStruct((pairs // size, held, width), jnp.bfloat16)] * size,
        ],
        scratch_shapes=[
            pltpu.VMEM((count, width), jnp.bfloat16),
            pltpu.VMEM(pieces, jnp.bfloat16),
            pltpu.VMEM((pairs, 2, held, width), jnp.bfloat16),
            pltpu.VMEM((pairs, held, width), jnp.bfloat16),
            pltpu.SemaphoreType.DMA,
            pltpu.SemaphoreType.DMA((size,)),
            pltpu.SemaphoreType.DMA((size,)),
        ],
        compiler_params=pltpu.CompilerParams(
            collective_id=4, has_side_effects=True, vmem_limit_bytes=56 << 20
        ),
        cost_estimate=pl.CostEstimate(
            flops=4 * count * width * columns * size, bytes_accessed=30_000_000, transcendentals=0
        ),
        name="residual_back",
    )(grad_sum, residual, cot, gain, attended, weight, weights)


def qkv_terms_kernel(normed_ref, grad_ref, terms_ref, got_ref, send_sem, recv_sem):
    step = pl.program_id(0)
    size = lax.axis_size("heads")
    head, blk = lax.axis_index("heads"), lax.axis_index("blk")
    count = got_ref.shape[1]
    copies = [
        pltpu.make_async_remote_copy(
            src_ref=grad_ref.at[pl.ds(k * count, count)],
            dst_ref=got_ref.at[k - 1],
            send_sem=send_sem.at[k - 1],
            recv_sem=recv_sem.at[k - 1],
            device_id=(head ^ k, blk),
            device_id_type=MESH,
        )
        for k in range(1, size)
    ]

    @pl.when(step == 0)
    def _():
        barrier = pltpu.get_barrier_semaphore()
        for k in range(1, size):
            pl.semaphore_signal(barrier, inc=1, device_id=(head ^ k, blk), device_id_type=MESH)
        pl.semaphore_wait(barrier, size - 1)
        for copy in copies:
            copy.start()

    terms_ref[...] = lax.dot_general(
        normed_ref[...], grad_ref[...], (((0,), (0,)), ((), ())), preferred_element_type=jnp.float32
    ).astype(terms_ref.dtype)

    @pl.when(step == pl.num_programs(0) - 1)
    def _():
        for copy in copies:
            copy.wait()


def qkv_terms(normed, grad, rows):
    count, height = normed.shape
    width = grad.shape[1]
    size = lax.axis_size("heads")
    return pl.pallas_call(
        qkv_terms_kernel,
        grid=(height // rows,),
        in_specs=[
            pl.BlockSpec((count, rows), lambda i: (0, i)),
            pl.BlockSpec((count, width), lambda i: (0, 0)),
        ],
        out_specs=[
            pl.BlockSpec((rows, width), lambda i: (i, 0)),
            pl.BlockSpec(memory_space=pl.ANY),
        ],
        out_shape=[
            jax.ShapeDtypeStruct((height, width), jnp.bfloat16),
            jax.ShapeDtypeStruct((size - 1, count // size, width), jnp.bfloat16),
        ],
        scratch_shapes=[pltpu.SemaphoreType.DMA((size - 1,))] * 2,
        compiler_params=pltpu.CompilerParams(
            collective_id=7, has_side_effects=True, vmem_limit_bytes=48 << 20
        ),
        cost_estimate=pl.CostEstimate(
            flops=4 * count * height * width, bytes_accessed=20_000_000, transcendentals=0
        ),
        name="qkv_terms",
    )(normed, grad)


def finish_kernel(
    query_width, dim, got_ref, qkv_ref, gain_ref, ffn_ref, head_ref, out_own_ref, out_one_ref, out_two_ref, out_three_ref, *refs
):
    size, blk_size = lax.axis_size("heads"), lax.axis_size("blk")
    out_refs = (out_own_ref, out_one_ref, out_two_ref, out_three_ref)
    sources, refs = refs[:12], refs[12:]
    (
        grad_ref, qkv_grad_ref, gains_ref, out_grad_ref, in_grad_ref, layer_ref, *refs
    ) = refs
    held, refs = refs[:12], refs[12:]
    weight_ref, weights_ref, x_ref, residual_grad_ref, sent_ref, in_ref, residual_ref, rest_ref = held[:8]
    (
        qkv_other_ref, qkv_sum_ref, qkv_got_ref, part_ref, gain_got_ref, out_part_ref,
        out_got_ref, in_got_ref, load_sem, c_send, c_recv, q_send, q_recv, g_send,
        g_recv, o_send, o_recv, i_send, i_recv,
    ) = refs
    devices = size * blk_size
    pairs = blk_size // 2
    head, blk = lax.axis_index("heads"), lax.axis_index("blk")
    core, pair = lax.rem(blk, 2), blk // 2
    own = head * blk_size + blk
    own_pair = head * pairs + pair
    count, width = x_ref.shape
    depth = width // devices
    barrier = pltpu.get_barrier_semaphore()
    loads = [
        pltpu.make_async_copy(
            source.at[pl.ds(0, target.shape[0]), pl.ds(0, target.shape[1])]
            if index in (0, 4, 6)
            else source.at[pl.ds(target.shape[0], target.shape[0])]
            if index == 7
            else source,
            target,
            load_sem.at[index],
        )
        for index, (source, target) in enumerate(zip(sources, held))
    ]
    for load in loads:
        load.start()

    def place_of(index):
        return (index // blk_size, lax.rem(index, blk_size))

    def greet(k, carried):
        pl.semaphore_signal(
            barrier, inc=1, device_id=place_of(lax.rem(own + k, devices)), device_id_type=MESH
        )
        return carried

    lax.fori_loop(1, devices, greet, 0)
    pl.semaphore_wait(barrier, devices - 1)

    def copy(source, target, place, send, recv):
        return pltpu.make_async_remote_copy(
            src_ref=source,
            dst_ref=target,
            send_sem=send,
            recv_sem=recv,
            device_id=place,
            device_id_type=MESH,
        )

    across = copy(qkv_ref.at[:, 1 - core], qkv_other_ref, (head, blk ^ 1), c_send, c_recv)
    across.start()
    def wide_of(block):
        return block.astype(jnp.float32)

    across.wait_recv()

    def qkv_copy(k, slot):
        other = lax.rem(own_pair + k, size * pairs)
        return copy(
            qkv_sum_ref.at[other],
            qkv_got_ref.at[slot],
            (other // pairs, lax.rem(other, pairs) * 2 + core),
            q_send.at[k],
            q_recv.at[slot],
        )

    def qkv_sum(index, carried):
        qkv_sum_ref[index] = (
            wide_of(qkv_ref[index, core]) + wide_of(qkv_other_ref[index])
        ).astype(jnp.bfloat16)
        return carried

    def start_qkv(k, carried):
        qkv_copy(k, own_pair).start()
        return carried

    lax.fori_loop(0, size * pairs, qkv_sum, 0)
    lax.fori_loop(1, size * pairs, start_qkv, 0)
    qkv_got_ref[own_pair] = qkv_sum_ref[own_pair]

    def out_copy(k, slot):
        other = lax.rem(pair + k, pairs)
        return copy(
            out_part_ref.at[other],
            out_got_ref.at[slot],
            (head, other * 2 + core),
            o_send.at[k],
            o_recv.at[slot],
        )

    out_rows = out_grad_ref.shape[0]

    def out_sum(index, carried):
        here = pl.ds(pl.multiple_of(index * out_rows, out_rows), out_rows)
        total = wide_of(out_refs[0][here])
        for ref in out_refs[1:]:
            total += wide_of(ref[here])
        out_part_ref[index, :out_rows] = total.astype(jnp.bfloat16)
        return carried

    def start_out(k, carried):
        out_copy(k, pair).start()
        return carried

    lax.fori_loop(0, pairs, out_sum, 0)
    lax.fori_loop(1, pairs, start_out, 0)
    out_got_ref[pair] = out_part_ref[pair]

    loads[5].wait()
    in_sends = [
        copy(
            in_ref.at[head ^ k],
            in_got_ref.at[k - 1],
            (head ^ k, blk),
            i_send.at[k - 1],
            i_recv.at[k - 1],
        )
        for k in range(1, size)
    ]
    for sent in in_sends:
        sent.start()

    for load in loads[:5]:
        load.wait()
    rows = min(128, count)

    def tile(index, gain_sum):
        here = pl.ds(pl.multiple_of(index * rows, rows), rows)
        normed_grad = lax.dot_general(
            sent_ref[here], weight_ref[...], ROWS_IN_BOTH, preferred_element_type=jnp.float32
        )
        for k in range(1, size):
            normed_grad += lax.dot_general(
                got_ref[k - 1, here],
                weights_ref[k - 1],
                ROWS_IN_BOTH,
                preferred_element_type=jnp.float32,
            )
        values = wide_of(x_ref[here])
        inverse = lax.rsqrt(jnp.mean(values * values, axis=-1, keepdims=True) + EPS)
        scaled = normed_grad * gain_ref[...]
        moment = jnp.mean(scaled * values, axis=-1, keepdims=True)
        grad_ref[here] = (
            residual_grad_ref[here]
            + inverse * scaled
            - values * (inverse * inverse * inverse * moment)
        )
        return gain_sum + jnp.sum(normed_grad * values * inverse, axis=0, keepdims=True)

    attn_sum = lax.fori_loop(0, count // rows, tile, jnp.zeros((1, width), jnp.float32))

    def by_device(row):
        lanes = jnp.concatenate(
            [row[:, d * depth : (d + 1) * depth] for d in range(devices)], axis=0
        )
        if depth < 64:
            lanes = jnp.concatenate(
                [lanes, jnp.zeros((devices, 64 - depth), jnp.float32)], axis=1
            )
        return lanes

    head_row = head_ref[...]
    query_sum = head_row[:, :dim]
    for c in range(dim, query_width, dim):
        query_sum += head_row[:, c : c + dim]
    key_sum = head_row[:, query_width : query_width + dim]
    for c in range(query_width + dim, head_row.shape[1], dim):
        key_sum += head_row[:, c : c + dim]
    both = jnp.concatenate([query_sum, key_sum], axis=1)
    part_ref[...] = jnp.zeros_like(part_ref)
    part_ref[:, 0, :] = jnp.concatenate([by_device(attn_sum), by_device(ffn_ref[...])], axis=1)
    part_ref[:, 1, :] = jnp.broadcast_to(both, (devices, 2 * dim))

    def gain_copy(k, slot):
        other = lax.rem(own + k, devices)
        return copy(
            part_ref.at[other], gain_got_ref.at[slot], place_of(other), g_send.at[k], g_recv.at[slot]
        )

    def start_gain(k, carried):
        gain_copy(k, own).start()
        return carried

    lax.fori_loop(1, devices, start_gain, 0)
    gain_got_ref[own] = part_ref[own]

    units = in_ref.shape[2] // 2
    for k in range(size):
        if k:
            in_sends[k - 1].wait_recv()
        for part in range(2):
            columns = pl.ds(pl.multiple_of((part * size + (head ^ k)) * units, units), units)
            piece = slice(part * units, (part + 1) * units)
            got = in_got_ref[k - 1, :, piece] if k else in_ref[head, :, piece]
            in_grad_ref[:, columns] = wide_of(got)

    for load in loads[6:]:
        load.wait()
    half = count // 2
    for part in range(2):
        here = slice(part * half, (part + 1) * half)
        layer_ref[here] = (
            residual_ref[here] + wide_of(rest_ref[here]) + wide_of(held[8 + part][...])
            + wide_of(held[10 + part][...])
        ).astype(jnp.bfloat16)

    def finish_qkv(k, carried):
        qkv_copy(k, lax.rem(own_pair + size * pairs - k, size * pairs)).wait()
        return carried

    lax.fori_loop(1, size * pairs, finish_qkv, 0)

    def group_sum(h):
        total = wide_of(qkv_got_ref[h * pairs])
        for b in range(1, pairs):
            total += wide_of(qkv_got_ref[h * pairs + b])
        return total

    sums = [group_sum(h) for h in range(size)]
    key_end = query_width + (sums[0].shape[1] - query_width) // 2
    qkv_grad_ref[...] = jnp.concatenate(
        [total[:, :query_width] for total in sums]
        + [total[:, query_width:key_end] for total in sums]
        + [total[:, key_end:] for total in sums],
        axis=1,
    )

    def finish_out(k, carried):
        out_copy(k, lax.rem(pair + pairs - k, pairs)).wait()
        return carried

    lax.fori_loop(1, pairs, finish_out, 0)
    out_total = wide_of(out_got_ref[0, :out_rows])
    for b in range(1, pairs):
        out_total += wide_of(out_got_ref[b, :out_rows])
    out_grad_ref[...] = out_total

    def finish_gain(k, carried):
        gain_copy(k, lax.rem(own + devices - k, devices)).wait()
        return carried

    lax.fori_loop(1, devices, finish_gain, 0)
    gains_ref[...] = jnp.sum(gain_got_ref[...], axis=0)
    across.wait_send()
    for sent in in_sends:
        sent.wait_send()


def finish(
    sent, got, qkv_part, x, residual_grad, gain, ffn_sum, head_sum, weight, weights, outs, in_part,
    residual, rest, terms, query_width, dim
):
    size, blk_size = lax.axis_size("heads"), lax.axis_size("blk")
    devices = size * blk_size
    pairs = blk_size // 2
    count, width = x.shape
    depth, joined = width // devices, sent.shape[1]
    out_rows = outs[0].shape[0] // pairs
    held_rows = -(-out_rows // 16) * 16
    units = in_part.shape[2]
    vmem = pl.BlockSpec(memory_space=pltpu.VMEM)
    anywhere = pl.BlockSpec(memory_space=pl.ANY)
    sems = pltpu.SemaphoreType.DMA
    low = jnp.bfloat16
    loaded = (weights, x, residual_grad)
    return pl.pallas_call(
        functools.partial(finish_kernel, query_width, dim),
        out_shape=[
            jax.ShapeDtypeStruct((count, width), jnp.float32),
            jax.ShapeDtypeStruct((depth, size * joined), jnp.float32),
            jax.ShapeDtypeStruct((8, 128), jnp.float32),
            jax.ShapeDtypeStruct((out_rows, width), jnp.float32),
            jax.ShapeDtypeStruct((depth, size * units), jnp.float32),
            jax.ShapeDtypeStruct((count, width), low),
        ],
        in_specs=[vmem] * (5 + size) + [anywhere] * 12,
        out_specs=[vmem] * 6,
        scratch_shapes=[pltpu.VMEM((width, joined), low)]
        + [pltpu.VMEM(array.shape, array.dtype) for array in loaded]
        + [pltpu.VMEM((count, joined), low), pltpu.VMEM(in_part.shape, low)]
        + [pltpu.VMEM((count, width), jnp.float32), pltpu.VMEM((count, width), low)]
        + [pltpu.VMEM((count // 2, width), low)] * 4
        + [
            pltpu.VMEM((size * pairs, depth, joined), low),
            pltpu.VMEM((size * pairs, depth, joined), low),
            pltpu.VMEM((size * pairs, depth, joined), low),
            pltpu.VMEM((devices, 8, 128), jnp.float32),
            pltpu.VMEM((devices, 8, 128), jnp.float32),
            pltpu.VMEM((pairs, held_rows, width), low),
            pltpu.VMEM((pairs, held_rows, width), low),
            pltpu.VMEM((size - 1, depth, units), low),
            sems((12,)),
            sems,
            sems,
            sems((size * pairs,)),
            sems((size * pairs,)),
            sems((devices,)),
            sems((devices,)),
            sems((pairs,)),
            sems((pairs,)),
            sems((size - 1,)),
            sems((size - 1,)),
        ],
        compiler_params=pltpu.CompilerParams(
            collective_id=0, has_side_effects=True, vmem_limit_bytes=60 << 20
        ),
        name="finish",
    )(
        got, qkv_part.reshape(size * pairs, 2, depth, joined), gain, ffn_sum, head_sum, *outs,
        weight, *loaded, sent, in_part, residual, rest, *terms
    )


def permute(block, axis, k):
    return lax.ppermute(block, axis, [(i, i ^ k) for i in range(lax.axis_size(axis))])


def after(value, *done):
    return lax.optimization_barrier((value, *done))[0]


def pick(block, k, axis, dim):
    extent = block.shape[dim] // lax.axis_size(axis)
    return lax.dynamic_slice_in_dim(block, (lax.axis_index(axis) ^ k) * extent, extent, dim)


def wide(block):
    return block.astype(jnp.float32)


def local(
    inputs,
    positions,
    attn_gain,
    qkv_weight,
    q_gain,
    k_gain,
    out_weight,
    ffn_gain,
    ffn_in_weight,
    ffn_out_weight,
    cotangent,
):
    token_count, width = inputs.shape
    depth = qkv_weight.shape[0]
    head_dim = q_gain.shape[0]
    group_size = HEADS // KV_HEADS
    size = lax.axis_size("heads")
    blk_size = lax.axis_size("blk")
    query_all, key_all = HEADS * head_dim, KV_HEADS * head_dim
    query_width, key_width = query_all // size, key_all // size
    qkv_width = query_width + 2 * key_width
    block_len = token_count * size
    half = token_count // 2
    own = lax.axis_index("heads").astype(jnp.int32).reshape(1)

    qkv_parts = jnp.concatenate(
        [
            qkv_weight[:, :query_all].reshape(depth, size, query_width),
            qkv_weight[:, query_all : query_all + key_all].reshape(depth, size, key_width),
            qkv_weight[:, query_all + key_all :].reshape(depth, size, key_width),
            jnp.broadcast_to(attn_gain[:, None, None], (depth, size, 64)),
            jnp.broadcast_to(ffn_gain[:, None, None], (depth, size, 64)),
        ],
        axis=-1,
    ).transpose(1, 0, 2)
    out_group = lax.all_gather(out_weight, "blk", axis=0, tiled=True)
    in_rows = trade(ffn_in_weight)
    in_group = lax.all_gather(in_rows, "blk", axis=1, tiled=True).reshape(width, -1)

    inputs_blk, qkv_rows = begin(after(inputs, in_rows), qkv_parts)
    qkv_rows = qkv_rows.reshape(width, -1)
    cosine, sine = rotation(positions, head_dim)
    cosine = jnp.concatenate([cosine[:, 0], cosine[:, 0]], axis=-1)
    sine = jnp.concatenate([-sine[:, 0], sine[:, 0]], axis=-1)
    head_gain = jnp.concatenate(
        [jnp.tile(q_gain, HEADS // size), jnp.tile(k_gain, KV_HEADS // size)]
    ).astype(jnp.float32)[None, :]
    query_low, pair_blk, raw, normed, attn_scaling, ffn_scaling, out_peers = project(
        inputs_blk, qkv_rows, head_gain, cosine, sine, out_group, size, query_width, 256
    )
    pair_behind = from_behind(pair_blk, "blk", 1)
    pair_all = jnp.concatenate([pair_behind, pair_blk], axis=0)
    down_weight, pair_all = lax.optimization_barrier((ffn_out_weight, pair_all))
    down_group = lax.all_gather(down_weight, "blk", axis=0, tiled=True)
    query_rows, key_rows = token_count, 256
    low = block_len + jnp.arange(block_len, dtype=jnp.int32) - positions
    first = jnp.concatenate([low[::query_rows] // key_rows, own])
    low = low[None, :]
    attended_blk, logs = attend(query_low, pair_all, first, low, group_size, query_rows, key_rows)

    mine = jnp.concatenate([pick(attended_blk, k, "heads", 0) for k in range(size)], axis=0)
    late = after(cotangent, inputs_blk)
    one_top, two_bottom = permute(late[:half], "heads", 1), permute(late[half:], "heads", 2)
    mine, in_group = lax.optimization_barrier((mine, in_group))
    residual, ffn_normed, attended_own, one_bottom, two_top = join(
        inputs_blk, mine, out_group, out_peers, ffn_scaling, cotangent, 256
    )
    cot_near = (one_top, one_bottom, two_top, two_bottom)
    hidden, gate_grad, up_grad, in_sum, cot_far, qkv_peers = hidden_pass(
        ffn_normed, in_group, cotangent, cot_near, down_group, qkv_rows, qkv_width, 256
    )
    in_part = lax.psum_scatter(
        in_sum.reshape(size, blk_size * depth, -1), "blk", scatter_dimension=1, tiled=True
    )
    down_sum, one_far, two_far, one_near, two_near, out_rest, grad_sum = feed_tail(
        gate_grad, up_grad, hidden, in_group, down_group, (cotangent, *cot_near, cot_far)
    )
    through_top, through_bottom = permute(one_far, "heads", 1), permute(two_far, "heads", 2)
    residual_grad, ffn_sum, grads, *out_slices = residual_back(
        grad_sum, residual, cotangent, ffn_scaling, attended_own, out_group, out_peers,
        min(128, half)
    )
    down_sum, in_part, grads, through_top, through_bottom = lax.optimization_barrier(
        (down_sum, in_part, grads, through_top, through_bottom)
    )
    ffn_out_grad = wide(lax.psum_scatter(down_sum, "blk", scatter_dimension=0, tiled=True))
    top_send = (wide(out_rest[:half]) + wide(through_top)).astype(jnp.bfloat16)
    bottom_send = (wide(out_rest[half : 2 * half]) + wide(through_bottom)).astype(jnp.bfloat16)
    out_top_last = permute(top_send, "heads", 2)
    out_bottom_last = permute(bottom_send, "heads", 1)
    out_slices = [piece.reshape(-1, width) for piece in out_slices]
    out_slices = [out_slices[0]] + [permute(out_slices[k], "heads", k) for k in range(1, size)]
    query_grad, pair_sum, behind = attend_back(
        query_low, pair_all, first, low, grads, attended_blk, logs, group_size, query_rows, key_rows
    )
    pair_sum, out_top_last, out_bottom_last, *out_slices = lax.optimization_barrier(
        (pair_sum, out_top_last, out_bottom_last, *out_slices)
    )
    projected_grad, head_sum = project_back(
        query_grad, pair_sum, behind, raw, head_gain, cosine, sine, size, 256
    )
    out_top = permute(after(one_near, pair_sum), "heads", 1)
    out_bottom = permute(after(two_near, pair_sum), "heads", 2)
    qkv_part, got = qkv_terms(normed, projected_grad, 512)
    input_grad, qkv_grad, gains, out_grad, ffn_in_grad, layer_out = finish(
        projected_grad, got, qkv_part, inputs, residual_grad, attn_scaling, ffn_sum, head_sum,
        qkv_rows, qkv_peers, out_slices, in_part, residual, out_rest,
        (out_top, out_bottom, out_top_last, out_bottom_last), query_width, head_dim
    )
    return (
        layer_out,
        input_grad,
        gains[0, :depth],
        qkv_grad,
        gains[1, :head_dim],
        gains[1, head_dim : 2 * head_dim],
        out_grad,
        gains[0, 64 : 64 + depth],
        ffn_in_grad,
        ffn_out_grad,
    )


def solution(mesh):
    placed = (
        P(("blk", "heads"), None),
        P("blk"),
        P(("heads", "blk")),
        P(("heads", "blk"), None),
        P(),
        P(),
        P(("heads", "blk"), None),
        P(("heads", "blk")),
        P(("heads", "blk"), None),
        P(("heads", "blk"), None),
        P(("blk", "heads"), None),
    )
    return jax.shard_map(
        local,
        mesh=mesh,
        in_specs=placed,
        out_specs=(
            P(("blk", "heads"), None),
            P(("blk", "heads"), None),
            P(("heads", "blk")),
            P(("heads", "blk"), None),
            P(),
            P(),
            P(("heads", "blk"), None),
            P(("heads", "blk")),
            P(("heads", "blk"), None),
            P(("heads", "blk"), None),
        ),
        check_vma=False,
    )
```

```python
import functools

import jax
import jax.numpy as jnp
from jax import lax
from jax.experimental import pallas as pl
from jax.experimental.pallas import tpu as pltpu
from jax.sharding import PartitionSpec as P

HEADS = 16
KV_HEADS = 4


EPS = 1e-06
ROPE_BASE = 10000.0
NEG = -1e30
MESH = pl.DeviceIdType.MESH
ROWS_IN_BOTH = (((1,), (1,)), ((), ()))


def rotation(positions, head_dim):
    half_width = head_dim // 2
    frequency = ROPE_BASE ** (-2.0 * jnp.arange(half_width, dtype=jnp.float32) / head_dim)
    angles = positions.astype(jnp.float32)[:, None] * frequency[None, :]
    return (jnp.cos(angles)[:, None, :], jnp.sin(angles)[:, None, :])


def stack_heads(tile, heads, first):
    turned = tile.T
    dim = turned.shape[0] // heads
    wide = jnp.concatenate([turned[h * dim : (h + 1) * dim] for h in range(heads)], axis=1)
    zero = jnp.zeros_like(wide)
    return jnp.concatenate([wide, zero] if first else [zero, wide], axis=0)


def unstack_heads(wide, heads):
    count = wide.shape[1] // heads
    return jnp.concatenate([wide[:, h * count : (h + 1) * count] for h in range(heads)], axis=0).T


def scores_at(pair, query_ext, low, first_query, key_start, heads):
    scores = jnp.dot(pair, query_ext, preferred_element_type=jnp.float32)
    rows, columns = scores.shape
    shape = (rows, columns // heads)
    key = key_start + lax.broadcasted_iota(jnp.int32, shape, 0)
    query = first_query + lax.broadcasted_iota(jnp.int32, shape, 1)
    bias = jnp.where((key <= query) & (key >= low), 0.0, NEG)
    return scores + jnp.concatenate([bias] * heads, axis=1)


def transpose_into(pair_ref, turned_ref):
    for start in range(0, pair_ref.shape[0], 512):
        turned_ref[:, start : start + 512] = pair_ref[start : start + 512, :].T


def attend_kernel(
    heads, key_rows, scale, first_ref, query_ref, low_ref, pair_ref, out_ref, log_ref, turned_ref,
    mixed_ref, total_ref
):
    step = pl.program_id(0)
    query_rows = query_ref.shape[0]

    @pl.when(step == 0)
    def _():
        transpose_into(pair_ref, turned_ref)

    query_ext = stack_heads(query_ref[...] * jnp.bfloat16(scale), heads, True)
    low = low_ref[...]
    base = pair_ref.shape[0] // 2 + step * query_rows
    mixed_ref[...] = jnp.zeros_like(mixed_ref)
    total_ref[...] = jnp.zeros_like(total_ref)

    def tile(index, carried):
        start = pl.multiple_of(index * key_rows, key_rows)
        expo = jnp.exp(
            scores_at(pair_ref[pl.ds(start, key_rows), :], query_ext, low, base, start, heads)
        )
        total_ref[...] += jnp.sum(expo, axis=0, keepdims=True)
        mixed_ref[...] += jnp.dot(
            turned_ref[:, pl.ds(start, key_rows)],
            expo.astype(jnp.bfloat16),
            preferred_element_type=jnp.float32,
        )
        return carried

    lax.fori_loop(first_ref[step], (base + query_rows - 1) // key_rows + 1, tile, 0)
    total = total_ref[...]
    dim = pair_ref.shape[1] // 2
    out_ref[...] = unstack_heads(mixed_ref[dim:] / total, heads).astype(out_ref.dtype)
    log_ref[...] = jnp.log(total)[None]


def attend_back_kernel(
    heads, key_rows, scale, first_ref, query_ref, low_ref, pair_ref, out_ref, log_ref, *refs
):
    grads_ref, query_grad_ref, pair_grad_ref, behind_ref, turned_ref, sum_ref = refs
    step = pl.program_id(0)
    grad = grads_ref[first_ref[pl.num_programs(0)] ^ step]
    query_rows = query_ref.shape[0]
    dim = pair_ref.shape[1] // 2

    @pl.when(step == 0)
    def _():
        pair_grad_ref[...] = jnp.zeros_like(pair_grad_ref)
        transpose_into(pair_ref, turned_ref)

    query_ext = stack_heads(query_ref[...] * jnp.bfloat16(scale), heads, True)
    grad_ext = stack_heads(grad, heads, False)
    out_ext = stack_heads(out_ref[...], heads, False)
    inner = jnp.sum(
        grad_ext.astype(jnp.float32) * out_ext.astype(jnp.float32), axis=0, keepdims=True
    )
    log_sum = log_ref[0]
    low = low_ref[...]
    base = pair_ref.shape[0] // 2 + step * query_rows
    sum_ref[...] = jnp.zeros_like(sum_ref)

    def tile(index, carried):
        start = pl.multiple_of(index * key_rows, key_rows)
        pair = pair_ref[pl.ds(start, key_rows), :]
        probs = jnp.exp(scores_at(pair, query_ext, low, base, start, heads) - log_sum)
        probs_grad = jnp.dot(pair, grad_ext, preferred_element_type=jnp.float32)
        score_grad = (probs * (probs_grad - inner)).astype(jnp.bfloat16)
        sum_ref[...] += jnp.dot(
            turned_ref[:dim, pl.ds(start, key_rows)], score_grad, preferred_element_type=jnp.float32
        )
        pair_grad_ref[pl.ds(start, key_rows), :] += lax.dot_general(
            score_grad, query_ext, ROWS_IN_BOTH, preferred_element_type=jnp.float32
        ) + lax.dot_general(
            probs.astype(jnp.bfloat16), grad_ext, ROWS_IN_BOTH, preferred_element_type=jnp.float32
        )
        return carried

    lax.fori_loop(first_ref[step], (base + query_rows - 1) // key_rows + 1, tile, 0)
    query_grad_ref[...] = unstack_heads(sum_ref[...] * scale, heads).astype(query_grad_ref.dtype)

    @pl.when(step == pl.num_programs(0) - 1)
    def _():
        behind_ref[...] = pair_grad_ref[: behind_ref.shape[0]].astype(behind_ref.dtype)


def attention_specs(queries, pair, query_rows, heads):
    width = queries.shape[1]
    return (
        pl.BlockSpec((query_rows, width), lambda i, first: (i, 0)),
        pl.BlockSpec((1, query_rows), lambda i, first: (0, i)),
        pl.BlockSpec(pair.shape, lambda i, first: (0, 0)),
        pl.BlockSpec((1, 1, heads * query_rows), lambda i, first: (i, 0, 0)),
    )


def attend(queries, pair, first, low, heads, query_rows, key_rows):
    count, width = queries.shape
    tile, row, whole, logs = attention_specs(queries, pair, query_rows, heads)
    columns = heads * query_rows
    return pl.pallas_call(
        functools.partial(attend_kernel, heads, key_rows, (width // heads) ** -0.5),
        grid_spec=pltpu.PrefetchScalarGridSpec(
            num_scalar_prefetch=1,
            grid=(count // query_rows,),
            in_specs=[tile, row, whole],
            out_specs=[tile, logs],
            scratch_shapes=[
                pltpu.VMEM(pair.shape[::-1], jnp.bfloat16),
                pltpu.VMEM((pair.shape[1], columns), jnp.float32),
                pltpu.VMEM((1, columns), jnp.float32),
            ],
        ),
        out_shape=[
            jax.ShapeDtypeStruct((count, width), jnp.bfloat16),
            jax.ShapeDtypeStruct((count // query_rows, 1, columns), jnp.float32),
        ],
        compiler_params=pltpu.CompilerParams(vmem_limit_bytes=48 << 20),
        cost_estimate=pl.CostEstimate(
            flops=20_000_000_000, bytes_accessed=8_000_000, transcendentals=0
        ),
        name="attend",
    )(first, queries, low, pair)


def attend_back(queries, pair, first, low, grads, out, logs, heads, query_rows, key_rows):
    count, width = queries.shape
    tile, row, whole, log_spec = attention_specs(queries, pair, query_rows, heads)
    columns = heads * query_rows
    behind = (pair.shape[0] // 2, pair.shape[1])
    return pl.pallas_call(
        functools.partial(attend_back_kernel, heads, key_rows, (width // heads) ** -0.5),
        grid_spec=pltpu.PrefetchScalarGridSpec(
            num_scalar_prefetch=1,
            grid=(count // query_rows,),
            in_specs=[tile, row, whole, tile, log_spec]
            + [pl.BlockSpec(grads.shape, lambda i, first: (0, 0, 0))],
            out_specs=[tile, whole, pl.BlockSpec(behind, lambda i, first: (0, 0))],
            scratch_shapes=[
                pltpu.VMEM(pair.shape[::-1], jnp.bfloat16),
                pltpu.VMEM((pair.shape[1] // 2, columns), jnp.float32),
            ],
        ),
        out_shape=[
            jax.ShapeDtypeStruct((count, width), jnp.bfloat16),
            jax.ShapeDtypeStruct(pair.shape, jnp.float32),
            jax.ShapeDtypeStruct(behind, jnp.bfloat16),
        ],
        compiler_params=pltpu.CompilerParams(vmem_limit_bytes=48 << 20),
        cost_estimate=pl.CostEstimate(
            flops=40_000_000_000, bytes_accessed=12_000_000, transcendentals=0
        ),
        name="attend_back",
    )(first, queries, low, pair, out, logs, grads)


def heads_apart(wide, dim):
    rows = wide.shape[0]
    return jnp.concatenate(
        [
            jnp.broadcast_to(
                jnp.mean(jnp.square(wide[:, c : c + dim]), axis=-1, keepdims=True), (rows, dim)
            )
            for c in range(0, wide.shape[1], dim)
        ],
        axis=1,
    )


def spread_mean(wide, dim):
    rows = wide.shape[0]
    return jnp.concatenate(
        [
            jnp.broadcast_to(jnp.mean(wide[:, c : c + dim], axis=-1, keepdims=True), (rows, dim))
            for c in range(0, wide.shape[1], dim)
        ],
        axis=1,
    )


def turn(wide, cosine, sine, dim):
    count = wide.shape[1] // dim
    half = dim // 2
    swapped = jnp.concatenate(
        [
            wide[:, c + shift : c + shift + half]
            for c in range(0, wide.shape[1], dim)
            for shift in (half, 0)
        ],
        axis=1,
    )
    return wide * jnp.concatenate([cosine] * count, axis=1) + swapped * jnp.concatenate(
        [sine] * count, axis=1
    )


def project_kernel(
    dim, size, x_ref, weight_ref, head_gain_ref, cosine_ref, sine_ref, side_ref, query_ref, raw_ref,
    normed_ref, gain_ref, ffn_gain_ref, spread_ref, pair_ref, pair_held, send_sem, recv_sem,
    pair_sem, pair_send, pair_recv
):
    columns = raw_ref.shape[1]
    step, steps = pl.program_id(0), pl.num_programs(0)
    marks = (0, steps // 2, steps - 2)
    head, blk = lax.axis_index("heads"), lax.axis_index("blk")
    last = lax.axis_size("blk") - 1
    rows, block = x_ref.shape[0], pair_held.shape[0]
    tiles = block // size // rows

    @pl.when(step == 0)
    def _():
        barrier = pltpu.get_barrier_semaphore()
        for place in ((head ^ 1, blk), (head ^ 2, blk), (head, blk ^ 1)):
            pl.semaphore_signal(barrier, inc=1, device_id=place, device_id_type=MESH)

        @pl.when(blk > 0)
        def _():
            pl.semaphore_signal(barrier, inc=1, device_id=(head, blk - 1), device_id_type=MESH)

        @pl.when(blk < last)
        def _():
            pl.semaphore_wait(barrier, 4)

        @pl.when(blk == last)
        def _():
            pl.semaphore_wait(barrier, 3)

    end = spread_job(step, marks, side_ref, spread_ref, send_sem, recv_sem, False)

    def chunk_rows(k, first):
        return pl.ds(
            pl.multiple_of(first + (head ^ k) * (block // size), block // size), block // size
        )

    def keep(k):
        return pltpu.make_async_copy(
            pair_held.at[chunk_rows(k, 0)], pair_ref.at[chunk_rows(k, block)], pair_sem.at[k]
        )

    def pass_on(k):
        return pltpu.make_async_remote_copy(
            src_ref=pair_held.at[chunk_rows(k, 0)],
            dst_ref=pair_ref.at[chunk_rows(k, 0)],
            send_sem=pair_send.at[k],
            recv_sem=pair_recv.at[k],
            device_id=(head, jnp.minimum(blk + 1, last)),
            device_id_type=MESH,
        )

    @pl.when(pl.program_id(0) == 0)
    def _():
        gains = weight_ref[:, columns:].T.astype(jnp.float32)
        gain_ref[...] = gains[:1]
        ffn_gain_ref[...] = gains[64:65]

    values = x_ref[...].astype(jnp.float32)
    normed = values * lax.rsqrt(jnp.mean(values * values, axis=-1, keepdims=True) + EPS)
    normed = (normed * gain_ref[...]).astype(jnp.bfloat16)
    normed_ref[...] = normed
    raw = jnp.dot(normed, weight_ref[:, :columns], preferred_element_type=jnp.float32)
    raw_ref[...] = raw
    turned_width = raw.shape[1] - pair_held.shape[1] // 2
    heads = raw[:, :turned_width]
    heads = heads * lax.rsqrt(heads_apart(heads, dim) + EPS) * head_gain_ref[...]
    heads = turn(heads, cosine_ref[...], sine_ref[...], dim).astype(jnp.bfloat16)
    query_width = query_ref.shape[1]
    query_ref[...] = heads[:, :query_width]
    place = ((head ^ (step // tiles)) * tiles + lax.rem(step, tiles)) * rows
    pair_held[pl.ds(pl.multiple_of(place, rows), rows)] = jnp.concatenate(
        [heads[:, query_width:], raw[:, turned_width:].astype(jnp.bfloat16)], axis=1
    )
    for k in range(size):

        @pl.when(step == (k + 1) * tiles - 1)
        def _(k=k):
            keep(k).start()

            @pl.when(blk < last)
            def _():
                pass_on(k).start()

    @pl.when(step == steps - 1)
    def _():
        end()
        for k in range(size):
            keep(k).wait()

        @pl.when(blk < last)
        def _():
            for k in range(size):
                pass_on(k).wait_send()

        @pl.when(blk > 0)
        def _():
            for k in range(size):
                pass_on(k).wait_recv()


def project(x, weight, head_gain, cosine, sine, side, size, query_width, rows):
    count, width = x.shape
    out_width = weight.shape[1] - 128
    pair_width = out_width - query_width
    dim = cosine.shape[1]
    tiles = count // size // rows

    def apart(i):
        return ((lax.axis_index("heads") ^ (i // tiles)) * tiles + i % tiles, 0)

    def there(i):
        return (i, 0)

    def whole(i):
        return (0, 0)

    anywhere = pl.BlockSpec(memory_space=pl.ANY)

    return pl.pallas_call(
        functools.partial(project_kernel, dim, size),
        grid=(count // rows,),
        in_specs=[
            pl.BlockSpec((rows, width), there),
            pl.BlockSpec(weight.shape, whole),
            pl.BlockSpec(head_gain.shape, whole),
            pl.BlockSpec((rows, dim), apart),
            pl.BlockSpec((rows, dim), apart),
            anywhere,
        ],
        out_specs=[
            pl.BlockSpec((rows, query_width), apart),
            pl.BlockSpec((rows, out_width), apart),
            pl.BlockSpec((rows, width), there),
            pl.BlockSpec((1, width), whole),
            pl.BlockSpec((1, width), whole),
            anywhere,
            anywhere,
        ],
        out_shape=[
            jax.ShapeDtypeStruct((count, query_width), jnp.bfloat16),
            jax.ShapeDtypeStruct((count, out_width), jnp.float32),
            jax.ShapeDtypeStruct((count, width), jnp.bfloat16),
            jax.ShapeDtypeStruct((1, width), jnp.float32),
            jax.ShapeDtypeStruct((1, width), jnp.float32),
            jax.ShapeDtypeStruct((3, *side.shape), side.dtype),
            jax.ShapeDtypeStruct((2 * count, pair_width), jnp.bfloat16),
        ],
        scratch_shapes=[pltpu.VMEM((count, pair_width), jnp.bfloat16)]
        + [pltpu.SemaphoreType.DMA((SPREAD_COUNT,))] * 2
        + [pltpu.SemaphoreType.DMA((size,))] * 3,
        compiler_params=pltpu.CompilerParams(
            collective_id=5, has_side_effects=True, vmem_limit_bytes=48 << 20
        ),
        cost_estimate=pl.CostEstimate(
            flops=4 * count * width * out_width, bytes_accessed=30_000_000, transcendentals=0
        ),
        name="project",
    )(x, weight, head_gain, cosine, sine, side)


def project_back_kernel(
    dim, size, query_grad_ref, pair_grad_ref, raw_ref, head_gain_ref, cosine_ref, sine_ref,
    behind_ref, grad_ref, gain_grad_ref, returned_ref, send_sem, recv_sem
):
    step = pl.program_id(0)
    head, blk = lax.axis_index("heads"), lax.axis_index("blk")
    last = lax.axis_size("blk") - 1
    rows = raw_ref.shape[0]
    tiles = returned_ref.shape[0] // size // rows
    back = pltpu.make_async_remote_copy(
        src_ref=behind_ref,
        dst_ref=returned_ref,
        send_sem=send_sem,
        recv_sem=recv_sem,
        device_id=(head, jnp.maximum(blk - 1, 0)),
        device_id_type=MESH,
    )

    @pl.when(step == 0)
    def _():
        barrier = pltpu.get_barrier_semaphore()

        @pl.when(blk < last)
        def _():
            pl.semaphore_signal(
                barrier, inc=1, device_id=(head, blk + 1), device_id_type=MESH
            )

        @pl.when(blk > 0)
        def _():
            pl.semaphore_wait(barrier, 1)
            back.start()

        @pl.when(blk == last)
        def _():
            returned_ref[...] = jnp.zeros_like(returned_ref)

        @pl.when(blk < last)
        def _():
            back.wait_recv()

        gain_grad_ref[...] = jnp.zeros_like(gain_grad_ref)

    place = ((head ^ (step // tiles)) * tiles + lax.rem(step, tiles)) * rows
    returned = returned_ref[pl.ds(pl.multiple_of(place, rows), rows)]
    pair_grad = pair_grad_ref[...] + returned.astype(jnp.float32)
    pair_grad = pair_grad.astype(jnp.bfloat16)
    half = pair_grad.shape[1] // 2
    grads = jnp.concatenate([query_grad_ref[...], pair_grad[:, :half]], axis=1).astype(jnp.float32)
    grads = turn(grads, cosine_ref[...], -sine_ref[...], dim)
    values = raw_ref[:, : grads.shape[1]]
    inverse = lax.rsqrt(heads_apart(values, dim) + EPS)
    gain_grad_ref[...] += jnp.sum(grads * values * inverse, axis=0, keepdims=True)
    scaled = grads * head_gain_ref[...]
    moment = spread_mean(scaled * values, dim)
    values_grad = inverse * scaled - values * inverse * inverse * inverse * moment
    grad_ref[...] = jnp.concatenate([values_grad.astype(jnp.bfloat16), pair_grad[:, half:]], axis=1)

    @pl.when((step == pl.num_programs(0) - 1) & (blk > 0))
    def _():
        back.wait_send()


def project_back(query_grad, pair_sum, behind, raw, head_gain, cosine, sine, size, rows):
    count, query_width = query_grad.shape
    pair_width = pair_sum.shape[1]
    out_width = raw.shape[1]
    dim = cosine.shape[1]
    tiles = count // size // rows

    def apart(i):
        return ((lax.axis_index("heads") ^ (i // tiles)) * tiles + i % tiles, 0)

    def after_behind(i):
        return (apart(i)[0] + count // rows, 0)

    def whole(i):
        return (0, 0)

    return pl.pallas_call(
        functools.partial(project_back_kernel, dim, size),
        grid=(count // rows,),
        in_specs=[
            pl.BlockSpec((rows, query_width), apart),
            pl.BlockSpec((rows, pair_width), after_behind),
            pl.BlockSpec((rows, out_width), apart),
            pl.BlockSpec(head_gain.shape, whole),
            pl.BlockSpec((rows, dim), apart),
            pl.BlockSpec((rows, dim), apart),
            pl.BlockSpec(memory_space=pl.ANY),
        ],
        out_specs=[
            pl.BlockSpec((rows, out_width), lambda i: (i, 0)),
            pl.BlockSpec(head_gain.shape, whole),
        ],
        scratch_shapes=[
            pltpu.VMEM(behind.shape, behind.dtype),
            pltpu.SemaphoreType.DMA,
            pltpu.SemaphoreType.DMA,
        ],
        out_shape=[
            jax.ShapeDtypeStruct((count, out_width), jnp.bfloat16),
            jax.ShapeDtypeStruct(head_gain.shape, jnp.float32),
        ],
        compiler_params=pltpu.CompilerParams(
            collective_id=9, has_side_effects=True, vmem_limit_bytes=48 << 20
        ),
        cost_estimate=pl.CostEstimate(
            flops=8_000_000_000, bytes_accessed=8_000_000, transcendentals=0
        ),
        name="project_back",
    )(query_grad, pair_sum, raw, head_gain, cosine, sine, behind)


def join_kernel(
    x_ref, weight_ref, weights_ref, gain_ref, mine_ref, cot_ref, residual_ref,
    normed_ref, attended_ref, cot_one_ref, cot_two_ref, held_ref, local_sem, send_sem, recv_sem
):
    step = pl.program_id(0)
    head, blk = lax.axis_index("heads"), lax.axis_index("blk")
    rows = x_ref.shape[0]
    count = held_ref.shape[1] // 4
    tiles = count // rows

    def copy(source, target, k, index):
        return pltpu.make_async_remote_copy(
            src_ref=source,
            dst_ref=target,
            send_sem=send_sem.at[index],
            recv_sem=recv_sem.at[index],
            device_id=(head ^ k, blk),
            device_id_type=MESH,
        )

    upper, lower = pl.ds(0, 2 * count), pl.ds(2 * count, 2 * count)
    near = [copy(mine_ref, held_ref.at[k], k, k - 1) for k in (1, 2)]
    far = [
        copy(held_ref.at[1, upper], held_ref.at[3, upper], 2, 2),
        copy(held_ref.at[2, lower], held_ref.at[3, lower], 1, 3),
    ]
    half = count // 2
    cot_near = [
        copy(cot_ref.at[pl.ds(half, half)], cot_one_ref, 1, 4),
        copy(cot_ref.at[pl.ds(0, half)], cot_two_ref, 2, 5),
    ]
    own = pltpu.make_async_copy(mine_ref, held_ref.at[0], local_sem)

    @pl.when(step == 0)
    def _():
        own.start()
        greet_near(False)
        for first in near:
            first.start()
        for first, second in zip(near, far):
            first.wait_recv()
            second.start()
        own.wait()
        for second in far:
            second.wait_recv()
        for last in cot_near:
            last.start()

    chunk = step // tiles
    parts = []
    total = x_ref[...].astype(jnp.float32)
    for k in range(4):
        start = ((chunk ^ k) * tiles + lax.rem(step, tiles)) * rows
        part = held_ref[k, pl.ds(pl.multiple_of(start, rows), rows)]
        weight = weight_ref[...] if k == 0 else weights_ref[k - 1]
        total += jnp.dot(part, weight, preferred_element_type=jnp.float32)
        parts.append(part)
    residual_ref[...] = total
    normed = total * lax.rsqrt(jnp.mean(total * total, axis=-1, keepdims=True) + EPS)
    normed_ref[...] = (normed * gain_ref[...]).astype(jnp.bfloat16)

    @pl.when(chunk == 0)
    def _():
        attended_ref[...] = jnp.concatenate(parts, axis=1)

    @pl.when(step == pl.num_programs(0) - 1)
    def _():
        for first in near + far:
            first.wait_send()
        for last in cot_near:
            last.wait()


def join(x, mine, weight, weights, gain, cot, rows):
    count, width = x.shape
    tokens = count // 4
    columns = mine.shape[1]
    tiles = tokens // rows
    anywhere = pl.BlockSpec(memory_space=pl.ANY)

    def there(i):
        return (i, 0)

    def whole(i):
        return (0, 0)

    sems = pltpu.SemaphoreType.DMA
    return pl.pallas_call(
        join_kernel,
        grid=(count // rows,),
        in_specs=[
            pl.BlockSpec((rows, width), there),
            pl.BlockSpec(weight.shape, whole),
            pl.BlockSpec(weights.shape, lambda i: (0, 0, 0)),
            pl.BlockSpec((1, width), whole),
            anywhere,
            anywhere,
        ],
        out_specs=[
            pl.BlockSpec((rows, width), there),
            pl.BlockSpec((rows, width), there),
            pl.BlockSpec((rows, 4 * columns), lambda i: (jnp.minimum(i, tiles - 1), 0)),
            anywhere,
            anywhere,
        ],
        out_shape=[
            jax.ShapeDtypeStruct((count, width), jnp.float32),
            jax.ShapeDtypeStruct((count, width), jnp.bfloat16),
            jax.ShapeDtypeStruct((tokens, 4 * columns), jnp.bfloat16),
            jax.ShapeDtypeStruct((tokens // 2, width), jnp.bfloat16),
            jax.ShapeDtypeStruct((tokens // 2, width), jnp.bfloat16),
        ],
        scratch_shapes=[
            pltpu.VMEM((4, count, columns), jnp.bfloat16),
            sems,
            sems((6,)),
            sems((6,)),
        ],
        compiler_params=pltpu.CompilerParams(
            collective_id=6, has_side_effects=True, vmem_limit_bytes=56 << 20
        ),
        cost_estimate=pl.CostEstimate(
            flops=16 * count * width * columns, bytes_accessed=50_000_000, transcendentals=0
        ),
        name="join",
    )(x, weight, weights, gain, mine, cot)


def trade_kernel(in_ref, out_ref, send_sem, recv_sem):
    head, blk = lax.axis_index("heads"), lax.axis_index("blk")
    size = lax.axis_size("heads")
    units = out_ref.shape[2] // 2
    barrier = pltpu.get_barrier_semaphore()
    for k in range(1, size):
        pl.semaphore_signal(barrier, inc=1, device_id=(head ^ k, blk), device_id_type=MESH)
    pl.semaphore_wait(barrier, size - 1)

    def columns(part, owner):
        return pl.ds(pl.multiple_of((part * size + owner) * units, units), units)

    copies = [
        pltpu.make_async_remote_copy(
            src_ref=in_ref.at[:, columns(part, head ^ k)],
            dst_ref=out_ref.at[head, :, pl.ds(part * units, units)],
            send_sem=send_sem.at[2 * k - 2 + part],
            recv_sem=recv_sem.at[2 * k - 2 + part],
            device_id=(head ^ k, blk),
            device_id_type=MESH,
        )
        for k in range(1, size)
        for part in range(2)
    ]
    for copy in copies:
        copy.start()
    for part in range(2):
        out_ref[head, :, part * units : (part + 1) * units] = in_ref[:, columns(part, head)]
    for copy in copies:
        copy.wait()


def trade(weight):
    size = lax.axis_size("heads")
    depth, width = weight.shape
    vmem = pl.BlockSpec(memory_space=pltpu.VMEM)
    return pl.pallas_call(
        trade_kernel,
        out_shape=jax.ShapeDtypeStruct((size, depth, width // size), weight.dtype),
        in_specs=[vmem],
        out_specs=vmem,
        scratch_shapes=[pltpu.SemaphoreType.DMA((2 * size - 2,))] * 2,
        compiler_params=pltpu.CompilerParams(
            collective_id=8, has_side_effects=True, vmem_limit_bytes=16 << 20
        ),
        name="trade",
    )(weight)


def begin_kernel(
    x_ref, qkv_ref, x_out, qkv_out, local_sem, x_send, x_recv, q_send, q_recv, b_send, b_recv,
    c_send, c_recv
):
    head, blk = lax.axis_index("heads"), lax.axis_index("blk")
    size, blk_size = lax.axis_size("heads"), lax.axis_size("blk")
    pairs = blk_size // 2
    count, depth = x_ref.shape[0], qkv_ref.shape[1]
    half = count // 2
    barrier = pltpu.get_barrier_semaphore()
    for k in range(1, size):
        pl.semaphore_signal(barrier, inc=1, device_id=(head ^ k, blk), device_id_type=MESH)
    pl.semaphore_signal(barrier, inc=1, device_id=(head, blk ^ 1), device_id_type=MESH)

    def same_core(k):
        return lax.rem(blk + 2 * k, blk_size)

    def greet(k, carried):
        pl.semaphore_signal(barrier, inc=1, device_id=(head, same_core(k)), device_id_type=MESH)
        return carried

    lax.fori_loop(1, pairs, greet, 0)
    pl.semaphore_wait(barrier, size + pairs - 1)

    def send(source, target, k, send_sem, recv_sem):
        return pltpu.make_async_remote_copy(
            src_ref=source,
            dst_ref=target,
            send_sem=send_sem,
            recv_sem=recv_sem,
            device_id=(head ^ k, blk),
            device_id_type=MESH,
        )

    def rows_of(index):
        return pl.ds(pl.multiple_of(index * depth, depth), depth)

    rows = rows_of(blk)
    qkv_copies = [
        send(
            qkv_ref.at[head ^ k], qkv_out.at[head, rows], k, q_send.at[k - 1], q_recv.at[k - 1]
        )
        for k in range(1, size)
    ]
    near = [
        send(x_ref, x_out.at[pl.ds(k * count, count)], k, x_send.at[k - 1], x_recv.at[k - 1])
        for k in (1, 2)
    ]
    far = [
        send(
            x_out.at[pl.ds(count, half)],
            x_out.at[pl.ds(3 * count, half)],
            2,
            x_send.at[2],
            x_recv.at[2],
        ),
        send(
            x_out.at[pl.ds(2 * count + half, half)],
            x_out.at[pl.ds(3 * count + half, half)],
            1,
            x_send.at[3],
            x_recv.at[3],
        ),
    ]
    own = [
        pltpu.make_async_copy(qkv_ref.at[head], qkv_out.at[head, rows], local_sem.at[0]),
        pltpu.make_async_copy(x_ref, x_out.at[pl.ds(0, count)], local_sem.at[1]),
    ]
    for copy in qkv_copies + near + own:
        copy.start()

    def along(k, source):
        return pltpu.make_async_remote_copy(
            src_ref=qkv_out.at[:, rows],
            dst_ref=qkv_out.at[:, rows_of(source)],
            send_sem=b_send.at[k],
            recv_sem=b_recv.at[k],
            device_id=(head, same_core(k)),
            device_id_type=MESH,
        )

    def behind(k):
        return lax.rem(blk + blk_size - 2 * k, blk_size)

    def across(k, core):
        source = behind(k) ^ core
        return pltpu.make_async_remote_copy(
            src_ref=qkv_out.at[:, rows_of(behind(k))],
            dst_ref=qkv_out.at[:, rows_of(source)],
            send_sem=c_send.at[k],
            recv_sem=c_recv.at[k],
            device_id=(head, blk ^ 1),
            device_id_type=MESH,
        )

    def start(k, carried):
        along(k, blk).start()
        return carried

    def pass_on(k, carried):
        along(k, behind(k)).wait_recv()
        across(k, 0).start()
        return carried

    def finish(k, carried):
        across(k, 0).wait_send()
        across(k, 1).wait_recv()
        return carried

    def sent(k, carried):
        along(k, blk).wait_send()
        return carried

    own[0].wait()
    for copy in qkv_copies:
        copy.wait_recv()
    lax.fori_loop(1, pairs, start, 0)
    across(0, 0).start()
    lax.fori_loop(1, pairs, pass_on, 0)
    for first, second in zip(near, far):
        first.wait_recv()
        second.start()
    for copy in qkv_copies + near:
        copy.wait_send()
    for copy in far:
        copy.wait()
    own[1].wait()
    lax.fori_loop(1, pairs, sent, 0)
    lax.fori_loop(0, pairs, finish, 0)


def begin(x, qkv_parts):
    size, blk_size = lax.axis_size("heads"), lax.axis_size("blk")
    count, width = x.shape
    depth, joined = qkv_parts.shape[1:]
    anywhere = pl.BlockSpec(memory_space=pl.ANY)
    sems = pltpu.SemaphoreType.DMA
    return pl.pallas_call(
        begin_kernel,
        out_shape=[
            jax.ShapeDtypeStruct((size * count, width), x.dtype),
            jax.ShapeDtypeStruct((size, blk_size * depth, joined), x.dtype),
        ],
        in_specs=[anywhere] * 2,
        out_specs=[anywhere] * 2,
        scratch_shapes=[
            sems((2,)),
            sems((4,)),
            sems((4,)),
            sems((size - 1,)),
            sems((size - 1,)),
            sems((blk_size // 2,)),
            sems((blk_size // 2,)),
            sems((blk_size // 2,)),
            sems((blk_size // 2,)),
        ],
        compiler_params=pltpu.CompilerParams(collective_id=1, has_side_effects=True),
        name="begin",
    )(x, qkv_parts)


def spread_copies(source_ref, target_ref, send_sem, recv_sem):
    head, blk = lax.axis_index("heads"), lax.axis_index("blk")
    rows = source_ref.shape[0] // 2
    quarter = rows // 2
    start = pl.multiple_of(lax.rem(blk, 2) * rows, rows)
    half = pl.ds(start, rows)
    first = source_ref.at[half, pl.ds(0, target_ref.shape[2])]
    count = [0]

    def copy(source, target, place):
        index = count[0]
        count[0] += 1
        return pltpu.make_async_remote_copy(
            src_ref=source,
            dst_ref=target,
            send_sem=send_sem.at[index],
            recv_sem=recv_sem.at[index],
            device_id=place,
            device_id_type=MESH,
        )

    near = [
        copy(first, target_ref.at[k - 1, half], (head ^ k, blk)) for k in (1, 2)
    ]
    upper = pl.ds(start, quarter)
    lower = pl.ds(pl.multiple_of(start + quarter, quarter), quarter)
    far = [
        copy(target_ref.at[0, upper], target_ref.at[2, upper], (head ^ 2, blk)),
        copy(target_ref.at[1, lower], target_ref.at[2, lower], (head ^ 1, blk)),
    ]
    other = [
        copy(target_ref.at[k, half], target_ref.at[k, half], (head, blk ^ 1)) for k in range(3)
    ]
    return near, far, other


def greet_near(partner):
    head, blk = lax.axis_index("heads"), lax.axis_index("blk")
    barrier = pltpu.get_barrier_semaphore()
    places = [(head ^ 1, blk), (head ^ 2, blk)] + ([(head, blk ^ 1)] if partner else [])
    for place in places:
        pl.semaphore_signal(barrier, inc=1, device_id=place, device_id_type=MESH)
    pl.semaphore_wait(barrier, len(places))


def spread_job(step, marks, source_ref, target_ref, send_sem, recv_sem, greet=True):
    near, far, other = spread_copies(source_ref, target_ref, send_sem, recv_sem)
    begin_at, far_at, other_at = marks

    @pl.when(step == begin_at)
    def _():
        if greet:
            greet_near(True)
        for copy in near:
            copy.start()

    @pl.when(step == far_at)
    def _():
        for k in range(2):
            near[k].wait_recv()
            far[k].start()
            other[k].start()

    @pl.when(step == other_at)
    def _():
        for copy in far:
            copy.wait_recv()
        other[2].start()

    def end():
        for copy in near + far:
            copy.wait_send()
        for copy in other:
            copy.wait()

    return end


SPREAD_COUNT = 7


def hidden_kernel(
    tiles, normed_ref, gate_ref, up_ref, down_ref, turned_ref, side_ref, cot_ref, one_top_ref,
    one_bottom_ref, two_top_ref, two_bottom_ref, hidden_ref, gate_grad_ref, up_grad_ref, in_sum_ref,
    cot_far_ref, spread_ref, held_ref, grads_ref, load_sem, far_send, far_recv, send_sem, recv_sem
):
    step, steps = pl.program_id(0), pl.num_programs(0)
    head, blk = lax.axis_index("heads"), lax.axis_index("blk")
    count = cot_ref.shape[0]
    half = count // 2
    rows, units = hidden_ref.shape
    far = [
        pltpu.make_async_remote_copy(
            src_ref=ref,
            dst_ref=held_ref.at[pl.ds(3 * count + part * half, half)],
            send_sem=far_send.at[part],
            recv_sem=far_recv.at[part],
            device_id=(head ^ k, blk),
            device_id_type=MESH,
        )
        for part, (ref, k) in enumerate(((one_top_ref, 2), (two_bottom_ref, 1)))
    ]
    keep = pltpu.make_async_copy(
        held_ref.at[pl.ds(3 * count, count)], cot_far_ref, load_sem.at[5]
    )
    near = ((one_top_ref, 2), (one_bottom_ref, 3), (two_top_ref, 4), (two_bottom_ref, 5))
    loads = [pltpu.make_async_copy(cot_ref, held_ref.at[pl.ds(0, count)], load_sem.at[0])] + [
        pltpu.make_async_copy(ref, held_ref.at[pl.ds(half * place, half)], load_sem.at[place - 1])
        for ref, place in near
    ]

    @pl.when(step == 0)
    def _():
        for load in loads:
            load.start()
        greet_near(True)
        for copy in far:
            copy.start()
        for load in loads:
            load.wait()

    @pl.when(step == tiles)
    def _():
        for copy in far:
            copy.wait()
        keep.start()

    marks = (tiles, 2 * tiles, 2 * tiles + 4)
    end = spread_job(step, marks, side_ref, spread_ref, send_sem, recv_sem, False)

    @pl.when(step < 2 * tiles)
    def _():
        here = pl.ds(pl.multiple_of(step // tiles * rows, rows), rows)
        normed = normed_ref[...]
        gate = jnp.dot(normed, gate_ref[...], preferred_element_type=jnp.float32)
        upward = jnp.dot(normed, up_ref[...], preferred_element_type=jnp.float32)
        grad = lax.dot_general(
            held_ref[here], down_ref[...], ROWS_IN_BOTH, preferred_element_type=jnp.float32
        )
        sigmoid = jax.nn.sigmoid(gate)
        activated = gate * sigmoid
        hidden_ref[...] = (activated * upward).astype(jnp.bfloat16)
        gate_grad = (grad * upward * sigmoid * (1.0 + gate * (1.0 - sigmoid))).astype(jnp.bfloat16)
        up_grad = (grad * activated).astype(jnp.bfloat16)
        gate_grad_ref[...] = gate_grad
        up_grad_ref[...] = up_grad
        for part, value in enumerate((gate_grad, up_grad)):
            place = (part * tiles + lax.rem(step, tiles)) * units
            grads_ref[here, pl.ds(pl.multiple_of(place, units), units)] = value

    @pl.when(step >= 2 * tiles)
    def _():
        in_sum_ref[...] = lax.dot_general(
            turned_ref[...],
            grads_ref[...],
            (((0,), (0,)), ((), ())),
            preferred_element_type=jnp.float32,
        ).astype(jnp.bfloat16)

    @pl.when(step == steps - 1)
    def _():
        end()
        keep.wait()


def hidden_pass(normed, weight, cot, cot_near, down, side, side_columns, units):
    count, width = normed.shape
    total = down.shape[0]
    tiles = total // units
    rows = count // 2
    columns = width // 8

    def row(s):
        return jnp.minimum(s // tiles, 1)

    def column(s):
        return jnp.where(s < 2 * tiles, lax.rem(s, tiles), tiles - 1)

    out_spec = pl.BlockSpec((rows, units), lambda s: (row(s), column(s)))
    out_shape = jax.ShapeDtypeStruct((count, total), jnp.bfloat16)
    anywhere = pl.BlockSpec(memory_space=pl.ANY)
    sems = pltpu.SemaphoreType.DMA
    return pl.pallas_call(
        functools.partial(hidden_kernel, tiles),
        grid=(2 * tiles + 8,),
        in_specs=[
            pl.BlockSpec((rows, width), lambda s: (row(s), 0)),
            pl.BlockSpec((width, units), lambda s: (0, column(s))),
            pl.BlockSpec((width, units), lambda s: (0, tiles + column(s))),
            pl.BlockSpec((units, width), lambda s: (column(s), 0)),
            pl.BlockSpec((count, columns), lambda s: (0, jnp.maximum(s - 2 * tiles, 0))),
        ]
        + [anywhere] * 6,
        out_specs=[out_spec] * 3
        + [
            pl.BlockSpec((columns, 2 * total), lambda s: (jnp.maximum(s - 2 * tiles, 0), 0)),
            anywhere,
            anywhere,
        ],
        out_shape=[out_shape] * 3
        + [
            jax.ShapeDtypeStruct((width, 2 * total), jnp.bfloat16),
            jax.ShapeDtypeStruct(cot.shape, jnp.bfloat16),
            jax.ShapeDtypeStruct((3, side.shape[0], side_columns), side.dtype),
        ],
        scratch_shapes=[
            pltpu.VMEM((count, width), jnp.bfloat16),
            pltpu.VMEM((count, 2 * total), jnp.bfloat16),
            sems((6,)),
            sems((2,)),
            sems((2,)),
            sems((SPREAD_COUNT,)),
            sems((SPREAD_COUNT,)),
        ],
        compiler_params=pltpu.CompilerParams(
            collective_id=2, has_side_effects=True, vmem_limit_bytes=58 << 20
        ),
        cost_estimate=pl.CostEstimate(
            flops=10 * count * width * total, bytes_accessed=70_000_000, transcendentals=0
        ),
        name="hidden_pass",
    )(normed, weight, weight, down, normed, side, cot, *cot_near)


def in_order(step):
    value = 1
    for index, half in enumerate((6, 7, 2, 5, 4, 3, 0)):
        value = jnp.where(step == index, half, value)
    return value


def tail_kernel(
    gate_ref, up_ref, hidden_ref, turned_ref, in_hbm, down_hbm, cot_ref, one_top_ref, one_bottom_ref,
    two_top_ref, two_bottom_ref, cot_far_ref, down_sum_ref, *refs
):
    first_refs, (out_rest_ref, grad_ref, *refs) = refs[:4], refs[4:]
    (
        weight_ref, down_ref, first_ref, rest_ref, got_ref, last_ref, last_got_ref, weight_sem,
        send_sem, recv_sem,
    ) = refs
    step = pl.program_id(0)
    head, blk = lax.axis_index("heads"), lax.axis_index("blk")
    rows, total = hidden_ref.shape
    width = grad_ref.shape[1]
    load_in = pltpu.make_async_copy(in_hbm, weight_ref, weight_sem.at[0])
    load_down = pltpu.make_async_copy(down_hbm, down_ref, weight_sem.at[1])
    pieces = (
        (cot_ref, 0, 2),
        (one_top_ref, 2, 1),
        (one_bottom_ref, 3, 1),
        (two_top_ref, 4, 1),
        (two_bottom_ref, 5, 1),
        (cot_far_ref, 6, 2),
    )
    cot_loads = [
        pltpu.make_async_copy(
            ref,
            weight_ref.at[pl.ds(place * rows, length * rows), pl.ds(0, width)],
            weight_sem.at[2 + index],
        )
        for index, (ref, place, length) in enumerate(pieces)
    ]

    def copy(source, target, k, index):
        return pltpu.make_async_remote_copy(
            src_ref=source,
            dst_ref=target,
            send_sem=send_sem.at[index],
            recv_sem=recv_sem.at[index],
            device_id=(head ^ k, blk),
            device_id_type=MESH,
        )

    firsts = [
        copy(first_ref.at[index], got_ref.at[index], k, index)
        for index, k in enumerate((1, 2, 1, 2))
    ]
    lasts = [copy(last_ref.at[part], last_got_ref.at[part], 2 - part, 4 + part) for part in range(2)]

    def wide_of(block):
        return block.astype(jnp.float32)

    @pl.when(step == 0)
    def _():
        load_in.start()
        load_down.start()
        greet_near(False)
        load_in.wait()

    @pl.when(step < 8)
    def _():
        value = lax.dot_general(
            gate_ref[...], weight_ref[:, :total], ROWS_IN_BOTH, preferred_element_type=jnp.float32
        ) + lax.dot_general(
            up_ref[...], weight_ref[:, total:], ROWS_IN_BOTH, preferred_element_type=jnp.float32
        )
        value = value.astype(jnp.bfloat16)

        for index in range(4):

            @pl.when(step == index)
            def _(index=index):
                first_ref[index] = value
                firsts[index].start()

        @pl.when(step >= 4)
        def _():
            rest_ref[pl.ds(pl.multiple_of((step - 4) * rows, rows), rows)] = value

        @pl.when(step == 7)
        def _():
            load_down.wait()
            for load in cot_loads:
                load.start()

    @pl.when((step >= 8) & (step < 16))
    def _():
        terms = jnp.dot(
            hidden_ref[...], down_ref[...], preferred_element_type=jnp.float32
        ).astype(jnp.bfloat16)

        for index, ref in enumerate(first_refs):

            @pl.when(step == 8 + index)
            def _(ref=ref):
                ref[...] = terms

        @pl.when(step >= 12)
        def _():
            out_rest_ref[...] = terms

        @pl.when(step == 15)
        def _():
            for load in cot_loads:
                load.wait()

    @pl.when(step >= 16)
    def _():
        down_sum_ref[...] = lax.dot_general(
            turned_ref[...],
            weight_ref[:, :width],
            (((0,), (0,)), ((), ())),
            preferred_element_type=jnp.float32,
        ).astype(jnp.bfloat16)

    for part, when in enumerate((8, 9)):

        @pl.when(step == when)
        def _(part=part):
            firsts[part].wait_recv()
            last_ref[part] = (
                wide_of(rest_ref[part * rows : (part + 1) * rows]) + wide_of(got_ref[part])
            ).astype(jnp.bfloat16)
            lasts[part].start()

    @pl.when(step == pl.num_programs(0) - 1)
    def _():
        for part in range(2):
            firsts[2 + part].wait_recv()
            lasts[part].wait_recv()
            grad_ref[part * rows : (part + 1) * rows] = (
                wide_of(rest_ref[(2 + part) * rows : (3 + part) * rows])
                + wide_of(got_ref[2 + part])
                + wide_of(last_got_ref[part])
            )
        for sent in firsts + lasts:
            sent.wait_send()


def feed_tail(gate_grad, up_grad, hidden, weight, down, cots):
    count, total = hidden.shape
    width = weight.shape[0]
    rows = count // 8
    units = 256
    anywhere = pl.BlockSpec(memory_space=pl.ANY)

    def stage(i, first, last):
        return jnp.clip(i - first, 0, last)

    def first_rows(i):
        return (in_order(stage(i, 0, 7)), 0)

    low = jnp.bfloat16
    return pl.pallas_call(
        tail_kernel,
        grid=(16 + total // units,),
        in_specs=[
            pl.BlockSpec((rows, total), first_rows),
            pl.BlockSpec((rows, total), first_rows),
            pl.BlockSpec((rows, total), lambda i: (in_order(stage(i, 8, 7)), 0)),
            pl.BlockSpec((count, units), lambda i: (0, jnp.maximum(i - 16, 0))),
        ]
        + [anywhere] * 8,
        out_specs=[
            pl.BlockSpec((units, width), lambda i: (jnp.maximum(i - 16, 0), 0)),
            *[pl.BlockSpec((rows, width), lambda i: (0, 0), pipeline_mode=pl.Buffered(1))] * 4,
            pl.BlockSpec((rows, width), lambda i: (stage(i, 12, 3), 0)),
            pl.BlockSpec((2 * rows, width), lambda i: (0, 0), pipeline_mode=pl.Buffered(1)),
        ],
        out_shape=[
            jax.ShapeDtypeStruct((total, width), low),
            *[jax.ShapeDtypeStruct((rows, width), low)] * 4,
            jax.ShapeDtypeStruct((4 * rows, width), low),
            jax.ShapeDtypeStruct((2 * rows, width), jnp.float32),
        ],
        scratch_shapes=[
            pltpu.VMEM(weight.shape, low),
            pltpu.VMEM(down.shape, low),
            pltpu.VMEM((4, rows, width), low),
            pltpu.VMEM((4 * rows, width), low),
            pltpu.VMEM((4, rows, width), low),
            pltpu.VMEM((2, rows, width), low),
            pltpu.VMEM((2, rows, width), low),
            pltpu.SemaphoreType.DMA((8,)),
            pltpu.SemaphoreType.DMA((6,)),
            pltpu.SemaphoreType.DMA((6,)),
        ],
        compiler_params=pltpu.CompilerParams(
            collective_id=3, has_side_effects=True, vmem_limit_bytes=60 << 20
        ),
        cost_estimate=pl.CostEstimate(
            flops=8 * count * width * total, bytes_accessed=70_000_000, transcendentals=0
        ),
        name="feed_tail",
    )(gate_grad, up_grad, hidden, hidden, weight, down, *cots)


def residual_back_kernel(
    grad_sum_ref, residual_ref, cot_ref, gain_ref, attended_ref, weight_ref, weights_ref, grad_ref,
    gain_grad_ref, pieces_ref, *refs
):
    *out_refs, branch_ref, mine_ref, terms_ref, terms_got_ref, own_sem, send_sem, recv_sem = refs
    size = lax.axis_size("heads")
    core = lax.rem(lax.axis_index("blk"), 2)
    step = pl.program_id(0)
    last = pl.num_programs(0) - 1
    head, blk = lax.axis_index("heads"), lax.axis_index("blk")
    rows = cot_ref.shape[0]
    copies = [
        pltpu.make_async_remote_copy(
            src_ref=mine_ref.at[k],
            dst_ref=pieces_ref.at[k],
            send_sem=send_sem.at[k - 1],
            recv_sem=recv_sem.at[k - 1],
            device_id=(head ^ k, blk),
            device_id_type=MESH,
        )
        for k in range(1, size)
    ]
    keep = pltpu.make_async_copy(mine_ref.at[0], pieces_ref.at[0], own_sem)
    across = pltpu.make_async_remote_copy(
        src_ref=terms_ref.at[:, 1 - core],
        dst_ref=terms_got_ref,
        send_sem=send_sem.at[size - 1],
        recv_sem=recv_sem.at[size - 1],
        device_id=(head, blk ^ 1),
        device_id_type=MESH,
    )

    @pl.when(step == 0)
    def _():
        gain_grad_ref[...] = jnp.zeros_like(gain_grad_ref)
        barrier = pltpu.get_barrier_semaphore()
        for k in range(1, size):
            pl.semaphore_signal(barrier, inc=1, device_id=(head ^ k, blk), device_id_type=MESH)
        pl.semaphore_signal(barrier, inc=1, device_id=(head, blk ^ 1), device_id_type=MESH)
        pl.semaphore_wait(barrier, size)

    @pl.when(step < last)
    def _():
        here = pl.ds(pl.multiple_of(step * rows, rows), rows)
        gradient = grad_sum_ref[...]
        values = residual_ref[...]
        inverse = lax.rsqrt(jnp.mean(values * values, axis=-1, keepdims=True) + EPS)
        gain_grad_ref[...] += jnp.sum(gradient * values * inverse, axis=0, keepdims=True)
        scaled = gradient * gain_ref[...]
        moment = jnp.mean(scaled * values, axis=-1, keepdims=True)
        total = cot_ref[...].astype(jnp.float32) + (
            inverse * scaled - values * (inverse * inverse * inverse * moment)
        )
        grad_ref[...] = total
        branch = total.astype(jnp.bfloat16)
        branch_ref[here] = branch
        for k in range(size):
            weight = weight_ref[...] if k == 0 else weights_ref[k - 1]
            mine_ref[k, here] = lax.dot_general(
                branch, weight, ROWS_IN_BOTH, preferred_element_type=jnp.float32
            ).astype(jnp.bfloat16)

    @pl.when(step == last)
    def _():
        for copy in copies:
            copy.start()
        keep.start()
        columns = attended_ref.shape[1] // size
        pairs = terms_ref.shape[0] // size
        for k in range(size):
            terms = lax.dot_general(
                attended_ref[:, k * columns : (k + 1) * columns],
                branch_ref[...],
                (((0,), (0,)), ((), ())),
                preferred_element_type=jnp.float32,
            ).astype(jnp.bfloat16)
            terms_ref[k * pairs : (k + 1) * pairs] = terms.reshape(pairs, *terms_ref.shape[1:])
        across.start()
        across.wait()

        for k, out_ref in enumerate(out_refs):

            def add(index, carried, k=k, out_ref=out_ref):
                out_ref[index] = (
                    terms_ref[k * pairs + index, core].astype(jnp.float32)
                    + terms_got_ref[k * pairs + index].astype(jnp.float32)
                ).astype(jnp.bfloat16)
                return carried

            lax.fori_loop(0, pairs, add, 0)
        for copy in copies:
            copy.wait()
        keep.wait()


def residual_back(grad_sum, residual, cot, gain, attended, weight, weights, rows):
    count, width = cot.shape
    size, blk_size = lax.axis_size("heads"), lax.axis_size("blk")
    columns = weight.shape[0]
    pairs, held = size * blk_size // 2, columns // blk_size
    tiles = count // rows

    def there(i):
        return (jnp.minimum(i, tiles - 1), 0)

    def whole(i):
        return (0, 0)

    tile = pl.BlockSpec((rows, width), there)
    row = pl.BlockSpec((1, width), whole)
    pieces = (size, count, columns)
    return pl.pallas_call(
        residual_back_kernel,
        grid=(tiles + 1,),
        in_specs=[
            tile,
            tile,
            tile,
            row,
            pl.BlockSpec(attended.shape, whole),
            pl.BlockSpec(weight.shape, whole),
            pl.BlockSpec(weights.shape, lambda i: (0, 0, 0)),
        ],
        out_specs=[
            tile,
            row,
            pl.BlockSpec(memory_space=pl.ANY),
            *[pl.BlockSpec((pairs // size, held, width), lambda i: (0, 0, 0))] * size,
        ],
        out_shape=[
            jax.ShapeDtypeStruct((count, width), jnp.float32),
            jax.ShapeDtypeStruct((1, width), jnp.float32),
            jax.ShapeDtypeStruct(pieces, jnp.bfloat16),
            *[jax.ShapeDtypeStruct((pairs // size, held, width), jnp.bfloat16)] * size,
        ],
        scratch_shapes=[
            pltpu.VMEM((count, width), jnp.bfloat16),
            pltpu.VMEM(pieces, jnp.bfloat16),
            pltpu.VMEM((pairs, 2, held, width), jnp.bfloat16),
            pltpu.VMEM((pairs, held, width), jnp.bfloat16),
            pltpu.SemaphoreType.DMA,
            pltpu.SemaphoreType.DMA((size,)),
            pltpu.SemaphoreType.DMA((size,)),
        ],
        compiler_params=pltpu.CompilerParams(
            collective_id=4, has_side_effects=True, vmem_limit_bytes=56 << 20
        ),
        cost_estimate=pl.CostEstimate(
            flops=4 * count * width * columns * size, bytes_accessed=30_000_000, transcendentals=0
        ),
        name="residual_back",
    )(grad_sum, residual, cot, gain, attended, weight, weights)


def qkv_terms_kernel(normed_ref, grad_ref, *refs):
    size, blk_size = lax.axis_size("heads"), lax.axis_size("blk")
    out_refs, refs = refs[:size], refs[size:]
    (
        terms_ref, got_ref, out_grad_ref, out_part_ref, out_got_ref, send_sem, recv_sem, o_send,
        o_recv,
    ) = refs
    step = pl.program_id(0)
    pairs = blk_size // 2
    head, blk = lax.axis_index("heads"), lax.axis_index("blk")
    core, pair = lax.rem(blk, 2), blk // 2
    count = got_ref.shape[1]
    out_rows = out_grad_ref.shape[0]
    copies = [
        pltpu.make_async_remote_copy(
            src_ref=grad_ref.at[pl.ds(k * count, count)],
            dst_ref=got_ref.at[k - 1],
            send_sem=send_sem.at[k - 1],
            recv_sem=recv_sem.at[k - 1],
            device_id=(head ^ k, blk),
            device_id_type=MESH,
        )
        for k in range(1, size)
    ]

    def wide_of(block):
        return block.astype(jnp.float32)

    def out_copy(k, slot):
        other = lax.rem(pair + k, pairs)
        return pltpu.make_async_remote_copy(
            src_ref=out_part_ref.at[other],
            dst_ref=out_got_ref.at[slot],
            send_sem=o_send.at[k],
            recv_sem=o_recv.at[slot],
            device_id=(head, other * 2 + core),
            device_id_type=MESH,
        )

    @pl.when(step == 0)
    def _():
        barrier = pltpu.get_barrier_semaphore()
        for k in range(1, size):
            pl.semaphore_signal(barrier, inc=1, device_id=(head ^ k, blk), device_id_type=MESH)

        def greet(k, carried):
            place = (head, lax.rem(pair + k, pairs) * 2 + core)
            pl.semaphore_signal(barrier, inc=1, device_id=place, device_id_type=MESH)
            return carried

        lax.fori_loop(1, pairs, greet, 0)
        pl.semaphore_wait(barrier, size + pairs - 2)
        for copy in copies:
            copy.start()

        def out_sum(index, carried):
            here = pl.ds(pl.multiple_of(index * out_rows, out_rows), out_rows)
            total = wide_of(out_refs[0][here])
            for ref in out_refs[1:]:
                total += wide_of(ref[here])
            out_part_ref[index, :out_rows] = total.astype(jnp.bfloat16)
            return carried

        def start(k, carried):
            out_copy(k, pair).start()
            return carried

        lax.fori_loop(0, pairs, out_sum, 0)
        lax.fori_loop(1, pairs, start, 0)
        out_got_ref[pair] = out_part_ref[pair]

    terms_ref[...] = lax.dot_general(
        normed_ref[...], grad_ref[...], (((0,), (0,)), ((), ())), preferred_element_type=jnp.float32
    ).astype(terms_ref.dtype)

    @pl.when(step == pl.num_programs(0) - 1)
    def _():
        for copy in copies:
            copy.wait()

        def finish(k, carried):
            out_copy(k, lax.rem(pair + pairs - k, pairs)).wait()
            return carried

        lax.fori_loop(1, pairs, finish, 0)
        total = wide_of(out_got_ref[0, :out_rows])
        for b in range(1, pairs):
            total += wide_of(out_got_ref[b, :out_rows])
        out_grad_ref[...] = total


def qkv_terms(normed, grad, outs, rows):
    count, height = normed.shape
    width = grad.shape[1]
    size, blk_size = lax.axis_size("heads"), lax.axis_size("blk")
    pairs = blk_size // 2
    out_rows, out_width = outs[0].shape[0] // pairs, outs[0].shape[1]
    held_rows = -(-out_rows // 16) * 16

    def whole(i):
        return (0, 0)

    sems = pltpu.SemaphoreType.DMA
    return pl.pallas_call(
        qkv_terms_kernel,
        grid=(height // rows,),
        in_specs=[
            pl.BlockSpec((count, rows), lambda i: (0, i)),
            pl.BlockSpec((count, width), whole),
        ]
        + [pl.BlockSpec(out.shape, whole) for out in outs],
        out_specs=[
            pl.BlockSpec((rows, width), lambda i: (i, 0)),
            pl.BlockSpec(memory_space=pl.ANY),
            pl.BlockSpec((out_rows, out_width), whole),
        ],
        out_shape=[
            jax.ShapeDtypeStruct((height, width), jnp.bfloat16),
            jax.ShapeDtypeStruct((size - 1, count // size, width), jnp.bfloat16),
            jax.ShapeDtypeStruct((out_rows, out_width), jnp.float32),
        ],
        scratch_shapes=[
            pltpu.VMEM((pairs, held_rows, out_width), jnp.bfloat16),
            pltpu.VMEM((pairs, held_rows, out_width), jnp.bfloat16),
            sems((size - 1,)),
            sems((size - 1,)),
            sems((pairs,)),
            sems((pairs,)),
        ],
        compiler_params=pltpu.CompilerParams(
            collective_id=7, has_side_effects=True, vmem_limit_bytes=48 << 20
        ),
        cost_estimate=pl.CostEstimate(
            flops=4 * count * height * width, bytes_accessed=20_000_000, transcendentals=0
        ),
        name="qkv_terms",
    )(normed, grad, *outs)


def finish_kernel(
    query_width, dim, got_ref, qkv_ref, gain_ref, ffn_ref, head_ref, *refs
):
    size, blk_size = lax.axis_size("heads"), lax.axis_size("blk")
    sources, refs = refs[:12], refs[12:]
    (
        grad_ref, qkv_grad_ref, gains_ref, in_grad_ref, layer_ref, *refs
    ) = refs
    held, refs = refs[:12], refs[12:]
    weight_ref, weights_ref, x_ref, residual_grad_ref, sent_ref, in_ref, residual_ref, rest_ref = held[:8]
    (
        qkv_other_ref, qkv_sum_ref, qkv_z_ref, qkv_mine_ref, qkv_got_ref, gain_mine_ref,
        gain_away_ref, gain_other_ref, gain_sum_ref, gain_z_ref, gain_part_ref, gain_got_ref,
        in_got_ref, load_sem, c_send, c_recv, z_send, z_recv, h_send,
        h_recv, gc_send, gc_recv, gz_send, gz_recv, gh_send, gh_recv, i_send, i_recv,
    ) = refs
    devices = size * blk_size
    pairs = blk_size // 2
    head, blk = lax.axis_index("heads"), lax.axis_index("blk")
    core, pair = lax.rem(blk, 2), blk // 2
    count, width = x_ref.shape
    depth = width // devices
    barrier = pltpu.get_barrier_semaphore()
    loads = [
        pltpu.make_async_copy(
            source.at[pl.ds(0, target.shape[0]), pl.ds(0, target.shape[1])]
            if index in (0, 4, 6)
            else source.at[pl.ds(target.shape[0], target.shape[0])]
            if index == 7
            else source,
            target,
            load_sem.at[index],
        )
        for index, (source, target) in enumerate(zip(sources, held))
    ]
    for load in loads:
        load.start()

    def same_core(k):
        return (head, lax.rem(pair + k, pairs) * 2 + core)

    for k in range(1, size):
        pl.semaphore_signal(barrier, inc=1, device_id=(head ^ k, blk), device_id_type=MESH)
    pl.semaphore_signal(barrier, inc=1, device_id=(head, blk ^ 1), device_id_type=MESH)

    def greet(k, carried):
        pl.semaphore_signal(barrier, inc=1, device_id=same_core(k), device_id_type=MESH)
        return carried

    lax.fori_loop(1, pairs, greet, 0)
    pl.semaphore_wait(barrier, size + pairs - 1)

    def copy(source, target, place, send, recv):
        return pltpu.make_async_remote_copy(
            src_ref=source,
            dst_ref=target,
            send_sem=send,
            recv_sem=recv,
            device_id=place,
            device_id_type=MESH,
        )

    in_sends = [
        copy(
            sources[5].at[head ^ k],
            in_got_ref.at[k - 1],
            (head ^ k, blk),
            i_send.at[k - 1],
            i_recv.at[k - 1],
        )
        for k in range(1, size)
    ]
    for sent in in_sends:
        sent.start()

    across = copy(qkv_ref.at[:, 1 - core], qkv_other_ref, (head, blk ^ 1), c_send, c_recv)
    across.start()
    def wide_of(block):
        return block.astype(jnp.float32)

    across.wait_recv()

    def along(k, source_ref, target_ref, slot, send, recv):
        return copy(
            source_ref.at[:, lax.rem(pair + k, pairs)],
            target_ref.at[slot],
            same_core(k),
            send.at[k],
            recv.at[slot],
        )

    def around(source_ref, target_ref, slots, send, recv):
        return [
            copy(
                source_ref.at[head ^ k],
                target_ref.at[slots[k]],
                (head ^ k, blk),
                send.at[k - 1],
                recv.at[slots[k]],
            )
            for k in range(1, size)
        ]

    def start_along(source_ref, target_ref, send, recv):
        def start(k, carried):
            along(k, source_ref, target_ref, pair, send, recv).start()
            return carried

        lax.fori_loop(1, pairs, start, 0)
        target_ref[pair] = source_ref[:, pair]

    def finish_along(source_ref, target_ref, send, recv):
        def finish(k, carried):
            slot = lax.rem(pair + pairs - k, pairs)
            along(k, source_ref, target_ref, slot, send, recv).wait()
            return carried

        lax.fori_loop(1, pairs, finish, 0)
        total = wide_of(target_ref[0])
        for k in range(1, pairs):
            total += wide_of(target_ref[k])
        return total

    here, there = [head] * size, [head ^ k for k in range(size)]

    def start_around(source_ref, target_ref, send, recv):
        for sent in around(source_ref, target_ref, here, send, recv):
            sent.start()
        target_ref[head] = source_ref[head]

    def finish_around(source_ref, target_ref, send, recv):
        for sent in around(source_ref, target_ref, there, send, recv):
            sent.wait()

    def qkv_sum(index, carried):
        qkv_sum_ref[index // pairs, lax.rem(index, pairs)] = (
            wide_of(qkv_ref[index, core]) + wide_of(qkv_other_ref[index])
        ).astype(jnp.bfloat16)
        return carried

    lax.fori_loop(0, size * pairs, qkv_sum, 0)
    start_along(qkv_sum_ref, qkv_z_ref, z_send, z_recv)

    for load in loads[:5]:
        load.wait()
    rows = min(128, count)

    def tile(index, gain_sum):
        here = pl.ds(pl.multiple_of(index * rows, rows), rows)
        normed_grad = lax.dot_general(
            sent_ref[here], weight_ref[...], ROWS_IN_BOTH, preferred_element_type=jnp.float32
        )
        for k in range(1, size):
            normed_grad += lax.dot_general(
                got_ref[k - 1, here],
                weights_ref[k - 1],
                ROWS_IN_BOTH,
                preferred_element_type=jnp.float32,
            )
        values = wide_of(x_ref[here])
        inverse = lax.rsqrt(jnp.mean(values * values, axis=-1, keepdims=True) + EPS)
        scaled = normed_grad * gain_ref[...]
        moment = jnp.mean(scaled * values, axis=-1, keepdims=True)
        grad_ref[here] = (
            residual_grad_ref[here]
            + inverse * scaled
            - values * (inverse * inverse * inverse * moment)
        )
        return gain_sum + jnp.sum(normed_grad * values * inverse, axis=0, keepdims=True)

    attn_sum = lax.fori_loop(0, count // rows, tile, jnp.zeros((1, width), jnp.float32))

    def by_device(row, which):
        lanes = jnp.concatenate(
            [row[:, d * depth : (d + 1) * depth] for d in range(which, devices, 2)], axis=0
        )
        if depth < 64:
            lanes = jnp.concatenate(
                [lanes, jnp.zeros((devices // 2, 64 - depth), jnp.float32)], axis=1
            )
        return lanes

    head_row = head_ref[...]
    query_sum = head_row[:, :dim]
    for c in range(dim, query_width, dim):
        query_sum += head_row[:, c : c + dim]
    key_sum = head_row[:, query_width : query_width + dim]
    for c in range(query_width + dim, head_row.shape[1], dim):
        key_sum += head_row[:, c : c + dim]
    both = jnp.concatenate([query_sum, key_sum], axis=1)
    gains = [
        jnp.concatenate([by_device(attn_sum, c), by_device(ffn_ref[...], c)], axis=1)
        for c in range(2)
    ]
    for ref, mine in ((gain_mine_ref, 0), (gain_away_ref, 1)):
        ref[...] = jnp.zeros_like(ref)
        ref[:, 0, :] = jnp.where(core == mine, gains[0], gains[1])
        ref[:, 1, :] = jnp.broadcast_to(both, (devices // 2, 2 * dim))
    gain_across = copy(gain_away_ref, gain_other_ref, (head, blk ^ 1), gc_send, gc_recv)
    gain_across.start()
    gain_across.wait()
    gain_sum_ref[...] = (gain_mine_ref[...] + gain_other_ref[...]).reshape(gain_sum_ref.shape)
    start_along(gain_sum_ref, gain_z_ref, gz_send, gz_recv)

    qkv_mine_ref[...] = finish_along(qkv_sum_ref, qkv_z_ref, z_send, z_recv).astype(jnp.bfloat16)
    start_around(qkv_mine_ref, qkv_got_ref, h_send, h_recv)
    gain_part_ref[...] = finish_along(gain_sum_ref, gain_z_ref, gz_send, gz_recv)
    start_around(gain_part_ref, gain_got_ref, gh_send, gh_recv)

    loads[5].wait()
    units = in_ref.shape[2] // 2
    for k in range(size):
        if k:
            in_sends[k - 1].wait_recv()
        for part in range(2):
            columns = pl.ds(pl.multiple_of((part * size + (head ^ k)) * units, units), units)
            piece = slice(part * units, (part + 1) * units)
            got = in_got_ref[k - 1, :, piece] if k else in_ref[head, :, piece]
            in_grad_ref[:, columns] = wide_of(got)

    for load in loads[6:]:
        load.wait()
    half = count // 2
    for part in range(2):
        here = slice(part * half, (part + 1) * half)
        layer_ref[here] = (
            residual_ref[here] + wide_of(rest_ref[here]) + wide_of(held[8 + part][...])
            + wide_of(held[10 + part][...])
        ).astype(jnp.bfloat16)

    finish_around(qkv_mine_ref, qkv_got_ref, h_send, h_recv)
    sums = [wide_of(qkv_got_ref[h]) for h in range(size)]
    key_end = query_width + (sums[0].shape[1] - query_width) // 2
    qkv_grad_ref[...] = jnp.concatenate(
        [total[:, :query_width] for total in sums]
        + [total[:, query_width:key_end] for total in sums]
        + [total[:, key_end:] for total in sums],
        axis=1,
    )

    finish_around(gain_part_ref, gain_got_ref, gh_send, gh_recv)
    gains_ref[...] = jnp.sum(gain_got_ref[...], axis=0)
    across.wait_send()
    for sent in in_sends:
        sent.wait_send()


def finish(
    sent, got, qkv_part, x, residual_grad, gain, ffn_sum, head_sum, weight, weights, in_part,
    residual, rest, terms, query_width, dim
):
    size, blk_size = lax.axis_size("heads"), lax.axis_size("blk")
    devices = size * blk_size
    pairs = blk_size // 2
    count, width = x.shape
    depth, joined = width // devices, sent.shape[1]
    units = in_part.shape[2]
    vmem = pl.BlockSpec(memory_space=pltpu.VMEM)
    anywhere = pl.BlockSpec(memory_space=pl.ANY)
    sems = pltpu.SemaphoreType.DMA
    low = jnp.bfloat16
    loaded = (weights, x, residual_grad)
    return pl.pallas_call(
        functools.partial(finish_kernel, query_width, dim),
        out_shape=[
            jax.ShapeDtypeStruct((count, width), jnp.float32),
            jax.ShapeDtypeStruct((depth, size * joined), jnp.float32),
            jax.ShapeDtypeStruct((8, 128), jnp.float32),
            jax.ShapeDtypeStruct((depth, size * units), jnp.float32),
            jax.ShapeDtypeStruct((count, width), low),
        ],
        in_specs=[vmem] * 5 + [anywhere] * 12,
        out_specs=[vmem] * 5,
        scratch_shapes=[pltpu.VMEM((width, joined), low)]
        + [pltpu.VMEM(array.shape, array.dtype) for array in loaded]
        + [pltpu.VMEM((count, joined), low), pltpu.VMEM(in_part.shape, low)]
        + [pltpu.VMEM((count, width), jnp.float32), pltpu.VMEM((count, width), low)]
        + [pltpu.VMEM((count // 2, width), low)] * 4
        + [
            pltpu.VMEM((size * pairs, depth, joined), low),
            pltpu.VMEM((size, pairs, depth, joined), low),
            pltpu.VMEM((pairs, size, depth, joined), low),
            pltpu.VMEM((size, depth, joined), low),
            pltpu.VMEM((size, depth, joined), low),
            pltpu.VMEM((devices // 2, 8, 128), jnp.float32),
            pltpu.VMEM((devices // 2, 8, 128), jnp.float32),
            pltpu.VMEM((devices // 2, 8, 128), jnp.float32),
            pltpu.VMEM((size, pairs, 8, 128), jnp.float32),
            pltpu.VMEM((pairs, size, 8, 128), jnp.float32),
            pltpu.VMEM((size, 8, 128), jnp.float32),
            pltpu.VMEM((size, 8, 128), jnp.float32),
            pltpu.VMEM((size - 1, depth, units), low),
            sems((12,)),
            sems,
            sems,
            sems((pairs,)),
            sems((pairs,)),
            sems((size - 1,)),
            sems((size,)),
            sems,
            sems,
            sems((pairs,)),
            sems((pairs,)),
            sems((size - 1,)),
            sems((size,)),
            sems((size - 1,)),
            sems((size - 1,)),
        ],
        compiler_params=pltpu.CompilerParams(
            collective_id=0, has_side_effects=True, vmem_limit_bytes=60 << 20
        ),
        name="finish",
    )(
        got, qkv_part.reshape(size * pairs, 2, depth, joined), gain, ffn_sum, head_sum,
        weight, *loaded, sent, in_part, residual, rest, *terms
    )


def permute(block, axis, k):
    return lax.ppermute(block, axis, [(i, i ^ k) for i in range(lax.axis_size(axis))])


def after(value, *done):
    return lax.optimization_barrier((value, *done))[0]


def pick(block, k, axis, dim):
    extent = block.shape[dim] // lax.axis_size(axis)
    return lax.dynamic_slice_in_dim(block, (lax.axis_index(axis) ^ k) * extent, extent, dim)


def wide(block):
    return block.astype(jnp.float32)


def local(
    inputs,
    positions,
    attn_gain,
    qkv_weight,
    q_gain,
    k_gain,
    out_weight,
    ffn_gain,
    ffn_in_weight,
    ffn_out_weight,
    cotangent,
):
    token_count, width = inputs.shape
    depth = qkv_weight.shape[0]
    head_dim = q_gain.shape[0]
    group_size = HEADS // KV_HEADS
    size = lax.axis_size("heads")
    blk_size = lax.axis_size("blk")
    query_all, key_all = HEADS * head_dim, KV_HEADS * head_dim
    query_width, key_width = query_all // size, key_all // size
    qkv_width = query_width + 2 * key_width
    block_len = token_count * size
    half = token_count // 2
    own = lax.axis_index("heads").astype(jnp.int32).reshape(1)

    qkv_parts = jnp.concatenate(
        [
            qkv_weight[:, :query_all].reshape(depth, size, query_width),
            qkv_weight[:, query_all : query_all + key_all].reshape(depth, size, key_width),
            qkv_weight[:, query_all + key_all :].reshape(depth, size, key_width),
            jnp.broadcast_to(attn_gain[:, None, None], (depth, size, 64)),
            jnp.broadcast_to(ffn_gain[:, None, None], (depth, size, 64)),
        ],
        axis=-1,
    ).transpose(1, 0, 2)
    out_group = lax.all_gather(out_weight, "blk", axis=0, tiled=True)
    in_rows = trade(ffn_in_weight)
    in_group = lax.all_gather(in_rows, "blk", axis=1, tiled=True).reshape(width, -1)

    inputs_blk, qkv_rows = begin(after(inputs, in_rows), qkv_parts)
    qkv_rows = qkv_rows.reshape(width, -1)
    cosine, sine = rotation(positions, head_dim)
    cosine = jnp.concatenate([cosine[:, 0], cosine[:, 0]], axis=-1)
    sine = jnp.concatenate([-sine[:, 0], sine[:, 0]], axis=-1)
    head_gain = jnp.concatenate(
        [jnp.tile(q_gain, HEADS // size), jnp.tile(k_gain, KV_HEADS // size)]
    ).astype(jnp.float32)[None, :]
    query_low, raw, normed, attn_scaling, ffn_scaling, out_peers, pair_all = project(
        inputs_blk, qkv_rows, head_gain, cosine, sine, out_group, size, query_width, 256
    )
    down_weight, pair_all = lax.optimization_barrier((ffn_out_weight, pair_all))
    down_group = lax.all_gather(down_weight, "blk", axis=0, tiled=True)
    query_rows, key_rows = token_count, 256
    low = block_len + jnp.arange(block_len, dtype=jnp.int32) - positions
    first = jnp.concatenate([low[::query_rows] // key_rows, own])
    low = low[None, :]
    attended_blk, logs = attend(query_low, pair_all, first, low, group_size, query_rows, key_rows)

    mine = jnp.concatenate([pick(attended_blk, k, "heads", 0) for k in range(size)], axis=0)
    late = after(cotangent, inputs_blk)
    one_top, two_bottom = permute(late[:half], "heads", 1), permute(late[half:], "heads", 2)
    mine, in_group = lax.optimization_barrier((mine, in_group))
    residual, ffn_normed, attended_own, one_bottom, two_top = join(
        inputs_blk, mine, out_group, out_peers, ffn_scaling, cotangent, 256
    )
    cot_near = (one_top, one_bottom, two_top, two_bottom)
    hidden, gate_grad, up_grad, in_sum, cot_far, qkv_peers = hidden_pass(
        ffn_normed, in_group, cotangent, cot_near, down_group, qkv_rows, qkv_width, 256
    )
    in_part = lax.psum_scatter(
        in_sum.reshape(size, blk_size * depth, -1), "blk", scatter_dimension=1, tiled=True
    )
    down_sum, one_far, two_far, one_near, two_near, out_rest, grad_sum = feed_tail(
        gate_grad, up_grad, hidden, in_group, down_group, (cotangent, *cot_near, cot_far)
    )
    through_top, through_bottom = permute(one_far, "heads", 1), permute(two_far, "heads", 2)
    residual_grad, ffn_sum, grads, *out_slices = residual_back(
        grad_sum, residual, cotangent, ffn_scaling, attended_own, out_group, out_peers,
        min(128, half)
    )
    down_sum, in_part, grads, through_top, through_bottom = lax.optimization_barrier(
        (down_sum, in_part, grads, through_top, through_bottom)
    )
    ffn_out_grad = wide(lax.psum_scatter(down_sum, "blk", scatter_dimension=0, tiled=True))
    top_send = (wide(out_rest[:half]) + wide(through_top)).astype(jnp.bfloat16)
    bottom_send = (wide(out_rest[half : 2 * half]) + wide(through_bottom)).astype(jnp.bfloat16)
    out_top_last = permute(top_send, "heads", 2)
    out_bottom_last = permute(bottom_send, "heads", 1)
    out_slices = [piece.reshape(-1, width) for piece in out_slices]
    out_slices = [out_slices[0]] + [permute(out_slices[k], "heads", k) for k in range(1, size)]
    query_grad, pair_sum, behind = attend_back(
        query_low, pair_all, first, low, grads, attended_blk, logs, group_size, query_rows, key_rows
    )
    pair_sum, out_top_last, out_bottom_last, *out_slices = lax.optimization_barrier(
        (pair_sum, out_top_last, out_bottom_last, *out_slices)
    )
    projected_grad, head_sum = project_back(
        query_grad, pair_sum, behind, raw, head_gain, cosine, sine, size, 256
    )
    out_top = permute(after(one_near, pair_sum), "heads", 1)
    out_bottom = permute(after(two_near, pair_sum), "heads", 2)
    qkv_part, got, out_grad = qkv_terms(normed, projected_grad, out_slices, 512)
    input_grad, qkv_grad, gains, ffn_in_grad, layer_out = finish(
        projected_grad, got, qkv_part, inputs, residual_grad, attn_scaling, ffn_sum, head_sum,
        qkv_rows, qkv_peers, in_part, residual, out_rest,
        (out_top, out_bottom, out_top_last, out_bottom_last), query_width, head_dim
    )
    return (
        layer_out,
        input_grad,
        gains[0, :depth],
        qkv_grad,
        gains[1, :head_dim],
        gains[1, head_dim : 2 * head_dim],
        out_grad,
        gains[0, 64 : 64 + depth],
        ffn_in_grad,
        ffn_out_grad,
    )


def solution(mesh):
    placed = (
        P(("blk", "heads"), None),
        P("blk"),
        P(("heads", "blk")),
        P(("heads", "blk"), None),
        P(),
        P(),
        P(("heads", "blk"), None),
        P(("heads", "blk")),
        P(("heads", "blk"), None),
        P(("heads", "blk"), None),
        P(("blk", "heads"), None),
    )
    return jax.shard_map(
        local,
        mesh=mesh,
        in_specs=placed,
        out_specs=(
            P(("blk", "heads"), None),
            P(("blk", "heads"), None),
            P(("heads", "blk")),
            P(("heads", "blk"), None),
            P(),
            P(),
            P(("heads", "blk"), None),
            P(("heads", "blk")),
            P(("heads", "blk"), None),
            P(("heads", "blk"), None),
        ),
        check_vma=False,
    )
```

```python
import functools

import jax
import jax.numpy as jnp
from jax import lax
from jax.experimental import pallas as pl
from jax.experimental.pallas import tpu as pltpu
from jax.sharding import PartitionSpec as P

HEADS = 16
KV_HEADS = 4


EPS = 1e-06
ROPE_BASE = 10000.0
NEG = -1e30
MESH = pl.DeviceIdType.MESH
ROWS_IN_BOTH = (((1,), (1,)), ((), ()))


def stack_heads(tile, heads, first):
    turned = tile.T
    dim = turned.shape[0] // heads
    wide = jnp.concatenate([turned[h * dim : (h + 1) * dim] for h in range(heads)], axis=1)
    zero = jnp.zeros_like(wide)
    return jnp.concatenate([wide, zero] if first else [zero, wide], axis=0)


def unstack_heads(wide, heads):
    count = wide.shape[1] // heads
    return jnp.concatenate([wide[:, h * count : (h + 1) * count] for h in range(heads)], axis=0).T


def scores_at(pair, query_ext, low, first_query, key_start, heads):
    scores = jnp.dot(pair, query_ext, preferred_element_type=jnp.float32)
    rows, columns = scores.shape
    shape = (rows, columns // heads)
    key = key_start + lax.broadcasted_iota(jnp.int32, shape, 0)
    query = first_query + lax.broadcasted_iota(jnp.int32, shape, 1)
    bias = jnp.where((key <= query) & (key >= low), 0.0, NEG)
    return scores + jnp.concatenate([bias] * heads, axis=1)


def transpose_into(pair_ref, turned_ref):
    for start in range(0, pair_ref.shape[0], 512):
        turned_ref[:, start : start + 512] = pair_ref[start : start + 512, :].T


def attend_kernel(
    heads, key_rows, scale, first_ref, query_ref, low_ref, pair_ref, out_ref, log_ref, turned_ref,
    mixed_ref, total_ref
):
    step = pl.program_id(0)
    query_rows = query_ref.shape[0]

    @pl.when(step == 0)
    def _():
        transpose_into(pair_ref, turned_ref)

    query_ext = stack_heads(query_ref[...] * jnp.bfloat16(scale), heads, True)
    low = low_ref[...]
    base = pair_ref.shape[0] // 2 + step * query_rows
    mixed_ref[...] = jnp.zeros_like(mixed_ref)
    total_ref[...] = jnp.zeros_like(total_ref)

    def tile(index, carried):
        start = pl.multiple_of(index * key_rows, key_rows)
        expo = jnp.exp(
            scores_at(pair_ref[pl.ds(start, key_rows), :], query_ext, low, base, start, heads)
        )
        total_ref[...] += jnp.sum(expo, axis=0, keepdims=True)
        mixed_ref[...] += jnp.dot(
            turned_ref[:, pl.ds(start, key_rows)],
            expo.astype(jnp.bfloat16),
            preferred_element_type=jnp.float32,
        )
        return carried

    lax.fori_loop(first_ref[step], (base + query_rows - 1) // key_rows + 1, tile, 0)
    total = total_ref[...]
    dim = pair_ref.shape[1] // 2
    out_ref[...] = unstack_heads(mixed_ref[dim:] / total, heads).astype(out_ref.dtype)
    log_ref[...] = jnp.log(total)[None]


def attend_back_kernel(
    heads, key_rows, scale, first_ref, query_ref, low_ref, pair_ref, out_ref, log_ref, *refs
):
    grads_ref, query_grad_ref, pair_grad_ref, behind_ref, turned_ref, sum_ref = refs
    step = pl.program_id(0)
    grad = grads_ref[first_ref[pl.num_programs(0)] ^ step]
    query_rows = query_ref.shape[0]
    dim = pair_ref.shape[1] // 2

    @pl.when(step == 0)
    def _():
        pair_grad_ref[...] = jnp.zeros_like(pair_grad_ref)
        transpose_into(pair_ref, turned_ref)

    query_ext = stack_heads(query_ref[...] * jnp.bfloat16(scale), heads, True)
    grad_ext = stack_heads(grad, heads, False)
    out_ext = stack_heads(out_ref[...], heads, False)
    inner = jnp.sum(
        grad_ext.astype(jnp.float32) * out_ext.astype(jnp.float32), axis=0, keepdims=True
    )
    log_sum = log_ref[0]
    low = low_ref[...]
    base = pair_ref.shape[0] // 2 + step * query_rows
    sum_ref[...] = jnp.zeros_like(sum_ref)

    def tile(index, carried):
        start = pl.multiple_of(index * key_rows, key_rows)
        pair = pair_ref[pl.ds(start, key_rows), :]
        probs = jnp.exp(scores_at(pair, query_ext, low, base, start, heads) - log_sum)
        probs_grad = jnp.dot(pair, grad_ext, preferred_element_type=jnp.float32)
        score_grad = (probs * (probs_grad - inner)).astype(jnp.bfloat16)
        sum_ref[...] += jnp.dot(
            turned_ref[:dim, pl.ds(start, key_rows)], score_grad, preferred_element_type=jnp.float32
        )
        pair_grad_ref[pl.ds(start, key_rows), :] += lax.dot_general(
            score_grad, query_ext, ROWS_IN_BOTH, preferred_element_type=jnp.float32
        ) + lax.dot_general(
            probs.astype(jnp.bfloat16), grad_ext, ROWS_IN_BOTH, preferred_element_type=jnp.float32
        )
        return carried

    lax.fori_loop(first_ref[step], (base + query_rows - 1) // key_rows + 1, tile, 0)
    query_grad_ref[...] = unstack_heads(sum_ref[...] * scale, heads).astype(query_grad_ref.dtype)

    @pl.when(step == pl.num_programs(0) - 1)
    def _():
        behind_ref[...] = pair_grad_ref[: behind_ref.shape[0]].astype(behind_ref.dtype)


def attention_specs(queries, pair, query_rows, heads):
    width = queries.shape[1]
    return (
        pl.BlockSpec((query_rows, width), lambda i, first: (i, 0)),
        pl.BlockSpec((1, query_rows), lambda i, first: (0, i)),
        pl.BlockSpec(pair.shape, lambda i, first: (0, 0)),
        pl.BlockSpec((1, 1, heads * query_rows), lambda i, first: (i, 0, 0)),
    )


def attend(queries, pair, first, low, heads, query_rows, key_rows):
    count, width = queries.shape
    tile, row, whole, logs = attention_specs(queries, pair, query_rows, heads)
    columns = heads * query_rows
    return pl.pallas_call(
        functools.partial(attend_kernel, heads, key_rows, (width // heads) ** -0.5),
        grid_spec=pltpu.PrefetchScalarGridSpec(
            num_scalar_prefetch=1,
            grid=(count // query_rows,),
            in_specs=[tile, row, whole],
            out_specs=[tile, logs],
            scratch_shapes=[
                pltpu.VMEM(pair.shape[::-1], jnp.bfloat16),
                pltpu.VMEM((pair.shape[1], columns), jnp.float32),
                pltpu.VMEM((1, columns), jnp.float32),
            ],
        ),
        out_shape=[
            jax.ShapeDtypeStruct((count, width), jnp.bfloat16),
            jax.ShapeDtypeStruct((count // query_rows, 1, columns), jnp.float32),
        ],
        compiler_params=pltpu.CompilerParams(vmem_limit_bytes=60 << 20),
        cost_estimate=pl.CostEstimate(
            flops=20_000_000_000, bytes_accessed=8_000_000, transcendentals=0
        ),
        name="attend",
    )(first, queries, low, pair)


def attend_back(queries, pair, first, low, grads, out, logs, heads, query_rows, key_rows):
    count, width = queries.shape
    tile, row, whole, log_spec = attention_specs(queries, pair, query_rows, heads)
    columns = heads * query_rows
    behind = (pair.shape[0] // 2, pair.shape[1])
    return pl.pallas_call(
        functools.partial(attend_back_kernel, heads, key_rows, (width // heads) ** -0.5),
        grid_spec=pltpu.PrefetchScalarGridSpec(
            num_scalar_prefetch=1,
            grid=(count // query_rows,),
            in_specs=[tile, row, whole, tile, log_spec]
            + [pl.BlockSpec(grads.shape, lambda i, first: (0, 0, 0))],
            out_specs=[tile, whole, pl.BlockSpec(behind, lambda i, first: (0, 0))],
            scratch_shapes=[
                pltpu.VMEM(pair.shape[::-1], jnp.bfloat16),
                pltpu.VMEM((pair.shape[1] // 2, columns), jnp.float32),
            ],
        ),
        out_shape=[
            jax.ShapeDtypeStruct((count, width), jnp.bfloat16),
            jax.ShapeDtypeStruct(pair.shape, jnp.float32),
            jax.ShapeDtypeStruct(behind, jnp.bfloat16),
        ],
        compiler_params=pltpu.CompilerParams(vmem_limit_bytes=60 << 20),
        cost_estimate=pl.CostEstimate(
            flops=40_000_000_000, bytes_accessed=12_000_000, transcendentals=0
        ),
        name="attend_back",
    )(first, queries, low, pair, out, logs, grads)


def heads_apart(wide, dim):
    rows = wide.shape[0]
    return jnp.concatenate(
        [
            jnp.broadcast_to(
                jnp.mean(jnp.square(wide[:, c : c + dim]), axis=-1, keepdims=True), (rows, dim)
            )
            for c in range(0, wide.shape[1], dim)
        ],
        axis=1,
    )


def spread_mean(wide, dim):
    rows = wide.shape[0]
    return jnp.concatenate(
        [
            jnp.broadcast_to(jnp.mean(wide[:, c : c + dim], axis=-1, keepdims=True), (rows, dim))
            for c in range(0, wide.shape[1], dim)
        ],
        axis=1,
    )


def turn(wide, cosine, sine, dim):
    count = wide.shape[1] // dim
    half = dim // 2
    swapped = jnp.concatenate(
        [
            wide[:, c + shift : c + shift + half]
            for c in range(0, wide.shape[1], dim)
            for shift in (half, 0)
        ],
        axis=1,
    )
    return wide * jnp.concatenate([cosine] * count, axis=1) + swapped * jnp.concatenate(
        [sine] * count, axis=1
    )


def project_kernel(
    dim, size, x_ref, weight_ref, head_gain_ref, cosine_ref, sine_ref, side_ref, query_ref, raw_ref,
    normed_ref, gain_ref, ffn_gain_ref, spread_ref, pair_ref, pair_held, send_sem, recv_sem,
    pair_sem, pair_send, pair_recv
):
    columns = raw_ref.shape[1]
    step, steps = pl.program_id(0), pl.num_programs(0)
    marks = (0, steps // 2, steps - 2)
    head, blk = lax.axis_index("heads"), lax.axis_index("blk")
    last = lax.axis_size("blk") - 1
    rows, block = x_ref.shape[0], pair_held.shape[0]
    tiles = block // size // rows

    @pl.when(step == 0)
    def _():
        barrier = pltpu.get_barrier_semaphore()
        for place in ((head ^ 1, blk), (head ^ 2, blk), (head, blk ^ 1)):
            pl.semaphore_signal(barrier, inc=1, device_id=place, device_id_type=MESH)

        @pl.when(blk > 0)
        def _():
            pl.semaphore_signal(barrier, inc=1, device_id=(head, blk - 1), device_id_type=MESH)

        @pl.when(blk < last)
        def _():
            pl.semaphore_wait(barrier, 4)

        @pl.when(blk == last)
        def _():
            pl.semaphore_wait(barrier, 3)

    end = spread_job(step, marks, side_ref, spread_ref, send_sem, recv_sem, False)

    def chunk_rows(k, first):
        return pl.ds(
            pl.multiple_of(first + (head ^ k) * (block // size), block // size), block // size
        )

    def keep(k):
        return pltpu.make_async_copy(
            pair_held.at[chunk_rows(k, 0)], pair_ref.at[chunk_rows(k, block)], pair_sem.at[k]
        )

    def pass_on(k):
        return pltpu.make_async_remote_copy(
            src_ref=pair_held.at[chunk_rows(k, 0)],
            dst_ref=pair_ref.at[chunk_rows(k, 0)],
            send_sem=pair_send.at[k],
            recv_sem=pair_recv.at[k],
            device_id=(head, jnp.minimum(blk + 1, last)),
            device_id_type=MESH,
        )

    @pl.when(pl.program_id(0) == 0)
    def _():
        gains = weight_ref[:, columns:].T.astype(jnp.float32)
        gain_ref[...] = gains[:1]
        ffn_gain_ref[...] = gains[64:65]

    values = x_ref[...].astype(jnp.float32)
    normed = values * lax.rsqrt(jnp.mean(values * values, axis=-1, keepdims=True) + EPS)
    normed = (normed * gain_ref[...]).astype(jnp.bfloat16)
    normed_ref[...] = normed
    raw = jnp.dot(normed, weight_ref[:, :columns], preferred_element_type=jnp.float32)
    raw_ref[...] = raw
    turned_width = raw.shape[1] - pair_held.shape[1] // 2
    heads = raw[:, :turned_width]
    heads = heads * lax.rsqrt(heads_apart(heads, dim) + EPS) * head_gain_ref[...]
    heads = turn(heads, cosine_ref[...], sine_ref[...], dim).astype(jnp.bfloat16)
    query_width = query_ref.shape[1]
    query_ref[...] = heads[:, :query_width]
    place = ((head ^ (step // tiles)) * tiles + lax.rem(step, tiles)) * rows
    pair_held[pl.ds(pl.multiple_of(place, rows), rows)] = jnp.concatenate(
        [heads[:, query_width:], raw[:, turned_width:].astype(jnp.bfloat16)], axis=1
    )
    for k in range(size):

        @pl.when(step == (k + 1) * tiles - 1)
        def _(k=k):
            keep(k).start()

            @pl.when(blk < last)
            def _():
                pass_on(k).start()

    @pl.when(step == steps - 1)
    def _():
        end()
        for k in range(size):
            keep(k).wait()

        @pl.when(blk < last)
        def _():
            for k in range(size):
                pass_on(k).wait_send()

        @pl.when(blk > 0)
        def _():
            for k in range(size):
                pass_on(k).wait_recv()


def project(x, weight, head_gain, cosine, sine, side, size, query_width, rows):
    count, width = x.shape
    out_width = weight.shape[1] - 128
    pair_width = out_width - query_width
    dim = cosine.shape[1]
    tiles = count // size // rows

    def apart(i):
        return ((lax.axis_index("heads") ^ (i // tiles)) * tiles + i % tiles, 0)

    def there(i):
        return (i, 0)

    def whole(i):
        return (0, 0)

    anywhere = pl.BlockSpec(memory_space=pl.ANY)

    return pl.pallas_call(
        functools.partial(project_kernel, dim, size),
        grid=(count // rows,),
        in_specs=[
            pl.BlockSpec((rows, width), there),
            pl.BlockSpec(weight.shape, whole),
            pl.BlockSpec(head_gain.shape, whole),
            pl.BlockSpec((rows, dim), apart),
            pl.BlockSpec((rows, dim), apart),
            anywhere,
        ],
        out_specs=[
            pl.BlockSpec((rows, query_width), apart),
            pl.BlockSpec((rows, out_width), apart),
            pl.BlockSpec((rows, width), there),
            pl.BlockSpec((1, width), whole),
            pl.BlockSpec((1, width), whole),
            anywhere,
            anywhere,
        ],
        out_shape=[
            jax.ShapeDtypeStruct((count, query_width), jnp.bfloat16),
            jax.ShapeDtypeStruct((count, out_width), jnp.float32),
            jax.ShapeDtypeStruct((count, width), jnp.bfloat16),
            jax.ShapeDtypeStruct((1, width), jnp.float32),
            jax.ShapeDtypeStruct((1, width), jnp.float32),
            jax.ShapeDtypeStruct((3, *side.shape), side.dtype),
            jax.ShapeDtypeStruct((2 * count, pair_width), jnp.bfloat16),
        ],
        scratch_shapes=[pltpu.VMEM((count, pair_width), jnp.bfloat16)]
        + [pltpu.SemaphoreType.DMA((SPREAD_COUNT,))] * 2
        + [pltpu.SemaphoreType.DMA((size,))] * 3,
        compiler_params=pltpu.CompilerParams(
            collective_id=5, has_side_effects=True, vmem_limit_bytes=60 << 20
        ),
        cost_estimate=pl.CostEstimate(
            flops=4 * count * width * out_width, bytes_accessed=30_000_000, transcendentals=0
        ),
        name="project",
    )(x, weight, head_gain, cosine, sine, side)


def project_back_kernel(
    dim, size, query_grad_ref, pair_grad_ref, raw_ref, head_gain_ref, cosine_ref, sine_ref,
    behind_ref, grad_ref, gain_grad_ref, returned_ref, send_sem, recv_sem
):
    step = pl.program_id(0)
    head, blk = lax.axis_index("heads"), lax.axis_index("blk")
    last = lax.axis_size("blk") - 1
    rows = raw_ref.shape[0]
    tiles = returned_ref.shape[0] // size // rows
    back = pltpu.make_async_remote_copy(
        src_ref=behind_ref,
        dst_ref=returned_ref,
        send_sem=send_sem,
        recv_sem=recv_sem,
        device_id=(head, jnp.maximum(blk - 1, 0)),
        device_id_type=MESH,
    )

    @pl.when(step == 0)
    def _():
        barrier = pltpu.get_barrier_semaphore()

        @pl.when(blk < last)
        def _():
            pl.semaphore_signal(
                barrier, inc=1, device_id=(head, blk + 1), device_id_type=MESH
            )

        @pl.when(blk > 0)
        def _():
            pl.semaphore_wait(barrier, 1)
            back.start()

        @pl.when(blk == last)
        def _():
            returned_ref[...] = jnp.zeros_like(returned_ref)

        @pl.when(blk < last)
        def _():
            back.wait_recv()

        gain_grad_ref[...] = jnp.zeros_like(gain_grad_ref)

    place = ((head ^ (step // tiles)) * tiles + lax.rem(step, tiles)) * rows
    returned = returned_ref[pl.ds(pl.multiple_of(place, rows), rows)]
    pair_grad = pair_grad_ref[...] + returned.astype(jnp.float32)
    pair_grad = pair_grad.astype(jnp.bfloat16)
    half = pair_grad.shape[1] // 2
    grads = jnp.concatenate([query_grad_ref[...], pair_grad[:, :half]], axis=1).astype(jnp.float32)
    grads = turn(grads, cosine_ref[...], -sine_ref[...], dim)
    values = raw_ref[:, : grads.shape[1]]
    inverse = lax.rsqrt(heads_apart(values, dim) + EPS)
    gain_grad_ref[...] += jnp.sum(grads * values * inverse, axis=0, keepdims=True)
    scaled = grads * head_gain_ref[...]
    moment = spread_mean(scaled * values, dim)
    values_grad = inverse * scaled - values * inverse * inverse * inverse * moment
    grad_ref[...] = jnp.concatenate([values_grad.astype(jnp.bfloat16), pair_grad[:, half:]], axis=1)

    @pl.when((step == pl.num_programs(0) - 1) & (blk > 0))
    def _():
        back.wait_send()


def project_back(query_grad, pair_sum, behind, raw, head_gain, cosine, sine, size, rows):
    count, query_width = query_grad.shape
    pair_width = pair_sum.shape[1]
    out_width = raw.shape[1]
    dim = cosine.shape[1]
    tiles = count // size // rows

    def apart(i):
        return ((lax.axis_index("heads") ^ (i // tiles)) * tiles + i % tiles, 0)

    def after_behind(i):
        return (apart(i)[0] + count // rows, 0)

    def whole(i):
        return (0, 0)

    return pl.pallas_call(
        functools.partial(project_back_kernel, dim, size),
        grid=(count // rows,),
        in_specs=[
            pl.BlockSpec((rows, query_width), apart),
            pl.BlockSpec((rows, pair_width), after_behind),
            pl.BlockSpec((rows, out_width), apart),
            pl.BlockSpec(head_gain.shape, whole),
            pl.BlockSpec((rows, dim), apart),
            pl.BlockSpec((rows, dim), apart),
            pl.BlockSpec(memory_space=pl.ANY),
        ],
        out_specs=[
            pl.BlockSpec((rows, out_width), lambda i: (i, 0)),
            pl.BlockSpec(head_gain.shape, whole),
        ],
        scratch_shapes=[
            pltpu.VMEM(behind.shape, behind.dtype),
            pltpu.SemaphoreType.DMA,
            pltpu.SemaphoreType.DMA,
        ],
        out_shape=[
            jax.ShapeDtypeStruct((count, out_width), jnp.bfloat16),
            jax.ShapeDtypeStruct(head_gain.shape, jnp.float32),
        ],
        compiler_params=pltpu.CompilerParams(
            collective_id=9, has_side_effects=True, vmem_limit_bytes=60 << 20
        ),
        cost_estimate=pl.CostEstimate(
            flops=8_000_000_000, bytes_accessed=8_000_000, transcendentals=0
        ),
        name="project_back",
    )(query_grad, pair_sum, raw, head_gain, cosine, sine, behind)


def join_kernel(
    x_ref, weight_ref, weights_ref, gain_ref, mine_ref, cot_ref, residual_ref,
    normed_ref, attended_ref, cot_one_ref, cot_two_ref, held_ref, local_sem, send_sem, recv_sem
):
    step = pl.program_id(0)
    head, blk = lax.axis_index("heads"), lax.axis_index("blk")
    rows = x_ref.shape[0]
    count = held_ref.shape[1] // 4
    tiles = count // rows

    def copy(source, target, k, index):
        return pltpu.make_async_remote_copy(
            src_ref=source,
            dst_ref=target,
            send_sem=send_sem.at[index],
            recv_sem=recv_sem.at[index],
            device_id=(head ^ k, blk),
            device_id_type=MESH,
        )

    upper, lower = pl.ds(0, 2 * count), pl.ds(2 * count, 2 * count)
    near = [copy(mine_ref, held_ref.at[k], k, k - 1) for k in (1, 2)]
    far = [
        copy(held_ref.at[1, upper], held_ref.at[3, upper], 2, 2),
        copy(held_ref.at[2, lower], held_ref.at[3, lower], 1, 3),
    ]
    half = count // 2
    cot_near = [
        copy(cot_ref.at[pl.ds(half, half)], cot_one_ref, 1, 4),
        copy(cot_ref.at[pl.ds(0, half)], cot_two_ref, 2, 5),
    ]
    own = pltpu.make_async_copy(mine_ref, held_ref.at[0], local_sem)

    @pl.when(step == 0)
    def _():
        own.start()
        greet_near(False)
        for first in near:
            first.start()
        for first, second in zip(near, far):
            first.wait_recv()
            second.start()
        own.wait()
        for second in far:
            second.wait_recv()
        for last in cot_near:
            last.start()

    chunk = step // tiles
    parts = []
    total = x_ref[...].astype(jnp.float32)
    for k in range(4):
        start = ((chunk ^ k) * tiles + lax.rem(step, tiles)) * rows
        part = held_ref[k, pl.ds(pl.multiple_of(start, rows), rows)]
        weight = weight_ref[...] if k == 0 else weights_ref[k - 1]
        total += jnp.dot(part, weight, preferred_element_type=jnp.float32)
        parts.append(part)
    residual_ref[...] = total
    normed = total * lax.rsqrt(jnp.mean(total * total, axis=-1, keepdims=True) + EPS)
    normed_ref[...] = (normed * gain_ref[...]).astype(jnp.bfloat16)

    @pl.when(chunk == 0)
    def _():
        attended_ref[...] = jnp.concatenate(parts, axis=1)

    @pl.when(step == pl.num_programs(0) - 1)
    def _():
        for first in near + far:
            first.wait_send()
        for last in cot_near:
            last.wait()


def join(x, mine, weight, weights, gain, cot, rows):
    count, width = x.shape
    tokens = count // 4
    columns = mine.shape[1]
    tiles = tokens // rows
    anywhere = pl.BlockSpec(memory_space=pl.ANY)

    def there(i):
        return (i, 0)

    def whole(i):
        return (0, 0)

    sems = pltpu.SemaphoreType.DMA
    return pl.pallas_call(
        join_kernel,
        grid=(count // rows,),
        in_specs=[
            pl.BlockSpec((rows, width), there),
            pl.BlockSpec(weight.shape, whole),
            pl.BlockSpec(weights.shape, lambda i: (0, 0, 0)),
            pl.BlockSpec((1, width), whole),
            anywhere,
            anywhere,
        ],
        out_specs=[
            pl.BlockSpec((rows, width), there),
            pl.BlockSpec((rows, width), there),
            pl.BlockSpec((rows, 4 * columns), lambda i: (jnp.minimum(i, tiles - 1), 0)),
            anywhere,
            anywhere,
        ],
        out_shape=[
            jax.ShapeDtypeStruct((count, width), jnp.float32),
            jax.ShapeDtypeStruct((count, width), jnp.bfloat16),
            jax.ShapeDtypeStruct((tokens, 4 * columns), jnp.bfloat16),
            jax.ShapeDtypeStruct((tokens // 2, width), jnp.bfloat16),
            jax.ShapeDtypeStruct((tokens // 2, width), jnp.bfloat16),
        ],
        scratch_shapes=[
            pltpu.VMEM((4, count, columns), jnp.bfloat16),
            sems,
            sems((6,)),
            sems((6,)),
        ],
        compiler_params=pltpu.CompilerParams(
            collective_id=6, has_side_effects=True, vmem_limit_bytes=60 << 20
        ),
        cost_estimate=pl.CostEstimate(
            flops=16 * count * width * columns, bytes_accessed=50_000_000, transcendentals=0
        ),
        name="join",
    )(x, weight, weights, gain, mine, cot)


def trade_kernel(in_ref, out_ref, send_sem, recv_sem):
    head, blk = lax.axis_index("heads"), lax.axis_index("blk")
    size = lax.axis_size("heads")
    units = out_ref.shape[2] // 2
    barrier = pltpu.get_barrier_semaphore()
    for k in range(1, size):
        pl.semaphore_signal(barrier, inc=1, device_id=(head ^ k, blk), device_id_type=MESH)
    pl.semaphore_wait(barrier, size - 1)

    def columns(part, owner):
        return pl.ds(pl.multiple_of((part * size + owner) * units, units), units)

    copies = [
        pltpu.make_async_remote_copy(
            src_ref=in_ref.at[:, columns(part, head ^ k)],
            dst_ref=out_ref.at[head, :, pl.ds(part * units, units)],
            send_sem=send_sem.at[2 * k - 2 + part],
            recv_sem=recv_sem.at[2 * k - 2 + part],
            device_id=(head ^ k, blk),
            device_id_type=MESH,
        )
        for k in range(1, size)
        for part in range(2)
    ]
    for copy in copies:
        copy.start()
    for part in range(2):
        out_ref[head, :, part * units : (part + 1) * units] = in_ref[:, columns(part, head)]
    for copy in copies:
        copy.wait()


def trade(weight):
    size = lax.axis_size("heads")
    depth, width = weight.shape
    vmem = pl.BlockSpec(memory_space=pltpu.VMEM)
    return pl.pallas_call(
        trade_kernel,
        out_shape=jax.ShapeDtypeStruct((size, depth, width // size), weight.dtype),
        in_specs=[vmem],
        out_specs=vmem,
        scratch_shapes=[pltpu.SemaphoreType.DMA((2 * size - 2,))] * 2,
        compiler_params=pltpu.CompilerParams(
            collective_id=8, has_side_effects=True, vmem_limit_bytes=60 << 20
        ),
        name="trade",
    )(weight)


def begin_kernel(
    x_ref, qkv_ref, cot_ref, position_ref, frequency_ref, x_out, qkv_out, cot_top, cot_bottom,
    cosine_ref, sine_ref, held_ref, local_sem, x_send, x_recv, q_send, q_recv, b_send, b_recv, c_send,
    c_recv
):
    head, blk = lax.axis_index("heads"), lax.axis_index("blk")
    size, blk_size = lax.axis_size("heads"), lax.axis_size("blk")
    pairs = blk_size // 2
    count, depth = x_ref.shape[0], qkv_ref.shape[1]
    half = count // 2
    barrier = pltpu.get_barrier_semaphore()
    for k in range(1, size):
        pl.semaphore_signal(barrier, inc=1, device_id=(head ^ k, blk), device_id_type=MESH)
    pl.semaphore_signal(barrier, inc=1, device_id=(head, blk ^ 1), device_id_type=MESH)

    def same_core(k):
        return lax.rem(blk + 2 * k, blk_size)

    def greet(k, carried):
        pl.semaphore_signal(barrier, inc=1, device_id=(head, same_core(k)), device_id_type=MESH)
        return carried

    lax.fori_loop(1, pairs, greet, 0)
    pl.semaphore_wait(barrier, size + pairs - 1)

    def send(source, target, k, send_sem, recv_sem):
        return pltpu.make_async_remote_copy(
            src_ref=source,
            dst_ref=target,
            send_sem=send_sem,
            recv_sem=recv_sem,
            device_id=(head ^ k, blk),
            device_id_type=MESH,
        )

    def rows_of(index):
        return pl.ds(pl.multiple_of(index * depth, depth), depth)

    rows = rows_of(blk)
    qkv_copies = [
        send(
            qkv_ref.at[head ^ k], qkv_out.at[head, rows], k, q_send.at[k - 1], q_recv.at[k - 1]
        )
        for k in range(1, size)
    ]
    near = [
        send(x_ref, x_out.at[pl.ds(k * count, count)], k, x_send.at[k - 1], x_recv.at[k - 1])
        for k in (1, 2)
    ]
    far = [
        send(
            x_out.at[pl.ds(count, half)],
            x_out.at[pl.ds(3 * count, half)],
            2,
            x_send.at[2],
            x_recv.at[2],
        ),
        send(
            x_out.at[pl.ds(2 * count + half, half)],
            x_out.at[pl.ds(3 * count + half, half)],
            1,
            x_send.at[3],
            x_recv.at[3],
        ),
    ]
    own = [
        pltpu.make_async_copy(qkv_ref.at[head], qkv_out.at[head, rows], local_sem.at[0]),
        pltpu.make_async_copy(x_ref, held_ref.at[0], local_sem.at[1]),
        pltpu.make_async_copy(cot_ref, held_ref.at[1], local_sem.at[2]),
    ]
    laid = [
        pltpu.make_async_copy(held_ref.at[0], x_out.at[pl.ds(0, count)], local_sem.at[3]),
        pltpu.make_async_copy(held_ref.at[1, pl.ds(0, half)], cot_top, local_sem.at[4]),
        pltpu.make_async_copy(held_ref.at[1, pl.ds(half, half)], cot_bottom, local_sem.at[5]),
    ]
    for copy in qkv_copies + near + own:
        copy.start()

    def along(k, source):
        return pltpu.make_async_remote_copy(
            src_ref=qkv_out.at[:, rows],
            dst_ref=qkv_out.at[:, rows_of(source)],
            send_sem=b_send.at[k],
            recv_sem=b_recv.at[k],
            device_id=(head, same_core(k)),
            device_id_type=MESH,
        )

    def behind(k):
        return lax.rem(blk + blk_size - 2 * k, blk_size)

    def across(k, core):
        source = behind(k) ^ core
        return pltpu.make_async_remote_copy(
            src_ref=qkv_out.at[:, rows_of(behind(k))],
            dst_ref=qkv_out.at[:, rows_of(source)],
            send_sem=c_send.at[k],
            recv_sem=c_recv.at[k],
            device_id=(head, blk ^ 1),
            device_id_type=MESH,
        )

    def start(k, carried):
        along(k, blk).start()
        return carried

    def pass_on(k, carried):
        along(k, behind(k)).wait_recv()
        across(k, 0).start()
        return carried

    def finish(k, carried):
        across(k, 0).wait_send()
        across(k, 1).wait_recv()
        return carried

    def sent(k, carried):
        along(k, blk).wait_send()
        return carried

    own[0].wait()
    for copy in qkv_copies:
        copy.wait_recv()
    lax.fori_loop(1, pairs, start, 0)
    across(0, 0).start()
    for copy in own[1:]:
        copy.wait()
    for copy in laid:
        copy.start()

    lanes = 512

    def table(index, carried):
        here = pl.ds(pl.multiple_of(index * lanes, lanes), lanes)
        angle = frequency_ref[...] * position_ref[:, here].astype(jnp.float32)
        cosine, sine = jnp.cos(angle).T, jnp.sin(angle).T
        cosine_ref[here] = jnp.concatenate([cosine, cosine], axis=1)
        sine_ref[here] = jnp.concatenate([-sine, sine], axis=1)
        return carried

    lax.fori_loop(0, position_ref.shape[1] // lanes, table, 0)
    lax.fori_loop(1, pairs, pass_on, 0)
    for first, second in zip(near, far):
        first.wait_recv()
        second.start()
    for copy in qkv_copies + near:
        copy.wait_send()
    for copy in far:
        copy.wait()
    for copy in laid:
        copy.wait()
    lax.fori_loop(1, pairs, sent, 0)
    lax.fori_loop(0, pairs, finish, 0)


def begin(x, qkv_parts, cot, positions, frequency):
    size, blk_size = lax.axis_size("heads"), lax.axis_size("blk")
    count, width = x.shape
    depth, joined = qkv_parts.shape[1:]
    anywhere = pl.BlockSpec(memory_space=pl.ANY)
    vmem = pl.BlockSpec(memory_space=pltpu.VMEM)
    table = jax.ShapeDtypeStruct((positions.shape[1], 2 * frequency.shape[0]), jnp.float32)
    sems = pltpu.SemaphoreType.DMA
    return pl.pallas_call(
        begin_kernel,
        out_shape=[
            jax.ShapeDtypeStruct((size * count, width), x.dtype),
            jax.ShapeDtypeStruct((size, blk_size * depth, joined), x.dtype),
            jax.ShapeDtypeStruct((count // 2, width), x.dtype),
            jax.ShapeDtypeStruct((count // 2, width), x.dtype),
            table,
            table,
        ],
        in_specs=[anywhere] * 3 + [vmem] * 2,
        out_specs=[anywhere] * 4 + [vmem] * 2,
        scratch_shapes=[
            pltpu.VMEM((2, count, width), x.dtype),
            sems((6,)),
            sems((4,)),
            sems((4,)),
            sems((size - 1,)),
            sems((size - 1,)),
            sems((blk_size // 2,)),
            sems((blk_size // 2,)),
            sems((blk_size // 2,)),
            sems((blk_size // 2,)),
        ],
        compiler_params=pltpu.CompilerParams(
            collective_id=1, has_side_effects=True, vmem_limit_bytes=60 << 20
        ),
        name="begin",
    )(x, qkv_parts, cot, positions, frequency)


def spread_copies(source_ref, target_ref, send_sem, recv_sem):
    head, blk = lax.axis_index("heads"), lax.axis_index("blk")
    rows = source_ref.shape[0] // 2
    quarter = rows // 2
    start = pl.multiple_of(lax.rem(blk, 2) * rows, rows)
    half = pl.ds(start, rows)
    first = source_ref.at[half, pl.ds(0, target_ref.shape[2])]
    count = [0]

    def copy(source, target, place):
        index = count[0]
        count[0] += 1
        return pltpu.make_async_remote_copy(
            src_ref=source,
            dst_ref=target,
            send_sem=send_sem.at[index],
            recv_sem=recv_sem.at[index],
            device_id=place,
            device_id_type=MESH,
        )

    near = [
        copy(first, target_ref.at[k - 1, half], (head ^ k, blk)) for k in (1, 2)
    ]
    upper = pl.ds(start, quarter)
    lower = pl.ds(pl.multiple_of(start + quarter, quarter), quarter)
    far = [
        copy(target_ref.at[0, upper], target_ref.at[2, upper], (head ^ 2, blk)),
        copy(target_ref.at[1, lower], target_ref.at[2, lower], (head ^ 1, blk)),
    ]
    other = [
        copy(target_ref.at[k, half], target_ref.at[k, half], (head, blk ^ 1)) for k in range(3)
    ]
    return near, far, other


def greet_near(partner):
    head, blk = lax.axis_index("heads"), lax.axis_index("blk")
    barrier = pltpu.get_barrier_semaphore()
    places = [(head ^ 1, blk), (head ^ 2, blk)] + ([(head, blk ^ 1)] if partner else [])
    for place in places:
        pl.semaphore_signal(barrier, inc=1, device_id=place, device_id_type=MESH)
    pl.semaphore_wait(barrier, len(places))


def spread_job(step, marks, source_ref, target_ref, send_sem, recv_sem, greet=True):
    near, far, other = spread_copies(source_ref, target_ref, send_sem, recv_sem)
    begin_at, far_at, other_at = marks

    @pl.when(step == begin_at)
    def _():
        if greet:
            greet_near(True)
        for copy in near:
            copy.start()

    @pl.when(step == far_at)
    def _():
        for k in range(2):
            near[k].wait_recv()
            far[k].start()
            other[k].start()

    @pl.when(step == other_at)
    def _():
        for copy in far:
            copy.wait_recv()
        other[2].start()

    def end():
        for copy in near + far:
            copy.wait_send()
        for copy in other:
            copy.wait()

    return end


SPREAD_COUNT = 7


def hidden_kernel(
    tiles, normed_ref, gate_ref, up_ref, down_ref, turned_ref, side_ref, cot_ref, one_top_ref,
    one_bottom_ref, two_top_ref, two_bottom_ref, hidden_ref, gate_grad_ref, up_grad_ref, in_sum_ref,
    cot_far_ref, spread_ref, held_ref, grads_ref, load_sem, far_send, far_recv, send_sem, recv_sem
):
    step, steps = pl.program_id(0), pl.num_programs(0)
    head, blk = lax.axis_index("heads"), lax.axis_index("blk")
    count = cot_ref.shape[0]
    half = count // 2
    rows, units = hidden_ref.shape
    far = [
        pltpu.make_async_remote_copy(
            src_ref=ref,
            dst_ref=held_ref.at[pl.ds(3 * count + part * half, half)],
            send_sem=far_send.at[part],
            recv_sem=far_recv.at[part],
            device_id=(head ^ k, blk),
            device_id_type=MESH,
        )
        for part, (ref, k) in enumerate(((one_top_ref, 2), (two_bottom_ref, 1)))
    ]
    keep = pltpu.make_async_copy(
        held_ref.at[pl.ds(3 * count, count)], cot_far_ref, load_sem.at[5]
    )
    near = ((one_top_ref, 2), (one_bottom_ref, 3), (two_top_ref, 4), (two_bottom_ref, 5))
    loads = [pltpu.make_async_copy(cot_ref, held_ref.at[pl.ds(0, count)], load_sem.at[0])] + [
        pltpu.make_async_copy(ref, held_ref.at[pl.ds(half * place, half)], load_sem.at[place - 1])
        for ref, place in near
    ]

    @pl.when(step == 0)
    def _():
        for load in loads:
            load.start()
        greet_near(True)
        for copy in far:
            copy.start()
        for load in loads:
            load.wait()

    @pl.when(step == tiles)
    def _():
        for copy in far:
            copy.wait()
        keep.start()

    marks = (tiles, 2 * tiles, 2 * tiles + 4)
    end = spread_job(step, marks, side_ref, spread_ref, send_sem, recv_sem, False)

    @pl.when(step < 2 * tiles)
    def _():
        here = pl.ds(pl.multiple_of(step // tiles * rows, rows), rows)
        normed = normed_ref[...]
        gate = jnp.dot(normed, gate_ref[...], preferred_element_type=jnp.float32)
        upward = jnp.dot(normed, up_ref[...], preferred_element_type=jnp.float32)
        grad = lax.dot_general(
            held_ref[here], down_ref[...], ROWS_IN_BOTH, preferred_element_type=jnp.float32
        )
        sigmoid = jax.nn.sigmoid(gate)
        activated = gate * sigmoid
        hidden_ref[...] = (activated * upward).astype(jnp.bfloat16)
        gate_grad = (grad * upward * sigmoid * (1.0 + gate * (1.0 - sigmoid))).astype(jnp.bfloat16)
        up_grad = (grad * activated).astype(jnp.bfloat16)
        gate_grad_ref[...] = gate_grad
        up_grad_ref[...] = up_grad
        for part, value in enumerate((gate_grad, up_grad)):
            place = (part * tiles + lax.rem(step, tiles)) * units
            grads_ref[here, pl.ds(pl.multiple_of(place, units), units)] = value

    @pl.when(step >= 2 * tiles)
    def _():
        in_sum_ref[...] = lax.dot_general(
            turned_ref[...],
            grads_ref[...],
            (((0,), (0,)), ((), ())),
            preferred_element_type=jnp.float32,
        ).astype(jnp.bfloat16)

    @pl.when(step == steps - 1)
    def _():
        end()
        keep.wait()


def hidden_pass(normed, weight, cot, cot_near, down, side, side_columns, units):
    count, width = normed.shape
    total = down.shape[0]
    tiles = total // units
    rows = count // 2
    columns = width // 8

    def row(s):
        return jnp.minimum(s // tiles, 1)

    def column(s):
        return jnp.where(s < 2 * tiles, lax.rem(s, tiles), tiles - 1)

    out_spec = pl.BlockSpec((rows, units), lambda s: (row(s), column(s)))
    out_shape = jax.ShapeDtypeStruct((count, total), jnp.bfloat16)
    anywhere = pl.BlockSpec(memory_space=pl.ANY)
    sems = pltpu.SemaphoreType.DMA
    return pl.pallas_call(
        functools.partial(hidden_kernel, tiles),
        grid=(2 * tiles + 8,),
        in_specs=[
            pl.BlockSpec((rows, width), lambda s: (row(s), 0)),
            pl.BlockSpec((width, units), lambda s: (0, column(s))),
            pl.BlockSpec((width, units), lambda s: (0, tiles + column(s))),
            pl.BlockSpec((units, width), lambda s: (column(s), 0)),
            pl.BlockSpec((count, columns), lambda s: (0, jnp.maximum(s - 2 * tiles, 0))),
        ]
        + [anywhere] * 6,
        out_specs=[out_spec] * 3
        + [
            pl.BlockSpec((columns, 2 * total), lambda s: (jnp.maximum(s - 2 * tiles, 0), 0)),
            anywhere,
            anywhere,
        ],
        out_shape=[out_shape] * 3
        + [
            jax.ShapeDtypeStruct((width, 2 * total), jnp.bfloat16),
            jax.ShapeDtypeStruct(cot.shape, jnp.bfloat16),
            jax.ShapeDtypeStruct((3, side.shape[0], side_columns), side.dtype),
        ],
        scratch_shapes=[
            pltpu.VMEM((count, width), jnp.bfloat16),
            pltpu.VMEM((count, 2 * total), jnp.bfloat16),
            sems((6,)),
            sems((2,)),
            sems((2,)),
            sems((SPREAD_COUNT,)),
            sems((SPREAD_COUNT,)),
        ],
        compiler_params=pltpu.CompilerParams(
            collective_id=2, has_side_effects=True, vmem_limit_bytes=60 << 20
        ),
        cost_estimate=pl.CostEstimate(
            flops=10 * count * width * total, bytes_accessed=70_000_000, transcendentals=0
        ),
        name="hidden_pass",
    )(normed, weight, weight, down, normed, side, cot, *cot_near)


def in_order(step):
    value = 1
    for index, half in enumerate((6, 7, 2, 5, 4, 3, 0)):
        value = jnp.where(step == index, half, value)
    return value


def tail_kernel(
    gate_ref, up_ref, hidden_ref, turned_ref, in_hbm, down_hbm, cot_ref, one_top_ref, one_bottom_ref,
    two_top_ref, two_bottom_ref, cot_far_ref, down_sum_ref, *refs
):
    first_refs, (out_rest_ref, grad_ref, *refs) = refs[:4], refs[4:]
    (
        weight_ref, down_ref, first_ref, rest_ref, got_ref, last_ref, last_got_ref, weight_sem,
        send_sem, recv_sem,
    ) = refs
    step = pl.program_id(0)
    head, blk = lax.axis_index("heads"), lax.axis_index("blk")
    rows, total = hidden_ref.shape
    width = grad_ref.shape[1]
    load_in = pltpu.make_async_copy(in_hbm, weight_ref, weight_sem.at[0])
    load_down = pltpu.make_async_copy(down_hbm, down_ref, weight_sem.at[1])
    pieces = (
        (cot_ref, 0, 2),
        (one_top_ref, 2, 1),
        (one_bottom_ref, 3, 1),
        (two_top_ref, 4, 1),
        (two_bottom_ref, 5, 1),
        (cot_far_ref, 6, 2),
    )
    cot_loads = [
        pltpu.make_async_copy(
            ref,
            weight_ref.at[pl.ds(place * rows, length * rows), pl.ds(0, width)],
            weight_sem.at[2 + index],
        )
        for index, (ref, place, length) in enumerate(pieces)
    ]

    def copy(source, target, k, index):
        return pltpu.make_async_remote_copy(
            src_ref=source,
            dst_ref=target,
            send_sem=send_sem.at[index],
            recv_sem=recv_sem.at[index],
            device_id=(head ^ k, blk),
            device_id_type=MESH,
        )

    firsts = [
        copy(first_ref.at[index], got_ref.at[index], k, index)
        for index, k in enumerate((1, 2, 1, 2))
    ]
    lasts = [copy(last_ref.at[part], last_got_ref.at[part], 2 - part, 4 + part) for part in range(2)]

    def wide_of(block):
        return block.astype(jnp.float32)

    @pl.when(step == 0)
    def _():
        load_in.start()
        load_down.start()
        greet_near(False)
        load_in.wait()

    @pl.when(step < 8)
    def _():
        value = lax.dot_general(
            gate_ref[...], weight_ref[:, :total], ROWS_IN_BOTH, preferred_element_type=jnp.float32
        ) + lax.dot_general(
            up_ref[...], weight_ref[:, total:], ROWS_IN_BOTH, preferred_element_type=jnp.float32
        )
        value = value.astype(jnp.bfloat16)

        for index in range(4):

            @pl.when(step == index)
            def _(index=index):
                first_ref[index] = value
                firsts[index].start()

        @pl.when(step >= 4)
        def _():
            rest_ref[pl.ds(pl.multiple_of((step - 4) * rows, rows), rows)] = value

        @pl.when(step == 7)
        def _():
            load_down.wait()
            for load in cot_loads:
                load.start()

    @pl.when((step >= 8) & (step < 16))
    def _():
        terms = jnp.dot(
            hidden_ref[...], down_ref[...], preferred_element_type=jnp.float32
        ).astype(jnp.bfloat16)

        for index, ref in enumerate(first_refs):

            @pl.when(step == 8 + index)
            def _(ref=ref):
                ref[...] = terms

        @pl.when(step >= 12)
        def _():
            out_rest_ref[...] = terms

        @pl.when(step == 15)
        def _():
            for load in cot_loads:
                load.wait()

    @pl.when(step >= 16)
    def _():
        down_sum_ref[...] = lax.dot_general(
            turned_ref[...],
            weight_ref[:, :width],
            (((0,), (0,)), ((), ())),
            preferred_element_type=jnp.float32,
        ).astype(jnp.bfloat16)

    for part, when in enumerate((8, 9)):

        @pl.when(step == when)
        def _(part=part):
            firsts[part].wait_recv()
            last_ref[part] = (
                wide_of(rest_ref[part * rows : (part + 1) * rows]) + wide_of(got_ref[part])
            ).astype(jnp.bfloat16)
            lasts[part].start()

    @pl.when(step == pl.num_programs(0) - 1)
    def _():
        for part in range(2):
            firsts[2 + part].wait_recv()
            lasts[part].wait_recv()
            grad_ref[part * rows : (part + 1) * rows] = (
                wide_of(rest_ref[(2 + part) * rows : (3 + part) * rows])
                + wide_of(got_ref[2 + part])
                + wide_of(last_got_ref[part])
            )
        for sent in firsts + lasts:
            sent.wait_send()


def feed_tail(gate_grad, up_grad, hidden, weight, down, cots):
    count, total = hidden.shape
    width = weight.shape[0]
    rows = count // 8
    units = 256
    anywhere = pl.BlockSpec(memory_space=pl.ANY)

    def stage(i, first, last):
        return jnp.clip(i - first, 0, last)

    def first_rows(i):
        return (in_order(stage(i, 0, 7)), 0)

    low = jnp.bfloat16
    return pl.pallas_call(
        tail_kernel,
        grid=(16 + total // units,),
        in_specs=[
            pl.BlockSpec((rows, total), first_rows),
            pl.BlockSpec((rows, total), first_rows),
            pl.BlockSpec((rows, total), lambda i: (in_order(stage(i, 8, 7)), 0)),
            pl.BlockSpec((count, units), lambda i: (0, jnp.maximum(i - 16, 0))),
        ]
        + [anywhere] * 8,
        out_specs=[
            pl.BlockSpec((units, width), lambda i: (jnp.maximum(i - 16, 0), 0)),
            *[pl.BlockSpec((rows, width), lambda i: (0, 0), pipeline_mode=pl.Buffered(1))] * 4,
            pl.BlockSpec((rows, width), lambda i: (stage(i, 12, 3), 0)),
            pl.BlockSpec((2 * rows, width), lambda i: (0, 0), pipeline_mode=pl.Buffered(1)),
        ],
        out_shape=[
            jax.ShapeDtypeStruct((total, width), low),
            *[jax.ShapeDtypeStruct((rows, width), low)] * 4,
            jax.ShapeDtypeStruct((4 * rows, width), low),
            jax.ShapeDtypeStruct((2 * rows, width), jnp.float32),
        ],
        scratch_shapes=[
            pltpu.VMEM(weight.shape, low),
            pltpu.VMEM(down.shape, low),
            pltpu.VMEM((4, rows, width), low),
            pltpu.VMEM((4 * rows, width), low),
            pltpu.VMEM((4, rows, width), low),
            pltpu.VMEM((2, rows, width), low),
            pltpu.VMEM((2, rows, width), low),
            pltpu.SemaphoreType.DMA((8,)),
            pltpu.SemaphoreType.DMA((6,)),
            pltpu.SemaphoreType.DMA((6,)),
        ],
        compiler_params=pltpu.CompilerParams(
            collective_id=3, has_side_effects=True, vmem_limit_bytes=60 << 20
        ),
        cost_estimate=pl.CostEstimate(
            flops=8 * count * width * total, bytes_accessed=70_000_000, transcendentals=0
        ),
        name="feed_tail",
    )(gate_grad, up_grad, hidden, hidden, weight, down, *cots)


def residual_back_kernel(
    grad_sum_ref, residual_ref, cot_ref, gain_ref, attended_ref, weight_ref, weights_ref, grad_ref,
    gain_grad_ref, pieces_ref, *refs
):
    *out_refs, branch_ref, mine_ref, terms_ref, terms_got_ref, own_sem, send_sem, recv_sem = refs
    size = lax.axis_size("heads")
    core = lax.rem(lax.axis_index("blk"), 2)
    step = pl.program_id(0)
    last = pl.num_programs(0) - 1
    head, blk = lax.axis_index("heads"), lax.axis_index("blk")
    rows = cot_ref.shape[0]
    copies = [
        pltpu.make_async_remote_copy(
            src_ref=mine_ref.at[k],
            dst_ref=pieces_ref.at[k],
            send_sem=send_sem.at[k - 1],
            recv_sem=recv_sem.at[k - 1],
            device_id=(head ^ k, blk),
            device_id_type=MESH,
        )
        for k in range(1, size)
    ]
    keep = pltpu.make_async_copy(mine_ref.at[0], pieces_ref.at[0], own_sem)
    across = pltpu.make_async_remote_copy(
        src_ref=terms_ref.at[:, 1 - core],
        dst_ref=terms_got_ref,
        send_sem=send_sem.at[size - 1],
        recv_sem=recv_sem.at[size - 1],
        device_id=(head, blk ^ 1),
        device_id_type=MESH,
    )

    @pl.when(step == 0)
    def _():
        gain_grad_ref[...] = jnp.zeros_like(gain_grad_ref)
        barrier = pltpu.get_barrier_semaphore()
        for k in range(1, size):
            pl.semaphore_signal(barrier, inc=1, device_id=(head ^ k, blk), device_id_type=MESH)
        pl.semaphore_signal(barrier, inc=1, device_id=(head, blk ^ 1), device_id_type=MESH)
        pl.semaphore_wait(barrier, size)

    @pl.when(step < last)
    def _():
        here = pl.ds(pl.multiple_of(step * rows, rows), rows)
        gradient = grad_sum_ref[...]
        values = residual_ref[...]
        inverse = lax.rsqrt(jnp.mean(values * values, axis=-1, keepdims=True) + EPS)
        gain_grad_ref[...] += jnp.sum(gradient * values * inverse, axis=0, keepdims=True)
        scaled = gradient * gain_ref[...]
        moment = jnp.mean(scaled * values, axis=-1, keepdims=True)
        total = cot_ref[...].astype(jnp.float32) + (
            inverse * scaled - values * (inverse * inverse * inverse * moment)
        )
        grad_ref[...] = total
        branch = total.astype(jnp.bfloat16)
        branch_ref[here] = branch
        for k in range(size):
            weight = weight_ref[...] if k == 0 else weights_ref[k - 1]
            mine_ref[k, here] = lax.dot_general(
                branch, weight, ROWS_IN_BOTH, preferred_element_type=jnp.float32
            ).astype(jnp.bfloat16)

    @pl.when(step == last)
    def _():
        for copy in copies:
            copy.start()
        keep.start()
        columns = attended_ref.shape[1] // size
        pairs = terms_ref.shape[0] // size
        for k in range(size):
            terms = lax.dot_general(
                attended_ref[:, k * columns : (k + 1) * columns],
                branch_ref[...],
                (((0,), (0,)), ((), ())),
                preferred_element_type=jnp.float32,
            ).astype(jnp.bfloat16)
            terms_ref[k * pairs : (k + 1) * pairs] = terms.reshape(pairs, *terms_ref.shape[1:])
        across.start()
        across.wait()

        for k, out_ref in enumerate(out_refs):

            def add(index, carried, k=k, out_ref=out_ref):
                out_ref[index] = (
                    terms_ref[k * pairs + index, core].astype(jnp.float32)
                    + terms_got_ref[k * pairs + index].astype(jnp.float32)
                ).astype(jnp.bfloat16)
                return carried

            lax.fori_loop(0, pairs, add, 0)
        for copy in copies:
            copy.wait()
        keep.wait()


def residual_back(grad_sum, residual, cot, gain, attended, weight, weights, rows):
    count, width = cot.shape
    size, blk_size = lax.axis_size("heads"), lax.axis_size("blk")
    columns = weight.shape[0]
    pairs, held = size * blk_size // 2, columns // blk_size
    tiles = count // rows

    def there(i):
        return (jnp.minimum(i, tiles - 1), 0)

    def whole(i):
        return (0, 0)

    tile = pl.BlockSpec((rows, width), there)
    row = pl.BlockSpec((1, width), whole)
    pieces = (size, count, columns)
    return pl.pallas_call(
        residual_back_kernel,
        grid=(tiles + 1,),
        in_specs=[
            tile,
            tile,
            tile,
            row,
            pl.BlockSpec(attended.shape, whole),
            pl.BlockSpec(weight.shape, whole),
            pl.BlockSpec(weights.shape, lambda i: (0, 0, 0)),
        ],
        out_specs=[
            tile,
            row,
            pl.BlockSpec(memory_space=pl.ANY),
            *[pl.BlockSpec((pairs // size, held, width), lambda i: (0, 0, 0))] * size,
        ],
        out_shape=[
            jax.ShapeDtypeStruct((count, width), jnp.float32),
            jax.ShapeDtypeStruct((1, width), jnp.float32),
            jax.ShapeDtypeStruct(pieces, jnp.bfloat16),
            *[jax.ShapeDtypeStruct((pairs // size, held, width), jnp.bfloat16)] * size,
        ],
        scratch_shapes=[
            pltpu.VMEM((count, width), jnp.bfloat16),
            pltpu.VMEM(pieces, jnp.bfloat16),
            pltpu.VMEM((pairs, 2, held, width), jnp.bfloat16),
            pltpu.VMEM((pairs, held, width), jnp.bfloat16),
            pltpu.SemaphoreType.DMA,
            pltpu.SemaphoreType.DMA((size,)),
            pltpu.SemaphoreType.DMA((size,)),
        ],
        compiler_params=pltpu.CompilerParams(
            collective_id=4, has_side_effects=True, vmem_limit_bytes=60 << 20
        ),
        cost_estimate=pl.CostEstimate(
            flops=4 * count * width * columns * size, bytes_accessed=30_000_000, transcendentals=0
        ),
        name="residual_back",
    )(grad_sum, residual, cot, gain, attended, weight, weights)


def qkv_terms_kernel(normed_ref, grad_ref, *refs):
    size, blk_size = lax.axis_size("heads"), lax.axis_size("blk")
    out_refs, refs = refs[:size], refs[size:]
    (
        terms_ref, got_ref, out_grad_ref, out_part_ref, out_got_ref, send_sem, recv_sem, o_send,
        o_recv,
    ) = refs
    step = pl.program_id(0)
    pairs = blk_size // 2
    head, blk = lax.axis_index("heads"), lax.axis_index("blk")
    core, pair = lax.rem(blk, 2), blk // 2
    count = got_ref.shape[1]
    out_rows = out_grad_ref.shape[0]
    copies = [
        pltpu.make_async_remote_copy(
            src_ref=grad_ref.at[pl.ds(k * count, count)],
            dst_ref=got_ref.at[k - 1],
            send_sem=send_sem.at[k - 1],
            recv_sem=recv_sem.at[k - 1],
            device_id=(head ^ k, blk),
            device_id_type=MESH,
        )
        for k in range(1, size)
    ]

    def wide_of(block):
        return block.astype(jnp.float32)

    def out_copy(k, slot):
        other = lax.rem(pair + k, pairs)
        return pltpu.make_async_remote_copy(
            src_ref=out_part_ref.at[other],
            dst_ref=out_got_ref.at[slot],
            send_sem=o_send.at[k],
            recv_sem=o_recv.at[slot],
            device_id=(head, other * 2 + core),
            device_id_type=MESH,
        )

    @pl.when(step == 0)
    def _():
        barrier = pltpu.get_barrier_semaphore()
        for k in range(1, size):
            pl.semaphore_signal(barrier, inc=1, device_id=(head ^ k, blk), device_id_type=MESH)

        def greet(k, carried):
            place = (head, lax.rem(pair + k, pairs) * 2 + core)
            pl.semaphore_signal(barrier, inc=1, device_id=place, device_id_type=MESH)
            return carried

        lax.fori_loop(1, pairs, greet, 0)
        pl.semaphore_wait(barrier, size + pairs - 2)
        for copy in copies:
            copy.start()

        def out_sum(index, carried):
            here = pl.ds(pl.multiple_of(index * out_rows, out_rows), out_rows)
            total = wide_of(out_refs[0][here])
            for ref in out_refs[1:]:
                total += wide_of(ref[here])
            out_part_ref[index, :out_rows] = total.astype(jnp.bfloat16)
            return carried

        def start(k, carried):
            out_copy(k, pair).start()
            return carried

        lax.fori_loop(0, pairs, out_sum, 0)
        lax.fori_loop(1, pairs, start, 0)
        out_got_ref[pair] = out_part_ref[pair]

    terms_ref[...] = lax.dot_general(
        normed_ref[...], grad_ref[...], (((0,), (0,)), ((), ())), preferred_element_type=jnp.float32
    ).astype(terms_ref.dtype)

    @pl.when(step == pl.num_programs(0) - 1)
    def _():
        for copy in copies:
            copy.wait()

        def finish(k, carried):
            out_copy(k, lax.rem(pair + pairs - k, pairs)).wait()
            return carried

        lax.fori_loop(1, pairs, finish, 0)
        total = wide_of(out_got_ref[0, :out_rows])
        for b in range(1, pairs):
            total += wide_of(out_got_ref[b, :out_rows])
        out_grad_ref[...] = total


def qkv_terms(normed, grad, outs, rows):
    count, height = normed.shape
    width = grad.shape[1]
    size, blk_size = lax.axis_size("heads"), lax.axis_size("blk")
    pairs = blk_size // 2
    out_rows, out_width = outs[0].shape[0] // pairs, outs[0].shape[1]
    held_rows = -(-out_rows // 16) * 16

    def whole(i):
        return (0, 0)

    sems = pltpu.SemaphoreType.DMA
    return pl.pallas_call(
        qkv_terms_kernel,
        grid=(height // rows,),
        in_specs=[
            pl.BlockSpec((count, rows), lambda i: (0, i)),
            pl.BlockSpec((count, width), whole),
        ]
        + [pl.BlockSpec(out.shape, whole) for out in outs],
        out_specs=[
            pl.BlockSpec((rows, width), lambda i: (i, 0)),
            pl.BlockSpec(memory_space=pl.ANY),
            pl.BlockSpec((out_rows, out_width), whole),
        ],
        out_shape=[
            jax.ShapeDtypeStruct((height, width), jnp.bfloat16),
            jax.ShapeDtypeStruct((size - 1, count // size, width), jnp.bfloat16),
            jax.ShapeDtypeStruct((out_rows, out_width), jnp.float32),
        ],
        scratch_shapes=[
            pltpu.VMEM((pairs, held_rows, out_width), jnp.bfloat16),
            pltpu.VMEM((pairs, held_rows, out_width), jnp.bfloat16),
            sems((size - 1,)),
            sems((size - 1,)),
            sems((pairs,)),
            sems((pairs,)),
        ],
        compiler_params=pltpu.CompilerParams(
            collective_id=7, has_side_effects=True, vmem_limit_bytes=60 << 20
        ),
        cost_estimate=pl.CostEstimate(
            flops=4 * count * height * width, bytes_accessed=20_000_000, transcendentals=0
        ),
        name="qkv_terms",
    )(normed, grad, *outs)


def finish_kernel(
    query_width, dim, got_ref, qkv_ref, gain_ref, ffn_ref, head_ref, *refs
):
    size, blk_size = lax.axis_size("heads"), lax.axis_size("blk")
    sources, refs = refs[:12], refs[12:]
    (
        grad_ref, qkv_grad_ref, gains_ref, in_grad_ref, layer_ref, *refs
    ) = refs
    held, refs = refs[:12], refs[12:]
    weight_ref, weights_ref, x_ref, residual_grad_ref, sent_ref, in_ref, residual_ref, rest_ref = held[:8]
    (
        qkv_other_ref, qkv_sum_ref, qkv_z_ref, qkv_mine_ref, qkv_got_ref, gain_mine_ref,
        gain_away_ref, gain_other_ref, gain_sum_ref, gain_z_ref, gain_part_ref, gain_got_ref,
        in_got_ref, load_sem, c_send, c_recv, z_send, z_recv, h_send,
        h_recv, gc_send, gc_recv, gz_send, gz_recv, gh_send, gh_recv, i_send, i_recv,
    ) = refs
    devices = size * blk_size
    pairs = blk_size // 2
    head, blk = lax.axis_index("heads"), lax.axis_index("blk")
    core, pair = lax.rem(blk, 2), blk // 2
    count, width = x_ref.shape
    depth = width // devices
    barrier = pltpu.get_barrier_semaphore()
    loads = [
        pltpu.make_async_copy(
            source.at[pl.ds(0, target.shape[0]), pl.ds(0, target.shape[1])]
            if index in (0, 4, 6)
            else source.at[pl.ds(target.shape[0], target.shape[0])]
            if index == 7
            else source,
            target,
            load_sem.at[index],
        )
        for index, (source, target) in enumerate(zip(sources, held))
    ]
    for load in loads:
        load.start()

    def same_core(k):
        return (head, lax.rem(pair + k, pairs) * 2 + core)

    for k in range(1, size):
        pl.semaphore_signal(barrier, inc=1, device_id=(head ^ k, blk), device_id_type=MESH)
    pl.semaphore_signal(barrier, inc=1, device_id=(head, blk ^ 1), device_id_type=MESH)

    def greet(k, carried):
        pl.semaphore_signal(barrier, inc=1, device_id=same_core(k), device_id_type=MESH)
        return carried

    lax.fori_loop(1, pairs, greet, 0)
    pl.semaphore_wait(barrier, size + pairs - 1)

    def copy(source, target, place, send, recv):
        return pltpu.make_async_remote_copy(
            src_ref=source,
            dst_ref=target,
            send_sem=send,
            recv_sem=recv,
            device_id=place,
            device_id_type=MESH,
        )

    in_sends = [
        copy(
            sources[5].at[head ^ k],
            in_got_ref.at[k - 1],
            (head ^ k, blk),
            i_send.at[k - 1],
            i_recv.at[k - 1],
        )
        for k in range(1, size)
    ]
    for sent in in_sends:
        sent.start()

    across = copy(qkv_ref.at[:, 1 - core], qkv_other_ref, (head, blk ^ 1), c_send, c_recv)
    across.start()
    def wide_of(block):
        return block.astype(jnp.float32)

    across.wait_recv()

    def along(k, source_ref, target_ref, slot, send, recv):
        return copy(
            source_ref.at[:, lax.rem(pair + k, pairs)],
            target_ref.at[slot],
            same_core(k),
            send.at[k],
            recv.at[slot],
        )

    def around(source_ref, target_ref, slots, send, recv):
        return [
            copy(
                source_ref.at[head ^ k],
                target_ref.at[slots[k]],
                (head ^ k, blk),
                send.at[k - 1],
                recv.at[slots[k]],
            )
            for k in range(1, size)
        ]

    def start_along(source_ref, target_ref, send, recv):
        def start(k, carried):
            along(k, source_ref, target_ref, pair, send, recv).start()
            return carried

        lax.fori_loop(1, pairs, start, 0)
        target_ref[pair] = source_ref[:, pair]

    def finish_along(source_ref, target_ref, send, recv):
        def finish(k, carried):
            slot = lax.rem(pair + pairs - k, pairs)
            along(k, source_ref, target_ref, slot, send, recv).wait()
            return carried

        lax.fori_loop(1, pairs, finish, 0)
        total = wide_of(target_ref[0])
        for k in range(1, pairs):
            total += wide_of(target_ref[k])
        return total

    here, there = [head] * size, [head ^ k for k in range(size)]

    def start_around(source_ref, target_ref, send, recv):
        for sent in around(source_ref, target_ref, here, send, recv):
            sent.start()
        target_ref[head] = source_ref[head]

    def finish_around(source_ref, target_ref, send, recv):
        for sent in around(source_ref, target_ref, there, send, recv):
            sent.wait()

    def qkv_sum(index, carried):
        qkv_sum_ref[index // pairs, lax.rem(index, pairs)] = (
            wide_of(qkv_ref[index, core]) + wide_of(qkv_other_ref[index])
        ).astype(jnp.bfloat16)
        return carried

    lax.fori_loop(0, size * pairs, qkv_sum, 0)
    start_along(qkv_sum_ref, qkv_z_ref, z_send, z_recv)

    for load in loads[:5]:
        load.wait()
    rows = min(128, count)

    def tile(index, gain_sum):
        here = pl.ds(pl.multiple_of(index * rows, rows), rows)
        normed_grad = lax.dot_general(
            sent_ref[here], weight_ref[...], ROWS_IN_BOTH, preferred_element_type=jnp.float32
        )
        for k in range(1, size):
            normed_grad += lax.dot_general(
                got_ref[k - 1, here],
                weights_ref[k - 1],
                ROWS_IN_BOTH,
                preferred_element_type=jnp.float32,
            )
        values = wide_of(x_ref[here])
        inverse = lax.rsqrt(jnp.mean(values * values, axis=-1, keepdims=True) + EPS)
        scaled = normed_grad * gain_ref[...]
        moment = jnp.mean(scaled * values, axis=-1, keepdims=True)
        grad_ref[here] = (
            residual_grad_ref[here]
            + inverse * scaled
            - values * (inverse * inverse * inverse * moment)
        )
        return gain_sum + jnp.sum(normed_grad * values * inverse, axis=0, keepdims=True)

    attn_sum = lax.fori_loop(0, count // rows, tile, jnp.zeros((1, width), jnp.float32))

    def by_device(row, which):
        lanes = jnp.concatenate(
            [row[:, d * depth : (d + 1) * depth] for d in range(which, devices, 2)], axis=0
        )
        if depth < 64:
            lanes = jnp.concatenate(
                [lanes, jnp.zeros((devices // 2, 64 - depth), jnp.float32)], axis=1
            )
        return lanes

    head_row = head_ref[...]
    query_sum = head_row[:, :dim]
    for c in range(dim, query_width, dim):
        query_sum += head_row[:, c : c + dim]
    key_sum = head_row[:, query_width : query_width + dim]
    for c in range(query_width + dim, head_row.shape[1], dim):
        key_sum += head_row[:, c : c + dim]
    both = jnp.concatenate([query_sum, key_sum], axis=1)
    gains = [
        jnp.concatenate([by_device(attn_sum, c), by_device(ffn_ref[...], c)], axis=1)
        for c in range(2)
    ]
    for ref, mine in ((gain_mine_ref, 0), (gain_away_ref, 1)):
        ref[...] = jnp.zeros_like(ref)
        ref[:, 0, :] = jnp.where(core == mine, gains[0], gains[1])
        ref[:, 1, :] = jnp.broadcast_to(both, (devices // 2, 2 * dim))
    gain_across = copy(gain_away_ref, gain_other_ref, (head, blk ^ 1), gc_send, gc_recv)
    gain_across.start()
    gain_across.wait()
    gain_sum_ref[...] = (gain_mine_ref[...] + gain_other_ref[...]).reshape(gain_sum_ref.shape)
    start_along(gain_sum_ref, gain_z_ref, gz_send, gz_recv)

    qkv_mine_ref[...] = finish_along(qkv_sum_ref, qkv_z_ref, z_send, z_recv).astype(jnp.bfloat16)
    start_around(qkv_mine_ref, qkv_got_ref, h_send, h_recv)
    gain_part_ref[...] = finish_along(gain_sum_ref, gain_z_ref, gz_send, gz_recv)
    start_around(gain_part_ref, gain_got_ref, gh_send, gh_recv)

    loads[5].wait()
    units = in_ref.shape[2] // 2
    for k in range(size):
        if k:
            in_sends[k - 1].wait_recv()
        for part in range(2):
            columns = pl.ds(pl.multiple_of((part * size + (head ^ k)) * units, units), units)
            piece = slice(part * units, (part + 1) * units)
            got = in_got_ref[k - 1, :, piece] if k else in_ref[head, :, piece]
            in_grad_ref[:, columns] = wide_of(got)

    for load in loads[6:]:
        load.wait()
    half = count // 2
    for part in range(2):
        here = slice(part * half, (part + 1) * half)
        layer_ref[here] = (
            residual_ref[here] + wide_of(rest_ref[here]) + wide_of(held[8 + part][...])
            + wide_of(held[10 + part][...])
        ).astype(jnp.bfloat16)

    finish_around(qkv_mine_ref, qkv_got_ref, h_send, h_recv)
    sums = [wide_of(qkv_got_ref[h]) for h in range(size)]
    key_end = query_width + (sums[0].shape[1] - query_width) // 2
    qkv_grad_ref[...] = jnp.concatenate(
        [total[:, :query_width] for total in sums]
        + [total[:, query_width:key_end] for total in sums]
        + [total[:, key_end:] for total in sums],
        axis=1,
    )

    finish_around(gain_part_ref, gain_got_ref, gh_send, gh_recv)
    gains_ref[...] = jnp.sum(gain_got_ref[...], axis=0)
    across.wait_send()
    for sent in in_sends:
        sent.wait_send()


def finish(
    sent, got, qkv_part, x, residual_grad, gain, ffn_sum, head_sum, weight, weights, in_part,
    residual, rest, terms, query_width, dim
):
    size, blk_size = lax.axis_size("heads"), lax.axis_size("blk")
    devices = size * blk_size
    pairs = blk_size // 2
    count, width = x.shape
    depth, joined = width // devices, sent.shape[1]
    units = in_part.shape[2]
    vmem = pl.BlockSpec(memory_space=pltpu.VMEM)
    anywhere = pl.BlockSpec(memory_space=pl.ANY)
    sems = pltpu.SemaphoreType.DMA
    low = jnp.bfloat16
    loaded = (weights, x, residual_grad)
    return pl.pallas_call(
        functools.partial(finish_kernel, query_width, dim),
        out_shape=[
            jax.ShapeDtypeStruct((count, width), jnp.float32),
            jax.ShapeDtypeStruct((depth, size * joined), jnp.float32),
            jax.ShapeDtypeStruct((8, 128), jnp.float32),
            jax.ShapeDtypeStruct((depth, size * units), jnp.float32),
            jax.ShapeDtypeStruct((count, width), low),
        ],
        in_specs=[vmem] * 5 + [anywhere] * 12,
        out_specs=[vmem] * 5,
        scratch_shapes=[pltpu.VMEM((width, joined), low)]
        + [pltpu.VMEM(array.shape, array.dtype) for array in loaded]
        + [pltpu.VMEM((count, joined), low), pltpu.VMEM(in_part.shape, low)]
        + [pltpu.VMEM((count, width), jnp.float32), pltpu.VMEM((count, width), low)]
        + [pltpu.VMEM((count // 2, width), low)] * 4
        + [
            pltpu.VMEM((size * pairs, depth, joined), low),
            pltpu.VMEM((size, pairs, depth, joined), low),
            pltpu.VMEM((pairs, size, depth, joined), low),
            pltpu.VMEM((size, depth, joined), low),
            pltpu.VMEM((size, depth, joined), low),
            pltpu.VMEM((devices // 2, 8, 128), jnp.float32),
            pltpu.VMEM((devices // 2, 8, 128), jnp.float32),
            pltpu.VMEM((devices // 2, 8, 128), jnp.float32),
            pltpu.VMEM((size, pairs, 8, 128), jnp.float32),
            pltpu.VMEM((pairs, size, 8, 128), jnp.float32),
            pltpu.VMEM((size, 8, 128), jnp.float32),
            pltpu.VMEM((size, 8, 128), jnp.float32),
            pltpu.VMEM((size - 1, depth, units), low),
            sems((12,)),
            sems,
            sems,
            sems((pairs,)),
            sems((pairs,)),
            sems((size - 1,)),
            sems((size,)),
            sems,
            sems,
            sems((pairs,)),
            sems((pairs,)),
            sems((size - 1,)),
            sems((size,)),
            sems((size - 1,)),
            sems((size - 1,)),
        ],
        compiler_params=pltpu.CompilerParams(
            collective_id=0, has_side_effects=True, vmem_limit_bytes=60 << 20
        ),
        name="finish",
    )(
        got, qkv_part.reshape(size * pairs, 2, depth, joined), gain, ffn_sum, head_sum,
        weight, *loaded, sent, in_part, residual, rest, *terms
    )


def permute(block, axis, k):
    return lax.ppermute(block, axis, [(i, i ^ k) for i in range(lax.axis_size(axis))])


def after(value, *done):
    return lax.optimization_barrier((value, *done))[0]


def pick(block, k, axis, dim):
    extent = block.shape[dim] // lax.axis_size(axis)
    return lax.dynamic_slice_in_dim(block, (lax.axis_index(axis) ^ k) * extent, extent, dim)


def wide(block):
    return block.astype(jnp.float32)


def local(
    inputs,
    positions,
    attn_gain,
    qkv_weight,
    q_gain,
    k_gain,
    out_weight,
    ffn_gain,
    ffn_in_weight,
    ffn_out_weight,
    cotangent,
):
    token_count, width = inputs.shape
    depth = qkv_weight.shape[0]
    head_dim = q_gain.shape[0]
    group_size = HEADS // KV_HEADS
    size = lax.axis_size("heads")
    blk_size = lax.axis_size("blk")
    query_all, key_all = HEADS * head_dim, KV_HEADS * head_dim
    query_width, key_width = query_all // size, key_all // size
    qkv_width = query_width + 2 * key_width
    block_len = token_count * size
    half = token_count // 2
    own = lax.axis_index("heads").astype(jnp.int32).reshape(1)

    qkv_parts = jnp.concatenate(
        [
            qkv_weight[:, :query_all].reshape(depth, size, query_width),
            qkv_weight[:, query_all : query_all + key_all].reshape(depth, size, key_width),
            qkv_weight[:, query_all + key_all :].reshape(depth, size, key_width),
            jnp.broadcast_to(attn_gain[:, None, None], (depth, size, 64)),
            jnp.broadcast_to(ffn_gain[:, None, None], (depth, size, 64)),
        ],
        axis=-1,
    ).transpose(1, 0, 2)
    out_group = lax.all_gather(out_weight, "blk", axis=0, tiled=True)
    in_rows = trade(ffn_in_weight)
    in_group = lax.all_gather(in_rows, "blk", axis=1, tiled=True).reshape(width, -1)

    half_dim = jnp.arange(head_dim // 2, dtype=jnp.float32)
    frequency = (ROPE_BASE ** (-2.0 * half_dim / head_dim))[:, None]
    inputs_blk, qkv_rows, cot_top, cot_bottom, cosine, sine = begin(
        after(inputs, in_rows), qkv_parts, cotangent, positions[None, :], frequency
    )
    qkv_rows = qkv_rows.reshape(width, -1)
    head_gain = jnp.concatenate(
        [jnp.tile(q_gain, HEADS // size), jnp.tile(k_gain, KV_HEADS // size)]
    ).astype(jnp.float32)[None, :]
    query_low, raw, normed, attn_scaling, ffn_scaling, out_peers, pair_all = project(
        inputs_blk, qkv_rows, head_gain, cosine, sine, out_group, size, query_width, 256
    )
    down_weight, pair_all = lax.optimization_barrier((ffn_out_weight, pair_all))
    down_group = lax.all_gather(down_weight, "blk", axis=0, tiled=True)
    query_rows, key_rows = token_count, 256
    low = block_len + jnp.arange(block_len, dtype=jnp.int32) - positions
    first = jnp.concatenate([low[::query_rows] // key_rows, own])
    low = low[None, :]
    attended_blk, logs = attend(query_low, pair_all, first, low, group_size, query_rows, key_rows)

    mine = jnp.concatenate([pick(attended_blk, k, "heads", 0) for k in range(size)], axis=0)
    one_top, two_bottom = permute(cot_top, "heads", 1), permute(cot_bottom, "heads", 2)
    mine, in_group = lax.optimization_barrier((mine, in_group))
    residual, ffn_normed, attended_own, one_bottom, two_top = join(
        inputs_blk, mine, out_group, out_peers, ffn_scaling, cotangent, 256
    )
    cot_near = (one_top, one_bottom, two_top, two_bottom)
    hidden, gate_grad, up_grad, in_sum, cot_far, qkv_peers = hidden_pass(
        ffn_normed, in_group, cotangent, cot_near, down_group, qkv_rows, qkv_width, 256
    )
    in_part = lax.psum_scatter(
        in_sum.reshape(size, blk_size * depth, -1), "blk", scatter_dimension=1, tiled=True
    )
    down_sum, one_far, two_far, one_near, two_near, out_rest, grad_sum = feed_tail(
        gate_grad, up_grad, hidden, in_group, down_group, (cotangent, *cot_near, cot_far)
    )
    down_part = lax.psum_scatter(down_sum, "blk", scatter_dimension=0, tiled=True)
    through_top, through_bottom = permute(one_far, "heads", 1), permute(two_far, "heads", 2)
    residual_grad, ffn_sum, grads, *out_slices = residual_back(
        grad_sum, residual, cotangent, ffn_scaling, attended_own, out_group, out_peers,
        min(128, half)
    )
    in_part, grads, through_top, through_bottom = lax.optimization_barrier(
        (in_part, grads, through_top, through_bottom)
    )
    top_send = (wide(out_rest[:half]) + wide(through_top)).astype(jnp.bfloat16)
    bottom_send = (wide(out_rest[half : 2 * half]) + wide(through_bottom)).astype(jnp.bfloat16)
    out_top_last = permute(top_send, "heads", 2)
    out_bottom_last = permute(bottom_send, "heads", 1)
    out_slices = [piece.reshape(-1, width) for piece in out_slices]
    out_slices = [out_slices[0]] + [permute(out_slices[k], "heads", k) for k in range(1, size)]
    query_grad, pair_sum, behind = attend_back(
        query_low, pair_all, first, low, grads, attended_blk, logs, group_size, query_rows, key_rows
    )
    pair_sum, out_top_last, out_bottom_last, *out_slices = lax.optimization_barrier(
        (pair_sum, out_top_last, out_bottom_last, *out_slices)
    )
    projected_grad, head_sum = project_back(
        query_grad, pair_sum, behind, raw, head_gain, cosine, sine, size, 256
    )
    out_top = permute(after(one_near, pair_sum), "heads", 1)
    out_bottom = permute(after(two_near, pair_sum), "heads", 2)
    qkv_part, got, out_grad = qkv_terms(normed, projected_grad, out_slices, 512)
    input_grad, qkv_grad, gains, ffn_in_grad, layer_out = finish(
        projected_grad, got, qkv_part, inputs, residual_grad, attn_scaling, ffn_sum, head_sum,
        qkv_rows, qkv_peers, in_part, residual, out_rest,
        (out_top, out_bottom, out_top_last, out_bottom_last), query_width, head_dim
    )
    down_part, gains = lax.optimization_barrier((down_part, gains))
    ffn_out_grad = wide(down_part)
    return (
        layer_out,
        input_grad,
        gains[0, :depth],
        qkv_grad,
        gains[1, :head_dim],
        gains[1, head_dim : 2 * head_dim],
        out_grad,
        gains[0, 64 : 64 + depth],
        ffn_in_grad,
        ffn_out_grad,
    )


def solution(mesh):
    placed = (
        P(("blk", "heads"), None),
        P("blk"),
        P(("heads", "blk")),
        P(("heads", "blk"), None),
        P(),
        P(),
        P(("heads", "blk"), None),
        P(("heads", "blk")),
        P(("heads", "blk"), None),
        P(("heads", "blk"), None),
        P(("blk", "heads"), None),
    )
    return jax.shard_map(
        local,
        mesh=mesh,
        in_specs=placed,
        out_specs=(
            P(("blk", "heads"), None),
            P(("blk", "heads"), None),
            P(("heads", "blk")),
            P(("heads", "blk"), None),
            P(),
            P(),
            P(("heads", "blk"), None),
            P(("heads", "blk")),
            P(("heads", "blk"), None),
            P(("heads", "blk"), None),
        ),
        check_vma=False,
    )
```

```python
import functools

import jax
import jax.numpy as jnp
from jax import lax
from jax.experimental import pallas as pl
from jax.experimental.pallas import tpu as pltpu
from jax.sharding import PartitionSpec as P

HEADS = 16
KV_HEADS = 4


EPS = 1e-06
ROPE_BASE = 10000.0
NEG = -1e30
MESH = pl.DeviceIdType.MESH
ROWS_IN_BOTH = (((1,), (1,)), ((), ()))


def stack_heads(tile, heads, first):
    turned = tile.T
    dim = turned.shape[0] // heads
    wide = jnp.concatenate([turned[h * dim : (h + 1) * dim] for h in range(heads)], axis=1)
    zero = jnp.zeros_like(wide)
    return jnp.concatenate([wide, zero] if first else [zero, wide], axis=0)


def unstack_heads(wide, heads):
    count = wide.shape[1] // heads
    return jnp.concatenate([wide[:, h * count : (h + 1) * count] for h in range(heads)], axis=0).T


def scores_at(pair, query_ext, low, first_query, key_start, heads):
    scores = jnp.dot(pair, query_ext, preferred_element_type=jnp.float32)
    rows, columns = scores.shape
    shape = (rows, columns // heads)
    key = key_start + lax.broadcasted_iota(jnp.int32, shape, 0)
    query = first_query + lax.broadcasted_iota(jnp.int32, shape, 1)
    bias = jnp.where((key <= query) & (key >= low), 0.0, NEG)
    return scores + jnp.concatenate([bias] * heads, axis=1)


def transpose_into(pair_ref, turned_ref):
    for start in range(0, pair_ref.shape[0], 512):
        turned_ref[:, start : start + 512] = pair_ref[start : start + 512, :].T


def attend_kernel(
    heads, key_rows, scale, first_ref, query_ref, low_ref, pair_ref, out_ref, log_ref, turned_ref,
    mixed_ref, total_ref
):
    step = pl.program_id(0)
    query_rows = query_ref.shape[0]

    @pl.when(step == 0)
    def _():
        transpose_into(pair_ref, turned_ref)

    query_ext = stack_heads(query_ref[...] * jnp.bfloat16(scale), heads, True)
    low = low_ref[...]
    base = pair_ref.shape[0] // 2 + step * query_rows
    mixed_ref[...] = jnp.zeros_like(mixed_ref)
    total_ref[...] = jnp.zeros_like(total_ref)

    def tile(index, carried):
        start = pl.multiple_of(index * key_rows, key_rows)
        expo = jnp.exp(
            scores_at(pair_ref[pl.ds(start, key_rows), :], query_ext, low, base, start, heads)
        )
        total_ref[...] += jnp.sum(expo, axis=0, keepdims=True)
        mixed_ref[...] += jnp.dot(
            turned_ref[:, pl.ds(start, key_rows)],
            expo.astype(jnp.bfloat16),
            preferred_element_type=jnp.float32,
        )
        return carried

    lax.fori_loop(first_ref[step], (base + query_rows - 1) // key_rows + 1, tile, 0)
    total = total_ref[...]
    dim = pair_ref.shape[1] // 2
    out_ref[...] = unstack_heads(mixed_ref[dim:] / total, heads).astype(out_ref.dtype)
    log_ref[...] = jnp.log(total)[None]


def attend_back_kernel(
    heads, key_rows, scale, first_ref, query_ref, low_ref, pair_ref, out_ref, log_ref, *refs
):
    grads_ref, query_grad_ref, pair_grad_ref, behind_ref, turned_ref, sum_ref = refs
    step = pl.program_id(0)
    grad = grads_ref[first_ref[pl.num_programs(0)] ^ step]
    query_rows = query_ref.shape[0]
    dim = pair_ref.shape[1] // 2

    @pl.when(step == 0)
    def _():
        pair_grad_ref[...] = jnp.zeros_like(pair_grad_ref)
        transpose_into(pair_ref, turned_ref)

    query_ext = stack_heads(query_ref[...] * jnp.bfloat16(scale), heads, True)
    grad_ext = stack_heads(grad, heads, False)
    out_ext = stack_heads(out_ref[...], heads, False)
    inner = jnp.sum(
        grad_ext.astype(jnp.float32) * out_ext.astype(jnp.float32), axis=0, keepdims=True
    )
    log_sum = log_ref[0]
    low = low_ref[...]
    base = pair_ref.shape[0] // 2 + step * query_rows
    sum_ref[...] = jnp.zeros_like(sum_ref)

    def tile(index, carried):
        start = pl.multiple_of(index * key_rows, key_rows)
        pair = pair_ref[pl.ds(start, key_rows), :]
        probs = jnp.exp(scores_at(pair, query_ext, low, base, start, heads) - log_sum)
        probs_grad = jnp.dot(pair, grad_ext, preferred_element_type=jnp.float32)
        score_grad = (probs * (probs_grad - inner)).astype(jnp.bfloat16)
        sum_ref[...] += jnp.dot(
            turned_ref[:dim, pl.ds(start, key_rows)], score_grad, preferred_element_type=jnp.float32
        )
        pair_grad_ref[pl.ds(start, key_rows), :] += lax.dot_general(
            score_grad, query_ext, ROWS_IN_BOTH, preferred_element_type=jnp.float32
        ) + lax.dot_general(
            probs.astype(jnp.bfloat16), grad_ext, ROWS_IN_BOTH, preferred_element_type=jnp.float32
        )
        return carried

    lax.fori_loop(first_ref[step], (base + query_rows - 1) // key_rows + 1, tile, 0)
    query_grad_ref[...] = unstack_heads(sum_ref[...] * scale, heads).astype(query_grad_ref.dtype)

    @pl.when(step == pl.num_programs(0) - 1)
    def _():
        behind_ref[...] = pair_grad_ref[: behind_ref.shape[0]].astype(behind_ref.dtype)


def attention_specs(queries, pair, query_rows, heads):
    width = queries.shape[1]
    return (
        pl.BlockSpec((query_rows, width), lambda i, first: (i, 0)),
        pl.BlockSpec((1, query_rows), lambda i, first: (0, i)),
        pl.BlockSpec(pair.shape, lambda i, first: (0, 0)),
        pl.BlockSpec((1, 1, heads * query_rows), lambda i, first: (i, 0, 0)),
    )


def attend(queries, pair, first, low, heads, query_rows, key_rows):
    count, width = queries.shape
    tile, row, whole, logs = attention_specs(queries, pair, query_rows, heads)
    columns = heads * query_rows
    return pl.pallas_call(
        functools.partial(attend_kernel, heads, key_rows, (width // heads) ** -0.5),
        grid_spec=pltpu.PrefetchScalarGridSpec(
            num_scalar_prefetch=1,
            grid=(count // query_rows,),
            in_specs=[tile, row, whole],
            out_specs=[tile, logs],
            scratch_shapes=[
                pltpu.VMEM(pair.shape[::-1], jnp.bfloat16),
                pltpu.VMEM((pair.shape[1], columns), jnp.float32),
                pltpu.VMEM((1, columns), jnp.float32),
            ],
        ),
        out_shape=[
            jax.ShapeDtypeStruct((count, width), jnp.bfloat16),
            jax.ShapeDtypeStruct((count // query_rows, 1, columns), jnp.float32),
        ],
        compiler_params=pltpu.CompilerParams(vmem_limit_bytes=60 << 20),
        cost_estimate=pl.CostEstimate(
            flops=20_000_000_000, bytes_accessed=8_000_000, transcendentals=0
        ),
        name="attend",
    )(first, queries, low, pair)


def attend_back(queries, pair, first, low, grads, out, logs, heads, query_rows, key_rows):
    count, width = queries.shape
    tile, row, whole, log_spec = attention_specs(queries, pair, query_rows, heads)
    columns = heads * query_rows
    behind = (pair.shape[0] // 2, pair.shape[1])
    return pl.pallas_call(
        functools.partial(attend_back_kernel, heads, key_rows, (width // heads) ** -0.5),
        grid_spec=pltpu.PrefetchScalarGridSpec(
            num_scalar_prefetch=1,
            grid=(count // query_rows,),
            in_specs=[tile, row, whole, tile, log_spec]
            + [pl.BlockSpec(grads.shape, lambda i, first: (0, 0, 0))],
            out_specs=[tile, whole, pl.BlockSpec(behind, lambda i, first: (0, 0))],
            scratch_shapes=[
                pltpu.VMEM(pair.shape[::-1], jnp.bfloat16),
                pltpu.VMEM((pair.shape[1] // 2, columns), jnp.float32),
            ],
        ),
        out_shape=[
            jax.ShapeDtypeStruct((count, width), jnp.bfloat16),
            jax.ShapeDtypeStruct(pair.shape, jnp.float32),
            jax.ShapeDtypeStruct(behind, jnp.bfloat16),
        ],
        compiler_params=pltpu.CompilerParams(vmem_limit_bytes=60 << 20),
        cost_estimate=pl.CostEstimate(
            flops=40_000_000_000, bytes_accessed=12_000_000, transcendentals=0
        ),
        name="attend_back",
    )(first, queries, low, pair, out, logs, grads)


def heads_apart(wide, dim):
    rows = wide.shape[0]
    return jnp.concatenate(
        [
            jnp.broadcast_to(
                jnp.mean(jnp.square(wide[:, c : c + dim]), axis=-1, keepdims=True), (rows, dim)
            )
            for c in range(0, wide.shape[1], dim)
        ],
        axis=1,
    )


def spread_mean(wide, dim):
    rows = wide.shape[0]
    return jnp.concatenate(
        [
            jnp.broadcast_to(jnp.mean(wide[:, c : c + dim], axis=-1, keepdims=True), (rows, dim))
            for c in range(0, wide.shape[1], dim)
        ],
        axis=1,
    )


def turn(wide, cosine, sine, dim):
    count = wide.shape[1] // dim
    half = dim // 2
    swapped = jnp.concatenate(
        [
            wide[:, c + shift : c + shift + half]
            for c in range(0, wide.shape[1], dim)
            for shift in (half, 0)
        ],
        axis=1,
    )
    return wide * jnp.concatenate([cosine] * count, axis=1) + swapped * jnp.concatenate(
        [sine] * count, axis=1
    )


def project_kernel(
    dim, size, x_ref, weight_ref, head_gain_ref, cosine_ref, sine_ref, side_ref, query_ref, raw_ref,
    normed_ref, gain_ref, ffn_gain_ref, spread_ref, pair_ref, pair_held, send_sem, recv_sem,
    pair_sem, pair_send, pair_recv
):
    columns = raw_ref.shape[1]
    step, steps = pl.program_id(0), pl.num_programs(0)
    marks = (0, steps // 2, steps - 2)
    head, blk = lax.axis_index("heads"), lax.axis_index("blk")
    last = lax.axis_size("blk") - 1
    rows, block = x_ref.shape[0], pair_held.shape[0]
    tiles = block // size // rows

    @pl.when(step == 0)
    def _():
        barrier = pltpu.get_barrier_semaphore()
        for place in ((head ^ 1, blk), (head ^ 2, blk), (head, blk ^ 1)):
            pl.semaphore_signal(barrier, inc=1, device_id=place, device_id_type=MESH)

        @pl.when(blk > 0)
        def _():
            pl.semaphore_signal(barrier, inc=1, device_id=(head, blk - 1), device_id_type=MESH)

        @pl.when(blk < last)
        def _():
            pl.semaphore_wait(barrier, 4)

        @pl.when(blk == last)
        def _():
            pl.semaphore_wait(barrier, 3)

    end = spread_job(step, marks, side_ref, spread_ref, send_sem, recv_sem, False)

    def chunk_rows(k, first):
        return pl.ds(
            pl.multiple_of(first + (head ^ k) * (block // size), block // size), block // size
        )

    def keep(k):
        return pltpu.make_async_copy(
            pair_held.at[chunk_rows(k, 0)], pair_ref.at[chunk_rows(k, block)], pair_sem.at[k]
        )

    def pass_on(k):
        return pltpu.make_async_remote_copy(
            src_ref=pair_held.at[chunk_rows(k, 0)],
            dst_ref=pair_ref.at[chunk_rows(k, 0)],
            send_sem=pair_send.at[k],
            recv_sem=pair_recv.at[k],
            device_id=(head, jnp.minimum(blk + 1, last)),
            device_id_type=MESH,
        )

    @pl.when(pl.program_id(0) == 0)
    def _():
        gains = weight_ref[:, columns:].T.astype(jnp.float32)
        gain_ref[...] = gains[:1]
        ffn_gain_ref[...] = gains[64:65]

    values = x_ref[...].astype(jnp.float32)
    normed = values * lax.rsqrt(jnp.mean(values * values, axis=-1, keepdims=True) + EPS)
    normed = (normed * gain_ref[...]).astype(jnp.bfloat16)
    normed_ref[...] = normed
    raw = jnp.dot(normed, weight_ref[:, :columns], preferred_element_type=jnp.float32)
    raw_ref[...] = raw
    turned_width = raw.shape[1] - pair_held.shape[1] // 2
    heads = raw[:, :turned_width]
    heads = heads * lax.rsqrt(heads_apart(heads, dim) + EPS) * head_gain_ref[...]
    heads = turn(heads, cosine_ref[...], sine_ref[...], dim).astype(jnp.bfloat16)
    query_width = query_ref.shape[1]
    query_ref[...] = heads[:, :query_width]
    place = ((head ^ (step // tiles)) * tiles + lax.rem(step, tiles)) * rows
    pair_held[pl.ds(pl.multiple_of(place, rows), rows)] = jnp.concatenate(
        [heads[:, query_width:], raw[:, turned_width:].astype(jnp.bfloat16)], axis=1
    )
    for k in range(size):

        @pl.when(step == (k + 1) * tiles - 1)
        def _(k=k):
            keep(k).start()

            @pl.when(blk < last)
            def _():
                pass_on(k).start()

    @pl.when(step == steps - 1)
    def _():
        end()
        for k in range(size):
            keep(k).wait()

        @pl.when(blk < last)
        def _():
            for k in range(size):
                pass_on(k).wait_send()

        @pl.when(blk > 0)
        def _():
            for k in range(size):
                pass_on(k).wait_recv()


def project(x, weight, head_gain, cosine, sine, side, size, query_width, rows):
    count, width = x.shape
    out_width = weight.shape[1] - 128
    pair_width = out_width - query_width
    dim = cosine.shape[1]
    tiles = count // size // rows

    def apart(i):
        return ((lax.axis_index("heads") ^ (i // tiles)) * tiles + i % tiles, 0)

    def there(i):
        return (i, 0)

    def whole(i):
        return (0, 0)

    anywhere = pl.BlockSpec(memory_space=pl.ANY)

    return pl.pallas_call(
        functools.partial(project_kernel, dim, size),
        grid=(count // rows,),
        in_specs=[
            pl.BlockSpec((rows, width), there),
            pl.BlockSpec(weight.shape, whole),
            pl.BlockSpec(head_gain.shape, whole),
            pl.BlockSpec((rows, dim), apart),
            pl.BlockSpec((rows, dim), apart),
            anywhere,
        ],
        out_specs=[
            pl.BlockSpec((rows, query_width), apart),
            pl.BlockSpec((rows, out_width), apart),
            pl.BlockSpec((rows, width), there),
            pl.BlockSpec((1, width), whole),
            pl.BlockSpec((1, width), whole),
            anywhere,
            anywhere,
        ],
        out_shape=[
            jax.ShapeDtypeStruct((count, query_width), jnp.bfloat16),
            jax.ShapeDtypeStruct((count, out_width), jnp.float32),
            jax.ShapeDtypeStruct((count, width), jnp.bfloat16),
            jax.ShapeDtypeStruct((1, width), jnp.float32),
            jax.ShapeDtypeStruct((1, width), jnp.float32),
            jax.ShapeDtypeStruct((3, *side.shape), side.dtype),
            jax.ShapeDtypeStruct((2 * count, pair_width), jnp.bfloat16),
        ],
        scratch_shapes=[pltpu.VMEM((count, pair_width), jnp.bfloat16)]
        + [pltpu.SemaphoreType.DMA((SPREAD_COUNT,))] * 2
        + [pltpu.SemaphoreType.DMA((size,))] * 3,
        compiler_params=pltpu.CompilerParams(
            collective_id=5, has_side_effects=True, vmem_limit_bytes=60 << 20
        ),
        cost_estimate=pl.CostEstimate(
            flops=4 * count * width * out_width, bytes_accessed=30_000_000, transcendentals=0
        ),
        name="project",
    )(x, weight, head_gain, cosine, sine, side)


def far_first(index):
    return jnp.where(index == 0, 3, jnp.where(index == 3, 0, index))


def back_terms_kernel(
    dim, query_grad_ref, pair_grad_ref, raw_ref, head_gain_ref, cosine_ref, sine_ref, normed_ref,
    behind_ref, one_ref, two_ref, *refs
):
    size, blk_size = lax.axis_size("heads"), lax.axis_size("blk")
    out_refs, refs = refs[:size], refs[size:]
    (
        own_grad_ref, gain_grad_ref, terms_ref, got_ref, out_grad_ref, early_ref, returned_ref, grads_ref,
        out_part_ref, out_got_ref, b_send, b_recv, s_send, s_recv, o_send, o_recv, n_send,
        n_recv,
    ) = refs
    step = pl.program_id(0)
    pairs, last = blk_size // 2, blk_size - 1
    head, blk = lax.axis_index("heads"), lax.axis_index("blk")
    core, pair = lax.rem(blk, 2), blk // 2
    rows = raw_ref.shape[0]
    block = returned_ref.shape[0]
    count = block // size
    tiles = count // rows
    out_rows = out_grad_ref.shape[0]
    chunk = far_first(jnp.minimum(step // tiles, size - 1))

    def copy(source, target, place, send, recv):
        return pltpu.make_async_remote_copy(
            src_ref=source,
            dst_ref=target,
            send_sem=send,
            recv_sem=recv,
            device_id=place,
            device_id_type=MESH,
        )

    def back(k):
        here = pl.ds(pl.multiple_of((head ^ k) * count, count), count)
        place = (head, jnp.maximum(blk - 1, 0))
        return copy(behind_ref.at[here], returned_ref.at[here], place, b_send.at[k], b_recv.at[k])

    def share(k):
        return copy(
            grads_ref.at[pl.ds(k * count, count)],
            got_ref.at[k - 1],
            (head ^ k, blk),
            s_send.at[k - 1],
            s_recv.at[k - 1],
        )

    near = [
        copy(
            ref.at[pl.ds(0, early_ref.shape[1])],
            early_ref.at[part],
            (head ^ (1 + part), blk),
            n_send.at[part],
            n_recv.at[part],
        )
        for part, ref in enumerate((one_ref, two_ref))
    ]

    def wide_of(value):
        return value.astype(jnp.float32)

    def out_copy(k, slot):
        other = lax.rem(pair + k, pairs)
        return copy(
            out_part_ref.at[other],
            out_got_ref.at[slot],
            (head, other * 2 + core),
            o_send.at[k],
            o_recv.at[slot],
        )

    @pl.when(step == 0)
    def _():
        gain_grad_ref[...] = jnp.zeros_like(gain_grad_ref)
        barrier = pltpu.get_barrier_semaphore()
        for k in range(1, size):
            pl.semaphore_signal(barrier, inc=1, device_id=(head ^ k, blk), device_id_type=MESH)

        def greet(k, carried):
            place = (head, lax.rem(pair + k, pairs) * 2 + core)
            pl.semaphore_signal(barrier, inc=1, device_id=place, device_id_type=MESH)
            return carried

        lax.fori_loop(1, pairs, greet, 0)

        @pl.when(blk < last)
        def _():
            pl.semaphore_signal(barrier, inc=1, device_id=(head, blk + 1), device_id_type=MESH)

        @pl.when(blk == 0)
        def _():
            pl.semaphore_wait(barrier, size + pairs - 2)

        @pl.when(blk > 0)
        def _():
            pl.semaphore_wait(barrier, size + pairs - 1)
            for k in (3, 1, 2, 0):
                back(k).start()

        @pl.when(blk == last)
        def _():
            returned_ref[...] = jnp.zeros_like(returned_ref)

        for sent in near:
            sent.start()

    for index, k in enumerate((3, 1, 2, 0)):

        @pl.when((step == index * tiles) & (blk < last))
        def _(k=k):
            back(k).wait_recv()

    @pl.when(step < size * tiles)
    def _():
        place = ((head ^ chunk) * tiles + lax.rem(step, tiles)) * rows
        returned = returned_ref[pl.ds(pl.multiple_of(place, rows), rows)]
        pair_grad = (pair_grad_ref[...] + wide_of(returned)).astype(jnp.bfloat16)
        half = pair_grad.shape[1] // 2
        grads = wide_of(jnp.concatenate([query_grad_ref[...], pair_grad[:, :half]], axis=1))
        grads = turn(grads, cosine_ref[...], -sine_ref[...], dim)
        values = raw_ref[:, : grads.shape[1]]
        inverse = lax.rsqrt(heads_apart(values, dim) + EPS)
        gain_grad_ref[...] += jnp.sum(grads * values * inverse, axis=0, keepdims=True)
        scaled = grads * head_gain_ref[...]
        moment = spread_mean(scaled * values, dim)
        values_grad = inverse * scaled - values * inverse * inverse * inverse * moment
        value = jnp.concatenate([values_grad.astype(jnp.bfloat16), pair_grad[:, half:]], axis=1)
        held = (chunk * tiles + lax.rem(step, tiles)) * rows
        grads_ref[pl.ds(pl.multiple_of(held, rows), rows)] = value

        @pl.when(chunk == 0)
        def _():
            own_grad_ref[...] = value

    for index, k in enumerate((3, 1, 2)):

        @pl.when(step == (index + 1) * tiles - 1)
        def _(k=k):
            share(k).start()

    @pl.when(step == size * tiles)
    def _():
        def out_sum(index, carried):
            here = pl.ds(pl.multiple_of(index * out_rows, out_rows), out_rows)
            total = wide_of(out_refs[0][here])
            for ref in out_refs[1:]:
                total += wide_of(ref[here])
            out_part_ref[index, :out_rows] = total.astype(jnp.bfloat16)
            return carried

        def start(k, carried):
            out_copy(k, pair).start()
            return carried

        lax.fori_loop(0, pairs, out_sum, 0)
        lax.fori_loop(1, pairs, start, 0)
        out_got_ref[pair] = out_part_ref[pair]

    @pl.when(step >= size * tiles)
    def _():
        terms_ref[...] = lax.dot_general(
            normed_ref[...],
            grads_ref[...],
            (((0,), (0,)), ((), ())),
            preferred_element_type=jnp.float32,
        ).astype(terms_ref.dtype)

    @pl.when(step == pl.num_programs(0) - 1)
    def _():
        def finish(k, carried):
            out_copy(k, lax.rem(pair + pairs - k, pairs)).wait()
            return carried

        lax.fori_loop(1, pairs, finish, 0)
        total = wide_of(out_got_ref[0, :out_rows])
        for b in range(1, pairs):
            total += wide_of(out_got_ref[b, :out_rows])
        out_grad_ref[...] = total
        for k in range(1, size):
            share(k).wait()
        for sent in near:
            sent.wait()

        @pl.when(blk > 0)
        def _():
            for k in range(size):
                back(k).wait_send()


def back_terms(
    query_grad, pair_sum, behind, raw, head_gain, cosine, sine, normed, near, outs, rows, columns
):
    count, query_width = query_grad.shape
    pair_width = pair_sum.shape[1]
    out_width = raw.shape[1]
    height = normed.shape[1]
    dim = cosine.shape[1]
    size, blk_size = lax.axis_size("heads"), lax.axis_size("blk")
    pairs = blk_size // 2
    tokens = count // size
    tiles = tokens // rows
    first = size * tiles
    out_rows, out_columns = outs[0].shape[0] // pairs, outs[0].shape[1]
    held_rows = -(-out_rows // 16) * 16

    def apart(i):
        i = jnp.minimum(i, first - 1)
        return ((lax.axis_index("heads") ^ far_first(i // tiles)) * tiles + i % tiles, 0)

    def after_behind(i):
        return (apart(i)[0] + count // rows, 0)

    def later(i):
        return jnp.maximum(i - first, 0)

    def whole(i):
        return (0, 0)

    sems = pltpu.SemaphoreType.DMA
    low = jnp.bfloat16
    return pl.pallas_call(
        functools.partial(back_terms_kernel, dim),
        grid=(first + height // columns,),
        in_specs=[
            pl.BlockSpec((rows, query_width), apart),
            pl.BlockSpec((rows, pair_width), after_behind),
            pl.BlockSpec((rows, out_width), apart),
            pl.BlockSpec(head_gain.shape, whole),
            pl.BlockSpec((rows, dim), apart),
            pl.BlockSpec((rows, dim), apart),
            pl.BlockSpec((count, columns), lambda i: (0, later(i))),
            pl.BlockSpec(memory_space=pl.ANY),
            pl.BlockSpec(memory_space=pl.ANY),
            pl.BlockSpec(memory_space=pl.ANY),
        ]
        + [pl.BlockSpec(out.shape, whole) for out in outs],
        out_specs=[
            pl.BlockSpec(
                (rows, out_width), lambda i: (jnp.clip(i - (size - 1) * tiles, 0, tiles - 1), 0)
            ),
            pl.BlockSpec(head_gain.shape, whole),
            pl.BlockSpec((columns, out_width), lambda i: (later(i), 0)),
            pl.BlockSpec(memory_space=pl.ANY),
            pl.BlockSpec((out_rows, out_columns), whole),
            pl.BlockSpec(memory_space=pl.ANY),
        ],
        out_shape=[
            jax.ShapeDtypeStruct((tokens, out_width), low),
            jax.ShapeDtypeStruct(head_gain.shape, jnp.float32),
            jax.ShapeDtypeStruct((height, out_width), low),
            jax.ShapeDtypeStruct((size - 1, tokens, out_width), low),
            jax.ShapeDtypeStruct((out_rows, out_columns), jnp.float32),
            jax.ShapeDtypeStruct((2, near[0].shape[0] // 2, near[0].shape[1]), low),
        ],
        scratch_shapes=[
            pltpu.VMEM(behind.shape, low),
            pltpu.VMEM((count, out_width), low),
            pltpu.VMEM((pairs, held_rows, out_columns), low),
            pltpu.VMEM((pairs, held_rows, out_columns), low),
            sems((size,)),
            sems((size,)),
            sems((size - 1,)),
            sems((size - 1,)),
            sems((pairs,)),
            sems((pairs,)),
            sems((2,)),
            sems((2,)),
        ],
        compiler_params=pltpu.CompilerParams(
            collective_id=9, has_side_effects=True, vmem_limit_bytes=60 << 20
        ),
        cost_estimate=pl.CostEstimate(
            flops=20_000_000_000, bytes_accessed=20_000_000, transcendentals=0
        ),
        name="back_terms",
    )(query_grad, pair_sum, raw, head_gain, cosine, sine, normed, behind, *near, *outs)


def join_kernel(
    x_ref, weight_ref, weights_ref, gain_ref, mine_ref, cot_ref, residual_ref,
    normed_ref, attended_ref, cot_one_ref, cot_two_ref, held_ref, local_sem, send_sem, recv_sem
):
    step = pl.program_id(0)
    head, blk = lax.axis_index("heads"), lax.axis_index("blk")
    rows = x_ref.shape[0]
    count = held_ref.shape[1] // 4
    tiles = count // rows

    def copy(source, target, k, index):
        return pltpu.make_async_remote_copy(
            src_ref=source,
            dst_ref=target,
            send_sem=send_sem.at[index],
            recv_sem=recv_sem.at[index],
            device_id=(head ^ k, blk),
            device_id_type=MESH,
        )

    upper, lower = pl.ds(0, 2 * count), pl.ds(2 * count, 2 * count)
    near = [copy(mine_ref, held_ref.at[k], k, k - 1) for k in (1, 2)]
    far = [
        copy(held_ref.at[1, upper], held_ref.at[3, upper], 2, 2),
        copy(held_ref.at[2, lower], held_ref.at[3, lower], 1, 3),
    ]
    half = count // 2
    cot_near = [
        copy(cot_ref.at[pl.ds(half, half)], cot_one_ref, 1, 4),
        copy(cot_ref.at[pl.ds(0, half)], cot_two_ref, 2, 5),
    ]
    own = pltpu.make_async_copy(mine_ref, held_ref.at[0], local_sem)

    @pl.when(step == 0)
    def _():
        own.start()
        greet_near(False)
        for first in near:
            first.start()
        for first, second in zip(near, far):
            first.wait_recv()
            second.start()
        own.wait()
        for second in far:
            second.wait_recv()
        for last in cot_near:
            last.start()

    chunk = step // tiles
    parts = []
    total = x_ref[...].astype(jnp.float32)
    for k in range(4):
        start = ((chunk ^ k) * tiles + lax.rem(step, tiles)) * rows
        part = held_ref[k, pl.ds(pl.multiple_of(start, rows), rows)]
        weight = weight_ref[...] if k == 0 else weights_ref[k - 1]
        total += jnp.dot(part, weight, preferred_element_type=jnp.float32)
        parts.append(part)
    residual_ref[...] = total
    normed = total * lax.rsqrt(jnp.mean(total * total, axis=-1, keepdims=True) + EPS)
    normed_ref[...] = (normed * gain_ref[...]).astype(jnp.bfloat16)

    @pl.when(chunk == 0)
    def _():
        attended_ref[...] = jnp.concatenate(parts, axis=1)

    @pl.when(step == pl.num_programs(0) - 1)
    def _():
        for first in near + far:
            first.wait_send()
        for last in cot_near:
            last.wait()


def join(x, mine, weight, weights, gain, cot, rows):
    count, width = x.shape
    tokens = count // 4
    columns = mine.shape[1]
    tiles = tokens // rows
    anywhere = pl.BlockSpec(memory_space=pl.ANY)

    def there(i):
        return (i, 0)

    def whole(i):
        return (0, 0)

    sems = pltpu.SemaphoreType.DMA
    return pl.pallas_call(
        join_kernel,
        grid=(count // rows,),
        in_specs=[
            pl.BlockSpec((rows, width), there),
            pl.BlockSpec(weight.shape, whole),
            pl.BlockSpec(weights.shape, lambda i: (0, 0, 0)),
            pl.BlockSpec((1, width), whole),
            anywhere,
            anywhere,
        ],
        out_specs=[
            pl.BlockSpec((rows, width), there),
            pl.BlockSpec((rows, width), there),
            pl.BlockSpec((rows, 4 * columns), lambda i: (jnp.minimum(i, tiles - 1), 0)),
            anywhere,
            anywhere,
        ],
        out_shape=[
            jax.ShapeDtypeStruct((count, width), jnp.float32),
            jax.ShapeDtypeStruct((count, width), jnp.bfloat16),
            jax.ShapeDtypeStruct((tokens, 4 * columns), jnp.bfloat16),
            jax.ShapeDtypeStruct((tokens // 2, width), jnp.bfloat16),
            jax.ShapeDtypeStruct((tokens // 2, width), jnp.bfloat16),
        ],
        scratch_shapes=[
            pltpu.VMEM((4, count, columns), jnp.bfloat16),
            sems,
            sems((6,)),
            sems((6,)),
        ],
        compiler_params=pltpu.CompilerParams(
            collective_id=6, has_side_effects=True, vmem_limit_bytes=60 << 20
        ),
        cost_estimate=pl.CostEstimate(
            flops=16 * count * width * columns, bytes_accessed=50_000_000, transcendentals=0
        ),
        name="join",
    )(x, weight, weights, gain, mine, cot)


def trade_kernel(in_ref, out_ref, send_sem, recv_sem):
    head, blk = lax.axis_index("heads"), lax.axis_index("blk")
    size = lax.axis_size("heads")
    units = out_ref.shape[2] // 2
    barrier = pltpu.get_barrier_semaphore()
    for k in range(1, size):
        pl.semaphore_signal(barrier, inc=1, device_id=(head ^ k, blk), device_id_type=MESH)
    pl.semaphore_wait(barrier, size - 1)

    def columns(part, owner):
        return pl.ds(pl.multiple_of((part * size + owner) * units, units), units)

    copies = [
        pltpu.make_async_remote_copy(
            src_ref=in_ref.at[:, columns(part, head ^ k)],
            dst_ref=out_ref.at[head, :, pl.ds(part * units, units)],
            send_sem=send_sem.at[2 * k - 2 + part],
            recv_sem=recv_sem.at[2 * k - 2 + part],
            device_id=(head ^ k, blk),
            device_id_type=MESH,
        )
        for k in range(1, size)
        for part in range(2)
    ]
    for copy in copies:
        copy.start()
    for part in range(2):
        out_ref[head, :, part * units : (part + 1) * units] = in_ref[:, columns(part, head)]
    for copy in copies:
        copy.wait()


def trade(weight):
    size = lax.axis_size("heads")
    depth, width = weight.shape
    vmem = pl.BlockSpec(memory_space=pltpu.VMEM)
    return pl.pallas_call(
        trade_kernel,
        out_shape=jax.ShapeDtypeStruct((size, depth, width // size), weight.dtype),
        in_specs=[vmem],
        out_specs=vmem,
        scratch_shapes=[pltpu.SemaphoreType.DMA((2 * size - 2,))] * 2,
        compiler_params=pltpu.CompilerParams(
            collective_id=8, has_side_effects=True, vmem_limit_bytes=60 << 20
        ),
        name="trade",
    )(weight)


def begin_kernel(
    x_ref, qkv_ref, cot_ref, position_ref, frequency_ref, x_out, qkv_out, cot_top, cot_bottom,
    cosine_ref, sine_ref, held_ref, local_sem, x_send, x_recv, q_send, q_recv, b_send, b_recv, c_send,
    c_recv
):
    head, blk = lax.axis_index("heads"), lax.axis_index("blk")
    size, blk_size = lax.axis_size("heads"), lax.axis_size("blk")
    pairs = blk_size // 2
    count, depth = x_ref.shape[0], qkv_ref.shape[1]
    half = count // 2
    barrier = pltpu.get_barrier_semaphore()
    for k in range(1, size):
        pl.semaphore_signal(barrier, inc=1, device_id=(head ^ k, blk), device_id_type=MESH)
    pl.semaphore_signal(barrier, inc=1, device_id=(head, blk ^ 1), device_id_type=MESH)

    def same_core(k):
        return lax.rem(blk + 2 * k, blk_size)

    def greet(k, carried):
        pl.semaphore_signal(barrier, inc=1, device_id=(head, same_core(k)), device_id_type=MESH)
        return carried

    lax.fori_loop(1, pairs, greet, 0)
    pl.semaphore_wait(barrier, size + pairs - 1)

    def send(source, target, k, send_sem, recv_sem):
        return pltpu.make_async_remote_copy(
            src_ref=source,
            dst_ref=target,
            send_sem=send_sem,
            recv_sem=recv_sem,
            device_id=(head ^ k, blk),
            device_id_type=MESH,
        )

    def rows_of(index):
        return pl.ds(pl.multiple_of(index * depth, depth), depth)

    rows = rows_of(blk)
    qkv_copies = [
        send(
            qkv_ref.at[head ^ k], qkv_out.at[head, rows], k, q_send.at[k - 1], q_recv.at[k - 1]
        )
        for k in range(1, size)
    ]
    near = [
        send(x_ref, x_out.at[pl.ds(k * count, count)], k, x_send.at[k - 1], x_recv.at[k - 1])
        for k in (1, 2)
    ]
    far = [
        send(
            x_out.at[pl.ds(count, half)],
            x_out.at[pl.ds(3 * count, half)],
            2,
            x_send.at[2],
            x_recv.at[2],
        ),
        send(
            x_out.at[pl.ds(2 * count + half, half)],
            x_out.at[pl.ds(3 * count + half, half)],
            1,
            x_send.at[3],
            x_recv.at[3],
        ),
    ]
    own = [
        pltpu.make_async_copy(qkv_ref.at[head], qkv_out.at[head, rows], local_sem.at[0]),
        pltpu.make_async_copy(x_ref, held_ref.at[0], local_sem.at[1]),
        pltpu.make_async_copy(cot_ref, held_ref.at[1], local_sem.at[2]),
    ]
    laid = [
        pltpu.make_async_copy(held_ref.at[0], x_out.at[pl.ds(0, count)], local_sem.at[3]),
        pltpu.make_async_copy(held_ref.at[1, pl.ds(0, half)], cot_top, local_sem.at[4]),
        pltpu.make_async_copy(held_ref.at[1, pl.ds(half, half)], cot_bottom, local_sem.at[5]),
    ]
    for copy in qkv_copies + near + own:
        copy.start()

    def along(k, source):
        return pltpu.make_async_remote_copy(
            src_ref=qkv_out.at[:, rows],
            dst_ref=qkv_out.at[:, rows_of(source)],
            send_sem=b_send.at[k],
            recv_sem=b_recv.at[k],
            device_id=(head, same_core(k)),
            device_id_type=MESH,
        )

    def behind(k):
        return lax.rem(blk + blk_size - 2 * k, blk_size)

    def across(k, core):
        source = behind(k) ^ core
        return pltpu.make_async_remote_copy(
            src_ref=qkv_out.at[:, rows_of(behind(k))],
            dst_ref=qkv_out.at[:, rows_of(source)],
            send_sem=c_send.at[k],
            recv_sem=c_recv.at[k],
            device_id=(head, blk ^ 1),
            device_id_type=MESH,
        )

    def start(k, carried):
        along(k, blk).start()
        return carried

    def pass_on(k, carried):
        along(k, behind(k)).wait_recv()
        across(k, 0).start()
        return carried

    def finish(k, carried):
        across(k, 0).wait_send()
        across(k, 1).wait_recv()
        return carried

    def sent(k, carried):
        along(k, blk).wait_send()
        return carried

    own[0].wait()
    for copy in qkv_copies:
        copy.wait_recv()
    lax.fori_loop(1, pairs, start, 0)
    across(0, 0).start()
    for copy in own[1:]:
        copy.wait()
    for copy in laid:
        copy.start()

    lanes = 512

    def table(index, carried):
        here = pl.ds(pl.multiple_of(index * lanes, lanes), lanes)
        angle = frequency_ref[...] * position_ref[:, here].astype(jnp.float32)
        cosine, sine = jnp.cos(angle).T, jnp.sin(angle).T
        cosine_ref[here] = jnp.concatenate([cosine, cosine], axis=1)
        sine_ref[here] = jnp.concatenate([-sine, sine], axis=1)
        return carried

    lax.fori_loop(0, position_ref.shape[1] // lanes, table, 0)
    lax.fori_loop(1, pairs, pass_on, 0)
    for first, second in zip(near, far):
        first.wait_recv()
        second.start()
    for copy in qkv_copies + near:
        copy.wait_send()
    for copy in far:
        copy.wait()
    for copy in laid:
        copy.wait()
    lax.fori_loop(1, pairs, sent, 0)
    lax.fori_loop(0, pairs, finish, 0)


def begin(x, qkv_parts, cot, positions, frequency):
    size, blk_size = lax.axis_size("heads"), lax.axis_size("blk")
    count, width = x.shape
    depth, joined = qkv_parts.shape[1:]
    anywhere = pl.BlockSpec(memory_space=pl.ANY)
    vmem = pl.BlockSpec(memory_space=pltpu.VMEM)
    table = jax.ShapeDtypeStruct((positions.shape[1], 2 * frequency.shape[0]), jnp.float32)
    sems = pltpu.SemaphoreType.DMA
    return pl.pallas_call(
        begin_kernel,
        out_shape=[
            jax.ShapeDtypeStruct((size * count, width), x.dtype),
            jax.ShapeDtypeStruct((size, blk_size * depth, joined), x.dtype),
            jax.ShapeDtypeStruct((count // 2, width), x.dtype),
            jax.ShapeDtypeStruct((count // 2, width), x.dtype),
            table,
            table,
        ],
        in_specs=[anywhere] * 3 + [vmem] * 2,
        out_specs=[anywhere] * 4 + [vmem] * 2,
        scratch_shapes=[
            pltpu.VMEM((2, count, width), x.dtype),
            sems((6,)),
            sems((4,)),
            sems((4,)),
            sems((size - 1,)),
            sems((size - 1,)),
            sems((blk_size // 2,)),
            sems((blk_size // 2,)),
            sems((blk_size // 2,)),
            sems((blk_size // 2,)),
        ],
        compiler_params=pltpu.CompilerParams(
            collective_id=1, has_side_effects=True, vmem_limit_bytes=60 << 20
        ),
        name="begin",
    )(x, qkv_parts, cot, positions, frequency)


def spread_copies(source_ref, target_ref, send_sem, recv_sem):
    head, blk = lax.axis_index("heads"), lax.axis_index("blk")
    rows = source_ref.shape[0] // 2
    quarter = rows // 2
    start = pl.multiple_of(lax.rem(blk, 2) * rows, rows)
    half = pl.ds(start, rows)
    first = source_ref.at[half, pl.ds(0, target_ref.shape[2])]
    count = [0]

    def copy(source, target, place):
        index = count[0]
        count[0] += 1
        return pltpu.make_async_remote_copy(
            src_ref=source,
            dst_ref=target,
            send_sem=send_sem.at[index],
            recv_sem=recv_sem.at[index],
            device_id=place,
            device_id_type=MESH,
        )

    near = [
        copy(first, target_ref.at[k - 1, half], (head ^ k, blk)) for k in (1, 2)
    ]
    upper = pl.ds(start, quarter)
    lower = pl.ds(pl.multiple_of(start + quarter, quarter), quarter)
    far = [
        copy(target_ref.at[0, upper], target_ref.at[2, upper], (head ^ 2, blk)),
        copy(target_ref.at[1, lower], target_ref.at[2, lower], (head ^ 1, blk)),
    ]
    other = [
        copy(target_ref.at[k, half], target_ref.at[k, half], (head, blk ^ 1)) for k in range(3)
    ]
    return near, far, other


def greet_near(partner):
    head, blk = lax.axis_index("heads"), lax.axis_index("blk")
    barrier = pltpu.get_barrier_semaphore()
    places = [(head ^ 1, blk), (head ^ 2, blk)] + ([(head, blk ^ 1)] if partner else [])
    for place in places:
        pl.semaphore_signal(barrier, inc=1, device_id=place, device_id_type=MESH)
    pl.semaphore_wait(barrier, len(places))


def spread_job(step, marks, source_ref, target_ref, send_sem, recv_sem, greet=True):
    near, far, other = spread_copies(source_ref, target_ref, send_sem, recv_sem)
    begin_at, far_at, other_at = marks

    @pl.when(step == begin_at)
    def _():
        if greet:
            greet_near(True)
        for copy in near:
            copy.start()

    @pl.when(step == far_at)
    def _():
        for k in range(2):
            near[k].wait_recv()
            far[k].start()
            other[k].start()

    @pl.when(step == other_at)
    def _():
        for copy in far:
            copy.wait_recv()
        other[2].start()

    def end():
        for copy in near + far:
            copy.wait_send()
        for copy in other:
            copy.wait()

    return end


SPREAD_COUNT = 7


def hidden_kernel(
    tiles, normed_ref, gate_ref, up_ref, down_ref, turned_ref, side_ref, cot_ref, one_top_ref,
    one_bottom_ref, two_top_ref, two_bottom_ref, hidden_ref, gate_grad_ref, up_grad_ref, in_sum_ref,
    cot_far_ref, spread_ref, held_ref, grads_ref, load_sem, far_send, far_recv, send_sem, recv_sem
):
    step, steps = pl.program_id(0), pl.num_programs(0)
    head, blk = lax.axis_index("heads"), lax.axis_index("blk")
    count = cot_ref.shape[0]
    half = count // 2
    rows, units = hidden_ref.shape
    far = [
        pltpu.make_async_remote_copy(
            src_ref=ref,
            dst_ref=held_ref.at[pl.ds(3 * count + part * half, half)],
            send_sem=far_send.at[part],
            recv_sem=far_recv.at[part],
            device_id=(head ^ k, blk),
            device_id_type=MESH,
        )
        for part, (ref, k) in enumerate(((one_top_ref, 2), (two_bottom_ref, 1)))
    ]
    keep = pltpu.make_async_copy(
        held_ref.at[pl.ds(3 * count, count)], cot_far_ref, load_sem.at[5]
    )
    near = ((one_top_ref, 2), (one_bottom_ref, 3), (two_top_ref, 4), (two_bottom_ref, 5))
    loads = [pltpu.make_async_copy(cot_ref, held_ref.at[pl.ds(0, count)], load_sem.at[0])] + [
        pltpu.make_async_copy(ref, held_ref.at[pl.ds(half * place, half)], load_sem.at[place - 1])
        for ref, place in near
    ]

    @pl.when(step == 0)
    def _():
        for load in loads:
            load.start()
        greet_near(True)
        for copy in far:
            copy.start()
        for load in loads[:3]:
            load.wait()

    @pl.when(step == tiles)
    def _():
        for load in loads[3:]:
            load.wait()
        for copy in far:
            copy.wait()
        keep.start()

    marks = (tiles, 2 * tiles, 2 * tiles + 4)
    end = spread_job(step, marks, side_ref, spread_ref, send_sem, recv_sem, False)

    @pl.when(step < 2 * tiles)
    def _():
        here = pl.ds(pl.multiple_of(step // tiles * rows, rows), rows)
        normed = normed_ref[...]
        gate = jnp.dot(normed, gate_ref[...], preferred_element_type=jnp.float32)
        upward = jnp.dot(normed, up_ref[...], preferred_element_type=jnp.float32)
        grad = lax.dot_general(
            held_ref[here], down_ref[...], ROWS_IN_BOTH, preferred_element_type=jnp.float32
        )
        sigmoid = jax.nn.sigmoid(gate)
        activated = gate * sigmoid
        hidden_ref[...] = (activated * upward).astype(jnp.bfloat16)
        gate_grad = (grad * upward * sigmoid * (1.0 + gate * (1.0 - sigmoid))).astype(jnp.bfloat16)
        up_grad = (grad * activated).astype(jnp.bfloat16)
        gate_grad_ref[...] = gate_grad
        up_grad_ref[...] = up_grad
        for part, value in enumerate((gate_grad, up_grad)):
            place = (part * tiles + lax.rem(step, tiles)) * units
            grads_ref[here, pl.ds(pl.multiple_of(place, units), units)] = value

    @pl.when(step >= 2 * tiles)
    def _():
        in_sum_ref[...] = lax.dot_general(
            turned_ref[...],
            grads_ref[...],
            (((0,), (0,)), ((), ())),
            preferred_element_type=jnp.float32,
        ).astype(jnp.bfloat16)

    @pl.when(step == steps - 1)
    def _():
        end()
        keep.wait()


def hidden_pass(normed, weight, cot, cot_near, down, side, side_columns, units):
    count, width = normed.shape
    total = down.shape[0]
    tiles = total // units
    rows = count // 2
    columns = width // 8

    def row(s):
        return jnp.minimum(s // tiles, 1)

    def column(s):
        return jnp.where(s < 2 * tiles, lax.rem(s, tiles), tiles - 1)

    out_spec = pl.BlockSpec((rows, units), lambda s: (row(s), column(s)))
    out_shape = jax.ShapeDtypeStruct((count, total), jnp.bfloat16)
    anywhere = pl.BlockSpec(memory_space=pl.ANY)
    sems = pltpu.SemaphoreType.DMA
    return pl.pallas_call(
        functools.partial(hidden_kernel, tiles),
        grid=(2 * tiles + 8,),
        in_specs=[
            pl.BlockSpec((rows, width), lambda s: (row(s), 0)),
            pl.BlockSpec((width, units), lambda s: (0, column(s))),
            pl.BlockSpec((width, units), lambda s: (0, tiles + column(s))),
            pl.BlockSpec((units, width), lambda s: (column(s), 0)),
            pl.BlockSpec((count, columns), lambda s: (0, jnp.maximum(s - 2 * tiles, 0))),
        ]
        + [anywhere] * 6,
        out_specs=[out_spec] * 3
        + [
            pl.BlockSpec((columns, 2 * total), lambda s: (jnp.maximum(s - 2 * tiles, 0), 0)),
            anywhere,
            anywhere,
        ],
        out_shape=[out_shape] * 3
        + [
            jax.ShapeDtypeStruct((width, 2 * total), jnp.bfloat16),
            jax.ShapeDtypeStruct(cot.shape, jnp.bfloat16),
            jax.ShapeDtypeStruct((3, side.shape[0], side_columns), side.dtype),
        ],
        scratch_shapes=[
            pltpu.VMEM((count, width), jnp.bfloat16),
            pltpu.VMEM((count, 2 * total), jnp.bfloat16),
            sems((6,)),
            sems((2,)),
            sems((2,)),
            sems((SPREAD_COUNT,)),
            sems((SPREAD_COUNT,)),
        ],
        compiler_params=pltpu.CompilerParams(
            collective_id=2, has_side_effects=True, vmem_limit_bytes=60 << 20
        ),
        cost_estimate=pl.CostEstimate(
            flops=10 * count * width * total, bytes_accessed=70_000_000, transcendentals=0
        ),
        name="hidden_pass",
    )(normed, weight, weight, down, normed, side, cot, *cot_near)


def in_order(step):
    value = 1
    for index, half in enumerate((6, 7, 2, 5, 4, 3, 0)):
        value = jnp.where(step == index, half, value)
    return value


def tail_kernel(
    gate_ref, up_ref, hidden_ref, turned_ref, in_hbm, down_hbm, cot_ref, one_top_ref, one_bottom_ref,
    two_top_ref, two_bottom_ref, cot_far_ref, down_sum_ref, *refs
):
    first_refs, (out_rest_ref, grad_ref, *refs) = refs[:4], refs[4:]
    (
        weight_ref, down_ref, first_ref, rest_ref, got_ref, last_ref, last_got_ref, weight_sem,
        send_sem, recv_sem,
    ) = refs
    step = pl.program_id(0)
    head, blk = lax.axis_index("heads"), lax.axis_index("blk")
    rows, total = hidden_ref.shape
    width = grad_ref.shape[1]
    load_in = pltpu.make_async_copy(in_hbm, weight_ref, weight_sem.at[0])
    load_down = pltpu.make_async_copy(down_hbm, down_ref, weight_sem.at[1])
    pieces = (
        (cot_ref, 0, 2),
        (one_top_ref, 2, 1),
        (one_bottom_ref, 3, 1),
        (two_top_ref, 4, 1),
        (two_bottom_ref, 5, 1),
        (cot_far_ref, 6, 2),
    )
    cot_loads = [
        pltpu.make_async_copy(
            ref,
            weight_ref.at[pl.ds(place * rows, length * rows), pl.ds(0, width)],
            weight_sem.at[2 + index],
        )
        for index, (ref, place, length) in enumerate(pieces)
    ]

    def copy(source, target, k, index):
        return pltpu.make_async_remote_copy(
            src_ref=source,
            dst_ref=target,
            send_sem=send_sem.at[index],
            recv_sem=recv_sem.at[index],
            device_id=(head ^ k, blk),
            device_id_type=MESH,
        )

    firsts = [
        copy(first_ref.at[index], got_ref.at[index], k, index)
        for index, k in enumerate((1, 2, 1, 2))
    ]
    lasts = [copy(last_ref.at[part], last_got_ref.at[part], 2 - part, 4 + part) for part in range(2)]

    def wide_of(block):
        return block.astype(jnp.float32)

    @pl.when(step == 0)
    def _():
        load_in.start()
        load_down.start()
        greet_near(False)
        load_in.wait()

    @pl.when(step < 8)
    def _():
        value = lax.dot_general(
            gate_ref[...], weight_ref[:, :total], ROWS_IN_BOTH, preferred_element_type=jnp.float32
        ) + lax.dot_general(
            up_ref[...], weight_ref[:, total:], ROWS_IN_BOTH, preferred_element_type=jnp.float32
        )
        value = value.astype(jnp.bfloat16)

        for index in range(4):

            @pl.when(step == index)
            def _(index=index):
                first_ref[index] = value
                firsts[index].start()

        @pl.when(step >= 4)
        def _():
            rest_ref[pl.ds(pl.multiple_of((step - 4) * rows, rows), rows)] = value

        @pl.when(step == 7)
        def _():
            load_down.wait()
            for load in cot_loads:
                load.start()

    @pl.when((step >= 8) & (step < 16))
    def _():
        terms = jnp.dot(
            hidden_ref[...], down_ref[...], preferred_element_type=jnp.float32
        ).astype(jnp.bfloat16)

        for index, ref in enumerate(first_refs):

            @pl.when(step == 8 + index)
            def _(ref=ref):
                ref[...] = terms

        @pl.when(step >= 12)
        def _():
            out_rest_ref[...] = terms

        @pl.when(step == 15)
        def _():
            for load in cot_loads:
                load.wait()

    @pl.when(step >= 16)
    def _():
        down_sum_ref[...] = lax.dot_general(
            turned_ref[...],
            weight_ref[:, :width],
            (((0,), (0,)), ((), ())),
            preferred_element_type=jnp.float32,
        ).astype(jnp.bfloat16)

    for part, when in enumerate((8, 9)):

        @pl.when(step == when)
        def _(part=part):
            firsts[part].wait_recv()
            last_ref[part] = (
                wide_of(rest_ref[part * rows : (part + 1) * rows]) + wide_of(got_ref[part])
            ).astype(jnp.bfloat16)
            lasts[part].start()

    @pl.when(step == pl.num_programs(0) - 1)
    def _():
        for part in range(2):
            firsts[2 + part].wait_recv()
            lasts[part].wait_recv()
            grad_ref[part * rows : (part + 1) * rows] = (
                wide_of(rest_ref[(2 + part) * rows : (3 + part) * rows])
                + wide_of(got_ref[2 + part])
                + wide_of(last_got_ref[part])
            )
        for sent in firsts + lasts:
            sent.wait_send()


def feed_tail(gate_grad, up_grad, hidden, weight, down, cots):
    count, total = hidden.shape
    width = weight.shape[0]
    rows = count // 8
    units = 256
    anywhere = pl.BlockSpec(memory_space=pl.ANY)

    def stage(i, first, last):
        return jnp.clip(i - first, 0, last)

    def first_rows(i):
        return (in_order(stage(i, 0, 7)), 0)

    low = jnp.bfloat16
    return pl.pallas_call(
        tail_kernel,
        grid=(16 + total // units,),
        in_specs=[
            pl.BlockSpec((rows, total), first_rows),
            pl.BlockSpec((rows, total), first_rows),
            pl.BlockSpec((rows, total), lambda i: (in_order(stage(i, 8, 7)), 0)),
            pl.BlockSpec((count, units), lambda i: (0, jnp.maximum(i - 16, 0))),
        ]
        + [anywhere] * 8,
        out_specs=[
            pl.BlockSpec((units, width), lambda i: (jnp.maximum(i - 16, 0), 0)),
            *[pl.BlockSpec((rows, width), lambda i: (0, 0), pipeline_mode=pl.Buffered(1))] * 4,
            pl.BlockSpec((rows, width), lambda i: (stage(i, 12, 3), 0)),
            pl.BlockSpec((2 * rows, width), lambda i: (0, 0), pipeline_mode=pl.Buffered(1)),
        ],
        out_shape=[
            jax.ShapeDtypeStruct((total, width), low),
            *[jax.ShapeDtypeStruct((rows, width), low)] * 4,
            jax.ShapeDtypeStruct((4 * rows, width), low),
            jax.ShapeDtypeStruct((2 * rows, width), jnp.float32),
        ],
        scratch_shapes=[
            pltpu.VMEM(weight.shape, low),
            pltpu.VMEM(down.shape, low),
            pltpu.VMEM((4, rows, width), low),
            pltpu.VMEM((4 * rows, width), low),
            pltpu.VMEM((4, rows, width), low),
            pltpu.VMEM((2, rows, width), low),
            pltpu.VMEM((2, rows, width), low),
            pltpu.SemaphoreType.DMA((8,)),
            pltpu.SemaphoreType.DMA((6,)),
            pltpu.SemaphoreType.DMA((6,)),
        ],
        compiler_params=pltpu.CompilerParams(
            collective_id=3, has_side_effects=True, vmem_limit_bytes=60 << 20
        ),
        cost_estimate=pl.CostEstimate(
            flops=8 * count * width * total, bytes_accessed=70_000_000, transcendentals=0
        ),
        name="feed_tail",
    )(gate_grad, up_grad, hidden, hidden, weight, down, *cots)


def residual_back_kernel(
    grad_sum_ref, residual_ref, cot_ref, gain_ref, attended_ref, weight_ref, weights_ref, grad_ref,
    gain_grad_ref, pieces_ref, *refs
):
    *out_refs, branch_ref, mine_ref, terms_ref, terms_got_ref, own_sem, send_sem, recv_sem = refs
    size = lax.axis_size("heads")
    core = lax.rem(lax.axis_index("blk"), 2)
    step = pl.program_id(0)
    last = pl.num_programs(0) - 1
    head, blk = lax.axis_index("heads"), lax.axis_index("blk")
    rows = cot_ref.shape[0]
    copies = [
        pltpu.make_async_remote_copy(
            src_ref=mine_ref.at[k],
            dst_ref=pieces_ref.at[k],
            send_sem=send_sem.at[k - 1],
            recv_sem=recv_sem.at[k - 1],
            device_id=(head ^ k, blk),
            device_id_type=MESH,
        )
        for k in range(1, size)
    ]
    keep = pltpu.make_async_copy(mine_ref.at[0], pieces_ref.at[0], own_sem)
    across = pltpu.make_async_remote_copy(
        src_ref=terms_ref.at[:, 1 - core],
        dst_ref=terms_got_ref,
        send_sem=send_sem.at[size - 1],
        recv_sem=recv_sem.at[size - 1],
        device_id=(head, blk ^ 1),
        device_id_type=MESH,
    )

    @pl.when(step == 0)
    def _():
        gain_grad_ref[...] = jnp.zeros_like(gain_grad_ref)
        barrier = pltpu.get_barrier_semaphore()
        for k in range(1, size):
            pl.semaphore_signal(barrier, inc=1, device_id=(head ^ k, blk), device_id_type=MESH)
        pl.semaphore_signal(barrier, inc=1, device_id=(head, blk ^ 1), device_id_type=MESH)
        pl.semaphore_wait(barrier, size)

    @pl.when(step < last)
    def _():
        here = pl.ds(pl.multiple_of(step * rows, rows), rows)
        gradient = grad_sum_ref[...]
        values = residual_ref[...]
        inverse = lax.rsqrt(jnp.mean(values * values, axis=-1, keepdims=True) + EPS)
        gain_grad_ref[...] += jnp.sum(gradient * values * inverse, axis=0, keepdims=True)
        scaled = gradient * gain_ref[...]
        moment = jnp.mean(scaled * values, axis=-1, keepdims=True)
        total = cot_ref[...].astype(jnp.float32) + (
            inverse * scaled - values * (inverse * inverse * inverse * moment)
        )
        grad_ref[...] = total
        branch = total.astype(jnp.bfloat16)
        branch_ref[here] = branch
        for k in range(size):
            weight = weight_ref[...] if k == 0 else weights_ref[k - 1]
            mine_ref[k, here] = lax.dot_general(
                branch, weight, ROWS_IN_BOTH, preferred_element_type=jnp.float32
            ).astype(jnp.bfloat16)

    @pl.when(step == last)
    def _():
        for copy in copies:
            copy.start()
        keep.start()
        columns = attended_ref.shape[1] // size
        pairs = terms_ref.shape[0] // size
        for k in range(size):
            terms = lax.dot_general(
                attended_ref[:, k * columns : (k + 1) * columns],
                branch_ref[...],
                (((0,), (0,)), ((), ())),
                preferred_element_type=jnp.float32,
            ).astype(jnp.bfloat16)
            terms_ref[k * pairs : (k + 1) * pairs] = terms.reshape(pairs, *terms_ref.shape[1:])
        across.start()
        across.wait()

        for k, out_ref in enumerate(out_refs):

            def add(index, carried, k=k, out_ref=out_ref):
                out_ref[index] = (
                    terms_ref[k * pairs + index, core].astype(jnp.float32)
                    + terms_got_ref[k * pairs + index].astype(jnp.float32)
                ).astype(jnp.bfloat16)
                return carried

            lax.fori_loop(0, pairs, add, 0)
        for copy in copies:
            copy.wait()
        keep.wait()


def residual_back(grad_sum, residual, cot, gain, attended, weight, weights, rows):
    count, width = cot.shape
    size, blk_size = lax.axis_size("heads"), lax.axis_size("blk")
    columns = weight.shape[0]
    pairs, held = size * blk_size // 2, columns // blk_size
    tiles = count // rows

    def there(i):
        return (jnp.minimum(i, tiles - 1), 0)

    def whole(i):
        return (0, 0)

    tile = pl.BlockSpec((rows, width), there)
    row = pl.BlockSpec((1, width), whole)
    pieces = (size, count, columns)
    return pl.pallas_call(
        residual_back_kernel,
        grid=(tiles + 1,),
        in_specs=[
            tile,
            tile,
            tile,
            row,
            pl.BlockSpec(attended.shape, whole),
            pl.BlockSpec(weight.shape, whole),
            pl.BlockSpec(weights.shape, lambda i: (0, 0, 0)),
        ],
        out_specs=[
            tile,
            row,
            pl.BlockSpec(memory_space=pl.ANY),
            *[pl.BlockSpec((pairs // size, held, width), lambda i: (0, 0, 0))] * size,
        ],
        out_shape=[
            jax.ShapeDtypeStruct((count, width), jnp.float32),
            jax.ShapeDtypeStruct((1, width), jnp.float32),
            jax.ShapeDtypeStruct(pieces, jnp.bfloat16),
            *[jax.ShapeDtypeStruct((pairs // size, held, width), jnp.bfloat16)] * size,
        ],
        scratch_shapes=[
            pltpu.VMEM((count, width), jnp.bfloat16),
            pltpu.VMEM(pieces, jnp.bfloat16),
            pltpu.VMEM((pairs, 2, held, width), jnp.bfloat16),
            pltpu.VMEM((pairs, held, width), jnp.bfloat16),
            pltpu.SemaphoreType.DMA,
            pltpu.SemaphoreType.DMA((size,)),
            pltpu.SemaphoreType.DMA((size,)),
        ],
        compiler_params=pltpu.CompilerParams(
            collective_id=4, has_side_effects=True, vmem_limit_bytes=60 << 20
        ),
        cost_estimate=pl.CostEstimate(
            flops=4 * count * width * columns * size, bytes_accessed=30_000_000, transcendentals=0
        ),
        name="residual_back",
    )(grad_sum, residual, cot, gain, attended, weight, weights)


def finish_kernel(
    query_width, dim, got_ref, qkv_ref, gain_ref, ffn_ref, head_ref, *refs
):
    size, blk_size = lax.axis_size("heads"), lax.axis_size("blk")
    sources, early_ref, refs = refs[:12], refs[12], refs[13:]
    (
        grad_ref, qkv_grad_ref, gains_ref, in_grad_ref, layer_ref, *refs
    ) = refs
    held, refs = refs[:12], refs[12:]
    weight_ref, weights_ref, x_ref, residual_grad_ref, sent_ref, in_ref, residual_ref, rest_ref = held[:8]
    (
        qkv_other_ref, qkv_sum_ref, qkv_z_ref, qkv_mine_ref, qkv_got_ref, gain_mine_ref,
        gain_away_ref, gain_other_ref, gain_sum_ref, gain_z_ref, gain_part_ref, gain_got_ref,
        in_got_ref, load_sem, c_send, c_recv, z_send, z_recv, h_send,
        h_recv, gc_send, gc_recv, gz_send, gz_recv, gh_send, gh_recv, i_send, i_recv, n_send, n_recv,
    ) = refs
    devices = size * blk_size
    pairs = blk_size // 2
    head, blk = lax.axis_index("heads"), lax.axis_index("blk")
    core, pair = lax.rem(blk, 2), blk // 2
    count, width = x_ref.shape
    depth = width // devices
    barrier = pltpu.get_barrier_semaphore()
    loads = [
        pltpu.make_async_copy(
            source.at[pl.ds(0, target.shape[0]), pl.ds(0, target.shape[1])]
            if index in (0, 4, 6)
            else source.at[pl.ds(target.shape[0], target.shape[0])]
            if index == 7
            else source,
            target,
            load_sem.at[index],
        )
        for index, (source, target) in enumerate(zip(sources, held))
        if index not in (8, 9)
    ]
    early = early_ref.shape[1]
    loads += [
        pltpu.make_async_copy(
            early_ref.at[part], held[8 + part].at[pl.ds(0, early)], load_sem.at[8 + part]
        )
        for part in range(2)
    ]
    for load in loads:
        load.start()

    def same_core(k):
        return (head, lax.rem(pair + k, pairs) * 2 + core)

    for k in range(1, size):
        pl.semaphore_signal(barrier, inc=1, device_id=(head ^ k, blk), device_id_type=MESH)
    pl.semaphore_signal(barrier, inc=1, device_id=(head, blk ^ 1), device_id_type=MESH)

    def greet(k, carried):
        pl.semaphore_signal(barrier, inc=1, device_id=same_core(k), device_id_type=MESH)
        return carried

    lax.fori_loop(1, pairs, greet, 0)
    pl.semaphore_wait(barrier, size + pairs - 1)

    def copy(source, target, place, send, recv):
        return pltpu.make_async_remote_copy(
            src_ref=source,
            dst_ref=target,
            send_sem=send,
            recv_sem=recv,
            device_id=place,
            device_id_type=MESH,
        )

    in_sends = [
        copy(
            sources[5].at[head ^ k],
            in_got_ref.at[k - 1],
            (head ^ k, blk),
            i_send.at[k - 1],
            i_recv.at[k - 1],
        )
        for k in range(1, size)
    ]
    near_sends = [
        copy(
            sources[8 + part].at[pl.ds(early, count // 2 - early)],
            held[8 + part].at[pl.ds(early, count // 2 - early)],
            (head ^ (1 + part), blk),
            n_send.at[part],
            n_recv.at[part],
        )
        for part in range(2)
    ]
    for sent in in_sends + near_sends:
        sent.start()

    across = copy(qkv_ref.at[:, 1 - core], qkv_other_ref, (head, blk ^ 1), c_send, c_recv)
    across.start()
    def wide_of(block):
        return block.astype(jnp.float32)

    across.wait_recv()

    def along(k, source_ref, target_ref, slot, send, recv):
        return copy(
            source_ref.at[:, lax.rem(pair + k, pairs)],
            target_ref.at[slot],
            same_core(k),
            send.at[k],
            recv.at[slot],
        )

    def around(source_ref, target_ref, slots, send, recv):
        return [
            copy(
                source_ref.at[head ^ k],
                target_ref.at[slots[k]],
                (head ^ k, blk),
                send.at[k - 1],
                recv.at[slots[k]],
            )
            for k in range(1, size)
        ]

    def start_along(source_ref, target_ref, send, recv):
        def start(k, carried):
            along(k, source_ref, target_ref, pair, send, recv).start()
            return carried

        lax.fori_loop(1, pairs, start, 0)
        target_ref[pair] = source_ref[:, pair]

    def finish_along(source_ref, target_ref, send, recv):
        def finish(k, carried):
            slot = lax.rem(pair + pairs - k, pairs)
            along(k, source_ref, target_ref, slot, send, recv).wait()
            return carried

        lax.fori_loop(1, pairs, finish, 0)
        total = wide_of(target_ref[0])
        for k in range(1, pairs):
            total += wide_of(target_ref[k])
        return total

    here, there = [head] * size, [head ^ k for k in range(size)]

    def start_around(source_ref, target_ref, send, recv):
        for sent in around(source_ref, target_ref, here, send, recv):
            sent.start()
        target_ref[head] = source_ref[head]

    def finish_around(source_ref, target_ref, send, recv):
        for sent in around(source_ref, target_ref, there, send, recv):
            sent.wait()

    def qkv_sum(index, carried):
        qkv_sum_ref[index // pairs, lax.rem(index, pairs)] = (
            wide_of(qkv_ref[index, core]) + wide_of(qkv_other_ref[index])
        ).astype(jnp.bfloat16)
        return carried

    lax.fori_loop(0, size * pairs, qkv_sum, 0)
    start_along(qkv_sum_ref, qkv_z_ref, z_send, z_recv)

    for load in loads[:5]:
        load.wait()
    rows = min(128, count)

    def tile(index, gain_sum):
        here = pl.ds(pl.multiple_of(index * rows, rows), rows)
        normed_grad = lax.dot_general(
            sent_ref[here], weight_ref[...], ROWS_IN_BOTH, preferred_element_type=jnp.float32
        )
        for k in range(1, size):
            normed_grad += lax.dot_general(
                got_ref[k - 1, here],
                weights_ref[k - 1],
                ROWS_IN_BOTH,
                preferred_element_type=jnp.float32,
            )
        values = wide_of(x_ref[here])
        inverse = lax.rsqrt(jnp.mean(values * values, axis=-1, keepdims=True) + EPS)
        scaled = normed_grad * gain_ref[...]
        moment = jnp.mean(scaled * values, axis=-1, keepdims=True)
        grad_ref[here] = (
            residual_grad_ref[here]
            + inverse * scaled
            - values * (inverse * inverse * inverse * moment)
        )
        return gain_sum + jnp.sum(normed_grad * values * inverse, axis=0, keepdims=True)

    attn_sum = lax.fori_loop(0, count // rows, tile, jnp.zeros((1, width), jnp.float32))

    def by_device(row, which):
        lanes = jnp.concatenate(
            [row[:, d * depth : (d + 1) * depth] for d in range(which, devices, 2)], axis=0
        )
        if depth < 64:
            lanes = jnp.concatenate(
                [lanes, jnp.zeros((devices // 2, 64 - depth), jnp.float32)], axis=1
            )
        return lanes

    head_row = head_ref[...]
    query_sum = head_row[:, :dim]
    for c in range(dim, query_width, dim):
        query_sum += head_row[:, c : c + dim]
    key_sum = head_row[:, query_width : query_width + dim]
    for c in range(query_width + dim, head_row.shape[1], dim):
        key_sum += head_row[:, c : c + dim]
    both = jnp.concatenate([query_sum, key_sum], axis=1)
    gains = [
        jnp.concatenate([by_device(attn_sum, c), by_device(ffn_ref[...], c)], axis=1)
        for c in range(2)
    ]
    for ref, mine in ((gain_mine_ref, 0), (gain_away_ref, 1)):
        ref[...] = jnp.zeros_like(ref)
        ref[:, 0, :] = jnp.where(core == mine, gains[0], gains[1])
        ref[:, 1, :] = jnp.broadcast_to(both, (devices // 2, 2 * dim))
    gain_across = copy(gain_away_ref, gain_other_ref, (head, blk ^ 1), gc_send, gc_recv)
    gain_across.start()
    gain_across.wait()
    gain_sum_ref[...] = (gain_mine_ref[...] + gain_other_ref[...]).reshape(gain_sum_ref.shape)
    start_along(gain_sum_ref, gain_z_ref, gz_send, gz_recv)

    qkv_mine_ref[...] = finish_along(qkv_sum_ref, qkv_z_ref, z_send, z_recv).astype(jnp.bfloat16)
    start_around(qkv_mine_ref, qkv_got_ref, h_send, h_recv)
    gain_part_ref[...] = finish_along(gain_sum_ref, gain_z_ref, gz_send, gz_recv)
    start_around(gain_part_ref, gain_got_ref, gh_send, gh_recv)

    loads[5].wait()
    units = in_ref.shape[2] // 2
    for k in range(size):
        if k:
            in_sends[k - 1].wait_recv()
        for part in range(2):
            columns = pl.ds(pl.multiple_of((part * size + (head ^ k)) * units, units), units)
            piece = slice(part * units, (part + 1) * units)
            got = in_got_ref[k - 1, :, piece] if k else in_ref[head, :, piece]
            in_grad_ref[:, columns] = wide_of(got)

    for load in loads[6:]:
        load.wait()
    for sent in near_sends:
        sent.wait_recv()
    half = count // 2
    for part in range(2):
        here = slice(part * half, (part + 1) * half)
        layer_ref[here] = (
            residual_ref[here] + wide_of(rest_ref[here]) + wide_of(held[8 + part][...])
            + wide_of(held[10 + part][...])
        ).astype(jnp.bfloat16)

    finish_around(qkv_mine_ref, qkv_got_ref, h_send, h_recv)
    sums = [wide_of(qkv_got_ref[h]) for h in range(size)]
    key_end = query_width + (sums[0].shape[1] - query_width) // 2
    qkv_grad_ref[...] = jnp.concatenate(
        [total[:, :query_width] for total in sums]
        + [total[:, query_width:key_end] for total in sums]
        + [total[:, key_end:] for total in sums],
        axis=1,
    )

    finish_around(gain_part_ref, gain_got_ref, gh_send, gh_recv)
    gains_ref[...] = jnp.sum(gain_got_ref[...], axis=0)
    across.wait_send()
    for sent in in_sends + near_sends:
        sent.wait_send()


def finish(
    sent, got, qkv_part, x, residual_grad, gain, ffn_sum, head_sum, weight, weights, in_part,
    residual, rest, terms, early, query_width, dim
):
    size, blk_size = lax.axis_size("heads"), lax.axis_size("blk")
    devices = size * blk_size
    pairs = blk_size // 2
    count, width = x.shape
    depth, joined = width // devices, sent.shape[1]
    units = in_part.shape[2]
    vmem = pl.BlockSpec(memory_space=pltpu.VMEM)
    anywhere = pl.BlockSpec(memory_space=pl.ANY)
    sems = pltpu.SemaphoreType.DMA
    low = jnp.bfloat16
    loaded = (weights, x, residual_grad)
    return pl.pallas_call(
        functools.partial(finish_kernel, query_width, dim),
        out_shape=[
            jax.ShapeDtypeStruct((count, width), jnp.float32),
            jax.ShapeDtypeStruct((depth, size * joined), jnp.float32),
            jax.ShapeDtypeStruct((8, 128), jnp.float32),
            jax.ShapeDtypeStruct((depth, size * units), jnp.float32),
            jax.ShapeDtypeStruct((count, width), low),
        ],
        in_specs=[vmem] * 5 + [anywhere] * 13,
        out_specs=[vmem] * 5,
        scratch_shapes=[pltpu.VMEM((width, joined), low)]
        + [pltpu.VMEM(array.shape, array.dtype) for array in loaded]
        + [pltpu.VMEM((count, joined), low), pltpu.VMEM(in_part.shape, low)]
        + [pltpu.VMEM((count, width), jnp.float32), pltpu.VMEM((count, width), low)]
        + [pltpu.VMEM((count // 2, width), low)] * 4
        + [
            pltpu.VMEM((size * pairs, depth, joined), low),
            pltpu.VMEM((size, pairs, depth, joined), low),
            pltpu.VMEM((pairs, size, depth, joined), low),
            pltpu.VMEM((size, depth, joined), low),
            pltpu.VMEM((size, depth, joined), low),
            pltpu.VMEM((devices // 2, 8, 128), jnp.float32),
            pltpu.VMEM((devices // 2, 8, 128), jnp.float32),
            pltpu.VMEM((devices // 2, 8, 128), jnp.float32),
            pltpu.VMEM((size, pairs, 8, 128), jnp.float32),
            pltpu.VMEM((pairs, size, 8, 128), jnp.float32),
            pltpu.VMEM((size, 8, 128), jnp.float32),
            pltpu.VMEM((size, 8, 128), jnp.float32),
            pltpu.VMEM((size - 1, depth, units), low),
            sems((12,)),
            sems,
            sems,
            sems((pairs,)),
            sems((pairs,)),
            sems((size - 1,)),
            sems((size,)),
            sems,
            sems,
            sems((pairs,)),
            sems((pairs,)),
            sems((size - 1,)),
            sems((size,)),
            sems((size - 1,)),
            sems((size - 1,)),
            sems((2,)),
            sems((2,)),
        ],
        compiler_params=pltpu.CompilerParams(
            collective_id=0, has_side_effects=True, vmem_limit_bytes=60 << 20
        ),
        name="finish",
    )(
        got, qkv_part.reshape(size * pairs, 2, depth, joined), gain, ffn_sum, head_sum,
        weight, *loaded, sent, in_part, residual, rest, *terms, early
    )


def permute(block, axis, k):
    return lax.ppermute(block, axis, [(i, i ^ k) for i in range(lax.axis_size(axis))])


def after(value, *done):
    return lax.optimization_barrier((value, *done))[0]


def pick(block, k, axis, dim):
    extent = block.shape[dim] // lax.axis_size(axis)
    return lax.dynamic_slice_in_dim(block, (lax.axis_index(axis) ^ k) * extent, extent, dim)


def wide(block):
    return block.astype(jnp.float32)


def local(
    inputs,
    positions,
    attn_gain,
    qkv_weight,
    q_gain,
    k_gain,
    out_weight,
    ffn_gain,
    ffn_in_weight,
    ffn_out_weight,
    cotangent,
):
    token_count, width = inputs.shape
    depth = qkv_weight.shape[0]
    head_dim = q_gain.shape[0]
    group_size = HEADS // KV_HEADS
    size = lax.axis_size("heads")
    blk_size = lax.axis_size("blk")
    query_all, key_all = HEADS * head_dim, KV_HEADS * head_dim
    query_width, key_width = query_all // size, key_all // size
    qkv_width = query_width + 2 * key_width
    block_len = token_count * size
    half = token_count // 2
    own = lax.axis_index("heads").astype(jnp.int32).reshape(1)

    qkv_parts = jnp.concatenate(
        [
            qkv_weight[:, :query_all].reshape(depth, size, query_width),
            qkv_weight[:, query_all : query_all + key_all].reshape(depth, size, key_width),
            qkv_weight[:, query_all + key_all :].reshape(depth, size, key_width),
            jnp.broadcast_to(attn_gain[:, None, None], (depth, size, 64)),
            jnp.broadcast_to(ffn_gain[:, None, None], (depth, size, 64)),
        ],
        axis=-1,
    ).transpose(1, 0, 2)
    out_group = lax.all_gather(out_weight, "blk", axis=0, tiled=True)
    in_rows = trade(ffn_in_weight)
    in_group = lax.all_gather(in_rows, "blk", axis=1, tiled=True).reshape(width, -1)

    half_dim = jnp.arange(head_dim // 2, dtype=jnp.float32)
    frequency = (ROPE_BASE ** (-2.0 * half_dim / head_dim))[:, None]
    inputs_blk, qkv_rows, cot_top, cot_bottom, cosine, sine = begin(
        after(inputs, in_rows), qkv_parts, cotangent, positions[None, :], frequency
    )
    qkv_rows = qkv_rows.reshape(width, -1)
    head_gain = jnp.concatenate(
        [jnp.tile(q_gain, HEADS // size), jnp.tile(k_gain, KV_HEADS // size)]
    ).astype(jnp.float32)[None, :]
    query_low, raw, normed, attn_scaling, ffn_scaling, out_peers, pair_all = project(
        inputs_blk, qkv_rows, head_gain, cosine, sine, out_group, size, query_width, 256
    )
    down_weight, pair_all = lax.optimization_barrier((ffn_out_weight, pair_all))
    down_group = lax.all_gather(down_weight, "blk", axis=0, tiled=True)
    query_rows, key_rows = token_count, 256
    low = block_len + jnp.arange(block_len, dtype=jnp.int32) - positions
    first = jnp.concatenate([low[::query_rows] // key_rows, own])
    low = low[None, :]
    attended_blk, logs = attend(query_low, pair_all, first, low, group_size, query_rows, key_rows)

    mine = jnp.concatenate([pick(attended_blk, k, "heads", 0) for k in range(size)], axis=0)
    one_top, two_bottom = permute(cot_top, "heads", 1), permute(cot_bottom, "heads", 2)
    mine, in_group = lax.optimization_barrier((mine, in_group))
    residual, ffn_normed, attended_own, one_bottom, two_top = join(
        inputs_blk, mine, out_group, out_peers, ffn_scaling, cotangent, 256
    )
    cot_near = (one_top, one_bottom, two_top, two_bottom)
    hidden, gate_grad, up_grad, in_sum, cot_far, qkv_peers = hidden_pass(
        ffn_normed, in_group, cotangent, cot_near, down_group, qkv_rows, qkv_width, 256
    )
    in_part = lax.psum_scatter(
        in_sum.reshape(size, blk_size * depth, -1), "blk", scatter_dimension=1, tiled=True
    )
    down_sum, one_far, two_far, one_near, two_near, out_rest, grad_sum = feed_tail(
        gate_grad, up_grad, hidden, in_group, down_group, (cotangent, *cot_near, cot_far)
    )
    down_part = lax.psum_scatter(down_sum, "blk", scatter_dimension=0, tiled=True)
    through_top, through_bottom = permute(one_far, "heads", 1), permute(two_far, "heads", 2)
    residual_grad, ffn_sum, grads, *out_slices = residual_back(
        grad_sum, residual, cotangent, ffn_scaling, attended_own, out_group, out_peers,
        min(128, half)
    )
    in_part, grads, through_top, through_bottom = lax.optimization_barrier(
        (in_part, grads, through_top, through_bottom)
    )
    top_send = (wide(out_rest[:half]) + wide(through_top)).astype(jnp.bfloat16)
    bottom_send = (wide(out_rest[half : 2 * half]) + wide(through_bottom)).astype(jnp.bfloat16)
    out_top_last = permute(top_send, "heads", 2)
    out_bottom_last = permute(bottom_send, "heads", 1)
    out_slices = [piece.reshape(-1, width) for piece in out_slices]
    out_slices = [out_slices[0]] + [permute(out_slices[k], "heads", k) for k in range(1, size)]
    query_grad, pair_sum, behind = attend_back(
        query_low, pair_all, first, low, grads, attended_blk, logs, group_size, query_rows, key_rows
    )
    pair_sum, out_top_last, out_bottom_last, *out_slices = lax.optimization_barrier(
        (pair_sum, out_top_last, out_bottom_last, *out_slices)
    )
    projected_grad, head_sum, qkv_part, got, out_grad, early = back_terms(
        query_grad, pair_sum, behind, raw, head_gain, cosine, sine, normed, (one_near, two_near),
        out_slices, 256, 512
    )
    input_grad, qkv_grad, gains, ffn_in_grad, layer_out = finish(
        projected_grad, got, qkv_part, inputs, residual_grad, attn_scaling, ffn_sum, head_sum,
        qkv_rows, qkv_peers, in_part, residual, out_rest,
        (one_near, two_near, out_top_last, out_bottom_last), early, query_width, head_dim
    )
    down_part, gains = lax.optimization_barrier((down_part, gains))
    ffn_out_grad = wide(down_part)
    return (
        layer_out,
        input_grad,
        gains[0, :depth],
        qkv_grad,
        gains[1, :head_dim],
        gains[1, head_dim : 2 * head_dim],
        out_grad,
        gains[0, 64 : 64 + depth],
        ffn_in_grad,
        ffn_out_grad,
    )


def solution(mesh):
    placed = (
        P(("blk", "heads"), None),
        P("blk"),
        P(("heads", "blk")),
        P(("heads", "blk"), None),
        P(),
        P(),
        P(("heads", "blk"), None),
        P(("heads", "blk")),
        P(("heads", "blk"), None),
        P(("heads", "blk"), None),
        P(("blk", "heads"), None),
    )
    return jax.shard_map(
        local,
        mesh=mesh,
        in_specs=placed,
        out_specs=(
            P(("blk", "heads"), None),
            P(("blk", "heads"), None),
            P(("heads", "blk")),
            P(("heads", "blk"), None),
            P(),
            P(),
            P(("heads", "blk"), None),
            P(("heads", "blk")),
            P(("heads", "blk"), None),
            P(("heads", "blk"), None),
        ),
        check_vma=False,
    )
```

```python
import functools

import jax
import jax.numpy as jnp
from jax import lax
from jax.experimental import pallas as pl
from jax.experimental.pallas import tpu as pltpu
from jax.sharding import PartitionSpec as P

HEADS = 16
KV_HEADS = 4


EPS = 1e-06
ROPE_BASE = 10000.0
NEG = -1e30
MESH = pl.DeviceIdType.MESH
ROWS_IN_BOTH = (((1,), (1,)), ((), ()))


def stack_heads(tile, heads, first):
    turned = tile.T
    dim = turned.shape[0] // heads
    wide = jnp.concatenate([turned[h * dim : (h + 1) * dim] for h in range(heads)], axis=1)
    zero = jnp.zeros_like(wide)
    return jnp.concatenate([wide, zero] if first else [zero, wide], axis=0)


def unstack_heads(wide, heads):
    count = wide.shape[1] // heads
    return jnp.concatenate([wide[:, h * count : (h + 1) * count] for h in range(heads)], axis=0).T


def scores_at(pair, query_ext, low, first_query, key_start, heads):
    scores = jnp.dot(pair, query_ext, preferred_element_type=jnp.float32)
    rows, columns = scores.shape
    shape = (rows, columns // heads)
    key = key_start + lax.broadcasted_iota(jnp.int32, shape, 0)
    query = first_query + lax.broadcasted_iota(jnp.int32, shape, 1)
    bias = jnp.where((key <= query) & (key >= low), 0.0, NEG)
    return scores + jnp.concatenate([bias] * heads, axis=1)


def transpose_into(pair_ref, turned_ref):
    for start in range(0, pair_ref.shape[0], 512):
        turned_ref[:, start : start + 512] = pair_ref[start : start + 512, :].T


def attend_kernel(
    heads, key_rows, scale, first_ref, query_ref, low_ref, pair_ref, out_ref, log_ref, turned_ref,
    mixed_ref, total_ref
):
    step = pl.program_id(0)
    query_rows = query_ref.shape[0]

    @pl.when(step == 0)
    def _():
        transpose_into(pair_ref, turned_ref)

    query_ext = stack_heads(query_ref[...] * jnp.bfloat16(scale), heads, True)
    low = low_ref[...]
    base = pair_ref.shape[0] // 2 + step * query_rows
    mixed_ref[...] = jnp.zeros_like(mixed_ref)
    total_ref[...] = jnp.zeros_like(total_ref)

    def tile(index, carried):
        start = pl.multiple_of(index * key_rows, key_rows)
        expo = jnp.exp(
            scores_at(pair_ref[pl.ds(start, key_rows), :], query_ext, low, base, start, heads)
        )
        total_ref[...] += jnp.sum(expo, axis=0, keepdims=True)
        mixed_ref[...] += jnp.dot(
            turned_ref[:, pl.ds(start, key_rows)],
            expo.astype(jnp.bfloat16),
            preferred_element_type=jnp.float32,
        )
        return carried

    lax.fori_loop(first_ref[step], (base + query_rows - 1) // key_rows + 1, tile, 0)
    total = total_ref[...]
    dim = pair_ref.shape[1] // 2
    out_ref[...] = unstack_heads(mixed_ref[dim:] / total, heads).astype(out_ref.dtype)
    log_ref[...] = jnp.log(total)[None]


def attend_back_kernel(
    heads, key_rows, scale, first_ref, query_ref, low_ref, pair_ref, out_ref, log_ref, *refs
):
    grads_ref, query_grad_ref, pair_grad_ref, behind_ref, turned_ref, sum_ref = refs
    step = pl.program_id(0)
    grad = grads_ref[first_ref[pl.num_programs(0)] ^ step]
    query_rows = query_ref.shape[0]
    dim = pair_ref.shape[1] // 2

    @pl.when(step == 0)
    def _():
        pair_grad_ref[...] = jnp.zeros_like(pair_grad_ref)
        transpose_into(pair_ref, turned_ref)

    query_ext = stack_heads(query_ref[...] * jnp.bfloat16(scale), heads, True)
    grad_ext = stack_heads(grad, heads, False)
    out_ext = stack_heads(out_ref[...], heads, False)
    inner = jnp.sum(
        grad_ext.astype(jnp.float32) * out_ext.astype(jnp.float32), axis=0, keepdims=True
    )
    log_sum = log_ref[0]
    low = low_ref[...]
    base = pair_ref.shape[0] // 2 + step * query_rows
    sum_ref[...] = jnp.zeros_like(sum_ref)

    def tile(index, carried):
        start = pl.multiple_of(index * key_rows, key_rows)
        pair = pair_ref[pl.ds(start, key_rows), :]
        probs = jnp.exp(scores_at(pair, query_ext, low, base, start, heads) - log_sum)
        probs_grad = jnp.dot(pair, grad_ext, preferred_element_type=jnp.float32)
        score_grad = (probs * (probs_grad - inner)).astype(jnp.bfloat16)
        sum_ref[...] += jnp.dot(
            turned_ref[:dim, pl.ds(start, key_rows)], score_grad, preferred_element_type=jnp.float32
        )
        pair_grad_ref[pl.ds(start, key_rows), :] += lax.dot_general(
            score_grad, query_ext, ROWS_IN_BOTH, preferred_element_type=jnp.float32
        ) + lax.dot_general(
            probs.astype(jnp.bfloat16), grad_ext, ROWS_IN_BOTH, preferred_element_type=jnp.float32
        )
        return carried

    lax.fori_loop(first_ref[step], (base + query_rows - 1) // key_rows + 1, tile, 0)
    query_grad_ref[...] = unstack_heads(sum_ref[...] * scale, heads).astype(query_grad_ref.dtype)

    @pl.when(step == pl.num_programs(0) - 1)
    def _():
        behind_ref[...] = pair_grad_ref[: behind_ref.shape[0]].astype(behind_ref.dtype)


def attention_specs(queries, pair, query_rows, heads):
    width = queries.shape[1]
    return (
        pl.BlockSpec((query_rows, width), lambda i, first: (i, 0)),
        pl.BlockSpec((1, query_rows), lambda i, first: (0, i)),
        pl.BlockSpec(pair.shape, lambda i, first: (0, 0)),
        pl.BlockSpec((1, 1, heads * query_rows), lambda i, first: (i, 0, 0)),
    )


def attend(queries, pair, first, low, heads, query_rows, key_rows):
    count, width = queries.shape
    tile, row, whole, logs = attention_specs(queries, pair, query_rows, heads)
    columns = heads * query_rows
    return pl.pallas_call(
        functools.partial(attend_kernel, heads, key_rows, (width // heads) ** -0.5),
        grid_spec=pltpu.PrefetchScalarGridSpec(
            num_scalar_prefetch=1,
            grid=(count // query_rows,),
            in_specs=[tile, row, whole],
            out_specs=[tile, logs],
            scratch_shapes=[
                pltpu.VMEM(pair.shape[::-1], jnp.bfloat16),
                pltpu.VMEM((pair.shape[1], columns), jnp.float32),
                pltpu.VMEM((1, columns), jnp.float32),
            ],
        ),
        out_shape=[
            jax.ShapeDtypeStruct((count, width), jnp.bfloat16),
            jax.ShapeDtypeStruct((count // query_rows, 1, columns), jnp.float32),
        ],
        compiler_params=pltpu.CompilerParams(vmem_limit_bytes=60 << 20),
        cost_estimate=pl.CostEstimate(
            flops=20_000_000_000, bytes_accessed=8_000_000, transcendentals=0
        ),
        name="attend",
    )(first, queries, low, pair)


def attend_back(queries, pair, first, low, grads, out, logs, heads, query_rows, key_rows):
    count, width = queries.shape
    tile, row, whole, log_spec = attention_specs(queries, pair, query_rows, heads)
    columns = heads * query_rows
    behind = (pair.shape[0] // 2, pair.shape[1])
    return pl.pallas_call(
        functools.partial(attend_back_kernel, heads, key_rows, (width // heads) ** -0.5),
        grid_spec=pltpu.PrefetchScalarGridSpec(
            num_scalar_prefetch=1,
            grid=(count // query_rows,),
            in_specs=[tile, row, whole, tile, log_spec]
            + [pl.BlockSpec(grads.shape, lambda i, first: (0, 0, 0))],
            out_specs=[tile, whole, pl.BlockSpec(behind, lambda i, first: (0, 0))],
            scratch_shapes=[
                pltpu.VMEM(pair.shape[::-1], jnp.bfloat16),
                pltpu.VMEM((pair.shape[1] // 2, columns), jnp.float32),
            ],
        ),
        out_shape=[
            jax.ShapeDtypeStruct((count, width), jnp.bfloat16),
            jax.ShapeDtypeStruct(pair.shape, jnp.float32),
            jax.ShapeDtypeStruct(behind, jnp.bfloat16),
        ],
        compiler_params=pltpu.CompilerParams(vmem_limit_bytes=60 << 20),
        cost_estimate=pl.CostEstimate(
            flops=40_000_000_000, bytes_accessed=12_000_000, transcendentals=0
        ),
        name="attend_back",
    )(first, queries, low, pair, out, logs, grads)


def heads_apart(wide, dim):
    rows = wide.shape[0]
    return jnp.concatenate(
        [
            jnp.broadcast_to(
                jnp.mean(jnp.square(wide[:, c : c + dim]), axis=-1, keepdims=True), (rows, dim)
            )
            for c in range(0, wide.shape[1], dim)
        ],
        axis=1,
    )


def spread_mean(wide, dim):
    rows = wide.shape[0]
    return jnp.concatenate(
        [
            jnp.broadcast_to(jnp.mean(wide[:, c : c + dim], axis=-1, keepdims=True), (rows, dim))
            for c in range(0, wide.shape[1], dim)
        ],
        axis=1,
    )


def turn(wide, cosine, sine, dim):
    count = wide.shape[1] // dim
    half = dim // 2
    swapped = jnp.concatenate(
        [
            wide[:, c + shift : c + shift + half]
            for c in range(0, wide.shape[1], dim)
            for shift in (half, 0)
        ],
        axis=1,
    )
    return wide * jnp.concatenate([cosine] * count, axis=1) + swapped * jnp.concatenate(
        [sine] * count, axis=1
    )


def project_kernel(
    dim, size, x_ref, weight_ref, head_gain_ref, cosine_ref, sine_ref, side_ref, query_ref, raw_ref,
    normed_ref, gain_ref, ffn_gain_ref, spread_ref, pair_ref, pair_held, send_sem, recv_sem,
    pair_sem, pair_send, pair_recv
):
    columns = raw_ref.shape[1]
    step, steps = pl.program_id(0), pl.num_programs(0)
    marks = (0, steps // 2, steps - 2)
    head, blk = lax.axis_index("heads"), lax.axis_index("blk")
    last = lax.axis_size("blk") - 1
    rows, block = x_ref.shape[0], pair_held.shape[0]
    tiles = block // size // rows

    @pl.when(step == 0)
    def _():
        barrier = pltpu.get_barrier_semaphore()
        for place in ((head ^ 1, blk), (head ^ 2, blk), (head, blk ^ 1)):
            pl.semaphore_signal(barrier, inc=1, device_id=place, device_id_type=MESH)

        @pl.when(blk > 0)
        def _():
            pl.semaphore_signal(barrier, inc=1, device_id=(head, blk - 1), device_id_type=MESH)

        @pl.when(blk < last)
        def _():
            pl.semaphore_wait(barrier, 4)

        @pl.when(blk == last)
        def _():
            pl.semaphore_wait(barrier, 3)

    end = spread_job(step, marks, side_ref, spread_ref, send_sem, recv_sem, False)

    def chunk_rows(k, first):
        return pl.ds(
            pl.multiple_of(first + (head ^ k) * (block // size), block // size), block // size
        )

    def keep(k):
        return pltpu.make_async_copy(
            pair_held.at[chunk_rows(k, 0)], pair_ref.at[chunk_rows(k, block)], pair_sem.at[k]
        )

    def pass_on(k):
        return pltpu.make_async_remote_copy(
            src_ref=pair_held.at[chunk_rows(k, 0)],
            dst_ref=pair_ref.at[chunk_rows(k, 0)],
            send_sem=pair_send.at[k],
            recv_sem=pair_recv.at[k],
            device_id=(head, jnp.minimum(blk + 1, last)),
            device_id_type=MESH,
        )

    @pl.when(pl.program_id(0) == 0)
    def _():
        gains = weight_ref[:, columns:].T.astype(jnp.float32)
        gain_ref[...] = gains[:1]
        ffn_gain_ref[...] = gains[64:65]

    values = x_ref[...].astype(jnp.float32)
    normed = values * lax.rsqrt(jnp.mean(values * values, axis=-1, keepdims=True) + EPS)
    normed = (normed * gain_ref[...]).astype(jnp.bfloat16)
    normed_ref[...] = normed
    raw = jnp.dot(normed, weight_ref[:, :columns], preferred_element_type=jnp.float32)
    raw_ref[...] = raw
    turned_width = raw.shape[1] - pair_held.shape[1] // 2
    heads = raw[:, :turned_width]
    heads = heads * lax.rsqrt(heads_apart(heads, dim) + EPS) * head_gain_ref[...]
    heads = turn(heads, cosine_ref[...], sine_ref[...], dim).astype(jnp.bfloat16)
    query_width = query_ref.shape[1]
    query_ref[...] = heads[:, :query_width]
    place = ((head ^ (step // tiles)) * tiles + lax.rem(step, tiles)) * rows
    pair_held[pl.ds(pl.multiple_of(place, rows), rows)] = jnp.concatenate(
        [heads[:, query_width:], raw[:, turned_width:].astype(jnp.bfloat16)], axis=1
    )
    for k in range(size):

        @pl.when(step == (k + 1) * tiles - 1)
        def _(k=k):
            keep(k).start()

            @pl.when(blk < last)
            def _():
                pass_on(k).start()

    @pl.when(step == steps - 1)
    def _():
        end()
        for k in range(size):
            keep(k).wait()

        @pl.when(blk < last)
        def _():
            for k in range(size):
                pass_on(k).wait_send()

        @pl.when(blk > 0)
        def _():
            for k in range(size):
                pass_on(k).wait_recv()


def project(x, weight, head_gain, cosine, sine, side, size, query_width, rows):
    count, width = x.shape
    out_width = weight.shape[1] - 128
    pair_width = out_width - query_width
    dim = cosine.shape[1]
    tiles = count // size // rows

    def apart(i):
        return ((lax.axis_index("heads") ^ (i // tiles)) * tiles + i % tiles, 0)

    def there(i):
        return (i, 0)

    def whole(i):
        return (0, 0)

    anywhere = pl.BlockSpec(memory_space=pl.ANY)

    return pl.pallas_call(
        functools.partial(project_kernel, dim, size),
        grid=(count // rows,),
        in_specs=[
            pl.BlockSpec((rows, width), there),
            pl.BlockSpec(weight.shape, whole),
            pl.BlockSpec(head_gain.shape, whole),
            pl.BlockSpec((rows, dim), apart),
            pl.BlockSpec((rows, dim), apart),
            anywhere,
        ],
        out_specs=[
            pl.BlockSpec((rows, query_width), apart),
            pl.BlockSpec((rows, out_width), apart),
            pl.BlockSpec((rows, width), there),
            pl.BlockSpec((1, width), whole),
            pl.BlockSpec((1, width), whole),
            anywhere,
            anywhere,
        ],
        out_shape=[
            jax.ShapeDtypeStruct((count, query_width), jnp.bfloat16),
            jax.ShapeDtypeStruct((count, out_width), jnp.float32),
            jax.ShapeDtypeStruct((count, width), jnp.bfloat16),
            jax.ShapeDtypeStruct((1, width), jnp.float32),
            jax.ShapeDtypeStruct((1, width), jnp.float32),
            jax.ShapeDtypeStruct((3, *side.shape), side.dtype),
            jax.ShapeDtypeStruct((2 * count, pair_width), jnp.bfloat16),
        ],
        scratch_shapes=[pltpu.VMEM((count, pair_width), jnp.bfloat16)]
        + [pltpu.SemaphoreType.DMA((SPREAD_COUNT,))] * 2
        + [pltpu.SemaphoreType.DMA((size,))] * 3,
        compiler_params=pltpu.CompilerParams(
            collective_id=5, has_side_effects=True, vmem_limit_bytes=60 << 20
        ),
        cost_estimate=pl.CostEstimate(
            flops=4 * count * width * out_width, bytes_accessed=30_000_000, transcendentals=0
        ),
        name="project",
    )(x, weight, head_gain, cosine, sine, side)


def far_first(index):
    return jnp.where(index == 0, 3, jnp.where(index == 3, 0, index))


def back_terms_kernel(
    dim, query_grad_ref, pair_grad_ref, raw_ref, head_gain_ref, cosine_ref, sine_ref, normed_ref,
    behind_ref, one_ref, two_ref, *refs
):
    size, blk_size = lax.axis_size("heads"), lax.axis_size("blk")
    out_refs, refs = refs[:size], refs[size:]
    (
        own_grad_ref, gain_grad_ref, terms_ref, got_ref, out_grad_ref, early_ref, returned_ref, grads_ref,
        out_part_ref, out_got_ref, b_send, b_recv, s_send, s_recv, o_send, o_recv, n_send,
        n_recv,
    ) = refs
    step = pl.program_id(0)
    pairs, last = blk_size // 2, blk_size - 1
    head, blk = lax.axis_index("heads"), lax.axis_index("blk")
    core, pair = lax.rem(blk, 2), blk // 2
    rows = raw_ref.shape[0]
    block = returned_ref.shape[0]
    count = block // size
    tiles = count // rows
    out_rows = out_grad_ref.shape[0]
    chunk = far_first(jnp.minimum(step // tiles, size - 1))

    def copy(source, target, place, send, recv):
        return pltpu.make_async_remote_copy(
            src_ref=source,
            dst_ref=target,
            send_sem=send,
            recv_sem=recv,
            device_id=place,
            device_id_type=MESH,
        )

    def back(k):
        here = pl.ds(pl.multiple_of((head ^ k) * count, count), count)
        place = (head, jnp.maximum(blk - 1, 0))
        return copy(behind_ref.at[here], returned_ref.at[here], place, b_send.at[k], b_recv.at[k])

    def share(k):
        return copy(
            grads_ref.at[pl.ds(k * count, count)],
            got_ref.at[k - 1],
            (head ^ k, blk),
            s_send.at[k - 1],
            s_recv.at[k - 1],
        )

    near = [
        copy(
            ref.at[pl.ds(0, early_ref.shape[1])],
            early_ref.at[part],
            (head ^ (1 + part), blk),
            n_send.at[part],
            n_recv.at[part],
        )
        for part, ref in enumerate((one_ref, two_ref))
    ]

    def wide_of(value):
        return value.astype(jnp.float32)

    def out_copy(k, slot):
        other = lax.rem(pair + k, pairs)
        return copy(
            out_part_ref.at[other],
            out_got_ref.at[slot],
            (head, other * 2 + core),
            o_send.at[k],
            o_recv.at[slot],
        )

    @pl.when(step == 0)
    def _():
        gain_grad_ref[...] = jnp.zeros_like(gain_grad_ref)
        barrier = pltpu.get_barrier_semaphore()
        for k in range(1, size):
            pl.semaphore_signal(barrier, inc=1, device_id=(head ^ k, blk), device_id_type=MESH)

        def greet(k, carried):
            place = (head, lax.rem(pair + k, pairs) * 2 + core)
            pl.semaphore_signal(barrier, inc=1, device_id=place, device_id_type=MESH)
            return carried

        lax.fori_loop(1, pairs, greet, 0)

        @pl.when(blk < last)
        def _():
            pl.semaphore_signal(barrier, inc=1, device_id=(head, blk + 1), device_id_type=MESH)

        @pl.when(blk == 0)
        def _():
            pl.semaphore_wait(barrier, size + pairs - 2)

        @pl.when(blk > 0)
        def _():
            pl.semaphore_wait(barrier, size + pairs - 1)
            for k in (3, 1, 2, 0):
                back(k).start()

        @pl.when(blk == last)
        def _():
            returned_ref[...] = jnp.zeros_like(returned_ref)

        for sent in near:
            sent.start()

    for index, k in enumerate((3, 1, 2, 0)):

        @pl.when((step == index * tiles) & (blk < last))
        def _(k=k):
            back(k).wait_recv()

    @pl.when(step < size * tiles)
    def _():
        place = ((head ^ chunk) * tiles + lax.rem(step, tiles)) * rows
        returned = returned_ref[pl.ds(pl.multiple_of(place, rows), rows)]
        pair_grad = (pair_grad_ref[...] + wide_of(returned)).astype(jnp.bfloat16)
        half = pair_grad.shape[1] // 2
        grads = wide_of(jnp.concatenate([query_grad_ref[...], pair_grad[:, :half]], axis=1))
        grads = turn(grads, cosine_ref[...], -sine_ref[...], dim)
        values = raw_ref[:, : grads.shape[1]]
        inverse = lax.rsqrt(heads_apart(values, dim) + EPS)
        gain_grad_ref[...] += jnp.sum(grads * values * inverse, axis=0, keepdims=True)
        scaled = grads * head_gain_ref[...]
        moment = spread_mean(scaled * values, dim)
        values_grad = inverse * scaled - values * inverse * inverse * inverse * moment
        value = jnp.concatenate([values_grad.astype(jnp.bfloat16), pair_grad[:, half:]], axis=1)
        held = (chunk * tiles + lax.rem(step, tiles)) * rows
        grads_ref[pl.ds(pl.multiple_of(held, rows), rows)] = value

        @pl.when(chunk == 0)
        def _():
            own_grad_ref[...] = value

    for index, k in enumerate((3, 1, 2)):

        @pl.when(step == (index + 1) * tiles - 1)
        def _(k=k):
            share(k).start()

    @pl.when(step == size * tiles)
    def _():
        def out_sum(index, carried):
            here = pl.ds(pl.multiple_of(index * out_rows, out_rows), out_rows)
            total = wide_of(out_refs[0][here])
            for ref in out_refs[1:]:
                total += wide_of(ref[here])
            out_part_ref[index, :out_rows] = total.astype(jnp.bfloat16)
            return carried

        def start(k, carried):
            out_copy(k, pair).start()
            return carried

        lax.fori_loop(0, pairs, out_sum, 0)
        lax.fori_loop(1, pairs, start, 0)
        out_got_ref[pair] = out_part_ref[pair]

    @pl.when(step >= size * tiles)
    def _():
        terms_ref[...] = lax.dot_general(
            normed_ref[...],
            grads_ref[...],
            (((0,), (0,)), ((), ())),
            preferred_element_type=jnp.float32,
        ).astype(terms_ref.dtype)

    @pl.when(step == pl.num_programs(0) - 1)
    def _():
        def finish(k, carried):
            out_copy(k, lax.rem(pair + pairs - k, pairs)).wait()
            return carried

        lax.fori_loop(1, pairs, finish, 0)
        total = wide_of(out_got_ref[0, :out_rows])
        for b in range(1, pairs):
            total += wide_of(out_got_ref[b, :out_rows])
        out_grad_ref[...] = total
        for k in range(1, size):
            share(k).wait()
        for sent in near:
            sent.wait()

        @pl.when(blk > 0)
        def _():
            for k in range(size):
                back(k).wait_send()


def back_terms(
    query_grad, pair_sum, behind, raw, head_gain, cosine, sine, normed, near, outs, rows, columns
):
    count, query_width = query_grad.shape
    pair_width = pair_sum.shape[1]
    out_width = raw.shape[1]
    height = normed.shape[1]
    dim = cosine.shape[1]
    size, blk_size = lax.axis_size("heads"), lax.axis_size("blk")
    pairs = blk_size // 2
    tokens = count // size
    tiles = tokens // rows
    first = size * tiles
    out_rows, out_columns = outs[0].shape[0] // pairs, outs[0].shape[1]
    held_rows = -(-out_rows // 16) * 16

    def apart(i):
        i = jnp.minimum(i, first - 1)
        return ((lax.axis_index("heads") ^ far_first(i // tiles)) * tiles + i % tiles, 0)

    def after_behind(i):
        return (apart(i)[0] + count // rows, 0)

    def later(i):
        return jnp.maximum(i - first, 0)

    def whole(i):
        return (0, 0)

    sems = pltpu.SemaphoreType.DMA
    low = jnp.bfloat16
    return pl.pallas_call(
        functools.partial(back_terms_kernel, dim),
        grid=(first + height // columns,),
        in_specs=[
            pl.BlockSpec((rows, query_width), apart),
            pl.BlockSpec((rows, pair_width), after_behind),
            pl.BlockSpec((rows, out_width), apart),
            pl.BlockSpec(head_gain.shape, whole),
            pl.BlockSpec((rows, dim), apart),
            pl.BlockSpec((rows, dim), apart),
            pl.BlockSpec((count, columns), lambda i: (0, later(i))),
            pl.BlockSpec(memory_space=pl.ANY),
            pl.BlockSpec(memory_space=pl.ANY),
            pl.BlockSpec(memory_space=pl.ANY),
        ]
        + [pl.BlockSpec(out.shape, whole) for out in outs],
        out_specs=[
            pl.BlockSpec(
                (rows, out_width), lambda i: (jnp.clip(i - (size - 1) * tiles, 0, tiles - 1), 0)
            ),
            pl.BlockSpec(head_gain.shape, whole),
            pl.BlockSpec((columns, out_width), lambda i: (later(i), 0)),
            pl.BlockSpec(memory_space=pl.ANY),
            pl.BlockSpec((out_rows, out_columns), whole),
            pl.BlockSpec(memory_space=pl.ANY),
        ],
        out_shape=[
            jax.ShapeDtypeStruct((tokens, out_width), low),
            jax.ShapeDtypeStruct(head_gain.shape, jnp.float32),
            jax.ShapeDtypeStruct((height, out_width), low),
            jax.ShapeDtypeStruct((size - 1, tokens, out_width), low),
            jax.ShapeDtypeStruct((out_rows, out_columns), jnp.float32),
            jax.ShapeDtypeStruct((2, near[0].shape[0] // 2, near[0].shape[1]), low),
        ],
        scratch_shapes=[
            pltpu.VMEM(behind.shape, low),
            pltpu.VMEM((count, out_width), low),
            pltpu.VMEM((pairs, held_rows, out_columns), low),
            pltpu.VMEM((pairs, held_rows, out_columns), low),
            sems((size,)),
            sems((size,)),
            sems((size - 1,)),
            sems((size - 1,)),
            sems((pairs,)),
            sems((pairs,)),
            sems((2,)),
            sems((2,)),
        ],
        compiler_params=pltpu.CompilerParams(
            collective_id=9, has_side_effects=True, vmem_limit_bytes=60 << 20
        ),
        cost_estimate=pl.CostEstimate(
            flops=20_000_000_000, bytes_accessed=20_000_000, transcendentals=0
        ),
        name="back_terms",
    )(query_grad, pair_sum, raw, head_gain, cosine, sine, normed, behind, *near, *outs)


def join_kernel(
    x_ref, weight_ref, weights_ref, gain_ref, mine_ref, cot_ref, residual_ref,
    normed_ref, attended_ref, cot_one_ref, cot_two_ref, held_ref, local_sem, send_sem, recv_sem
):
    step = pl.program_id(0)
    head, blk = lax.axis_index("heads"), lax.axis_index("blk")
    rows = x_ref.shape[0]
    count = held_ref.shape[1] // 4
    tiles = count // rows

    def copy(source, target, k, index):
        return pltpu.make_async_remote_copy(
            src_ref=source,
            dst_ref=target,
            send_sem=send_sem.at[index],
            recv_sem=recv_sem.at[index],
            device_id=(head ^ k, blk),
            device_id_type=MESH,
        )

    upper, lower = pl.ds(0, 2 * count), pl.ds(2 * count, 2 * count)
    near = [copy(mine_ref, held_ref.at[k], k, k - 1) for k in (1, 2)]
    far = [
        copy(held_ref.at[1, upper], held_ref.at[3, upper], 2, 2),
        copy(held_ref.at[2, lower], held_ref.at[3, lower], 1, 3),
    ]
    half = count // 2
    cot_near = [
        copy(cot_ref.at[pl.ds(half, half)], cot_one_ref, 1, 4),
        copy(cot_ref.at[pl.ds(0, half)], cot_two_ref, 2, 5),
    ]
    own = pltpu.make_async_copy(mine_ref, held_ref.at[0], local_sem)

    @pl.when(step == 0)
    def _():
        own.start()
        greet_near(False)
        for first in near:
            first.start()
        for first, second in zip(near, far):
            first.wait_recv()
            second.start()
        own.wait()
        for second in far:
            second.wait_recv()
        for last in cot_near:
            last.start()

    chunk = step // tiles
    parts = []
    total = x_ref[...].astype(jnp.float32)
    for k in range(4):
        start = ((chunk ^ k) * tiles + lax.rem(step, tiles)) * rows
        part = held_ref[k, pl.ds(pl.multiple_of(start, rows), rows)]
        weight = weight_ref[...] if k == 0 else weights_ref[k - 1]
        total += jnp.dot(part, weight, preferred_element_type=jnp.float32)
        parts.append(part)
    residual_ref[...] = total
    normed = total * lax.rsqrt(jnp.mean(total * total, axis=-1, keepdims=True) + EPS)
    normed_ref[...] = (normed * gain_ref[...]).astype(jnp.bfloat16)

    @pl.when(chunk == 0)
    def _():
        attended_ref[...] = jnp.concatenate(parts, axis=1)

    @pl.when(step == pl.num_programs(0) - 1)
    def _():
        for first in near + far:
            first.wait_send()
        for last in cot_near:
            last.wait()


def join(x, mine, weight, weights, gain, cot, rows):
    count, width = x.shape
    tokens = count // 4
    columns = mine.shape[1]
    tiles = tokens // rows
    anywhere = pl.BlockSpec(memory_space=pl.ANY)

    def there(i):
        return (i, 0)

    def whole(i):
        return (0, 0)

    sems = pltpu.SemaphoreType.DMA
    return pl.pallas_call(
        join_kernel,
        grid=(count // rows,),
        in_specs=[
            pl.BlockSpec((rows, width), there),
            pl.BlockSpec(weight.shape, whole),
            pl.BlockSpec(weights.shape, lambda i: (0, 0, 0)),
            pl.BlockSpec((1, width), whole),
            anywhere,
            anywhere,
        ],
        out_specs=[
            pl.BlockSpec((rows, width), there),
            pl.BlockSpec((rows, width), there),
            pl.BlockSpec((rows, 4 * columns), lambda i: (jnp.minimum(i, tiles - 1), 0)),
            anywhere,
            anywhere,
        ],
        out_shape=[
            jax.ShapeDtypeStruct((count, width), jnp.float32),
            jax.ShapeDtypeStruct((count, width), jnp.bfloat16),
            jax.ShapeDtypeStruct((tokens, 4 * columns), jnp.bfloat16),
            jax.ShapeDtypeStruct((tokens // 2, width), jnp.bfloat16),
            jax.ShapeDtypeStruct((tokens // 2, width), jnp.bfloat16),
        ],
        scratch_shapes=[
            pltpu.VMEM((4, count, columns), jnp.bfloat16),
            sems,
            sems((6,)),
            sems((6,)),
        ],
        compiler_params=pltpu.CompilerParams(
            collective_id=6, has_side_effects=True, vmem_limit_bytes=60 << 20
        ),
        cost_estimate=pl.CostEstimate(
            flops=16 * count * width * columns, bytes_accessed=50_000_000, transcendentals=0
        ),
        name="join",
    )(x, weight, weights, gain, mine, cot)


def trade_kernel(in_ref, out_ref, send_sem, recv_sem):
    head, blk = lax.axis_index("heads"), lax.axis_index("blk")
    size = lax.axis_size("heads")
    units = out_ref.shape[2] // 2
    barrier = pltpu.get_barrier_semaphore()
    for k in range(1, size):
        pl.semaphore_signal(barrier, inc=1, device_id=(head ^ k, blk), device_id_type=MESH)
    pl.semaphore_wait(barrier, size - 1)

    def columns(part, owner):
        return pl.ds(pl.multiple_of((part * size + owner) * units, units), units)

    copies = [
        pltpu.make_async_remote_copy(
            src_ref=in_ref.at[:, columns(part, head ^ k)],
            dst_ref=out_ref.at[head, :, pl.ds(part * units, units)],
            send_sem=send_sem.at[2 * k - 2 + part],
            recv_sem=recv_sem.at[2 * k - 2 + part],
            device_id=(head ^ k, blk),
            device_id_type=MESH,
        )
        for k in range(1, size)
        for part in range(2)
    ]
    for copy in copies:
        copy.start()
    for part in range(2):
        out_ref[head, :, part * units : (part + 1) * units] = in_ref[:, columns(part, head)]
    for copy in copies:
        copy.wait()


def trade(weight):
    size = lax.axis_size("heads")
    depth, width = weight.shape
    vmem = pl.BlockSpec(memory_space=pltpu.VMEM)
    return pl.pallas_call(
        trade_kernel,
        out_shape=jax.ShapeDtypeStruct((size, depth, width // size), weight.dtype),
        in_specs=[vmem],
        out_specs=vmem,
        scratch_shapes=[pltpu.SemaphoreType.DMA((2 * size - 2,))] * 2,
        compiler_params=pltpu.CompilerParams(
            collective_id=8, has_side_effects=True, vmem_limit_bytes=60 << 20
        ),
        name="trade",
    )(weight)


def begin_kernel(
    x_ref, qkv_ref, cot_ref, position_ref, frequency_ref, x_out, qkv_out, cot_top, cot_bottom,
    cosine_ref, sine_ref, held_ref, local_sem, x_send, x_recv, q_send, q_recv, b_send, b_recv, c_send,
    c_recv
):
    head, blk = lax.axis_index("heads"), lax.axis_index("blk")
    size, blk_size = lax.axis_size("heads"), lax.axis_size("blk")
    pairs = blk_size // 2
    count, depth = x_ref.shape[0], qkv_ref.shape[1]
    half = count // 2
    barrier = pltpu.get_barrier_semaphore()
    for k in range(1, size):
        pl.semaphore_signal(barrier, inc=1, device_id=(head ^ k, blk), device_id_type=MESH)
    pl.semaphore_signal(barrier, inc=1, device_id=(head, blk ^ 1), device_id_type=MESH)

    def same_core(k):
        return lax.rem(blk + 2 * k, blk_size)

    def greet(k, carried):
        pl.semaphore_signal(barrier, inc=1, device_id=(head, same_core(k)), device_id_type=MESH)
        return carried

    lax.fori_loop(1, pairs, greet, 0)
    pl.semaphore_wait(barrier, size + pairs - 1)

    def send(source, target, k, send_sem, recv_sem):
        return pltpu.make_async_remote_copy(
            src_ref=source,
            dst_ref=target,
            send_sem=send_sem,
            recv_sem=recv_sem,
            device_id=(head ^ k, blk),
            device_id_type=MESH,
        )

    def rows_of(index):
        return pl.ds(pl.multiple_of(index * depth, depth), depth)

    rows = rows_of(blk)
    qkv_copies = [
        send(
            qkv_ref.at[head ^ k], qkv_out.at[head, rows], k, q_send.at[k - 1], q_recv.at[k - 1]
        )
        for k in range(1, size)
    ]
    near = [
        send(x_ref, x_out.at[pl.ds(k * count, count)], k, x_send.at[k - 1], x_recv.at[k - 1])
        for k in (1, 2)
    ]
    far = [
        send(
            x_out.at[pl.ds(count, half)],
            x_out.at[pl.ds(3 * count, half)],
            2,
            x_send.at[2],
            x_recv.at[2],
        ),
        send(
            x_out.at[pl.ds(2 * count + half, half)],
            x_out.at[pl.ds(3 * count + half, half)],
            1,
            x_send.at[3],
            x_recv.at[3],
        ),
    ]
    own = [
        pltpu.make_async_copy(qkv_ref.at[head], qkv_out.at[head, rows], local_sem.at[0]),
        pltpu.make_async_copy(x_ref, held_ref.at[0], local_sem.at[1]),
        pltpu.make_async_copy(cot_ref, held_ref.at[1], local_sem.at[2]),
    ]
    laid = [
        pltpu.make_async_copy(held_ref.at[0], x_out.at[pl.ds(0, count)], local_sem.at[3]),
        pltpu.make_async_copy(held_ref.at[1, pl.ds(0, half)], cot_top, local_sem.at[4]),
        pltpu.make_async_copy(held_ref.at[1, pl.ds(half, half)], cot_bottom, local_sem.at[5]),
    ]
    for copy in qkv_copies + near + own:
        copy.start()

    def along(k, source):
        return pltpu.make_async_remote_copy(
            src_ref=qkv_out.at[:, rows],
            dst_ref=qkv_out.at[:, rows_of(source)],
            send_sem=b_send.at[k],
            recv_sem=b_recv.at[k],
            device_id=(head, same_core(k)),
            device_id_type=MESH,
        )

    def behind(k):
        return lax.rem(blk + blk_size - 2 * k, blk_size)

    def across(k, core):
        source = behind(k) ^ core
        return pltpu.make_async_remote_copy(
            src_ref=qkv_out.at[:, rows_of(behind(k))],
            dst_ref=qkv_out.at[:, rows_of(source)],
            send_sem=c_send.at[k],
            recv_sem=c_recv.at[k],
            device_id=(head, blk ^ 1),
            device_id_type=MESH,
        )

    def start(k, carried):
        along(k, blk).start()
        return carried

    def pass_on(k, carried):
        along(k, behind(k)).wait_recv()
        across(k, 0).start()
        return carried

    def finish(k, carried):
        across(k, 0).wait_send()
        across(k, 1).wait_recv()
        return carried

    def sent(k, carried):
        along(k, blk).wait_send()
        return carried

    own[0].wait()
    for copy in qkv_copies:
        copy.wait_recv()
    lax.fori_loop(1, pairs, start, 0)
    across(0, 0).start()
    for copy in own[1:]:
        copy.wait()
    for copy in laid:
        copy.start()

    lanes = 512

    def table(index, carried):
        here = pl.ds(pl.multiple_of(index * lanes, lanes), lanes)
        angle = frequency_ref[...] * position_ref[:, here].astype(jnp.float32)
        cosine, sine = jnp.cos(angle).T, jnp.sin(angle).T
        cosine_ref[here] = jnp.concatenate([cosine, cosine], axis=1)
        sine_ref[here] = jnp.concatenate([-sine, sine], axis=1)
        return carried

    lax.fori_loop(0, position_ref.shape[1] // lanes, table, 0)
    lax.fori_loop(1, pairs, pass_on, 0)
    for first, second in zip(near, far):
        first.wait_recv()
        second.start()
    for copy in qkv_copies + near:
        copy.wait_send()
    for copy in far:
        copy.wait()
    for copy in laid:
        copy.wait()
    lax.fori_loop(1, pairs, sent, 0)
    lax.fori_loop(0, pairs, finish, 0)


def begin(x, qkv_parts, cot, positions, frequency):
    size, blk_size = lax.axis_size("heads"), lax.axis_size("blk")
    count, width = x.shape
    depth, joined = qkv_parts.shape[1:]
    anywhere = pl.BlockSpec(memory_space=pl.ANY)
    vmem = pl.BlockSpec(memory_space=pltpu.VMEM)
    table = jax.ShapeDtypeStruct((positions.shape[1], 2 * frequency.shape[0]), jnp.float32)
    sems = pltpu.SemaphoreType.DMA
    return pl.pallas_call(
        begin_kernel,
        out_shape=[
            jax.ShapeDtypeStruct((size * count, width), x.dtype),
            jax.ShapeDtypeStruct((size, blk_size * depth, joined), x.dtype),
            jax.ShapeDtypeStruct((count // 2, width), x.dtype),
            jax.ShapeDtypeStruct((count // 2, width), x.dtype),
            table,
            table,
        ],
        in_specs=[anywhere] * 3 + [vmem] * 2,
        out_specs=[anywhere] * 4 + [vmem] * 2,
        scratch_shapes=[
            pltpu.VMEM((2, count, width), x.dtype),
            sems((6,)),
            sems((4,)),
            sems((4,)),
            sems((size - 1,)),
            sems((size - 1,)),
            sems((blk_size // 2,)),
            sems((blk_size // 2,)),
            sems((blk_size // 2,)),
            sems((blk_size // 2,)),
        ],
        compiler_params=pltpu.CompilerParams(
            collective_id=1, has_side_effects=True, vmem_limit_bytes=60 << 20
        ),
        name="begin",
    )(x, qkv_parts, cot, positions, frequency)


def spread_copies(source_ref, target_ref, send_sem, recv_sem):
    head, blk = lax.axis_index("heads"), lax.axis_index("blk")
    rows = source_ref.shape[0] // 2
    quarter = rows // 2
    start = pl.multiple_of(lax.rem(blk, 2) * rows, rows)
    half = pl.ds(start, rows)
    first = source_ref.at[half, pl.ds(0, target_ref.shape[2])]
    count = [0]

    def copy(source, target, place):
        index = count[0]
        count[0] += 1
        return pltpu.make_async_remote_copy(
            src_ref=source,
            dst_ref=target,
            send_sem=send_sem.at[index],
            recv_sem=recv_sem.at[index],
            device_id=place,
            device_id_type=MESH,
        )

    near = [
        copy(first, target_ref.at[k - 1, half], (head ^ k, blk)) for k in (1, 2)
    ]
    upper = pl.ds(start, quarter)
    lower = pl.ds(pl.multiple_of(start + quarter, quarter), quarter)
    far = [
        copy(target_ref.at[0, upper], target_ref.at[2, upper], (head ^ 2, blk)),
        copy(target_ref.at[1, lower], target_ref.at[2, lower], (head ^ 1, blk)),
    ]
    other = [
        copy(target_ref.at[k, half], target_ref.at[k, half], (head, blk ^ 1)) for k in range(3)
    ]
    return near, far, other


def greet_near(partner):
    head, blk = lax.axis_index("heads"), lax.axis_index("blk")
    barrier = pltpu.get_barrier_semaphore()
    places = [(head ^ 1, blk), (head ^ 2, blk)] + ([(head, blk ^ 1)] if partner else [])
    for place in places:
        pl.semaphore_signal(barrier, inc=1, device_id=place, device_id_type=MESH)
    pl.semaphore_wait(barrier, len(places))


def spread_job(step, marks, source_ref, target_ref, send_sem, recv_sem, greet=True):
    near, far, other = spread_copies(source_ref, target_ref, send_sem, recv_sem)
    begin_at, far_at, other_at = marks

    @pl.when(step == begin_at)
    def _():
        if greet:
            greet_near(True)
        for copy in near:
            copy.start()

    @pl.when(step == far_at)
    def _():
        for k in range(2):
            near[k].wait_recv()
            far[k].start()
            other[k].start()

    @pl.when(step == other_at)
    def _():
        for copy in far:
            copy.wait_recv()
        other[2].start()

    def end():
        for copy in near + far:
            copy.wait_send()
        for copy in other:
            copy.wait()

    return end


SPREAD_COUNT = 7


def hidden_kernel(
    tiles, normed_ref, gate_ref, up_ref, down_ref, turned_ref, side_ref, cot_ref, one_top_ref,
    one_bottom_ref, two_top_ref, two_bottom_ref, hidden_ref, gate_grad_ref, up_grad_ref, in_sum_ref,
    cot_far_ref, spread_ref, held_ref, grads_ref, load_sem, far_send, far_recv, send_sem, recv_sem
):
    step, steps = pl.program_id(0), pl.num_programs(0)
    head, blk = lax.axis_index("heads"), lax.axis_index("blk")
    count = cot_ref.shape[0]
    half = count // 2
    rows, units = hidden_ref.shape
    far = [
        pltpu.make_async_remote_copy(
            src_ref=ref,
            dst_ref=held_ref.at[pl.ds(3 * count + part * half, half)],
            send_sem=far_send.at[part],
            recv_sem=far_recv.at[part],
            device_id=(head ^ k, blk),
            device_id_type=MESH,
        )
        for part, (ref, k) in enumerate(((one_top_ref, 2), (two_bottom_ref, 1)))
    ]
    keep = pltpu.make_async_copy(
        held_ref.at[pl.ds(3 * count, count)], cot_far_ref, load_sem.at[5]
    )
    near = ((one_top_ref, 2), (one_bottom_ref, 3), (two_top_ref, 4), (two_bottom_ref, 5))
    loads = [pltpu.make_async_copy(cot_ref, held_ref.at[pl.ds(0, count)], load_sem.at[0])] + [
        pltpu.make_async_copy(ref, held_ref.at[pl.ds(half * place, half)], load_sem.at[place - 1])
        for ref, place in near
    ]

    @pl.when(step == 0)
    def _():
        for load in loads:
            load.start()
        greet_near(True)
        for copy in far:
            copy.start()
        for load in loads[:3]:
            load.wait()

    @pl.when(step == tiles)
    def _():
        for load in loads[3:]:
            load.wait()
        for copy in far:
            copy.wait()
        keep.start()

    marks = (tiles, 2 * tiles, 2 * tiles + 4)
    end = spread_job(step, marks, side_ref, spread_ref, send_sem, recv_sem, False)

    @pl.when(step < 2 * tiles)
    def _():
        here = pl.ds(pl.multiple_of(step // tiles * rows, rows), rows)
        normed = normed_ref[...]
        gate = jnp.dot(normed, gate_ref[...], preferred_element_type=jnp.float32)
        upward = jnp.dot(normed, up_ref[...], preferred_element_type=jnp.float32)
        grad = lax.dot_general(
            held_ref[here], down_ref[...], ROWS_IN_BOTH, preferred_element_type=jnp.float32
        )
        sigmoid = jax.nn.sigmoid(gate)
        activated = gate * sigmoid
        hidden_ref[...] = (activated * upward).astype(jnp.bfloat16)
        gate_grad = (grad * upward * sigmoid * (1.0 + gate * (1.0 - sigmoid))).astype(jnp.bfloat16)
        up_grad = (grad * activated).astype(jnp.bfloat16)
        gate_grad_ref[...] = gate_grad
        up_grad_ref[...] = up_grad
        for part, value in enumerate((gate_grad, up_grad)):
            place = (part * tiles + lax.rem(step, tiles)) * units
            grads_ref[here, pl.ds(pl.multiple_of(place, units), units)] = value

    @pl.when(step >= 2 * tiles)
    def _():
        in_sum_ref[...] = lax.dot_general(
            turned_ref[...],
            grads_ref[...],
            (((0,), (0,)), ((), ())),
            preferred_element_type=jnp.float32,
        ).astype(jnp.bfloat16)

    @pl.when(step == steps - 1)
    def _():
        end()
        keep.wait()


def hidden_pass(normed, weight, cot, cot_near, down, side, side_columns, units):
    count, width = normed.shape
    total = down.shape[0]
    tiles = total // units
    rows = count // 2
    columns = width // 8

    def row(s):
        return jnp.minimum(s // tiles, 1)

    def column(s):
        return jnp.where(s < 2 * tiles, lax.rem(s, tiles), tiles - 1)

    out_spec = pl.BlockSpec((rows, units), lambda s: (row(s), column(s)))
    out_shape = jax.ShapeDtypeStruct((count, total), jnp.bfloat16)
    anywhere = pl.BlockSpec(memory_space=pl.ANY)
    sems = pltpu.SemaphoreType.DMA
    return pl.pallas_call(
        functools.partial(hidden_kernel, tiles),
        grid=(2 * tiles + 8,),
        in_specs=[
            pl.BlockSpec((rows, width), lambda s: (row(s), 0)),
            pl.BlockSpec((width, units), lambda s: (0, column(s))),
            pl.BlockSpec((width, units), lambda s: (0, tiles + column(s))),
            pl.BlockSpec((units, width), lambda s: (column(s), 0)),
            pl.BlockSpec((count, columns), lambda s: (0, jnp.maximum(s - 2 * tiles, 0))),
        ]
        + [anywhere] * 6,
        out_specs=[out_spec] * 3
        + [
            pl.BlockSpec((columns, 2 * total), lambda s: (jnp.maximum(s - 2 * tiles, 0), 0)),
            anywhere,
            anywhere,
        ],
        out_shape=[out_shape] * 3
        + [
            jax.ShapeDtypeStruct((width, 2 * total), jnp.bfloat16),
            jax.ShapeDtypeStruct(cot.shape, jnp.bfloat16),
            jax.ShapeDtypeStruct((3, side.shape[0], side_columns), side.dtype),
        ],
        scratch_shapes=[
            pltpu.VMEM((count, width), jnp.bfloat16),
            pltpu.VMEM((count, 2 * total), jnp.bfloat16),
            sems((6,)),
            sems((2,)),
            sems((2,)),
            sems((SPREAD_COUNT,)),
            sems((SPREAD_COUNT,)),
        ],
        compiler_params=pltpu.CompilerParams(
            collective_id=2, has_side_effects=True, vmem_limit_bytes=60 << 20
        ),
        cost_estimate=pl.CostEstimate(
            flops=10 * count * width * total, bytes_accessed=70_000_000, transcendentals=0
        ),
        name="hidden_pass",
    )(normed, weight, weight, down, normed, side, cot, *cot_near)


def in_order(step):
    value = 1
    for index, half in enumerate((6, 7, 2, 5, 4, 3, 0)):
        value = jnp.where(step == index, half, value)
    return value


def tail_kernel(
    gate_ref, up_ref, hidden_ref, turned_ref, in_hbm, down_hbm, cot_ref, one_top_ref, one_bottom_ref,
    two_top_ref, two_bottom_ref, cot_far_ref, down_sum_ref, *refs
):
    first_refs, (out_rest_ref, grad_ref, *refs) = refs[:4], refs[4:]
    (
        weight_ref, down_ref, first_ref, rest_ref, got_ref, last_ref, last_got_ref, weight_sem,
        send_sem, recv_sem,
    ) = refs
    step = pl.program_id(0)
    head, blk = lax.axis_index("heads"), lax.axis_index("blk")
    rows, total = hidden_ref.shape
    width = grad_ref.shape[1]
    load_in = pltpu.make_async_copy(in_hbm, weight_ref, weight_sem.at[0])
    load_down = pltpu.make_async_copy(down_hbm, down_ref, weight_sem.at[1])
    pieces = (
        (cot_ref, 0, 2),
        (one_top_ref, 2, 1),
        (one_bottom_ref, 3, 1),
        (two_top_ref, 4, 1),
        (two_bottom_ref, 5, 1),
        (cot_far_ref, 6, 2),
    )
    cot_loads = [
        pltpu.make_async_copy(
            ref,
            weight_ref.at[pl.ds(place * rows, length * rows), pl.ds(0, width)],
            weight_sem.at[2 + index],
        )
        for index, (ref, place, length) in enumerate(pieces)
    ]

    def copy(source, target, k, index):
        return pltpu.make_async_remote_copy(
            src_ref=source,
            dst_ref=target,
            send_sem=send_sem.at[index],
            recv_sem=recv_sem.at[index],
            device_id=(head ^ k, blk),
            device_id_type=MESH,
        )

    firsts = [
        copy(first_ref.at[index], got_ref.at[index], k, index)
        for index, k in enumerate((1, 2, 1, 2))
    ]
    lasts = [copy(last_ref.at[part], last_got_ref.at[part], 2 - part, 4 + part) for part in range(2)]

    def wide_of(block):
        return block.astype(jnp.float32)

    @pl.when(step == 0)
    def _():
        load_in.start()
        load_down.start()
        greet_near(False)
        load_in.wait()

    @pl.when(step < 8)
    def _():
        value = lax.dot_general(
            gate_ref[...], weight_ref[:, :total], ROWS_IN_BOTH, preferred_element_type=jnp.float32
        ) + lax.dot_general(
            up_ref[...], weight_ref[:, total:], ROWS_IN_BOTH, preferred_element_type=jnp.float32
        )
        value = value.astype(jnp.bfloat16)

        for index in range(4):

            @pl.when(step == index)
            def _(index=index):
                first_ref[index] = value
                firsts[index].start()

        @pl.when(step >= 4)
        def _():
            rest_ref[pl.ds(pl.multiple_of((step - 4) * rows, rows), rows)] = value

        @pl.when(step == 7)
        def _():
            load_down.wait()
            for load in cot_loads:
                load.start()

    @pl.when((step >= 8) & (step < 16))
    def _():
        terms = jnp.dot(
            hidden_ref[...], down_ref[...], preferred_element_type=jnp.float32
        ).astype(jnp.bfloat16)

        for index, ref in enumerate(first_refs):

            @pl.when(step == 8 + index)
            def _(ref=ref):
                ref[...] = terms

        @pl.when(step >= 12)
        def _():
            out_rest_ref[...] = terms

        @pl.when(step == 15)
        def _():
            for load in cot_loads:
                load.wait()

    @pl.when(step >= 16)
    def _():
        down_sum_ref[...] = lax.dot_general(
            turned_ref[...],
            weight_ref[:, :width],
            (((0,), (0,)), ((), ())),
            preferred_element_type=jnp.float32,
        ).astype(jnp.bfloat16)

    for part, when in enumerate((8, 9)):

        @pl.when(step == when)
        def _(part=part):
            firsts[part].wait_recv()
            last_ref[part] = (
                wide_of(rest_ref[part * rows : (part + 1) * rows]) + wide_of(got_ref[part])
            ).astype(jnp.bfloat16)
            lasts[part].start()

    @pl.when(step == pl.num_programs(0) - 1)
    def _():
        for part in range(2):
            firsts[2 + part].wait_recv()
            lasts[part].wait_recv()
            grad_ref[part * rows : (part + 1) * rows] = (
                wide_of(rest_ref[(2 + part) * rows : (3 + part) * rows])
                + wide_of(got_ref[2 + part])
                + wide_of(last_got_ref[part])
            )
        for sent in firsts + lasts:
            sent.wait_send()


def feed_tail(gate_grad, up_grad, hidden, weight, down, cots):
    count, total = hidden.shape
    width = weight.shape[0]
    rows = count // 8
    units = 256
    anywhere = pl.BlockSpec(memory_space=pl.ANY)

    def stage(i, first, last):
        return jnp.clip(i - first, 0, last)

    def first_rows(i):
        return (in_order(stage(i, 0, 7)), 0)

    low = jnp.bfloat16
    return pl.pallas_call(
        tail_kernel,
        grid=(16 + total // units,),
        in_specs=[
            pl.BlockSpec((rows, total), first_rows),
            pl.BlockSpec((rows, total), first_rows),
            pl.BlockSpec((rows, total), lambda i: (in_order(stage(i, 8, 7)), 0)),
            pl.BlockSpec((count, units), lambda i: (0, jnp.maximum(i - 16, 0))),
        ]
        + [anywhere] * 8,
        out_specs=[
            pl.BlockSpec((units, width), lambda i: (jnp.maximum(i - 16, 0), 0)),
            *[pl.BlockSpec((rows, width), lambda i: (0, 0), pipeline_mode=pl.Buffered(1))] * 4,
            pl.BlockSpec((rows, width), lambda i: (stage(i, 12, 3), 0)),
            pl.BlockSpec((2 * rows, width), lambda i: (0, 0), pipeline_mode=pl.Buffered(1)),
        ],
        out_shape=[
            jax.ShapeDtypeStruct((total, width), low),
            *[jax.ShapeDtypeStruct((rows, width), low)] * 4,
            jax.ShapeDtypeStruct((4 * rows, width), low),
            jax.ShapeDtypeStruct((2 * rows, width), jnp.float32),
        ],
        scratch_shapes=[
            pltpu.VMEM(weight.shape, low),
            pltpu.VMEM(down.shape, low),
            pltpu.VMEM((4, rows, width), low),
            pltpu.VMEM((4 * rows, width), low),
            pltpu.VMEM((4, rows, width), low),
            pltpu.VMEM((2, rows, width), low),
            pltpu.VMEM((2, rows, width), low),
            pltpu.SemaphoreType.DMA((8,)),
            pltpu.SemaphoreType.DMA((6,)),
            pltpu.SemaphoreType.DMA((6,)),
        ],
        compiler_params=pltpu.CompilerParams(
            collective_id=3, has_side_effects=True, vmem_limit_bytes=60 << 20
        ),
        cost_estimate=pl.CostEstimate(
            flops=8 * count * width * total, bytes_accessed=70_000_000, transcendentals=0
        ),
        name="feed_tail",
    )(gate_grad, up_grad, hidden, hidden, weight, down, *cots)


def residual_back_kernel(
    grad_sum_ref, residual_ref, cot_ref, gain_ref, attended_ref, weight_ref, weights_ref, grad_ref,
    gain_grad_ref, pieces_ref, *refs
):
    *out_refs, branch_ref, mine_ref, terms_ref, terms_got_ref, own_sem, send_sem, recv_sem = refs
    size = lax.axis_size("heads")
    core = lax.rem(lax.axis_index("blk"), 2)
    step = pl.program_id(0)
    last = pl.num_programs(0) - 1
    head, blk = lax.axis_index("heads"), lax.axis_index("blk")
    rows = cot_ref.shape[0]
    copies = [
        pltpu.make_async_remote_copy(
            src_ref=mine_ref.at[k],
            dst_ref=pieces_ref.at[k],
            send_sem=send_sem.at[k - 1],
            recv_sem=recv_sem.at[k - 1],
            device_id=(head ^ k, blk),
            device_id_type=MESH,
        )
        for k in range(1, size)
    ]
    keep = pltpu.make_async_copy(mine_ref.at[0], pieces_ref.at[0], own_sem)
    across = pltpu.make_async_remote_copy(
        src_ref=terms_ref.at[:, 1 - core],
        dst_ref=terms_got_ref,
        send_sem=send_sem.at[size - 1],
        recv_sem=recv_sem.at[size - 1],
        device_id=(head, blk ^ 1),
        device_id_type=MESH,
    )

    @pl.when(step == 0)
    def _():
        gain_grad_ref[...] = jnp.zeros_like(gain_grad_ref)
        barrier = pltpu.get_barrier_semaphore()
        for k in range(1, size):
            pl.semaphore_signal(barrier, inc=1, device_id=(head ^ k, blk), device_id_type=MESH)
        pl.semaphore_signal(barrier, inc=1, device_id=(head, blk ^ 1), device_id_type=MESH)
        pl.semaphore_wait(barrier, size)

    @pl.when(step < last)
    def _():
        here = pl.ds(pl.multiple_of(step * rows, rows), rows)
        gradient = grad_sum_ref[...]
        values = residual_ref[...]
        inverse = lax.rsqrt(jnp.mean(values * values, axis=-1, keepdims=True) + EPS)
        gain_grad_ref[...] += jnp.sum(gradient * values * inverse, axis=0, keepdims=True)
        scaled = gradient * gain_ref[...]
        moment = jnp.mean(scaled * values, axis=-1, keepdims=True)
        total = cot_ref[...].astype(jnp.float32) + (
            inverse * scaled - values * (inverse * inverse * inverse * moment)
        )
        grad_ref[...] = total
        branch = total.astype(jnp.bfloat16)
        branch_ref[here] = branch
        for k in range(size):
            weight = weight_ref[...] if k == 0 else weights_ref[k - 1]
            mine_ref[k, here] = lax.dot_general(
                branch, weight, ROWS_IN_BOTH, preferred_element_type=jnp.float32
            ).astype(jnp.bfloat16)

    @pl.when(step == last)
    def _():
        for copy in copies:
            copy.start()
        keep.start()
        columns = attended_ref.shape[1] // size
        pairs = terms_ref.shape[0] // size
        for k in range(size):
            terms = lax.dot_general(
                attended_ref[:, k * columns : (k + 1) * columns],
                branch_ref[...],
                (((0,), (0,)), ((), ())),
                preferred_element_type=jnp.float32,
            ).astype(jnp.bfloat16)
            terms_ref[k * pairs : (k + 1) * pairs] = terms.reshape(pairs, *terms_ref.shape[1:])
        across.start()
        across.wait()

        for k, out_ref in enumerate(out_refs):

            def add(index, carried, k=k, out_ref=out_ref):
                out_ref[index] = (
                    terms_ref[k * pairs + index, core].astype(jnp.float32)
                    + terms_got_ref[k * pairs + index].astype(jnp.float32)
                ).astype(jnp.bfloat16)
                return carried

            lax.fori_loop(0, pairs, add, 0)
        for copy in copies:
            copy.wait()
        keep.wait()


def residual_back(grad_sum, residual, cot, gain, attended, weight, weights, rows):
    count, width = cot.shape
    size, blk_size = lax.axis_size("heads"), lax.axis_size("blk")
    columns = weight.shape[0]
    pairs, held = size * blk_size // 2, columns // blk_size
    tiles = count // rows

    def there(i):
        return (jnp.minimum(i, tiles - 1), 0)

    def whole(i):
        return (0, 0)

    tile = pl.BlockSpec((rows, width), there)
    row = pl.BlockSpec((1, width), whole)
    pieces = (size, count, columns)
    return pl.pallas_call(
        residual_back_kernel,
        grid=(tiles + 1,),
        in_specs=[
            tile,
            tile,
            tile,
            row,
            pl.BlockSpec(attended.shape, whole),
            pl.BlockSpec(weight.shape, whole),
            pl.BlockSpec(weights.shape, lambda i: (0, 0, 0)),
        ],
        out_specs=[
            tile,
            row,
            pl.BlockSpec(memory_space=pl.ANY),
            *[pl.BlockSpec((pairs // size, held, width), lambda i: (0, 0, 0))] * size,
        ],
        out_shape=[
            jax.ShapeDtypeStruct((count, width), jnp.float32),
            jax.ShapeDtypeStruct((1, width), jnp.float32),
            jax.ShapeDtypeStruct(pieces, jnp.bfloat16),
            *[jax.ShapeDtypeStruct((pairs // size, held, width), jnp.bfloat16)] * size,
        ],
        scratch_shapes=[
            pltpu.VMEM((count, width), jnp.bfloat16),
            pltpu.VMEM(pieces, jnp.bfloat16),
            pltpu.VMEM((pairs, 2, held, width), jnp.bfloat16),
            pltpu.VMEM((pairs, held, width), jnp.bfloat16),
            pltpu.SemaphoreType.DMA,
            pltpu.SemaphoreType.DMA((size,)),
            pltpu.SemaphoreType.DMA((size,)),
        ],
        compiler_params=pltpu.CompilerParams(
            collective_id=4, has_side_effects=True, vmem_limit_bytes=60 << 20
        ),
        cost_estimate=pl.CostEstimate(
            flops=4 * count * width * columns * size, bytes_accessed=30_000_000, transcendentals=0
        ),
        name="residual_back",
    )(grad_sum, residual, cot, gain, attended, weight, weights)


def finish_kernel(
    query_width, dim, got_ref, qkv_ref, gain_ref, ffn_ref, head_ref, *refs
):
    size, blk_size = lax.axis_size("heads"), lax.axis_size("blk")
    sources, early_ref, down_ref, refs = refs[:12], refs[12], refs[13], refs[14:]
    (
        grad_ref, qkv_grad_ref, gains_ref, in_grad_ref, layer_ref, down_grad_ref, *refs
    ) = refs
    held, down_held, refs = refs[:12], refs[12], refs[13:]
    weight_ref, weights_ref, x_ref, residual_grad_ref, sent_ref, in_ref, residual_ref, rest_ref = held[:8]
    (
        qkv_other_ref, qkv_sum_ref, qkv_z_ref, qkv_mine_ref, qkv_got_ref, gain_mine_ref,
        gain_away_ref, gain_other_ref, gain_sum_ref, gain_z_ref, gain_part_ref, gain_got_ref,
        in_got_ref, load_sem, c_send, c_recv, z_send, z_recv, h_send,
        h_recv, gc_send, gc_recv, gz_send, gz_recv, gh_send, gh_recv, i_send, i_recv, n_send, n_recv,
    ) = refs
    devices = size * blk_size
    pairs = blk_size // 2
    head, blk = lax.axis_index("heads"), lax.axis_index("blk")
    core, pair = lax.rem(blk, 2), blk // 2
    count, width = x_ref.shape
    depth = width // devices
    barrier = pltpu.get_barrier_semaphore()
    loads = [
        pltpu.make_async_copy(
            source.at[pl.ds(0, target.shape[0]), pl.ds(0, target.shape[1])]
            if index in (0, 4, 6)
            else source.at[pl.ds(target.shape[0], target.shape[0])]
            if index == 7
            else source,
            target,
            load_sem.at[index],
        )
        for index, (source, target) in enumerate(zip(sources, held))
        if index not in (8, 9)
    ]
    early = early_ref.shape[1]
    loads += [
        pltpu.make_async_copy(
            early_ref.at[part], held[8 + part].at[pl.ds(0, early)], load_sem.at[8 + part]
        )
        for part in range(2)
    ]
    loads.append(pltpu.make_async_copy(down_ref, down_held, load_sem.at[12]))
    for load in loads:
        load.start()

    def same_core(k):
        return (head, lax.rem(pair + k, pairs) * 2 + core)

    for k in range(1, size):
        pl.semaphore_signal(barrier, inc=1, device_id=(head ^ k, blk), device_id_type=MESH)
    pl.semaphore_signal(barrier, inc=1, device_id=(head, blk ^ 1), device_id_type=MESH)

    def greet(k, carried):
        pl.semaphore_signal(barrier, inc=1, device_id=same_core(k), device_id_type=MESH)
        return carried

    lax.fori_loop(1, pairs, greet, 0)
    pl.semaphore_wait(barrier, size + pairs - 1)

    def copy(source, target, place, send, recv):
        return pltpu.make_async_remote_copy(
            src_ref=source,
            dst_ref=target,
            send_sem=send,
            recv_sem=recv,
            device_id=place,
            device_id_type=MESH,
        )

    in_sends = [
        copy(
            sources[5].at[head ^ k],
            in_got_ref.at[k - 1],
            (head ^ k, blk),
            i_send.at[k - 1],
            i_recv.at[k - 1],
        )
        for k in range(1, size)
    ]
    near_sends = [
        copy(
            sources[8 + part].at[pl.ds(early, count // 2 - early)],
            held[8 + part].at[pl.ds(early, count // 2 - early)],
            (head ^ (1 + part), blk),
            n_send.at[part],
            n_recv.at[part],
        )
        for part in range(2)
    ]
    for sent in in_sends + near_sends:
        sent.start()

    across = copy(qkv_ref.at[:, 1 - core], qkv_other_ref, (head, blk ^ 1), c_send, c_recv)
    across.start()
    def wide_of(block):
        return block.astype(jnp.float32)

    across.wait_recv()

    def along(k, source_ref, target_ref, slot, send, recv):
        return copy(
            source_ref.at[:, lax.rem(pair + k, pairs)],
            target_ref.at[slot],
            same_core(k),
            send.at[k],
            recv.at[slot],
        )

    def around(source_ref, target_ref, slots, send, recv):
        return [
            copy(
                source_ref.at[head ^ k],
                target_ref.at[slots[k]],
                (head ^ k, blk),
                send.at[k - 1],
                recv.at[slots[k]],
            )
            for k in range(1, size)
        ]

    def start_along(source_ref, target_ref, send, recv):
        def start(k, carried):
            along(k, source_ref, target_ref, pair, send, recv).start()
            return carried

        lax.fori_loop(1, pairs, start, 0)
        target_ref[pair] = source_ref[:, pair]

    def finish_along(source_ref, target_ref, send, recv):
        def finish(k, carried):
            slot = lax.rem(pair + pairs - k, pairs)
            along(k, source_ref, target_ref, slot, send, recv).wait()
            return carried

        lax.fori_loop(1, pairs, finish, 0)
        total = wide_of(target_ref[0])
        for k in range(1, pairs):
            total += wide_of(target_ref[k])
        return total

    here, there = [head] * size, [head ^ k for k in range(size)]

    def start_around(source_ref, target_ref, send, recv):
        for sent in around(source_ref, target_ref, here, send, recv):
            sent.start()
        target_ref[head] = source_ref[head]

    def finish_around(source_ref, target_ref, send, recv):
        for sent in around(source_ref, target_ref, there, send, recv):
            sent.wait()

    def qkv_sum(index, carried):
        qkv_sum_ref[index // pairs, lax.rem(index, pairs)] = (
            wide_of(qkv_ref[index, core]) + wide_of(qkv_other_ref[index])
        ).astype(jnp.bfloat16)
        return carried

    lax.fori_loop(0, size * pairs, qkv_sum, 0)
    start_along(qkv_sum_ref, qkv_z_ref, z_send, z_recv)

    for load in loads[:5]:
        load.wait()
    rows = min(128, count)

    def tile(index, gain_sum):
        here = pl.ds(pl.multiple_of(index * rows, rows), rows)
        normed_grad = lax.dot_general(
            sent_ref[here], weight_ref[...], ROWS_IN_BOTH, preferred_element_type=jnp.float32
        )
        for k in range(1, size):
            normed_grad += lax.dot_general(
                got_ref[k - 1, here],
                weights_ref[k - 1],
                ROWS_IN_BOTH,
                preferred_element_type=jnp.float32,
            )
        values = wide_of(x_ref[here])
        inverse = lax.rsqrt(jnp.mean(values * values, axis=-1, keepdims=True) + EPS)
        scaled = normed_grad * gain_ref[...]
        moment = jnp.mean(scaled * values, axis=-1, keepdims=True)
        grad_ref[here] = (
            residual_grad_ref[here]
            + inverse * scaled
            - values * (inverse * inverse * inverse * moment)
        )
        return gain_sum + jnp.sum(normed_grad * values * inverse, axis=0, keepdims=True)

    attn_sum = lax.fori_loop(0, count // rows, tile, jnp.zeros((1, width), jnp.float32))

    def by_device(row, which):
        lanes = jnp.concatenate(
            [row[:, d * depth : (d + 1) * depth] for d in range(which, devices, 2)], axis=0
        )
        if depth < 64:
            lanes = jnp.concatenate(
                [lanes, jnp.zeros((devices // 2, 64 - depth), jnp.float32)], axis=1
            )
        return lanes

    head_row = head_ref[...]
    query_sum = head_row[:, :dim]
    for c in range(dim, query_width, dim):
        query_sum += head_row[:, c : c + dim]
    key_sum = head_row[:, query_width : query_width + dim]
    for c in range(query_width + dim, head_row.shape[1], dim):
        key_sum += head_row[:, c : c + dim]
    both = jnp.concatenate([query_sum, key_sum], axis=1)
    gains = [
        jnp.concatenate([by_device(attn_sum, c), by_device(ffn_ref[...], c)], axis=1)
        for c in range(2)
    ]
    for ref, mine in ((gain_mine_ref, 0), (gain_away_ref, 1)):
        ref[...] = jnp.zeros_like(ref)
        ref[:, 0, :] = jnp.where(core == mine, gains[0], gains[1])
        ref[:, 1, :] = jnp.broadcast_to(both, (devices // 2, 2 * dim))
    gain_across = copy(gain_away_ref, gain_other_ref, (head, blk ^ 1), gc_send, gc_recv)
    gain_across.start()
    gain_across.wait()
    gain_sum_ref[...] = (gain_mine_ref[...] + gain_other_ref[...]).reshape(gain_sum_ref.shape)
    start_along(gain_sum_ref, gain_z_ref, gz_send, gz_recv)

    qkv_mine_ref[...] = finish_along(qkv_sum_ref, qkv_z_ref, z_send, z_recv).astype(jnp.bfloat16)
    start_around(qkv_mine_ref, qkv_got_ref, h_send, h_recv)
    gain_part_ref[...] = finish_along(gain_sum_ref, gain_z_ref, gz_send, gz_recv)
    start_around(gain_part_ref, gain_got_ref, gh_send, gh_recv)

    loads[5].wait()
    units = in_ref.shape[2] // 2
    for k in range(size):
        if k:
            in_sends[k - 1].wait_recv()
        for part in range(2):
            columns = pl.ds(pl.multiple_of((part * size + (head ^ k)) * units, units), units)
            piece = slice(part * units, (part + 1) * units)
            got = in_got_ref[k - 1, :, piece] if k else in_ref[head, :, piece]
            in_grad_ref[:, columns] = wide_of(got)

    for load in loads[6:]:
        load.wait()
    down_grad_ref[...] = wide_of(down_held[...])
    for sent in near_sends:
        sent.wait_recv()
    half = count // 2
    for part in range(2):
        here = slice(part * half, (part + 1) * half)
        layer_ref[here] = (
            residual_ref[here] + wide_of(rest_ref[here]) + wide_of(held[8 + part][...])
            + wide_of(held[10 + part][...])
        ).astype(jnp.bfloat16)

    finish_around(qkv_mine_ref, qkv_got_ref, h_send, h_recv)
    sums = [wide_of(qkv_got_ref[h]) for h in range(size)]
    key_end = query_width + (sums[0].shape[1] - query_width) // 2
    qkv_grad_ref[...] = jnp.concatenate(
        [total[:, :query_width] for total in sums]
        + [total[:, query_width:key_end] for total in sums]
        + [total[:, key_end:] for total in sums],
        axis=1,
    )

    finish_around(gain_part_ref, gain_got_ref, gh_send, gh_recv)
    gains_ref[...] = jnp.sum(gain_got_ref[...], axis=0)
    across.wait_send()
    for sent in in_sends + near_sends:
        sent.wait_send()


def finish(
    sent, got, qkv_part, x, residual_grad, gain, ffn_sum, head_sum, weight, weights, in_part,
    residual, rest, terms, early, down_part, query_width, dim
):
    size, blk_size = lax.axis_size("heads"), lax.axis_size("blk")
    devices = size * blk_size
    pairs = blk_size // 2
    count, width = x.shape
    depth, joined = width // devices, sent.shape[1]
    units = in_part.shape[2]
    vmem = pl.BlockSpec(memory_space=pltpu.VMEM)
    anywhere = pl.BlockSpec(memory_space=pl.ANY)
    sems = pltpu.SemaphoreType.DMA
    low = jnp.bfloat16
    loaded = (weights, x, residual_grad)
    return pl.pallas_call(
        functools.partial(finish_kernel, query_width, dim),
        out_shape=[
            jax.ShapeDtypeStruct((count, width), jnp.float32),
            jax.ShapeDtypeStruct((depth, size * joined), jnp.float32),
            jax.ShapeDtypeStruct((8, 128), jnp.float32),
            jax.ShapeDtypeStruct((depth, size * units), jnp.float32),
            jax.ShapeDtypeStruct((count, width), low),
            jax.ShapeDtypeStruct(down_part.shape, jnp.float32),
        ],
        in_specs=[vmem] * 5 + [anywhere] * 14,
        out_specs=[vmem] * 6,
        scratch_shapes=[pltpu.VMEM((width, joined), low)]
        + [pltpu.VMEM(array.shape, array.dtype) for array in loaded]
        + [pltpu.VMEM((count, joined), low), pltpu.VMEM(in_part.shape, low)]
        + [pltpu.VMEM((count, width), jnp.float32), pltpu.VMEM((count, width), low)]
        + [pltpu.VMEM((count // 2, width), low)] * 4
        + [pltpu.VMEM(down_part.shape, low)]
        + [
            pltpu.VMEM((size * pairs, depth, joined), low),
            pltpu.VMEM((size, pairs, depth, joined), low),
            pltpu.VMEM((pairs, size, depth, joined), low),
            pltpu.VMEM((size, depth, joined), low),
            pltpu.VMEM((size, depth, joined), low),
            pltpu.VMEM((devices // 2, 8, 128), jnp.float32),
            pltpu.VMEM((devices // 2, 8, 128), jnp.float32),
            pltpu.VMEM((devices // 2, 8, 128), jnp.float32),
            pltpu.VMEM((size, pairs, 8, 128), jnp.float32),
            pltpu.VMEM((pairs, size, 8, 128), jnp.float32),
            pltpu.VMEM((size, 8, 128), jnp.float32),
            pltpu.VMEM((size, 8, 128), jnp.float32),
            pltpu.VMEM((size - 1, depth, units), low),
            sems((13,)),
            sems,
            sems,
            sems((pairs,)),
            sems((pairs,)),
            sems((size - 1,)),
            sems((size,)),
            sems,
            sems,
            sems((pairs,)),
            sems((pairs,)),
            sems((size - 1,)),
            sems((size,)),
            sems((size - 1,)),
            sems((size - 1,)),
            sems((2,)),
            sems((2,)),
        ],
        compiler_params=pltpu.CompilerParams(
            collective_id=0, has_side_effects=True, vmem_limit_bytes=60 << 20
        ),
        name="finish",
    )(
        got, qkv_part.reshape(size * pairs, 2, depth, joined), gain, ffn_sum, head_sum,
        weight, *loaded, sent, in_part, residual, rest, *terms, early, down_part
    )


def permute(block, axis, k):
    return lax.ppermute(block, axis, [(i, i ^ k) for i in range(lax.axis_size(axis))])


def after(value, *done):
    return lax.optimization_barrier((value, *done))[0]


def pick(block, k, axis, dim):
    extent = block.shape[dim] // lax.axis_size(axis)
    return lax.dynamic_slice_in_dim(block, (lax.axis_index(axis) ^ k) * extent, extent, dim)


def wide(block):
    return block.astype(jnp.float32)


def local(
    inputs,
    positions,
    attn_gain,
    qkv_weight,
    q_gain,
    k_gain,
    out_weight,
    ffn_gain,
    ffn_in_weight,
    ffn_out_weight,
    cotangent,
):
    token_count, width = inputs.shape
    depth = qkv_weight.shape[0]
    head_dim = q_gain.shape[0]
    group_size = HEADS // KV_HEADS
    size = lax.axis_size("heads")
    blk_size = lax.axis_size("blk")
    query_all, key_all = HEADS * head_dim, KV_HEADS * head_dim
    query_width, key_width = query_all // size, key_all // size
    qkv_width = query_width + 2 * key_width
    block_len = token_count * size
    half = token_count // 2
    own = lax.axis_index("heads").astype(jnp.int32).reshape(1)

    qkv_parts = jnp.concatenate(
        [
            qkv_weight[:, :query_all].reshape(depth, size, query_width),
            qkv_weight[:, query_all : query_all + key_all].reshape(depth, size, key_width),
            qkv_weight[:, query_all + key_all :].reshape(depth, size, key_width),
            jnp.broadcast_to(attn_gain[:, None, None], (depth, size, 64)),
            jnp.broadcast_to(ffn_gain[:, None, None], (depth, size, 64)),
        ],
        axis=-1,
    ).transpose(1, 0, 2)
    out_group = lax.all_gather(out_weight, "blk", axis=0, tiled=True)
    in_rows = trade(ffn_in_weight)
    in_group = lax.all_gather(in_rows, "blk", axis=1, tiled=True).reshape(width, -1)

    half_dim = jnp.arange(head_dim // 2, dtype=jnp.float32)
    frequency = (ROPE_BASE ** (-2.0 * half_dim / head_dim))[:, None]
    inputs_blk, qkv_rows, cot_top, cot_bottom, cosine, sine = begin(
        after(inputs, in_rows), qkv_parts, cotangent, positions[None, :], frequency
    )
    qkv_rows = qkv_rows.reshape(width, -1)
    head_gain = jnp.concatenate(
        [jnp.tile(q_gain, HEADS // size), jnp.tile(k_gain, KV_HEADS // size)]
    ).astype(jnp.float32)[None, :]
    query_low, raw, normed, attn_scaling, ffn_scaling, out_peers, pair_all = project(
        inputs_blk, qkv_rows, head_gain, cosine, sine, out_group, size, query_width, 256
    )
    down_weight, pair_all = lax.optimization_barrier((ffn_out_weight, pair_all))
    down_group = lax.all_gather(down_weight, "blk", axis=0, tiled=True)
    query_rows, key_rows = token_count, 256
    low = block_len + jnp.arange(block_len, dtype=jnp.int32) - positions
    first = jnp.concatenate([low[::query_rows] // key_rows, own])
    low = low[None, :]
    attended_blk, logs = attend(query_low, pair_all, first, low, group_size, query_rows, key_rows)

    mine = jnp.concatenate([pick(attended_blk, k, "heads", 0) for k in range(size)], axis=0)
    one_top, two_bottom = permute(cot_top, "heads", 1), permute(cot_bottom, "heads", 2)
    mine, in_group = lax.optimization_barrier((mine, in_group))
    residual, ffn_normed, attended_own, one_bottom, two_top = join(
        inputs_blk, mine, out_group, out_peers, ffn_scaling, cotangent, 256
    )
    cot_near = (one_top, one_bottom, two_top, two_bottom)
    hidden, gate_grad, up_grad, in_sum, cot_far, qkv_peers = hidden_pass(
        ffn_normed, in_group, cotangent, cot_near, down_group, qkv_rows, qkv_width, 256
    )
    in_part = lax.psum_scatter(
        in_sum.reshape(size, blk_size * depth, -1), "blk", scatter_dimension=1, tiled=True
    )
    down_sum, one_far, two_far, one_near, two_near, out_rest, grad_sum = feed_tail(
        gate_grad, up_grad, hidden, in_group, down_group, (cotangent, *cot_near, cot_far)
    )
    down_part = lax.psum_scatter(down_sum, "blk", scatter_dimension=0, tiled=True)
    through_top, through_bottom = permute(one_far, "heads", 1), permute(two_far, "heads", 2)
    residual_grad, ffn_sum, grads, *out_slices = residual_back(
        grad_sum, residual, cotangent, ffn_scaling, attended_own, out_group, out_peers,
        min(128, half)
    )
    in_part, grads, through_top, through_bottom = lax.optimization_barrier(
        (in_part, grads, through_top, through_bottom)
    )
    top_send = (wide(out_rest[:half]) + wide(through_top)).astype(jnp.bfloat16)
    bottom_send = (wide(out_rest[half : 2 * half]) + wide(through_bottom)).astype(jnp.bfloat16)
    out_top_last = permute(top_send, "heads", 2)
    out_bottom_last = permute(bottom_send, "heads", 1)
    out_slices = [piece.reshape(-1, width) for piece in out_slices]
    out_slices = [out_slices[0]] + [permute(out_slices[k], "heads", k) for k in range(1, size)]
    query_grad, pair_sum, behind = attend_back(
        query_low, pair_all, first, low, grads, attended_blk, logs, group_size, query_rows, key_rows
    )
    pair_sum, out_top_last, out_bottom_last, *out_slices = lax.optimization_barrier(
        (pair_sum, out_top_last, out_bottom_last, *out_slices)
    )
    projected_grad, head_sum, qkv_part, got, out_grad, early = back_terms(
        query_grad, pair_sum, behind, raw, head_gain, cosine, sine, normed, (one_near, two_near),
        out_slices, 256, 512
    )
    input_grad, qkv_grad, gains, ffn_in_grad, layer_out, ffn_out_grad = finish(
        projected_grad, got, qkv_part, inputs, residual_grad, attn_scaling, ffn_sum, head_sum,
        qkv_rows, qkv_peers, in_part, residual, out_rest,
        (one_near, two_near, out_top_last, out_bottom_last), early, down_part, query_width, head_dim
    )
    return (
        layer_out,
        input_grad,
        gains[0, :depth],
        qkv_grad,
        gains[1, :head_dim],
        gains[1, head_dim : 2 * head_dim],
        out_grad,
        gains[0, 64 : 64 + depth],
        ffn_in_grad,
        ffn_out_grad,
    )


def solution(mesh):
    placed = (
        P(("blk", "heads"), None),
        P("blk"),
        P(("heads", "blk")),
        P(("heads", "blk"), None),
        P(),
        P(),
        P(("heads", "blk"), None),
        P(("heads", "blk")),
        P(("heads", "blk"), None),
        P(("heads", "blk"), None),
        P(("blk", "heads"), None),
    )
    return jax.shard_map(
        local,
        mesh=mesh,
        in_specs=placed,
        out_specs=(
            P(("blk", "heads"), None),
            P(("blk", "heads"), None),
            P(("heads", "blk")),
            P(("heads", "blk"), None),
            P(),
            P(),
            P(("heads", "blk"), None),
            P(("heads", "blk")),
            P(("heads", "blk"), None),
            P(("heads", "blk"), None),
        ),
        check_vma=False,
    )
```
